32 devices in a mesh: row: 8 (over z, core), col: 4 (over y, x).
Axes of the slice: x: 2, y: 2, z: 4, core: 2. Of those that a mesh axis runs over, the one named last changes fastest.
Arguments:
- height: float32 [1024, 1024], P('row', 'col'), may hold values from 0.5 to 1.5
- noise: float32 [1024, 1024], P('row', 'col'), may hold values from -8 to 8
Outputs:
- solution_field: float32 [1024, 1024], P('row', 'col')
- residual: float32 [1024, 1024], P('row', 'col')
The draws below stay inside these ranges and needn't reach their ends.
All inputs are finite; a program needn't handle non-finite values.
Results may differ from the reference program's by a relative error of at most 0.0003.
Values sent between devices are 32-bit elements; how exact they have to be, the bound alone decides.
No kernel may reach another device: no remote copies, remote signals or barrier semaphores. Data moves between devices by JAX's collectives and lax.ppermute only.
A program may use at most 64 MiB of HBM per device.

```python
import jax
import jax.numpy as jnp
from jax import lax

SUB = 128
OV = 8
ITERS = 2
NR = 1024
NC = 1024


def draw_noise(key, part):
    key = jax.random.fold_in(key, 5)
    rough = jax.random.normal(key, (NR, NC), jnp.float32)
    return jnp.clip(rough, -6.0, 6.0)


def levels(stream_key, extent, split, least, high):
    level, own = 1.0, jax.random.fold_in(stream_key, 6)
    for position, blocks in split:
        draws = jnp.exp(jax.random.uniform(jax.random.fold_in(own, position), (blocks,), jnp.float32, least / len(split), high / len(split)))
        level = level * jnp.repeat(draws, extent[position] // blocks).reshape([-1 if axis == position else 1 for axis in range(len(extent))])
    return level


def setup_inputs(seed: int = 0) -> dict:
    keys = jax.random.split(jax.random.key(seed), 3)
    return {
        "height": jnp.clip(0.5 + 1.0 * jax.random.uniform(keys[0], (NR, NC), jnp.float32) ** levels(keys[0], (NR, NC), ((0, 8), (1, 4)), -0.2, 0.2), 0.5, 1.5),
        "noise": draw_noise(jax.random.fold_in(keys[2], 71), 0),
    }


damping = 2.0 ** (-28)
highest = lax.Precision.HIGHEST

def sine_basis(count):
    steps = jnp.arange(1, count + 1, dtype=jnp.float32)
    basis = jnp.sqrt(2.0 / (count + 1.0)) * jnp.sin(jnp.pi * steps[:, None] * steps[None, :] / (count + 1.0))
    eig = 2.0 - 2.0 * jnp.cos(jnp.pi * steps / (count + 1.0))
    return (basis, eig)

def minus_lap(field):
    padded = jnp.pad(field, 1)
    beside = padded[2:, 1:-1] + padded[:-2, 1:-1] + padded[1:-1, 2:] + padded[1:-1, :-2]
    return 4.0 * field - beside

def operate(field, mobility):
    return damping * field + minus_lap(mobility * minus_lap(field))

def eigen_solve(blocks, means, basis, eig):
    spectral = jnp.einsum('ba,nbc,cd->nad', basis, blocks, basis, precision=highest)
    spectral = spectral / (damping + means[:, None, None] * (eig[:, None] + eig[None, :]) ** 2)
    return jnp.einsum('ab,nbc,dc->nad', basis, spectral, basis, precision=highest)

def coarse_solve(sums):
    basis_r, eig_r = sine_basis(sums.shape[0])
    basis_c, eig_c = sine_basis(sums.shape[1])
    spectral = jnp.dot(jnp.dot(basis_r.T, sums, precision=highest), basis_c, precision=highest)
    scale = (eig_r[:, None] + eig_c[None, :]) / (SUB * SUB)
    spectral = spectral / (SUB * SUB * (damping + scale * scale))
    return jnp.dot(jnp.dot(basis_r, spectral, precision=highest), basis_c.T, precision=highest)

def schwarz(resid, mobility):
    total_r, total_c = resid.shape
    rows_n = total_r // SUB
    cols_n = total_c // SUB
    ext = SUB + 2 * OV
    basis, eig = sine_basis(ext)
    means_all = mobility.reshape(rows_n, SUB, cols_n, SUB).mean(axis=(1, 3))
    padded = jnp.pad(resid, OV)
    starts = jnp.arange(cols_n, dtype=jnp.int32) * SUB

    def one_row(acc, index):
        first = index.astype(jnp.int32) * SUB
        strip = lax.dynamic_slice_in_dim(padded, first, ext, 0)
        blocks = jax.vmap(lambda begin: lax.dynamic_slice_in_dim(strip, begin, ext, 1))(starts)
        means = lax.dynamic_index_in_dim(means_all, index, 0, keepdims=False)
        solved = eigen_solve(blocks, means, basis, eig)

        def place(col_index, inner):
            begin = col_index.astype(jnp.int32) * SUB
            piece = lax.dynamic_slice(inner, (first, begin), (ext, ext))
            return lax.dynamic_update_slice(inner, piece + solved[col_index], (first, begin))
        acc = lax.fori_loop(0, cols_n, place, acc)
        return (acc, None)
    start = jnp.zeros((total_r + 2 * OV, total_c + 2 * OV), jnp.float32)
    result, unused = lax.scan(one_row, start, jnp.arange(rows_n, dtype=jnp.int32))
    return result[OV:-OV, OV:-OV]

def precondition(resid, mobility):
    total_r, total_c = resid.shape
    rows_n = total_r // SUB
    cols_n = total_c // SUB
    sums = resid.reshape(rows_n, SUB, cols_n, SUB).sum(axis=(1, 3))
    coarse = coarse_solve(sums)
    spread = jnp.broadcast_to(coarse[:, None, :, None], (rows_n, SUB, cols_n, SUB)).reshape(total_r, total_c)
    return schwarz(resid, mobility) + spread

def reference(height, noise):
    mobility = height * height * height
    solution_field = jnp.zeros_like(noise)
    residual = noise
    direction = noise
    norm_old = jnp.float32(1.0)
    for step in range(ITERS):
        precond = precondition(residual, mobility)
        norm_now = jnp.sum(residual * precond)
        if step == 0:
            direction = precond
        else:
            direction = precond + norm_now / norm_old * direction
        image = operate(direction, mobility)
        alpha = norm_now / jnp.sum(direction * image)
        solution_field = solution_field + alpha * direction
        residual = residual - alpha * image
        norm_old = norm_now
    return (solution_field, residual)
```

```python
import functools

import jax
import jax.numpy as jnp
import numpy as np
from jax import lax
from jax.experimental import pallas as pl
from jax.experimental.pallas import tpu as pltpu
from jax.sharding import PartitionSpec as P

SUB = 128
OV = 8
EXT = SUB + 2 * OV
DAMP = 2.0**-28
SHRINK = 2.0**-20

TR, TC = 128, 256
FR, FC = 160, 384
SPEC = 192

highest = lax.Precision.HIGHEST


def sine(count):
    k = np.arange(1, count + 1, dtype=np.float64)
    basis = np.sqrt(2.0 / (count + 1.0)) * np.sin(np.pi * k[:, None] * k[None, :] / (count + 1.0))
    return basis, 2.0 - 2.0 * np.cos(np.pi * k / (count + 1.0))


def block_constants():
    basis, eig = sine(EXT)
    rows = np.zeros((FR, EXT))
    cols = np.zeros((FC, 2 * SPEC))
    for at in range(EXT):
        rows[(at - OV) % FR] = basis[at]
        for b in range(2):
            cols[(b * SUB + at - OV) % FC, b * SPEC : b * SPEC + EXT] = basis[at]
    scale = np.ones((EXT, 2 * SPEC))
    for b in range(2):
        scale[:, b * SPEC : b * SPEC + EXT] = (eig[:, None] + eig[None, :]) ** 2
    f32 = lambda x: np.ascontiguousarray(x, dtype=np.float32)
    return f32(rows), f32(rows.T), f32(cols), f32(cols.T), f32(scale)


def coarse_inverse(nr, nc, width):
    br, er = sine(nr)
    bc, ec = sine(nc)
    both = np.kron(br, bc)
    scale = (er[:, None] + ec[None, :]) / (SUB * SUB)
    values = (SUB * SUB * (DAMP + scale * scale)).reshape(-1)
    whole = np.zeros((width, width), np.float32)
    whole[: nr * nc, : nr * nc] = (both / values) @ both.T
    return whole


def dot(a, b):
    return lax.dot_general(
        a, b, (((1,), (0,)), ((), ())), precision=highest, preferred_element_type=jnp.float32
    )


def lap(x):
    rows, lanes = x.shape
    beside = pltpu.roll(x, 1, 0) + pltpu.roll(x, rows - 1, 0)
    beside = beside + (pltpu.roll(x, 1, 1) + pltpu.roll(x, lanes - 1, 1))
    return 4.0 * x - beside


def lanes_of(shape):
    return lax.broadcasted_iota(jnp.int32, shape, 1)


def rows_of(shape):
    return lax.broadcasted_iota(jnp.int32, shape, 0)


def total(x):
    return jnp.sum(jnp.sum(x, axis=0, keepdims=True), axis=1, keepdims=True)


def place():
    return lax.axis_index("row"), lax.axis_index("col")


def is_even(index):
    return lax.rem(index, 2) == 0


def grid_mask(shape, counts):
    i, j = place()
    rr, ll = rows_of(shape), lanes_of(shape)
    below = jnp.where(i < counts[0] - 1, 144, 128)
    above = jnp.where(i > 0, 144, 160)
    right = jnp.where(j < counts[1] - 1, 320, 256)
    left = jnp.where(j > 0, 320, 384)
    return ((rr < below) | (rr >= above)) & ((ll < right) | (ll >= left))


def table_at(values, counts):
    i, j = place()
    first = i * (2 * counts[1]) + 2 * j
    flat = rows_of((8, 128)) * 128 + lanes_of((8, 128))
    return jnp.where(flat == first, values[0], 0.0) + jnp.where(flat == first + 1, values[1], 0.0)


def as_row(table, width):
    return jnp.concatenate([table[k : k + 1] for k in range(width // 128)], axis=1)


def coarse_values(c_row, inverse):
    return dot(jnp.broadcast_to(c_row, (8, c_row.shape[1])), inverse)[:1]


def spread(g_row, counts):
    i, j = place()
    nr, nc = counts[0], 2 * counts[1]
    shape = (16, g_row.shape[1])
    which = rows_of(shape)
    r = i - 1 + which // 4
    c = 2 * j - 1 + which % 4
    inside = (r >= 0) & (r < nr) & (c >= 0) & (c < nc) & (which < 12)
    picked = jnp.where(inside & (lanes_of(shape) == r * nc + c), g_row, 0.0)
    picked = jnp.sum(picked, axis=1, keepdims=True)
    lane = lanes_of((1, 128))
    bands = []
    for d in range(3):
        left, first, second, right = (picked[4 * d + k : 4 * d + k + 1] for k in range(4))
        bands.append(
            jnp.concatenate(
                [
                    jnp.broadcast_to(first, (1, 128)),
                    jnp.broadcast_to(second, (1, 128)),
                    jnp.where(lane < 64, right, left),
                ],
                axis=1,
            )
        )
    return jnp.concatenate(
        [
            jnp.broadcast_to(bands[1], (128, FC)),
            jnp.broadcast_to(bands[2], (16, FC)),
            jnp.broadcast_to(bands[0], (16, FC)),
        ],
        axis=0,
    )


def local_solve(w, means, rows, rows_t, cols, cols_t, scale):
    lane = lanes_of((1, 2 * SPEC))
    mean = jnp.where(lane < SPEC, means[0], means[1])
    t = dot(dot(rows_t, w), cols)
    t = t / (DAMP + mean * scale)
    return dot(rows, dot(t, cols_t))


def core_sums(x):
    return [total(x[:, :128]), total(x[:, 128:256])]


def pack_columns(y):
    lane = lanes_of((FR, 128))
    packed = jnp.where(
        lane < 16,
        y[:, :128],
        jnp.where(lane >= 112, y[:, 128:256], pltpu.roll(y[:, 256:], 64, 1)),
    )
    turned = packed.T
    to_left = jnp.concatenate([turned[56:64], turned[:16]], axis=0)
    to_right = jnp.concatenate([turned[112:], turned[64:72]], axis=0)
    return to_left, to_right


def add_columns(y, from_left, from_right):
    turned = jnp.concatenate(
        [
            from_right[8:24],
            jnp.zeros((40, FR), jnp.float32),
            from_right[:8],
            from_left[16:24],
            jnp.zeros((40, FR), jnp.float32),
            from_left[:16],
        ],
        axis=0,
    )
    back = turned.T
    lane = lanes_of((FR, 128))
    rolled = pltpu.roll(back, 64, 1)
    first = y[:, :128] + jnp.where(lane < 8, rolled, 0.0)
    second = y[:, 128:256] + jnp.where(lane >= 120, rolled, 0.0)
    third = y[:, 256:] + jnp.where((lane < 16) | (lane >= 112), back, 0.0)
    return jnp.concatenate([first, second, third], axis=1)


def pack_rows(y):
    return jnp.concatenate([y[152:160], y[:16]], axis=0), y[112:136]


def add_rows(y, from_above, from_below):
    return jnp.concatenate(
        [
            y[:8] + from_above[16:24],
            y[8:120],
            y[120:144] + from_below,
            y[144:] + from_above[:16],
        ],
        axis=0,
    )


def begin_kernel(counts, r_ref, h_ref, a_ref, b_ref):
    j = lax.axis_index("col")
    even = is_even(j)
    r, h = r_ref[...], h_ref[...]
    lane = lanes_of((128, 128))
    packed = jnp.where(
        lane < 16,
        r[:, :128],
        jnp.where(
            lane < 64,
            pltpu.roll(h[:, :128], 16, 1),
            jnp.where(lane < 112, pltpu.roll(h[:, 128:], 112, 1), r[:, 128:]),
        ),
    )
    turned = packed.T
    left, right = turned[:32], turned[96:]
    table = table_at(core_sums(r), counts)
    a_ref[:32] = jnp.where(even, right, left)
    a_ref[32:] = table
    b_ref[:32] = jnp.where(even, left, right)
    b_ref[32:] = table


def widen_kernel(counts, r_ref, h_ref, ga_ref, gb_ref, tb_ref, r3_ref, h3_ref, a_ref, b_ref):
    i, j = place()
    even = is_even(j)
    ga, gb = ga_ref[:32], gb_ref[:32]
    from_right = jnp.where(even, ga, gb)
    from_left = jnp.where(even, gb, ga)
    turned = jnp.concatenate([from_right, jnp.zeros((64, 128), jnp.float32), from_left], axis=0)
    back = turned.T
    lane = lanes_of((128, 128))
    edge = (lane < 16) | (lane >= 112)
    r3 = jnp.where(edge, back, 0.0)
    h3 = jnp.where(
        lane < 16, pltpu.roll(back, 112, 1), jnp.where(lane >= 112, pltpu.roll(back, 16, 1), 0.0)
    )
    r3_ref[...] = r3
    h3_ref[...] = h3
    table = tb_ref[32:] + gb_ref[32:]
    r, h = r_ref[...], h_ref[...]
    even = is_even(i)
    top = [jnp.concatenate([r[:8], r3[:8]], axis=1), jnp.concatenate([h[:16], h3[:16]], axis=1)]
    low = [
        jnp.concatenate([r[120:], r3[120:]], axis=1),
        jnp.concatenate([h[112:], h3[112:]], axis=1),
    ]
    wide = jnp.concatenate([table, jnp.zeros((8, FC - 128), jnp.float32)], axis=1)
    a_ref[:8] = jnp.where(even, low[0], top[0])
    a_ref[8:24] = jnp.where(even, low[1], top[1])
    a_ref[24:] = wide
    b_ref[:8] = jnp.where(even, top[0], low[0])
    b_ref[8:24] = jnp.where(even, top[1], low[1])
    b_ref[24:] = wide


def first_kernel(
    counts,
    r_ref,
    h_ref,
    r3_ref,
    h3_ref,
    ga_ref,
    gb_ref,
    rows_ref,
    rows_t_ref,
    cols_ref,
    cols_t_ref,
    scale_ref,
    y_ref,
    m_ref,
    a_ref,
    b_ref,
):
    i, j = place()
    even = is_even(i)
    ga, gb = ga_ref[:24], gb_ref[:24]
    below = jnp.where(even, ga, gb)
    above = jnp.where(even, gb, ga)
    r = jnp.concatenate([r_ref[...], r3_ref[...]], axis=1)
    h = jnp.concatenate([h_ref[...], h3_ref[...]], axis=1)
    wide = jnp.concatenate([r, below[:8], jnp.zeros((16, FC), jnp.float32), above[:8]], axis=0)
    tall = jnp.concatenate([h, below[8:], above[8:]], axis=0)
    mobility = tall * tall * tall
    m_ref[...] = mobility
    means = [x / (SUB * SUB) for x in core_sums(mobility[:128])]
    y = local_solve(
        wide,
        means,
        rows_ref[...],
        rows_t_ref[...],
        cols_ref[...],
        cols_t_ref[...],
        scale_ref[...],
    )
    y_ref[...] = y
    to_left, to_right = pack_columns(y)
    even = is_even(j)
    a_ref[...] = jnp.where(even, to_right, to_left)
    b_ref[...] = jnp.where(even, to_left, to_right)


def columns_kernel(with_table, *refs):
    if with_table:
        y_ref, ga_ref, gb_ref, t_ref, gt_ref, out_ref, a_ref, b_ref, t_out = refs
    else:
        y_ref, ga_ref, gb_ref, out_ref, a_ref, b_ref = refs
    i, j = place()
    even = is_even(j)
    ga, gb = ga_ref[...], gb_ref[...]
    y = add_columns(y_ref[...], jnp.where(even, gb, ga), jnp.where(even, ga, gb))
    out_ref[...] = y
    to_above, to_below = pack_rows(y)
    even = is_even(i)
    a_ref[:24] = jnp.where(even, to_below, to_above)
    b_ref[...] = jnp.where(even, to_above, to_below)
    if with_table:
        inner = (lax.rem(j, 4) == 1) | (lax.rem(j, 4) == 2)
        table = jnp.where(inner, t_ref[...], gt_ref[...])
        t_out[...] = table
        a_ref[24:] = jnp.concatenate([table, jnp.zeros((8, FC - 128), jnp.float32)], axis=1)


def second_kernel(
    counts,
    width,
    y_ref,
    m_ref,
    ga_ref,
    gb_ref,
    t_ref,
    r_ref,
    inverse_ref,
    rows_ref,
    rows_t_ref,
    cols_ref,
    cols_t_ref,
    scale_ref,
    z_ref,
    w_ref,
    y2_ref,
    stats_ref,
    t_out,
    a_ref,
    b_ref,
):
    i, j = place()
    even = is_even(i)
    ga, gb = ga_ref[:24], gb_ref[...]
    s = add_rows(y_ref[...], jnp.where(even, gb, ga), jnp.where(even, ga, gb))
    mask = grid_mask((FR, FC), counts)
    s = jnp.where(mask, s, 0.0)
    inner = (lax.rem(i, 4) == 1) | (lax.rem(i, 4) == 2)
    table = jnp.where(inner, t_ref[...], ga_ref[24:, :128])
    t_out[...] = table
    coarse = spread(coarse_values(as_row(table, width), inverse_ref[...]), counts)
    mobility = m_ref[...]
    flow = mobility * (lap(s) + lap(coarse))
    z = s + coarse
    w = jnp.where(mask, DAMP * z + lap(flow), 0.0) * SHRINK
    zt, wt, rt, mt = z[:128, :256], w[:128, :256], r_ref[...], mobility[:128, :256]
    z_ref[...] = zt
    w_ref[...] = wt
    means = [x / (SUB * SUB) for x in core_sums(mt)]
    y = local_solve(
        w,
        means,
        rows_ref[...],
        rows_t_ref[...],
        cols_ref[...],
        cols_t_ref[...],
        scale_ref[...],
    )
    y2_ref[...] = y
    to_left, to_right = pack_columns(y)
    even = is_even(j)
    a_ref[...] = jnp.where(even, to_right, to_left)
    b_ref[...] = jnp.where(even, to_left, to_right)
    rz, zw = total(rt * zt), total(zt * wt)
    c1 = core_sums(wt)
    lane, row = lanes_of((1, 256)), rows_of((128, 1))
    along = (lane % 128 != 0) & (lane % 128 != 127)
    top, low = mt[:1], mt[127:]
    side = jnp.sum(jnp.where((row > 0) & (row < 127), mt, 0.0), axis=0, keepdims=True)

    def halves(x):
        return [
            jnp.sum(x[:, :128], axis=1, keepdims=True),
            jnp.sum(x[:, 128:], axis=1, keepdims=True),
        ]

    first, last = lane % 128 == 0, lane % 128 == 127
    zero = jnp.zeros((1, 1), jnp.float32)
    values = [
        [rz, zero],
        [zw, zero],
        c1,
        halves(jnp.where(along, top, 0.0)),
        halves(jnp.where(along, low, 0.0)),
        halves(jnp.where(first, side, 0.0)),
        halves(jnp.where(last, side, 0.0)),
        halves(jnp.where(first, top, 0.0)),
        halves(jnp.where(last, top, 0.0)),
        halves(jnp.where(first, low, 0.0)),
        halves(jnp.where(last, low, 0.0)),
    ]
    for k, pair in enumerate(values):
        stats_ref[k] = table_at(pair, counts)


def dots_kernel(
    counts, y_ref, m_ref, ga_ref, gb_ref, r_ref, w_ref, stats_ref, q_ref, v_ref, stats_out
):
    i, j = place()
    even = is_even(i)
    ga, gb = ga_ref[...], gb_ref[...]
    q = add_rows(y_ref[...], jnp.where(even, gb, ga), jnp.where(even, ga, gb))
    q = jnp.where(grid_mask((FR, FC), counts), q, 0.0)
    v = DAMP * q + lap(m_ref[...] * lap(q))
    qt, vt = q[:128, :256], v[:128, :256]
    q_ref[...] = qt
    v_ref[...] = vt
    zero = jnp.zeros((1, 1), jnp.float32)
    stats_out[:11] = stats_ref[:11]
    values = [
        core_sums(vt),
        [total(r_ref[...] * qt), zero],
        [total(w_ref[...] * qt), zero],
        [total(vt * qt), zero],
    ]
    for k, pair in enumerate(values):
        stats_out[11 + k] = table_at(pair, counts)
    stats_out[15] = jnp.zeros((8, 128), jnp.float32)


def end_kernel(
    counts,
    width,
    stats_ref,
    t_ref,
    inverse_ref,
    m_ref,
    r_ref,
    z_ref,
    w_ref,
    q_ref,
    v_ref,
    solution_ref,
    residual_ref,
):
    nc = 2 * counts[1]
    st = [as_row(stats_ref[k], width) for k in range(15)]

    def whole(x):
        return jnp.sum(x, axis=1, keepdims=True)

    rz, zw, rq, wq, qv = (whole(st[k]) for k in (0, 1, 12, 13, 14))
    c0, c1, sums_v = as_row(t_ref[...], width), st[2], st[11]
    g = coarse_values(c1, inverse_ref[...])
    lane = lanes_of((1, width))
    cell = lane < counts[0] * nc
    column = lane % nc
    up = jnp.where(lane >= nc, pltpu.roll(g, nc, 1), 0.0)
    down = jnp.where(lane < (counts[0] - 1) * nc, pltpu.roll(g, width - nc, 1), 0.0)
    left = jnp.where(column > 0, pltpu.roll(g, 1, 1), 0.0)
    right = jnp.where(column < nc - 1, pltpu.roll(g, width - 1, 1), 0.0)
    du, dd, dl, dr = g - up, g - down, g - left, g - right
    energy = DAMP * SUB * SUB * g * g
    energy = energy + st[3] * du * du + st[4] * dd * dd + st[5] * dl * dl + st[6] * dr * dr
    for weight, p, q in ((st[7], du, dl), (st[8], du, dr), (st[9], dd, dl), (st[10], dd, dr)):
        both = p + q
        energy = energy + weight * both * both
    ry = rq + whole(g * c0)
    yw = wq + whole(g * c1)
    yv = qv + whole(jnp.where(cell, 2.0 * g * sums_v + energy, 0.0))
    a = rz / zw
    rz1 = rz - a * ry - a * zw + a * a * yw
    beta1 = 1.0 + rz1 / rz
    dad = (beta1 * beta1 * zw - 2.0 * a * beta1 * yw) * (1.0 / SHRINK) + a * a * yv
    a1 = rz1 / dad
    coarse = spread(g, counts)
    y = q_ref[...] + coarse[:128, :256]
    image = DAMP * coarse + lap(m_ref[...] * lap(coarse))
    v = v_ref[...] + image[:128, :256]
    z, w = z_ref[...], w_ref[...]
    solution_ref[...] = (a * SHRINK) * z + a1 * (beta1 * z - a * y)
    residual_ref[...] = r_ref[...] - a * w - a1 * ((beta1 * (1.0 / SHRINK)) * w - a * v)


def call(kernel, outs, *args):
    shapes = [jax.ShapeDtypeStruct(s, jnp.float32) for s in outs]
    return pl.pallas_call(
        kernel,
        out_shape=shapes,
        compiler_params=pltpu.CompilerParams(vmem_limit_bytes=48 * 1024 * 1024),
    )(*args)


def swaps(count, offset):
    pairs = []
    for k in range(offset, count - 1, 2):
        pairs += [(k, k + 1), (k + 1, k)]
    return pairs


def across(count, bit):
    return [(k, k ^ bit) for k in range(count)]


def body(counts, height, noise):
    nr, nc = counts
    width = max(128, nr * nc * 2)
    rows, rows_t, cols, cols_t, scale = (jnp.asarray(x) for x in block_constants())
    inverse = jnp.asarray(coarse_inverse(nr, 2 * nc, width))
    basis = (rows, rows_t, cols, cols_t, scale)

    def swap_a(x, axis, count):
        return lax.ppermute(x, axis, swaps(count, 0))

    def swap_b(x, axis, count):
        return lax.ppermute(x, axis, swaps(count, 1))

    a, b = call(functools.partial(begin_kernel, counts), [(40, 128)] * 2, noise, height)
    ga = swap_a(a, "col", nc)
    b = b.at[32:].add(ga[32:])
    gb = swap_b(b, "col", nc)
    r3, h3, a, b = call(
        functools.partial(widen_kernel, counts),
        [(128, 128)] * 2 + [(32, FC)] * 2,
        noise,
        height,
        ga,
        gb,
        b,
    )
    ga = swap_a(a, "row", nr)
    b = b.at[24:].add(ga[24:])
    gb = swap_b(b, "row", nr)
    table = b[24:, :128] + gb[24:, :128]
    y, m, a, b = call(
        functools.partial(first_kernel, counts),
        [(FR, FC)] * 2 + [(24, FR)] * 2,
        noise,
        height,
        r3,
        h3,
        ga,
        gb,
        *basis,
    )
    for axis, count in (("row", nr), ("col", nc)):
        bit = 4
        while bit < count:
            table = table + lax.ppermute(table, axis, across(count, bit))
            bit *= 2
    whole_a = jnp.concatenate([a, jnp.pad(table, ((0, 0), (0, FR - 128)))], axis=0)
    ga = swap_a(whole_a, "col", nc)
    gb = swap_b(b, "col", nc)
    y, a, b, table = call(
        functools.partial(columns_kernel, True),
        [(FR, FC), (32, FC), (24, FC), (8, 128)],
        y,
        ga[:24],
        gb,
        table,
        ga[24:, :128],
    )
    ga = swap_a(a, "row", nr)
    gb = swap_b(b, "row", nr)
    z, w, y, stats, table, a, b = call(
        functools.partial(second_kernel, counts, width),
        [(TR, TC)] * 2 + [(FR, FC), (11, 8, 128), (8, 128)] + [(24, FR)] * 2,
        y,
        m,
        ga,
        gb,
        table,
        noise,
        inverse,
        *basis,
    )
    ga = swap_a(a, "col", nc)
    gb = swap_b(b, "col", nc)
    y, a, b = call(
        functools.partial(columns_kernel, False), [(FR, FC), (24, FC), (24, FC)], y, ga, gb
    )
    ga = swap_a(a, "row", nr)
    gb = swap_b(b, "row", nr)
    q, v, stats = call(
        functools.partial(dots_kernel, counts),
        [(TR, TC)] * 2 + [(16, 8, 128)],
        y,
        m,
        ga,
        gb,
        noise,
        w,
        stats,
    )
    used = width // 128
    stats = stats[:, :used]
    for axis, count in (("row", nr), ("col", nc)):
        bit = 1
        while bit < count:
            stats = stats + lax.ppermute(stats, axis, across(count, bit))
            bit *= 2
    return tuple(
        call(
            functools.partial(end_kernel, counts, width),
            [(TR, TC)] * 2,
            stats,
            table,
            inverse,
            m,
            noise,
            z,
            w,
            q,
            v,
        )
    )


def solution(mesh):
    counts = (mesh.shape["row"], mesh.shape["col"])
    spec = P("row", "col")
    return jax.shard_map(
        functools.partial(body, counts),
        mesh=mesh,
        in_specs=(spec, spec),
        out_specs=(spec, spec),
        check_vma=False,
    )
```

```python
import functools

import jax
import jax.numpy as jnp
import numpy as np
from jax import lax
from jax.experimental import pallas as pl
from jax.experimental.pallas import tpu as pltpu
from jax.sharding import PartitionSpec as P

SUB = 128
OV = 8
EXT = SUB + 2 * OV
DAMP = 2.0**-28
SHRINK = 2.0**-20

TR, TC = 128, 256
FR, FC = 160, 384
SPEC = 192

highest = lax.Precision.HIGHEST


def sine(count):
    k = np.arange(1, count + 1, dtype=np.float64)
    basis = np.sqrt(2.0 / (count + 1.0)) * np.sin(np.pi * k[:, None] * k[None, :] / (count + 1.0))
    return basis, 2.0 - 2.0 * np.cos(np.pi * k / (count + 1.0))


def block_constants():
    basis, eig = sine(EXT)
    rows = np.zeros((FR, EXT))
    cols = np.zeros((FC, 2 * SPEC))
    for at in range(EXT):
        rows[(at - OV) % FR] = basis[at]
        for b in range(2):
            cols[(b * SUB + at - OV) % FC, b * SPEC : b * SPEC + EXT] = basis[at]
    scale = np.ones((EXT, 2 * SPEC))
    for b in range(2):
        scale[:, b * SPEC : b * SPEC + EXT] = (eig[:, None] + eig[None, :]) ** 2
    wide = lambda x: np.pad(x, ((0, 0), (0, FC - x.shape[1])))
    return np.concatenate([cols, cols.T, scale, wide(rows), wide(rows.T)]).astype(np.float32)


def block_parts(ref):
    cols, cols_t, scale = ref[:FC], ref[FC : 2 * FC], ref[2 * FC : 2 * FC + EXT]
    at = 2 * FC + EXT
    return ref[at : at + FR, :EXT], ref[at + FR : at + FR + EXT, :FR], cols, cols_t, scale


def coarse_inverse(nr, nc, width):
    br, er = sine(nr)
    bc, ec = sine(nc)
    both = np.kron(br, bc).reshape(nr, nc // 2, 2, nr * nc).transpose(2, 0, 1, 3)
    both = both.reshape(nr * nc, nr * nc)
    scale = (er[:, None] + ec[None, :]) / (SUB * SUB)
    values = (SUB * SUB * (DAMP + scale * scale)).reshape(-1)
    whole = np.zeros((width, width), np.float32)
    whole[: nr * nc, : nr * nc] = (both / values) @ both.T
    return whole


def dot(a, b):
    return lax.dot_general(
        a, b, (((1,), (0,)), ((), ())), precision=highest, preferred_element_type=jnp.float32
    )


def lap(x):
    rows, lanes = x.shape
    beside = pltpu.roll(x, 1, 0) + pltpu.roll(x, rows - 1, 0)
    beside = beside + (pltpu.roll(x, 1, 1) + pltpu.roll(x, lanes - 1, 1))
    return 4.0 * x - beside


def lanes_of(shape):
    return lax.broadcasted_iota(jnp.int32, shape, 1)


def rows_of(shape):
    return lax.broadcasted_iota(jnp.int32, shape, 0)


def total(x):
    return jnp.sum(jnp.sum(x, axis=0, keepdims=True), axis=1, keepdims=True)


def place():
    return lax.axis_index("row"), lax.axis_index("col")


def is_even(index):
    return lax.rem(index, 2) == 0


def grid_mask(shape, counts):
    i, j = place()
    rr, ll = rows_of(shape), lanes_of(shape)
    below = jnp.where(i < counts[0] - 1, 144, 128)
    above = jnp.where(i > 0, 144, 160)
    right = jnp.where(j < counts[1] - 1, 320, 256)
    left = jnp.where(j > 0, 320, 384)
    return ((rr < below) | (rr >= above)) & ((ll < right) | (ll >= left))


def row_of(pairs):
    lane = lanes_of((1, 128))
    row = jnp.zeros((1, 128), jnp.float32)
    for k, (left, right) in enumerate(pairs):
        row = jnp.where(lane == k, left, jnp.where(lane == 64 + k, right, row))
    return row


def gathered(rows, width):
    devices = rows.shape[0]
    turned = rows.T
    parts = [turned[:16], turned[64:80]]
    if width > 2 * devices:
        parts.append(jnp.zeros((16, width - 2 * devices), jnp.float32))
    return jnp.concatenate(parts, axis=1)


def coarse_values(c_row, inverse):
    return dot(jnp.broadcast_to(c_row, (8, c_row.shape[1])), inverse)[:1]


def spread(g_row, counts):
    i, j = place()
    nr, nc = counts[0], 2 * counts[1]
    shape = (16, g_row.shape[1])
    which = rows_of(shape)
    r = i - 1 + which // 4
    c = 2 * j - 1 + which % 4
    inside = (r >= 0) & (r < nr) & (c >= 0) & (c < nc) & (which < 12)
    at = lax.rem(c + 2, 2) * (nr * counts[1]) + r * counts[1] + (c + 2) // 2 - 1
    picked = jnp.where(inside & (lanes_of(shape) == at), g_row, 0.0)
    picked = jnp.sum(picked, axis=1, keepdims=True)
    lane = lanes_of((1, 128))
    bands = []
    for d in range(3):
        left, first, second, right = (picked[4 * d + k : 4 * d + k + 1] for k in range(4))
        bands.append(
            jnp.concatenate(
                [
                    jnp.broadcast_to(first, (1, 128)),
                    jnp.broadcast_to(second, (1, 128)),
                    jnp.where(lane < 64, right, left),
                ],
                axis=1,
            )
        )
    return jnp.concatenate(
        [
            jnp.broadcast_to(bands[1], (128, FC)),
            jnp.broadcast_to(bands[2], (16, FC)),
            jnp.broadcast_to(bands[0], (16, FC)),
        ],
        axis=0,
    )


def local_solve(w, means, basis_ref):
    rows, rows_t, cols, cols_t, scale = block_parts(basis_ref)
    lane = lanes_of((1, 2 * SPEC))
    mean = jnp.where(lane < SPEC, means[0], means[1])
    t = dot(dot(rows_t, w), cols)
    t = t / (DAMP + mean * scale)
    return dot(rows, dot(t, cols_t))


def core_sums(x):
    return [total(x[:, :128]), total(x[:, 128:256])]


def pack_columns(y):
    lane = lanes_of((FR, 128))
    packed = jnp.where(
        lane < 16,
        y[:, :128],
        jnp.where(lane >= 112, y[:, 128:256], pltpu.roll(y[:, 256:], 64, 1)),
    )
    turned = packed.T
    to_left = jnp.concatenate([turned[56:64], turned[:16]], axis=0)
    to_right = jnp.concatenate([turned[112:], turned[64:72]], axis=0)
    return to_left, to_right


def add_columns(y, from_left, from_right):
    turned = jnp.concatenate(
        [
            from_right[8:24],
            jnp.zeros((40, FR), jnp.float32),
            from_right[:8],
            from_left[16:24],
            jnp.zeros((40, FR), jnp.float32),
            from_left[:16],
        ],
        axis=0,
    )
    back = turned.T
    lane = lanes_of((FR, 128))
    rolled = pltpu.roll(back, 64, 1)
    first = y[:, :128] + jnp.where(lane < 8, rolled, 0.0)
    second = y[:, 128:256] + jnp.where(lane >= 120, rolled, 0.0)
    third = y[:, 256:] + jnp.where((lane < 16) | (lane >= 112), back, 0.0)
    return jnp.concatenate([first, second, third], axis=1)


def pack_rows(y):
    return jnp.concatenate([y[152:160], y[:16]], axis=0), y[112:136]


def add_rows(y, from_above, from_below):
    return jnp.concatenate(
        [
            y[:8] + from_above[16:24],
            y[8:120],
            y[120:144] + from_below,
            y[144:] + from_above[:16],
        ],
        axis=0,
    )


def sides(index, count, a, b):
    even = is_even(index)
    before = jnp.where(index > 0, jnp.where(even, b, a), 0.0)
    after = jnp.where(index < count - 1, jnp.where(even, a, b), 0.0)
    return before, after


def send(index, a_ref, b_ref, before, after):
    even = is_even(index)
    a_ref[...] = jnp.where(even, after, before)
    b_ref[...] = jnp.where(even, before, after)


def begin_kernel(counts, r_hbm, h_hbm, r_ref, h_ref, a_ref, b_ref, sums_ref, sems):
    copies = [
        pltpu.make_async_copy(r_hbm, r_ref, sems.at[0]),
        pltpu.make_async_copy(h_hbm, h_ref, sems.at[1]),
    ]
    for copy in copies:
        copy.start()
    for copy in copies:
        copy.wait()
    r, h = r_ref[...], h_ref[...]
    lane = lanes_of((128, 128))
    packed = jnp.where(
        lane < 16,
        r[:, :128],
        jnp.where(
            lane < 64,
            pltpu.roll(h[:, :128], 16, 1),
            jnp.where(lane < 112, pltpu.roll(h[:, 128:], 112, 1), r[:, 128:]),
        ),
    )
    turned = packed.T
    send(lax.axis_index("col"), a_ref, b_ref, turned[:32], turned[96:])
    sums_ref[...] = row_of([core_sums(r)])


def widen_kernel(counts, r_ref, h_ref, ga_ref, gb_ref, r3_ref, h3_ref, a_ref, b_ref):
    i, j = place()
    from_left, from_right = sides(j, counts[1], ga_ref[...], gb_ref[...])
    turned = jnp.concatenate([from_right, jnp.zeros((64, 128), jnp.float32), from_left], axis=0)
    back = turned.T
    lane = lanes_of((128, 128))
    edge = (lane < 16) | (lane >= 112)
    r3 = jnp.where(edge, back, 0.0)
    h3 = jnp.where(
        lane < 16, pltpu.roll(back, 112, 1), jnp.where(lane >= 112, pltpu.roll(back, 16, 1), 0.0)
    )
    r3_ref[...] = r3
    h3_ref[...] = h3
    r, h = r_ref[...], h_ref[...]

    def strip(r_rows, h_rows):
        return jnp.concatenate(
            [
                jnp.concatenate([r[r_rows], r3[r_rows]], axis=1),
                jnp.concatenate([h[h_rows], h3[h_rows]], axis=1),
            ],
            axis=0,
        )

    send(i, a_ref, b_ref, strip(slice(0, 8), slice(0, 16)), strip(slice(120, 128), slice(112, 128)))


def first_kernel(
    counts, r_ref, h_ref, r3_ref, h3_ref, ga_ref, gb_ref, basis_ref, y_ref, m_ref, a_ref, b_ref
):
    i, j = place()
    above, below = sides(i, counts[0], ga_ref[...], gb_ref[...])
    r = jnp.concatenate([r_ref[...], r3_ref[...]], axis=1)
    h = jnp.concatenate([h_ref[...], h3_ref[...]], axis=1)
    wide = jnp.concatenate([r, below[:8], jnp.zeros((16, FC), jnp.float32), above[:8]], axis=0)
    tall = jnp.concatenate([h, below[8:], above[8:]], axis=0)
    mobility = tall * tall * tall
    m_ref[...] = mobility
    means = [x / (SUB * SUB) for x in core_sums(mobility[:128])]
    y = local_solve(wide, means, basis_ref)
    y_ref[...] = y
    send(j, a_ref, b_ref, *pack_columns(y))


def columns_kernel(counts, y_ref, ga_ref, gb_ref, out_ref, a_ref, b_ref):
    i, j = place()
    y = add_columns(y_ref[...], *sides(j, counts[1], ga_ref[...], gb_ref[...]))
    out_ref[...] = y
    send(i, a_ref, b_ref, *pack_rows(y))


def second_kernel(
    counts,
    width,
    y_ref,
    m_ref,
    ga_ref,
    gb_ref,
    sums_ref,
    r_ref,
    inverse_ref,
    basis_ref,
    z_ref,
    w_ref,
    y2_ref,
    stats_ref,
    a_ref,
    b_ref,
):
    i, j = place()
    s = add_rows(y_ref[...], *sides(i, counts[0], ga_ref[...], gb_ref[...]))
    mask = grid_mask((FR, FC), counts)
    s = jnp.where(mask, s, 0.0)
    c0 = gathered(sums_ref[...], width)[:1]
    coarse = spread(coarse_values(c0, inverse_ref[...]), counts)
    mobility = m_ref[...]
    flow = mobility * (lap(s) + lap(coarse))
    z = s + coarse
    w = jnp.where(mask, DAMP * z + lap(flow), 0.0) * SHRINK
    zt, wt, rt, mt = z[:128, :256], w[:128, :256], r_ref[...], mobility[:128, :256]
    z_ref[...] = zt
    w_ref[...] = wt
    means = [x / (SUB * SUB) for x in core_sums(mt)]
    y = local_solve(w, means, basis_ref)
    y2_ref[...] = y
    send(j, a_ref, b_ref, *pack_columns(y))
    lane, row = lanes_of((1, 256)), rows_of((128, 1))
    along = (lane % 128 != 0) & (lane % 128 != 127)
    top, low = mt[:1], mt[127:]
    side = jnp.sum(jnp.where((row > 0) & (row < 127), mt, 0.0), axis=0, keepdims=True)

    def halves(x):
        return [
            jnp.sum(x[:, :128], axis=1, keepdims=True),
            jnp.sum(x[:, 128:], axis=1, keepdims=True),
        ]

    first, last = lane % 128 == 0, lane % 128 == 127
    stats_ref[...] = row_of(
        [
            core_sums(rt * zt),
            core_sums(zt * wt),
            core_sums(wt),
            halves(jnp.where(along, top, 0.0)),
            halves(jnp.where(along, low, 0.0)),
            halves(jnp.where(first, side, 0.0)),
            halves(jnp.where(last, side, 0.0)),
            halves(jnp.where(first, top, 0.0)),
            halves(jnp.where(last, top, 0.0)),
            halves(jnp.where(first, low, 0.0)),
            halves(jnp.where(last, low, 0.0)),
        ]
    )


def dots_kernel(
    counts, y_ref, m_ref, ga_ref, gb_ref, r_ref, w_ref, stats_ref, q_ref, v_ref, stats_out
):
    i, j = place()
    q = add_rows(y_ref[...], *sides(i, counts[0], ga_ref[...], gb_ref[...]))
    q = jnp.where(grid_mask((FR, FC), counts), q, 0.0)
    v = DAMP * q + lap(m_ref[...] * lap(q))
    qt, vt = q[:128, :256], v[:128, :256]
    q_ref[...] = qt
    v_ref[...] = vt
    rest = [
        core_sums(vt),
        core_sums(r_ref[...] * qt),
        core_sums(w_ref[...] * qt),
        core_sums(vt * qt),
    ]
    zero = jnp.zeros((1, 1), jnp.float32)
    row = stats_ref[...] + row_of([[zero, zero]] * 11 + rest)
    stats_out[...] = jnp.broadcast_to(row, stats_out.shape)


def end_kernel(
    counts,
    width,
    stats_ref,
    sums_ref,
    inverse_ref,
    m_ref,
    r_ref,
    z_ref,
    w_ref,
    q_ref,
    v_ref,
    solution_ref,
    residual_ref,
):
    tiles_c = counts[1]
    devices = counts[0] * tiles_c
    table = gathered(stats_ref[...], width)
    st = [table[k : k + 1] for k in range(15)]

    def whole(x):
        return jnp.sum(x, axis=1, keepdims=True)

    rz, zw, rq, wq, qv = (whole(st[k]) for k in (0, 1, 12, 13, 14))
    c0, c1, sums_v = gathered(sums_ref[...], width)[:1], st[2], st[11]
    g = coarse_values(c1, inverse_ref[...])
    lane = lanes_of((1, width))
    cell = lane < 2 * devices
    on_left = lane < devices
    device = lane % devices
    column = device % tiles_c

    def from_lane(distance):
        return pltpu.roll(g, distance % width, 1)

    up = jnp.where(device >= tiles_c, from_lane(tiles_c), 0.0)
    down = jnp.where(device < devices - tiles_c, from_lane(-tiles_c), 0.0)
    left = jnp.where(
        on_left, jnp.where(column > 0, from_lane(1 - devices), 0.0), from_lane(devices)
    )
    right = jnp.where(
        on_left,
        from_lane(-devices),
        jnp.where(column < tiles_c - 1, from_lane(devices - 1), 0.0),
    )
    du, dd, dl, dr = g - up, g - down, g - left, g - right
    energy = DAMP * SUB * SUB * g * g
    energy = energy + st[3] * du * du + st[4] * dd * dd + st[5] * dl * dl + st[6] * dr * dr
    for weight, p, q in ((st[7], du, dl), (st[8], du, dr), (st[9], dd, dl), (st[10], dd, dr)):
        both = p + q
        energy = energy + weight * both * both
    ry = rq + whole(g * c0)
    yw = wq + whole(g * c1)
    yv = qv + whole(jnp.where(cell, 2.0 * g * sums_v + energy, 0.0))
    a = rz / zw
    rz1 = rz - a * ry - a * zw + a * a * yw
    beta1 = 1.0 + rz1 / rz
    dad = (beta1 * beta1 * zw - 2.0 * a * beta1 * yw) * (1.0 / SHRINK) + a * a * yv
    a1 = rz1 / dad
    coarse = spread(g, counts)
    y = q_ref[...] + coarse[:128, :256]
    image = DAMP * coarse + lap(m_ref[...] * lap(coarse))
    v = v_ref[...] + image[:128, :256]
    z, w = z_ref[...], w_ref[...]
    solution_ref[...] = (a * SHRINK) * z + a1 * (beta1 * z - a * y)
    residual_ref[...] = r_ref[...] - a * w - a1 * ((beta1 * (1.0 / SHRINK)) * w - a * v)


def call(kernel, outs, *args, **options):
    shapes = [jax.ShapeDtypeStruct(s, jnp.float32) for s in outs]
    return pl.pallas_call(
        kernel,
        out_shape=shapes,
        compiler_params=pltpu.CompilerParams(vmem_limit_bytes=48 * 1024 * 1024),
        **options,
    )(*args)


def pairs_from(count, offset):
    found = []
    for k in range(offset, count, 2):
        found += [(k, (k + 1) % count), ((k + 1) % count, k)]
    return found


def body(counts, height, noise):
    nr, nc = counts
    devices = nr * nc
    width = max(128, devices * 2)
    basis = jnp.asarray(block_constants())
    inverse = jnp.asarray(coarse_inverse(nr, 2 * nc, width))
    both = ("row", "col")

    def swap(a, b, axis):
        count = lax.axis_size(axis)
        return (
            lax.ppermute(a, axis, pairs_from(count, 0)),
            lax.ppermute(b, axis, pairs_from(count, 1)),
        )

    r, h, a, b, sums = call(
        functools.partial(begin_kernel, counts),
        [(TR, TC)] * 2 + [(32, 128)] * 2 + [(1, 128)],
        noise,
        height,
        in_specs=[pl.BlockSpec(memory_space=pltpu.HBM)] * 2,
        scratch_shapes=[pltpu.SemaphoreType.DMA((2,))],
    )
    sums = lax.all_gather(sums, both, axis=0, tiled=True)
    ga, gb = swap(a, b, "col")
    r3, h3, a, b = call(
        functools.partial(widen_kernel, counts),
        [(128, 128)] * 2 + [(24, FC)] * 2,
        r,
        h,
        ga,
        gb,
    )
    ga, gb = swap(a, b, "row")
    y, m, a, b = call(
        functools.partial(first_kernel, counts),
        [(FR, FC)] * 2 + [(24, FR)] * 2,
        r,
        h,
        r3,
        h3,
        ga,
        gb,
        basis,
    )
    ga, gb = swap(a, b, "col")
    y, a, b = call(
        functools.partial(columns_kernel, counts), [(FR, FC)] + [(24, FC)] * 2, y, ga, gb
    )
    ga, gb = swap(a, b, "row")
    z, w, y, stats, a, b = call(
        functools.partial(second_kernel, counts, width),
        [(TR, TC)] * 2 + [(FR, FC), (1, 128)] + [(24, FR)] * 2,
        y,
        m,
        ga,
        gb,
        sums,
        r,
        inverse,
        basis,
    )
    ga, gb = swap(a, b, "col")
    y, a, b = call(
        functools.partial(columns_kernel, counts), [(FR, FC)] + [(24, FC)] * 2, y, ga, gb
    )
    ga, gb = swap(a, b, "row")
    q, v, stats = call(
        functools.partial(dots_kernel, counts),
        [(TR, TC)] * 2 + [(devices, 128)],
        y,
        m,
        ga,
        gb,
        r,
        w,
        stats,
    )
    stats = lax.all_to_all(stats, both, 0, 0, tiled=True)
    return tuple(
        call(
            functools.partial(end_kernel, counts, width),
            [(TR, TC)] * 2,
            stats,
            sums,
            inverse,
            m,
            r,
            z,
            w,
            q,
            v,
        )
    )


def solution(mesh):
    counts = (mesh.shape["row"], mesh.shape["col"])
    spec = P("row", "col")
    return jax.shard_map(
        functools.partial(body, counts),
        mesh=mesh,
        in_specs=(spec, spec),
        out_specs=(spec, spec),
        check_vma=False,
    )
```

```python
import functools

import jax
import jax.numpy as jnp
import numpy as np
from jax import lax
from jax.experimental import pallas as pl
from jax.experimental.pallas import tpu as pltpu
from jax.sharding import PartitionSpec as P

SUB = 128
OV = 8
EXT = SUB + 2 * OV
DAMP = 2.0**-28
SHRINK = 2.0**-20

TR, TC = 128, 256
FR, FC = 160, 384
SPEC = 192

highest = lax.Precision.HIGHEST


def sine(count):
    k = np.arange(1, count + 1, dtype=np.float64)
    basis = np.sqrt(2.0 / (count + 1.0)) * np.sin(np.pi * k[:, None] * k[None, :] / (count + 1.0))
    return basis, 2.0 - 2.0 * np.cos(np.pi * k / (count + 1.0))


def block_constants():
    basis, eig = sine(EXT)
    rows = np.zeros((FR, EXT))
    cols = np.zeros((FC, 2 * SPEC))
    for at in range(EXT):
        rows[(at - OV) % FR] = basis[at]
        for b in range(2):
            cols[(b * SUB + at - OV) % FC, b * SPEC : b * SPEC + EXT] = basis[at]
    scale = np.ones((EXT, 2 * SPEC))
    for b in range(2):
        scale[:, b * SPEC : b * SPEC + EXT] = (eig[:, None] + eig[None, :]) ** 2
    wide = lambda x: np.pad(x, ((0, 0), (0, FC - x.shape[1])))
    return [cols, cols.T, scale, wide(rows), wide(rows.T)]


def block_parts(ref):
    cols, cols_t, scale = ref[:FC], ref[FC : 2 * FC], ref[2 * FC : 2 * FC + EXT]
    at = 2 * FC + EXT
    return ref[at : at + FR, :EXT], ref[at + FR : at + FR + EXT, :FR], cols, cols_t, scale


def coarse_part(ref, width):
    at = 2 * FC + 2 * EXT + FR
    parts = [ref[at + k * width : at + (k + 1) * width] for k in range(-(-width // FC))]
    return (parts[0] if len(parts) == 1 else jnp.concatenate(parts, axis=1))[:, :width]


def constants(nr, nc, width):
    inverse = coarse_inverse(nr, nc, -(-width // FC) * FC)[:width]
    return np.concatenate([*block_constants(), *np.split(inverse, inverse.shape[1] // FC, 1)], dtype=np.float32)


def coarse_inverse(nr, nc, width):
    br, er = sine(nr)
    bc, ec = sine(nc)
    both = np.kron(br, bc).reshape(nr, nc // 2, 2, nr * nc).transpose(2, 0, 1, 3)
    both = both.reshape(nr * nc, nr * nc)
    scale = (er[:, None] + ec[None, :]) / (SUB * SUB)
    values = (SUB * SUB * (DAMP + scale * scale)).reshape(-1)
    whole = np.zeros((width, width), np.float32)
    whole[: nr * nc, : nr * nc] = (both / values) @ both.T
    return whole


def dot(a, b):
    return lax.dot_general(
        a, b, (((1,), (0,)), ((), ())), precision=highest, preferred_element_type=jnp.float32
    )


def lap(x):
    rows, lanes = x.shape
    beside = pltpu.roll(x, 1, 0) + pltpu.roll(x, rows - 1, 0)
    beside = beside + (pltpu.roll(x, 1, 1) + pltpu.roll(x, lanes - 1, 1))
    return 4.0 * x - beside


def lanes_of(shape):
    return lax.broadcasted_iota(jnp.int32, shape, 1)


def rows_of(shape):
    return lax.broadcasted_iota(jnp.int32, shape, 0)


def total(x):
    return jnp.sum(jnp.sum(x, axis=0, keepdims=True), axis=1, keepdims=True)


def place():
    return lax.axis_index("row"), lax.axis_index("col")


def is_even(index):
    return lax.rem(index, 2) == 0


def grid_mask(shape, counts):
    i, j = place()
    rr, ll = rows_of(shape), lanes_of(shape)
    below = jnp.where(i < counts[0] - 1, 144, 128)
    above = jnp.where(i > 0, 144, 160)
    right = jnp.where(j < counts[1] - 1, 320, 256)
    left = jnp.where(j > 0, 320, 384)
    return ((rr < below) | (rr >= above)) & ((ll < right) | (ll >= left))


def flat_place(counts):
    i, j = place()
    nr, nc = counts
    shape = table_shape(counts)
    flat = rows_of(shape) * 128 + lanes_of(shape)
    device = flat % (nr * nc)
    return flat, (device // nc + nr - i) % nr, (device % nc + nc - j) % nc


def table_shape(counts):
    return (-(-2 * counts[0] * counts[1] // 1024) * 8, 128)


def table_of(values, counts):
    flat, rows, cols = flat_place(counts)
    devices = counts[0] * counts[1]
    own = jnp.where(flat < devices, values[0], jnp.where(flat < 2 * devices, values[1], 0.0))
    return jnp.where((rows == 0) & (cols == 0), own, 0.0)


def as_row(table, width):
    return jnp.concatenate([table[k : k + 1] for k in range(width // 128)], axis=1)


def row_of(pairs):
    lane = lanes_of((1, 128))
    row = jnp.zeros((1, 128), jnp.float32)
    for k, (left, right) in enumerate(pairs):
        row = jnp.where(lane == k, left, jnp.where(lane == 64 + k, right, row))
    return row


def gathered(rows, width):
    devices = rows.shape[0]
    turned = rows.T
    parts = [turned[:16], turned[64:80]]
    if width > 2 * devices:
        parts.append(jnp.zeros((16, width - 2 * devices), jnp.float32))
    return jnp.concatenate(parts, axis=1)


def coarse_values(c_row, inverse):
    return dot(jnp.broadcast_to(c_row, (8, c_row.shape[1])), inverse)[:1]


def spread(g_row, counts):
    i, j = place()
    nr, nc = counts[0], 2 * counts[1]
    shape = (16, g_row.shape[1])
    which = rows_of(shape)
    r = i - 1 + which // 4
    c = 2 * j - 1 + which % 4
    inside = (r >= 0) & (r < nr) & (c >= 0) & (c < nc) & (which < 12)
    at = lax.rem(c + 2, 2) * (nr * counts[1]) + r * counts[1] + (c + 2) // 2 - 1
    picked = jnp.where(inside & (lanes_of(shape) == at), g_row, 0.0)
    picked = jnp.sum(picked, axis=1, keepdims=True)
    lane = lanes_of((1, 128))
    bands = []
    for d in range(3):
        left, first, second, right = (picked[4 * d + k : 4 * d + k + 1] for k in range(4))
        bands.append(
            jnp.concatenate(
                [
                    jnp.broadcast_to(first, (1, 128)),
                    jnp.broadcast_to(second, (1, 128)),
                    jnp.where(lane < 64, right, left),
                ],
                axis=1,
            )
        )
    return jnp.concatenate(
        [
            jnp.broadcast_to(bands[1], (128, FC)),
            jnp.broadcast_to(bands[2], (16, FC)),
            jnp.broadcast_to(bands[0], (16, FC)),
        ],
        axis=0,
    )


def local_solve(w, means, basis_ref):
    rows, rows_t, cols, cols_t, scale = block_parts(basis_ref)
    lane = lanes_of((1, 2 * SPEC))
    mean = jnp.where(lane < SPEC, means[0], means[1])
    t = dot(dot(rows_t, w), cols)
    t = t / (DAMP + mean * scale)
    return dot(rows, dot(t, cols_t))


def core_sums(x):
    return [total(x[:, :128]), total(x[:, 128:256])]


def pack_columns(y):
    lane = lanes_of((FR, 128))
    packed = jnp.where(
        lane < 16,
        y[:, :128],
        jnp.where(lane >= 112, y[:, 128:256], pltpu.roll(y[:, 256:], 64, 1)),
    )
    turned = packed.T
    to_left = jnp.concatenate([turned[56:64], turned[:16]], axis=0)
    to_right = jnp.concatenate([turned[112:], turned[64:72]], axis=0)
    return to_left, to_right


def add_columns(y, from_left, from_right):
    turned = jnp.concatenate(
        [
            from_right[8:24],
            jnp.zeros((40, FR), jnp.float32),
            from_right[:8],
            from_left[16:24],
            jnp.zeros((40, FR), jnp.float32),
            from_left[:16],
        ],
        axis=0,
    )
    back = turned.T
    lane = lanes_of((FR, 128))
    rolled = pltpu.roll(back, 64, 1)
    first = y[:, :128] + jnp.where(lane < 8, rolled, 0.0)
    second = y[:, 128:256] + jnp.where(lane >= 120, rolled, 0.0)
    third = y[:, 256:] + jnp.where((lane < 16) | (lane >= 112), back, 0.0)
    return jnp.concatenate([first, second, third], axis=1)


def pack_rows(y):
    return jnp.concatenate([y[152:160], y[:16]], axis=0), y[112:136]


def add_rows(y, from_above, from_below):
    return jnp.concatenate(
        [
            y[:8] + from_above[16:24],
            y[8:120],
            y[120:144] + from_below,
            y[144:] + from_above[:16],
        ],
        axis=0,
    )


def sides(index, count, a, b):
    even = is_even(index)
    before = jnp.where(index > 0, jnp.where(even, b, a), 0.0)
    after = jnp.where(index < count - 1, jnp.where(even, a, b), 0.0)
    return before, after


def next_table(index, a, b):
    return jnp.where(is_even(index), a, b)[24:, :128]


def send(index, a_ref, b_ref, before, after):
    even = is_even(index)
    a_ref[...] = jnp.where(even, after, before)
    b_ref[...] = jnp.where(even, before, after)


def begin_kernel(counts, both_ref, a_ref, b_ref):
    r, h = both_ref[:TR], both_ref[TR:]
    lane = lanes_of((128, 128))
    packed = jnp.where(
        lane < 16,
        r[:, :128],
        jnp.where(
            lane < 64,
            pltpu.roll(h[:, :128], 16, 1),
            jnp.where(lane < 112, pltpu.roll(h[:, 128:], 112, 1), r[:, 128:]),
        ),
    )
    turned = packed.T
    table = table_of(core_sums(r), counts)
    send(
        lax.axis_index("col"),
        a_ref,
        b_ref,
        jnp.concatenate([turned[:32], table], axis=0),
        jnp.concatenate([turned[96:], table], axis=0),
    )


def widen_kernel(counts, both_ref, ga_ref, gb_ref, r3_ref, h3_ref, table_ref, a_ref, b_ref):
    i, j = place()
    from_left, from_right = sides(j, counts[1], ga_ref[:32], gb_ref[:32])
    turned = jnp.concatenate([from_right, jnp.zeros((64, 128), jnp.float32), from_left], axis=0)
    back = turned.T
    lane = lanes_of((128, 128))
    edge = (lane < 16) | (lane >= 112)
    r3 = jnp.where(edge, back, 0.0)
    h3 = jnp.where(
        lane < 16, pltpu.roll(back, 112, 1), jnp.where(lane >= 112, pltpu.roll(back, 16, 1), 0.0)
    )
    r3_ref[...] = r3
    h3_ref[...] = h3
    r, h = both_ref[:TR], both_ref[TR:]
    table = table_of(core_sums(r), counts) + ga_ref[32:] + gb_ref[32:]
    table_ref[...] = table
    wide = jnp.concatenate([table, jnp.zeros((table.shape[0], FC - 128), jnp.float32)], axis=1)

    def strip(r_rows, h_rows):
        return jnp.concatenate(
            [
                jnp.concatenate([r[r_rows], r3[r_rows]], axis=1),
                jnp.concatenate([h[h_rows], h3[h_rows]], axis=1),
                wide,
            ],
            axis=0,
        )

    send(i, a_ref, b_ref, strip(slice(0, 8), slice(0, 16)), strip(slice(120, 128), slice(112, 128)))


def first_kernel(
    counts, both_ref, r3_ref, h3_ref, ga_ref, gb_ref, basis_ref, y_ref, m_ref, a_ref, b_ref
):
    i, j = place()
    above, below = sides(i, counts[0], ga_ref[:24], gb_ref[:24])
    r = jnp.concatenate([both_ref[:TR], r3_ref[...]], axis=1)
    h = jnp.concatenate([both_ref[TR:], h3_ref[...]], axis=1)
    wide = jnp.concatenate([r, below[:8], jnp.zeros((16, FC), jnp.float32), above[:8]], axis=0)
    tall = jnp.concatenate([h, below[8:], above[8:]], axis=0)
    mobility = tall * tall * tall
    m_ref[...] = mobility
    means = [x / (SUB * SUB) for x in core_sums(mobility[:128])]
    y = local_solve(wide, means, basis_ref)
    y_ref[...] = y
    send(j, a_ref, b_ref, *pack_columns(y))


def columns_kernel(counts, y_ref, ga_ref, gb_ref, *refs):
    i, j = place()
    y = add_columns(y_ref[...], *sides(j, counts[1], ga_ref[:24], gb_ref[:24]))
    strips = pack_rows(y)
    if len(refs) == 5:
        table_ref, out_ref, table_out, a_ref, b_ref = refs
        cols = flat_place(counts)[2]
        table = table_ref[...] + jnp.where(
            cols % 4 == 2, next_table(j, ga_ref[...], gb_ref[...]), 0.0
        )
        table_out[...] = table
        wide = jnp.concatenate([table, jnp.zeros((table.shape[0], FC - 128), jnp.float32)], axis=1)
        strips = [jnp.concatenate([x, wide], axis=0) for x in strips]
    else:
        out_ref, a_ref, b_ref = refs
    out_ref[...] = y
    send(i, a_ref, b_ref, *strips)


def second_kernel(
    counts,
    width,
    y_ref,
    m_ref,
    ga_ref,
    gb_ref,
    table_ref,
    both_ref,
    basis_ref,
    z_ref,
    w_ref,
    y2_ref,
    table_out,
    stats_ref,
    a_ref,
    b_ref,
):
    i, j = place()
    s = add_rows(y_ref[...], *sides(i, counts[0], ga_ref[:24], gb_ref[:24]))
    mask = grid_mask((FR, FC), counts)
    s = jnp.where(mask, s, 0.0)
    rows = flat_place(counts)[1]
    table = table_ref[...] + jnp.where(rows % 4 == 2, next_table(i, ga_ref[...], gb_ref[...]), 0.0)
    table_out[...] = table
    c0 = as_row(table, width)
    coarse = spread(coarse_values(c0, coarse_part(basis_ref, width)), counts)
    mobility = m_ref[...]
    flow = mobility * (lap(s) + lap(coarse))
    z = s + coarse
    w = jnp.where(mask, DAMP * z + lap(flow), 0.0) * SHRINK
    zt, wt, rt, mt = z[:128, :256], w[:128, :256], both_ref[:TR], mobility[:128, :256]
    z_ref[...] = zt
    w_ref[...] = wt
    means = [x / (SUB * SUB) for x in core_sums(mt)]
    y = local_solve(w, means, basis_ref)
    y2_ref[...] = y
    send(j, a_ref, b_ref, *pack_columns(y))
    lane, row = lanes_of((1, 256)), rows_of((128, 1))
    along = (lane % 128 != 0) & (lane % 128 != 127)
    top, low = mt[:1], mt[127:]
    side = jnp.sum(jnp.where((row > 0) & (row < 127), mt, 0.0), axis=0, keepdims=True)

    def halves(x):
        return [
            jnp.sum(x[:, :128], axis=1, keepdims=True),
            jnp.sum(x[:, 128:], axis=1, keepdims=True),
        ]

    first, last = lane % 128 == 0, lane % 128 == 127
    stats_ref[...] = row_of(
        [
            core_sums(rt * zt),
            core_sums(zt * wt),
            core_sums(wt),
            halves(jnp.where(along, top, 0.0)),
            halves(jnp.where(along, low, 0.0)),
            halves(jnp.where(first, side, 0.0)),
            halves(jnp.where(last, side, 0.0)),
            halves(jnp.where(first, top, 0.0)),
            halves(jnp.where(last, top, 0.0)),
            halves(jnp.where(first, low, 0.0)),
            halves(jnp.where(last, low, 0.0)),
        ]
    )


def dots_kernel(
    counts, y_ref, m_ref, ga_ref, gb_ref, both_ref, w_ref, stats_ref, q_ref, v_ref, stats_out
):
    i, j = place()
    q = add_rows(y_ref[...], *sides(i, counts[0], ga_ref[...], gb_ref[...]))
    q = jnp.where(grid_mask((FR, FC), counts), q, 0.0)
    v = DAMP * q + lap(m_ref[...] * lap(q))
    qt, vt = q[:128, :256], v[:128, :256]
    q_ref[...] = qt
    v_ref[...] = vt
    rest = [
        core_sums(vt),
        core_sums(both_ref[:TR] * qt),
        core_sums(w_ref[...] * qt),
        core_sums(vt * qt),
    ]
    zero = jnp.zeros((1, 1), jnp.float32)
    row = stats_ref[...] + row_of([[zero, zero]] * 11 + rest)
    stats_out[...] = jnp.broadcast_to(row, stats_out.shape)


def end_kernel(
    counts,
    width,
    stats_ref,
    table_ref,
    basis_ref,
    m_ref,
    both_ref,
    z_ref,
    w_ref,
    q_ref,
    v_ref,
    solution_ref,
    residual_ref,
):
    tiles_c = counts[1]
    devices = counts[0] * tiles_c
    table = gathered(stats_ref[...], width)
    st = [table[k : k + 1] for k in range(15)]

    def whole(x):
        return jnp.sum(x, axis=1, keepdims=True)

    rz, zw, rq, wq, qv = (whole(st[k]) for k in (0, 1, 12, 13, 14))
    c0, c1, sums_v = as_row(table_ref[...], width), st[2], st[11]
    g = coarse_values(c1, coarse_part(basis_ref, width))
    lane = lanes_of((1, width))
    cell = lane < 2 * devices
    on_left = lane < devices
    device = lane % devices
    column = device % tiles_c

    def from_lane(distance):
        return pltpu.roll(g, distance % width, 1)

    up = jnp.where(device >= tiles_c, from_lane(tiles_c), 0.0)
    down = jnp.where(device < devices - tiles_c, from_lane(-tiles_c), 0.0)
    left = jnp.where(
        on_left, jnp.where(column > 0, from_lane(1 - devices), 0.0), from_lane(devices)
    )
    right = jnp.where(
        on_left,
        from_lane(-devices),
        jnp.where(column < tiles_c - 1, from_lane(devices - 1), 0.0),
    )
    du, dd, dl, dr = g - up, g - down, g - left, g - right
    energy = DAMP * SUB * SUB * g * g
    energy = energy + st[3] * du * du + st[4] * dd * dd + st[5] * dl * dl + st[6] * dr * dr
    for weight, p, q in ((st[7], du, dl), (st[8], du, dr), (st[9], dd, dl), (st[10], dd, dr)):
        both = p + q
        energy = energy + weight * both * both
    ry = rq + whole(g * c0)
    yw = wq + whole(g * c1)
    yv = qv + whole(jnp.where(cell, 2.0 * g * sums_v + energy, 0.0))
    a = rz / zw
    rz1 = rz - a * ry - a * zw + a * a * yw
    beta1 = 1.0 + rz1 / rz
    dad = (beta1 * beta1 * zw - 2.0 * a * beta1 * yw) * (1.0 / SHRINK) + a * a * yv
    a1 = rz1 / dad
    coarse = spread(g, counts)
    y = q_ref[...] + coarse[:128, :256]
    image = DAMP * coarse + lap(m_ref[...] * lap(coarse))
    v = v_ref[...] + image[:128, :256]
    z, w = z_ref[...], w_ref[...]
    solution_ref[...] = (a * SHRINK) * z + a1 * (beta1 * z - a * y)
    residual_ref[...] = both_ref[:TR] - a * w - a1 * ((beta1 * (1.0 / SHRINK)) * w - a * v)


def call(kernel, outs, *args, flops=10**9):
    shapes = [jax.ShapeDtypeStruct(s, jnp.float32) for s in outs]
    return pl.pallas_call(
        kernel,
        out_shape=shapes,
        compiler_params=pltpu.CompilerParams(vmem_limit_bytes=48 * 1024 * 1024),
        cost_estimate=pl.CostEstimate(flops=flops, bytes_accessed=10**6, transcendentals=0),
    )(*args)


def pairs_from(count, offset):
    found = []
    for k in range(offset, count, 2):
        found += [(k, (k + 1) % count), ((k + 1) % count, k)]
    return found


def body(counts, height, noise):
    nr, nc = counts
    devices = nr * nc
    width = max(128, devices * 2)
    basis = jnp.asarray(constants(nr, 2 * nc, width))
    both_axes = ("row", "col")
    depth = table_shape(counts)[0]

    def swap(a, b, axis):
        count = lax.axis_size(axis)
        return (
            lax.ppermute(a, axis, pairs_from(count, 0)),
            lax.ppermute(b, axis, pairs_from(count, 1)),
        )

    first = lax.broadcasted_iota(jnp.int32, (2, TR, TC), 0) == 0
    both = jnp.where(first, noise[None], height[None]).reshape(2 * TR, TC)
    a, b = call(functools.partial(begin_kernel, counts), [(32 + depth, 128)] * 2, both)
    ga, gb = swap(a, b, "col")
    r3, h3, table, a, b = call(
        functools.partial(widen_kernel, counts),
        [(128, 128)] * 2 + [(depth, 128)] + [(24 + depth, FC)] * 2,
        both,
        ga,
        gb,
    )
    ga, gb = swap(a, b, "row")
    table = table + ga[24:, :128] + gb[24:, :128]
    y, m, a, b = call(
        functools.partial(first_kernel, counts),
        [(FR, FC)] * 2 + [(24, FR)] * 2,
        both,
        r3,
        h3,
        ga,
        gb,
        basis,
    )
    for axis, count in (("row", nr), ("col", nc)):
        step = count // 2
        while step >= 4:
            shift = [(k, (k + step) % count) for k in range(count)]
            table = table + lax.ppermute(table, axis, shift)
            step //= 2
    wide = jnp.pad(table, ((0, 0), (0, FR - 128)))
    ga, gb = swap(*(jnp.concatenate([x, wide], axis=0) for x in (a, b)), "col")
    y, table, a, b = call(
        functools.partial(columns_kernel, counts),
        [(FR, FC), (depth, 128)] + [(24 + depth, FC)] * 2,
        y,
        ga,
        gb,
        table,
    )
    ga, gb = swap(a, b, "row")
    z, w, y, table, stats, a, b = call(
        functools.partial(second_kernel, counts, width),
        [(TR, TC)] * 2 + [(FR, FC), (depth, 128), (1, 128)] + [(24, FR)] * 2,
        y,
        m,
        ga,
        gb,
        table,
        both,
        basis,
    )
    ga, gb = swap(a, b, "col")
    y, a, b = call(
        functools.partial(columns_kernel, counts), [(FR, FC)] + [(24, FC)] * 2, y, ga, gb
    )
    ga, gb = swap(a, b, "row")
    q, v, stats = call(
        functools.partial(dots_kernel, counts),
        [(TR, TC)] * 2 + [(devices, 128)],
        y,
        m,
        ga,
        gb,
        both,
        w,
        stats,
    )
    stats = lax.all_to_all(stats, both_axes, 0, 0, tiled=True)
    return tuple(
        call(
            functools.partial(end_kernel, counts, width),
            [(TR, TC)] * 2,
            stats,
            table,
            basis,
            m,
            both,
            z,
            w,
            q,
            v,
        )
    )


def solution(mesh):
    counts = (mesh.shape["row"], mesh.shape["col"])
    spec = P("row", "col")
    return jax.shard_map(
        functools.partial(body, counts),
        mesh=mesh,
        in_specs=(spec, spec),
        out_specs=(spec, spec),
        check_vma=False,
    )
```

```python
import functools

import jax
import jax.numpy as jnp
import numpy as np
from jax import lax
from jax.experimental import pallas as pl
from jax.experimental.pallas import tpu as pltpu
from jax.sharding import PartitionSpec as P

SUB = 128
OV = 8
EXT = SUB + 2 * OV
DAMP = 2.0**-28
SHRINK = 2.0**-20

TR, TC = 128, 256
FR, FC = 160, 384
SPEC = 192

highest = lax.Precision.HIGHEST


def sine(count):
    k = np.arange(1, count + 1, dtype=np.float64)
    basis = np.sqrt(2.0 / (count + 1.0)) * np.sin(np.pi * k[:, None] * k[None, :] / (count + 1.0))
    return basis, 2.0 - 2.0 * np.cos(np.pi * k / (count + 1.0))


def block_constants():
    basis, eig = sine(EXT)
    rows = np.zeros((FR, EXT))
    cols = np.zeros((FC, 2 * SPEC))
    for at in range(EXT):
        rows[(at - OV) % FR] = basis[at]
        for b in range(2):
            cols[(b * SUB + at - OV) % FC, b * SPEC : b * SPEC + EXT] = basis[at]
    scale = np.ones((EXT, 2 * SPEC))
    for b in range(2):
        scale[:, b * SPEC : b * SPEC + EXT] = (eig[:, None] + eig[None, :]) ** 2
    wide = lambda x: np.pad(x, ((0, 0), (0, FC - x.shape[1])))
    return [cols, cols.T, scale, wide(rows), wide(rows.T)]


def block_parts(ref):
    cols, cols_t, scale = ref[:FC], ref[FC : 2 * FC], ref[2 * FC : 2 * FC + EXT]
    at = 2 * FC + EXT
    return ref[at : at + FR, :EXT], ref[at + FR : at + FR + EXT, :FR], cols, cols_t, scale


def coarse_part(ref, width):
    at = 2 * FC + 2 * EXT + FR
    parts = [ref[at + k * width : at + (k + 1) * width] for k in range(-(-width // FC))]
    return (parts[0] if len(parts) == 1 else jnp.concatenate(parts, axis=1))[:, :width]


def constants(nr, nc, width):
    inverse = coarse_inverse(nr, nc, -(-width // FC) * FC)[:width]
    return np.concatenate([*block_constants(), *np.split(inverse, inverse.shape[1] // FC, 1)], dtype=np.float32)


def coarse_inverse(nr, nc, width):
    br, er = sine(nr)
    bc, ec = sine(nc)
    both = np.kron(br, bc).reshape(nr, nc // 2, 2, nr * nc).transpose(2, 0, 1, 3)
    both = both.reshape(nr * nc, nr * nc)
    scale = (er[:, None] + ec[None, :]) / (SUB * SUB)
    values = (SUB * SUB * (DAMP + scale * scale)).reshape(-1)
    whole = np.zeros((width, width), np.float32)
    whole[: nr * nc, : nr * nc] = (both / values) @ both.T
    return whole


def dot(a, b):
    return lax.dot_general(
        a, b, (((1,), (0,)), ((), ())), precision=highest, preferred_element_type=jnp.float32
    )


def lap(x):
    rows, lanes = x.shape
    beside = pltpu.roll(x, 1, 0) + pltpu.roll(x, rows - 1, 0)
    beside = beside + (pltpu.roll(x, 1, 1) + pltpu.roll(x, lanes - 1, 1))
    return 4.0 * x - beside


def lanes_of(shape):
    return lax.broadcasted_iota(jnp.int32, shape, 1)


def rows_of(shape):
    return lax.broadcasted_iota(jnp.int32, shape, 0)


def total(x):
    return jnp.sum(jnp.sum(x, axis=0, keepdims=True), axis=1, keepdims=True)


def place():
    return lax.axis_index("row"), lax.axis_index("col")


def is_even(index):
    return lax.rem(index, 2) == 0


def grid_mask(shape, counts):
    i, j = place()
    rr, ll = rows_of(shape), lanes_of(shape)
    below = jnp.where(i < counts[0] - 1, 144, 128)
    above = jnp.where(i > 0, 144, 160)
    right = jnp.where(j < counts[1] - 1, 320, 256)
    left = jnp.where(j > 0, 320, 384)
    return ((rr < below) | (rr >= above)) & ((ll < right) | (ll >= left))


def flat_place(counts):
    i, j = place()
    nr, nc = counts
    shape = table_shape(counts)
    flat = rows_of(shape) * 128 + lanes_of(shape)
    device = flat % (nr * nc)
    return flat, (device // nc + nr - i) % nr, (device % nc + nc - j) % nc


def table_shape(counts):
    return (-(-2 * counts[0] * counts[1] // 1024) * 8, 128)


def table_of(values, counts):
    flat, rows, cols = flat_place(counts)
    devices = counts[0] * counts[1]
    own = jnp.where(flat < devices, values[0], jnp.where(flat < 2 * devices, values[1], 0.0))
    return jnp.where((rows == 0) & (cols == 0), own, 0.0)


def as_row(table, width):
    return jnp.concatenate([table[k : k + 1] for k in range(width // 128)], axis=1)


def row_of(pairs):
    lane = lanes_of((1, 128))
    row = jnp.zeros((1, 128), jnp.float32)
    for k, (left, right) in enumerate(pairs):
        row = jnp.where(lane == k, left, jnp.where(lane == 64 + k, right, row))
    return row


def gathered(rows, width):
    devices = rows.shape[0]
    turned = rows.T
    parts = [turned[:16], turned[64:80]]
    if width > 2 * devices:
        parts.append(jnp.zeros((16, width - 2 * devices), jnp.float32))
    return jnp.concatenate(parts, axis=1)


def coarse_values(c_row, inverse):
    return dot(jnp.broadcast_to(c_row, (8, c_row.shape[1])), inverse)[:1]


def spread(g_row, counts):
    i, j = place()
    nr, nc = counts[0], 2 * counts[1]
    shape = (16, g_row.shape[1])
    which = rows_of(shape)
    r = i - 1 + which // 4
    c = 2 * j - 1 + which % 4
    inside = (r >= 0) & (r < nr) & (c >= 0) & (c < nc) & (which < 12)
    at = lax.rem(c + 2, 2) * (nr * counts[1]) + r * counts[1] + (c + 2) // 2 - 1
    picked = jnp.where(inside & (lanes_of(shape) == at), g_row, 0.0)
    picked = jnp.sum(picked, axis=1, keepdims=True)
    lane = lanes_of((1, 128))
    bands = []
    for d in range(3):
        left, first, second, right = (picked[4 * d + k : 4 * d + k + 1] for k in range(4))
        bands.append(
            jnp.concatenate(
                [
                    jnp.broadcast_to(first, (1, 128)),
                    jnp.broadcast_to(second, (1, 128)),
                    jnp.where(lane < 64, right, left),
                ],
                axis=1,
            )
        )
    return jnp.concatenate(
        [
            jnp.broadcast_to(bands[1], (128, FC)),
            jnp.broadcast_to(bands[2], (16, FC)),
            jnp.broadcast_to(bands[0], (16, FC)),
        ],
        axis=0,
    )


def local_solve(w, means, basis_ref):
    rows, rows_t, cols, cols_t, scale = block_parts(basis_ref)
    lane = lanes_of((1, 2 * SPEC))
    mean = jnp.where(lane < SPEC, means[0], means[1])
    t = dot(dot(rows_t, w), cols)
    t = t / (DAMP + mean * scale)
    return dot(rows, dot(t, cols_t))


def core_sums(x):
    return [total(x[:, :128]), total(x[:, 128:256])]


def pack_columns(y):
    lane = lanes_of((FR, 128))
    packed = jnp.where(
        lane < 16,
        y[:, :128],
        jnp.where(lane >= 112, y[:, 128:256], pltpu.roll(y[:, 256:], 64, 1)),
    )
    turned = packed.T
    to_left = jnp.concatenate([turned[56:64], turned[:16]], axis=0)
    to_right = jnp.concatenate([turned[112:], turned[64:72]], axis=0)
    return to_left, to_right


def add_columns(y, from_left, from_right):
    turned = jnp.concatenate(
        [
            from_right[8:24],
            jnp.zeros((40, FR), jnp.float32),
            from_right[:8],
            from_left[16:24],
            jnp.zeros((40, FR), jnp.float32),
            from_left[:16],
        ],
        axis=0,
    )
    back = turned.T
    lane = lanes_of((FR, 128))
    rolled = pltpu.roll(back, 64, 1)
    first = y[:, :128] + jnp.where(lane < 8, rolled, 0.0)
    second = y[:, 128:256] + jnp.where(lane >= 120, rolled, 0.0)
    third = y[:, 256:] + jnp.where((lane < 16) | (lane >= 112), back, 0.0)
    return jnp.concatenate([first, second, third], axis=1)


def pack_rows(y):
    return jnp.concatenate([y[152:160], y[:16]], axis=0), y[112:136]


def add_rows(y, from_above, from_below):
    return jnp.concatenate(
        [
            y[:8] + from_above[16:24],
            y[8:120],
            y[120:144] + from_below,
            y[144:] + from_above[:16],
        ],
        axis=0,
    )


def sides(index, count, a, b):
    even = is_even(index)
    before = jnp.where(index > 0, jnp.where(even, b, a), 0.0)
    after = jnp.where(index < count - 1, jnp.where(even, a, b), 0.0)
    return before, after


def side_columns(ref, count, depth):
    j = lax.axis_index("col")
    left = ref[jnp.maximum(j - 1, 0), :depth]
    right = ref[jnp.minimum(j + 1, count - 1), :depth]
    return jnp.where(j > 0, left, 0.0), jnp.where(j < count - 1, right, 0.0)


def send_columns(ref, to_left, to_right):
    j = lax.axis_index("col")
    for k in range(ref.shape[0]):
        ref[k] = jnp.where(k > j, to_right, to_left)


def row_tables(index, nr, rows, a, b):
    even = is_even(index)
    after = jnp.where(even, a, b)[24:, :128]
    before = jnp.where(even, b, a)[24:, :128]
    if nr == 4:
        return jnp.where(rows == 2, after, 0.0)
    far = rows % 8
    return jnp.where(
        (far == 2) | (far == 5), after, jnp.where((far == 3) | (far == 6), before, 0.0)
    )


def send(index, a_ref, b_ref, before, after):
    even = is_even(index)
    a_ref[...] = jnp.where(even, after, before)
    b_ref[...] = jnp.where(even, before, after)


def begin_kernel(counts, both_ref, out_ref):
    r, h = both_ref[:TR], both_ref[TR:]
    lane = lanes_of((128, 128))
    packed = jnp.where(
        lane < 16,
        r[:, :128],
        jnp.where(
            lane < 64,
            pltpu.roll(h[:, :128], 16, 1),
            jnp.where(lane < 112, pltpu.roll(h[:, 128:], 112, 1), r[:, 128:]),
        ),
    )
    turned = packed.T
    table = table_of(core_sums(r), counts)
    send_columns(
        out_ref,
        jnp.concatenate([turned[:32], table], axis=0),
        jnp.concatenate([turned[96:], table], axis=0),
    )


def widen_kernel(counts, both_ref, got_ref, r3_ref, h3_ref, table_ref, a_ref, b_ref):
    i, j = place()
    from_left, from_right = side_columns(got_ref, counts[1], 32)
    turned = jnp.concatenate([from_right, jnp.zeros((64, 128), jnp.float32), from_left], axis=0)
    back = turned.T
    lane = lanes_of((128, 128))
    edge = (lane < 16) | (lane >= 112)
    r3 = jnp.where(edge, back, 0.0)
    h3 = jnp.where(
        lane < 16, pltpu.roll(back, 112, 1), jnp.where(lane >= 112, pltpu.roll(back, 16, 1), 0.0)
    )
    r3_ref[...] = r3
    h3_ref[...] = h3
    r, h = both_ref[:TR], both_ref[TR:]
    table = sum(got_ref[k, 32:] for k in range(counts[1]))
    table_ref[...] = table
    wide = jnp.concatenate([table, jnp.zeros((table.shape[0], FC - 128), jnp.float32)], axis=1)

    def strip(r_rows, h_rows):
        return jnp.concatenate(
            [
                jnp.concatenate([r[r_rows], r3[r_rows]], axis=1),
                jnp.concatenate([h[h_rows], h3[h_rows]], axis=1),
                wide,
            ],
            axis=0,
        )

    send(i, a_ref, b_ref, strip(slice(0, 8), slice(0, 16)), strip(slice(120, 128), slice(112, 128)))


def first_kernel(
    counts, both_ref, r3_ref, h3_ref, ga_ref, gb_ref, basis_ref, y_ref, m_ref, out_ref
):
    i, j = place()
    above, below = sides(i, counts[0], ga_ref[:24], gb_ref[:24])
    r = jnp.concatenate([both_ref[:TR], r3_ref[...]], axis=1)
    h = jnp.concatenate([both_ref[TR:], h3_ref[...]], axis=1)
    wide = jnp.concatenate([r, below[:8], jnp.zeros((16, FC), jnp.float32), above[:8]], axis=0)
    tall = jnp.concatenate([h, below[8:], above[8:]], axis=0)
    mobility = tall * tall * tall
    m_ref[...] = mobility
    means = [x / (SUB * SUB) for x in core_sums(mobility[:128])]
    y = local_solve(wide, means, basis_ref)
    y_ref[...] = y
    send_columns(out_ref, *pack_columns(y))


def columns_kernel(counts, y_ref, got_ref, *refs):
    y = add_columns(y_ref[...], *side_columns(got_ref, counts[1], 24))
    strips = pack_rows(y)
    if len(refs) == 4:
        table = refs[0][...]
        wide = jnp.concatenate([table, jnp.zeros((table.shape[0], FC - 128), jnp.float32)], axis=1)
        strips = [jnp.concatenate([x, wide], axis=0) for x in strips]
    out_ref, a_ref, b_ref = refs[-3:]
    out_ref[...] = y
    send(lax.axis_index("row"), a_ref, b_ref, *strips)


def second_kernel(
    counts,
    width,
    y_ref,
    m_ref,
    ga_ref,
    gb_ref,
    table_ref,
    both_ref,
    basis_ref,
    z_ref,
    w_ref,
    y2_ref,
    table_out,
    stats_ref,
    out_ref,
):
    i, j = place()
    s = add_rows(y_ref[...], *sides(i, counts[0], ga_ref[:24], gb_ref[:24]))
    mask = grid_mask((FR, FC), counts)
    s = jnp.where(mask, s, 0.0)
    rows = flat_place(counts)[1]
    table = table_ref[...] + row_tables(i, counts[0], rows, ga_ref[...], gb_ref[...])
    table_out[...] = table
    c0 = as_row(table, width)
    coarse = spread(coarse_values(c0, coarse_part(basis_ref, width)), counts)
    mobility = m_ref[...]
    flow = mobility * (lap(s) + lap(coarse))
    z = s + coarse
    w = jnp.where(mask, DAMP * z + lap(flow), 0.0) * SHRINK
    zt, wt, rt, mt = z[:128, :256], w[:128, :256], both_ref[:TR], mobility[:128, :256]
    z_ref[...] = zt
    w_ref[...] = wt
    means = [x / (SUB * SUB) for x in core_sums(mt)]
    y = local_solve(w, means, basis_ref)
    y2_ref[...] = y
    send_columns(out_ref, *pack_columns(y))
    lane, row = lanes_of((1, 256)), rows_of((128, 1))
    along = (lane % 128 != 0) & (lane % 128 != 127)
    top, low = mt[:1], mt[127:]
    side = jnp.sum(jnp.where((row > 0) & (row < 127), mt, 0.0), axis=0, keepdims=True)

    def halves(x):
        return [
            jnp.sum(x[:, :128], axis=1, keepdims=True),
            jnp.sum(x[:, 128:], axis=1, keepdims=True),
        ]

    first, last = lane % 128 == 0, lane % 128 == 127
    stats_ref[...] = row_of(
        [
            core_sums(rt * zt),
            core_sums(zt * wt),
            core_sums(wt),
            halves(jnp.where(along, top, 0.0)),
            halves(jnp.where(along, low, 0.0)),
            halves(jnp.where(first, side, 0.0)),
            halves(jnp.where(last, side, 0.0)),
            halves(jnp.where(first, top, 0.0)),
            halves(jnp.where(last, top, 0.0)),
            halves(jnp.where(first, low, 0.0)),
            halves(jnp.where(last, low, 0.0)),
        ]
    )


def dots_kernel(
    counts, y_ref, m_ref, ga_ref, gb_ref, both_ref, w_ref, stats_ref, q_ref, v_ref, stats_out
):
    i, j = place()
    q = add_rows(y_ref[...], *sides(i, counts[0], ga_ref[...], gb_ref[...]))
    q = jnp.where(grid_mask((FR, FC), counts), q, 0.0)
    v = DAMP * q + lap(m_ref[...] * lap(q))
    qt, vt = q[:128, :256], v[:128, :256]
    q_ref[...] = qt
    v_ref[...] = vt
    rest = [
        core_sums(vt),
        core_sums(both_ref[:TR] * qt),
        core_sums(w_ref[...] * qt),
        core_sums(vt * qt),
    ]
    zero = jnp.zeros((1, 1), jnp.float32)
    row = stats_ref[...] + row_of([[zero, zero]] * 11 + rest)
    stats_out[...] = jnp.broadcast_to(row, stats_out.shape)


def end_kernel(
    counts,
    width,
    stats_ref,
    table_ref,
    basis_ref,
    m_ref,
    both_ref,
    z_ref,
    w_ref,
    q_ref,
    v_ref,
    solution_ref,
    residual_ref,
):
    tiles_c = counts[1]
    devices = counts[0] * tiles_c
    table = gathered(stats_ref[...], width)
    st = [table[k : k + 1] for k in range(15)]

    def whole(x):
        return jnp.sum(x, axis=1, keepdims=True)

    rz, zw, rq, wq, qv = (whole(st[k]) for k in (0, 1, 12, 13, 14))
    c0, c1, sums_v = as_row(table_ref[...], width), st[2], st[11]
    g = coarse_values(c1, coarse_part(basis_ref, width))
    lane = lanes_of((1, width))
    cell = lane < 2 * devices
    on_left = lane < devices
    device = lane % devices
    column = device % tiles_c

    def from_lane(distance):
        return pltpu.roll(g, distance % width, 1)

    up = jnp.where(device >= tiles_c, from_lane(tiles_c), 0.0)
    down = jnp.where(device < devices - tiles_c, from_lane(-tiles_c), 0.0)
    left = jnp.where(
        on_left, jnp.where(column > 0, from_lane(1 - devices), 0.0), from_lane(devices)
    )
    right = jnp.where(
        on_left,
        from_lane(-devices),
        jnp.where(column < tiles_c - 1, from_lane(devices - 1), 0.0),
    )
    du, dd, dl, dr = g - up, g - down, g - left, g - right
    energy = DAMP * SUB * SUB * g * g
    energy = energy + st[3] * du * du + st[4] * dd * dd + st[5] * dl * dl + st[6] * dr * dr
    for weight, p, q in ((st[7], du, dl), (st[8], du, dr), (st[9], dd, dl), (st[10], dd, dr)):
        both = p + q
        energy = energy + weight * both * both
    ry = rq + whole(g * c0)
    yw = wq + whole(g * c1)
    yv = qv + whole(jnp.where(cell, 2.0 * g * sums_v + energy, 0.0))
    a = rz / zw
    rz1 = rz - a * ry - a * zw + a * a * yw
    beta1 = 1.0 + rz1 / rz
    dad = (beta1 * beta1 * zw - 2.0 * a * beta1 * yw) * (1.0 / SHRINK) + a * a * yv
    a1 = rz1 / dad
    coarse = spread(g, counts)
    y = q_ref[...] + coarse[:128, :256]
    image = DAMP * coarse + lap(m_ref[...] * lap(coarse))
    v = v_ref[...] + image[:128, :256]
    z, w = z_ref[...], w_ref[...]
    solution_ref[...] = (a * SHRINK) * z + a1 * (beta1 * z - a * y)
    residual_ref[...] = both_ref[:TR] - a * w - a1 * ((beta1 * (1.0 / SHRINK)) * w - a * v)


def call(kernel, outs, *args, flops=10**9):
    shapes = [jax.ShapeDtypeStruct(s, jnp.float32) for s in outs]
    return pl.pallas_call(
        kernel,
        out_shape=shapes,
        compiler_params=pltpu.CompilerParams(vmem_limit_bytes=48 * 1024 * 1024),
        cost_estimate=pl.CostEstimate(flops=flops, bytes_accessed=10**6, transcendentals=0),
    )(*args)


def pairs_from(count, offset):
    found = []
    for k in range(offset, count, 2):
        found += [(k, (k + 1) % count), ((k + 1) % count, k)]
    return found


def body(counts, height, noise):
    nr, nc = counts
    devices = nr * nc
    width = max(128, devices * 2)
    basis = jnp.asarray(constants(nr, 2 * nc, width))
    both_axes = ("row", "col")
    depth = table_shape(counts)[0]

    def columns(x):
        return lax.all_to_all(x, "col", 0, 0, tiled=True)

    def rows(a, b):
        return lax.ppermute(a, "row", pairs_from(nr, 0)), lax.ppermute(b, "row", pairs_from(nr, 1))

    def row_shift(x, step):
        return lax.ppermute(x, "row", [(k, (k + step) % nr) for k in range(nr)])

    both = jnp.pad(noise, ((0, TR), (0, 0))) + jnp.pad(height, ((TR, 0), (0, 0)))
    out = call(functools.partial(begin_kernel, counts), [(nc, 32 + depth, 128)], both)[0]
    r3, h3, table, a, b = call(
        functools.partial(widen_kernel, counts),
        [(128, 128)] * 2 + [(depth, 128)] + [(24 + depth, FC)] * 2,
        both,
        columns(out),
    )
    step = nr // 2
    while step >= 8:
        table = table + row_shift(table, step)
        step //= 2
    if nr > 8:
        a, b = (x.at[24:, :128].set(table) for x in (a, b))
    ga, gb = rows(a, b)
    far = row_shift(table, 4) if nr >= 8 else 0.0
    y, m, out = call(
        functools.partial(first_kernel, counts),
        [(FR, FC)] * 2 + [(nc, 24, FR)],
        both,
        r3,
        h3,
        ga,
        gb,
        basis,
    )
    table = table + ga[24:, :128] + gb[24:, :128] + far
    y, a, b = call(
        functools.partial(columns_kernel, counts),
        [(FR, FC)] + [(24 + depth, FC)] * 2,
        y,
        columns(out),
        table,
    )
    ga, gb = rows(a, b)
    z, w, y, table, stats, out = call(
        functools.partial(second_kernel, counts, width),
        [(TR, TC)] * 2 + [(FR, FC), (depth, 128), (1, 128), (nc, 24, FR)],
        y,
        m,
        ga,
        gb,
        table,
        both,
        basis,
    )
    y, a, b = call(
        functools.partial(columns_kernel, counts),
        [(FR, FC)] + [(24, FC)] * 2,
        y,
        columns(out),
    )
    ga, gb = rows(a, b)
    q, v, stats = call(
        functools.partial(dots_kernel, counts),
        [(TR, TC)] * 2 + [(devices, 128)],
        y,
        m,
        ga,
        gb,
        both,
        w,
        stats,
    )
    stats = lax.all_to_all(stats, both_axes, 0, 0, tiled=True)
    return tuple(
        call(
            functools.partial(end_kernel, counts, width),
            [(TR, TC)] * 2,
            stats,
            table,
            basis,
            m,
            both,
            z,
            w,
            q,
            v,
        )
    )


def solution(mesh):
    counts = (mesh.shape["row"], mesh.shape["col"])
    spec = P("row", "col")
    return jax.shard_map(
        functools.partial(body, counts),
        mesh=mesh,
        in_specs=(spec, spec),
        out_specs=(spec, spec),
        check_vma=False,
    )
```

```python
import functools

import jax
import jax.numpy as jnp
import numpy as np
from jax import lax
from jax.experimental import pallas as pl
from jax.experimental.pallas import tpu as pltpu
from jax.sharding import PartitionSpec as P

SUB = 128
OV = 8
EXT = SUB + 2 * OV
DAMP = 2.0**-28
SHRINK = 2.0**-20

TR, TC = 128, 256
FR, FC = 160, 384
SPEC = 256

highest = lax.Precision.HIGHEST


def sine(count):
    k = np.arange(1, count + 1, dtype=np.float64)
    basis = np.sqrt(2.0 / (count + 1.0)) * np.sin(np.pi * k[:, None] * k[None, :] / (count + 1.0))
    return basis, 2.0 - 2.0 * np.cos(np.pi * k / (count + 1.0))


def block_constants():
    basis, eig = sine(EXT)
    rows = np.roll(basis, -OV, 0)
    cols = np.pad(basis, ((0, SPEC - EXT), (0, SPEC - EXT)))
    scale = np.pad((eig[:, None] + eig[None, :]) ** 2, ((0, 0), (0, SPEC - EXT)))
    wide = lambda x: np.pad(x, ((0, 0), (0, 2 * SPEC - x.shape[1])))
    return [np.tile(scale, (1, 2)), wide(rows), wide(rows.T), wide(cols)]


def rows_part(ref):
    return ref[EXT : 2 * EXT, :EXT]


def rows_t_part(ref):
    return ref[2 * EXT : 3 * EXT, :EXT]


def cols_part(ref):
    return ref[3 * EXT : 3 * EXT + SPEC, :SPEC]


def coarse_part(ref, width):
    at, lanes = 3 * EXT + SPEC, 2 * SPEC
    parts = [ref[at + k * width : at + (k + 1) * width] for k in range(-(-width // lanes))]
    return (parts[0] if len(parts) == 1 else jnp.concatenate(parts, axis=1))[:, :width]


def constants(nr, nc, width):
    lanes = 2 * SPEC
    inverse = coarse_inverse(nr, nc, -(-width // lanes) * lanes)[:width]
    parts = [*block_constants(), *np.split(inverse, inverse.shape[1] // lanes, 1)]
    return np.concatenate(parts).astype(np.float32)


def coarse_inverse(nr, nc, width):
    br, er = sine(nr)
    bc, ec = sine(nc)
    both = np.kron(br, bc).reshape(nr, nc // 2, 2, nr * nc).transpose(2, 0, 1, 3)
    both = both.reshape(nr * nc, nr * nc)
    scale = (er[:, None] + ec[None, :]) / (SUB * SUB)
    values = (SUB * SUB * (DAMP + scale * scale)).reshape(-1)
    whole = np.zeros((width, width), np.float32)
    whole[: nr * nc, : nr * nc] = (both / values) @ both.T
    return whole


def dot(a, b, side=0):
    return lax.dot_general(
        a, b, (((1,), (side,)), ((), ())), precision=highest, preferred_element_type=jnp.float32
    )


def lap(x):
    rows, lanes = x.shape
    beside = pltpu.roll(x, 1, 0) + pltpu.roll(x, rows - 1, 0)
    beside = beside + (pltpu.roll(x, 1, 1) + pltpu.roll(x, lanes - 1, 1))
    return 4.0 * x - beside


def lanes_of(shape):
    return lax.broadcasted_iota(jnp.int32, shape, 1)


def rows_of(shape):
    return lax.broadcasted_iota(jnp.int32, shape, 0)


def total(x):
    return jnp.sum(jnp.sum(x, axis=0, keepdims=True), axis=1, keepdims=True)


def place():
    return lax.axis_index("row"), lax.axis_index("col")


def is_even(index):
    return lax.rem(index, 2) == 0


def grid_mask(shape, counts):
    i, j = place()
    rr, ll = rows_of(shape), lanes_of(shape)
    below = jnp.where(i < counts[0] - 1, 144, 128)
    above = jnp.where(i > 0, 144, 160)
    right = jnp.where(j < counts[1] - 1, 320, 256)
    left = jnp.where(j > 0, 320, 384)
    return ((rr < below) | (rr >= above)) & ((ll < right) | (ll >= left))


def flat_place(counts):
    i, j = place()
    nr, nc = counts
    shape = table_shape(counts)
    flat = rows_of(shape) * 128 + lanes_of(shape)
    device = flat % (nr * nc)
    return flat, (device // nc + nr - i) % nr, (device % nc + nc - j) % nc


def table_shape(counts):
    return (-(-2 * counts[0] * counts[1] // 1024) * 8, 128)


def table_of(values, counts):
    flat, rows, cols = flat_place(counts)
    devices = counts[0] * counts[1]
    own = jnp.where(flat < devices, values[0], jnp.where(flat < 2 * devices, values[1], 0.0))
    return jnp.where((rows == 0) & (cols == 0), own, 0.0)


def as_row(table, width):
    return jnp.concatenate([table[k : k + 1] for k in range(width // 128)], axis=1)


def row_of(pairs):
    lane = lanes_of((1, 128))
    row = jnp.zeros((1, 128), jnp.float32)
    for k, (left, right) in enumerate(pairs):
        row = jnp.where(lane == k, left, jnp.where(lane == 64 + k, right, row))
    return row


def gathered(rows, width):
    devices = rows.shape[0]
    turned = rows.T
    parts = [turned[:16], turned[64:80]]
    if width > 2 * devices:
        parts.append(jnp.zeros((16, width - 2 * devices), jnp.float32))
    return jnp.concatenate(parts, axis=1)


def coarse_values(c_row, inverse):
    return dot(jnp.broadcast_to(c_row, (8, c_row.shape[1])), inverse)[:1]


def spread(g_row, counts):
    i, j = place()
    nr, nc = counts[0], 2 * counts[1]
    shape = (16, g_row.shape[1])
    which = rows_of(shape)
    r = i - 1 + which // 4
    c = 2 * j - 1 + which % 4
    inside = (r >= 0) & (r < nr) & (c >= 0) & (c < nc) & (which < 12)
    at = lax.rem(c + 2, 2) * (nr * counts[1]) + r * counts[1] + (c + 2) // 2 - 1
    picked = jnp.where(inside & (lanes_of(shape) == at), g_row, 0.0)
    picked = jnp.sum(picked, axis=1, keepdims=True)
    lane = lanes_of((1, 128))
    bands = []
    for d in range(3):
        left, first, second, right = (picked[4 * d + k : 4 * d + k + 1] for k in range(4))
        bands.append(
            jnp.concatenate(
                [
                    jnp.broadcast_to(first, (1, 128)),
                    jnp.broadcast_to(second, (1, 128)),
                    jnp.where(lane < 64, right, left),
                ],
                axis=1,
            )
        )
    return jnp.concatenate(
        [
            jnp.broadcast_to(bands[1], (128, FC)),
            jnp.broadcast_to(bands[2], (16, FC)),
            jnp.broadcast_to(bands[0], (16, FC)),
        ],
        axis=0,
    )


def column_transform(w, basis_ref):
    w = pltpu.roll(w, OV, 1)
    cols = cols_part(basis_ref)
    return jnp.concatenate([dot(w[:, :256], cols), dot(w[:, 128:], cols)], axis=1)


def weights(means, basis_ref):
    lane = lanes_of((1, 2 * SPEC))
    mean = jnp.where(lane < SPEC, means[0], means[1])
    return 1.0 / (DAMP + mean * basis_ref[:EXT])


def strips_of(t, basis_ref):
    cols = cols_part(basis_ref)
    left = dot(cols[:24], t[:, :SPEC], 1)
    right = dot(cols[EXT - 24 : EXT], t[:, SPEC:], 1)
    both = dot(jnp.concatenate([left, right], axis=0), rows_t_part(basis_ref))
    return both[:24], both[24:]


def solution_of(t, basis_ref):
    v = dot(rows_part(basis_ref), t)
    cols = cols_part(basis_ref)
    first, second = dot(v[:, :SPEC], cols), dot(v[:, SPEC:], cols)
    y = jnp.concatenate(
        [first[:, :128], first[:, 128:] + second[:, :128], second[:, 128:]], axis=1
    )
    return pltpu.roll(y, FC - OV, 1)


def core_sums(x):
    return [total(x[:, :128]), total(x[:, 128:256])]


def add_columns(y, from_left, from_right):
    turned = jnp.concatenate(
        [
            from_right[8:24],
            jnp.zeros((40, EXT), jnp.float32),
            from_right[:8],
            from_left[16:24],
            jnp.zeros((40, EXT), jnp.float32),
            from_left[:16],
        ],
        axis=0,
    )
    back = turned.T
    lane = lanes_of((EXT, 128))
    rolled = pltpu.roll(back, 64, 1)
    first = y[:, :128] + jnp.where(lane < 8, rolled, 0.0)
    second = y[:, 128:256] + jnp.where(lane >= 120, rolled, 0.0)
    third = y[:, 256:] + jnp.where((lane < 16) | (lane >= 112), back, 0.0)
    return jnp.concatenate([first, second, third], axis=1)


def pack_rows(y):
    return jnp.concatenate([y[136:], y[:16]], axis=0), y[112:136]


def add_rows(y, from_above, from_below):
    return jnp.concatenate(
        [
            y[:8] + from_above[16:],
            y[8:120],
            y[120:136] + from_below[:16],
            from_below[16:],
            from_above[:8],
            y[136:] + from_above[8:16],
        ],
        axis=0,
    )


def sides(index, count, a, b):
    even = is_even(index)
    before = jnp.where(index > 0, jnp.where(even, b, a), 0.0)
    after = jnp.where(index < count - 1, jnp.where(even, a, b), 0.0)
    return before, after


def next_table(index, a, b):
    return jnp.where(is_even(index), a, b)[24:, :128]


def row_tables(index, nr, rows, a, b):
    even = is_even(index)
    after = jnp.where(even, a, b)[24:, :128]
    before = jnp.where(even, b, a)[24:, :128]
    if nr == 4:
        return jnp.where(rows == 2, after, 0.0)
    far = rows % 8
    return jnp.where(
        (far == 2) | (far == 5), after, jnp.where((far == 3) | (far == 6), before, 0.0)
    )


def send(index, a_ref, b_ref, before, after):
    even = is_even(index)
    a_ref[...] = jnp.where(even, after, before)
    b_ref[...] = jnp.where(even, before, after)


def begin_kernel(counts, both_ref, a_ref, b_ref):
    r, h = both_ref[:TR], both_ref[TR:]
    lane = lanes_of((128, 128))
    packed = jnp.where(
        lane < 16,
        r[:, :128],
        jnp.where(
            lane < 64,
            pltpu.roll(h[:, :128], 16, 1),
            jnp.where(lane < 112, pltpu.roll(h[:, 128:], 112, 1), r[:, 128:]),
        ),
    )
    turned = packed.T
    table = table_of(core_sums(r), counts)
    send(
        lax.axis_index("col"),
        a_ref,
        b_ref,
        jnp.concatenate([turned[:32], table], axis=0),
        jnp.concatenate([turned[96:], table], axis=0),
    )


def widen_kernel(counts, both_ref, ga_ref, gb_ref, r3_ref, h3_ref, table_ref, a_ref, b_ref):
    i, j = place()
    from_left, from_right = sides(j, counts[1], ga_ref[:32], gb_ref[:32])
    turned = jnp.concatenate([from_right, jnp.zeros((64, 128), jnp.float32), from_left], axis=0)
    back = turned.T
    lane = lanes_of((128, 128))
    edge = (lane < 16) | (lane >= 112)
    r3 = jnp.where(edge, back, 0.0)
    h3 = jnp.where(
        lane < 16, pltpu.roll(back, 112, 1), jnp.where(lane >= 112, pltpu.roll(back, 16, 1), 0.0)
    )
    r3_ref[...] = r3
    h3_ref[...] = h3
    r, h = both_ref[:TR], both_ref[TR:]
    table = table_of(core_sums(r), counts) + ga_ref[32:] + gb_ref[32:]
    table_ref[...] = table
    wide = jnp.concatenate([table, jnp.zeros((table.shape[0], FC - 128), jnp.float32)], axis=1)

    def strip(r_rows, h_rows):
        return jnp.concatenate(
            [
                jnp.concatenate([r[r_rows], r3[r_rows]], axis=1),
                jnp.concatenate([h[h_rows], h3[h_rows]], axis=1),
                wide,
            ],
            axis=0,
        )

    send(i, a_ref, b_ref, strip(slice(0, 8), slice(0, 16)), strip(slice(120, 128), slice(112, 128)))


def forward_kernel(both_ref, r3_ref, basis_ref, u_ref, weights_ref):
    r, h = both_ref[:TR], both_ref[TR:]
    u_ref[...] = column_transform(jnp.concatenate([r, r3_ref[...]], axis=1), basis_ref)
    means = [x / (SUB * SUB) for x in core_sums(h * h * h)]
    weights_ref[...] = weights(means, basis_ref)


def first_kernel(counts, ga_ref, gb_ref, u_ref, weights_ref, basis_ref, t_ref, a_ref, b_ref):
    i, j = place()
    above, below = sides(i, counts[0], ga_ref[:8], gb_ref[:8])
    halo = column_transform(jnp.concatenate([below, above], axis=0), basis_ref)
    u = jnp.concatenate([u_ref[...], halo], axis=0)
    t = dot(rows_t_part(basis_ref), u) * weights_ref[...]
    t_ref[...] = t
    send(j, a_ref, b_ref, *strips_of(t, basis_ref))


def inverse_kernel(counts, t_ref, basis_ref, both_ref, h3_ref, ga_ref, gb_ref, y_ref, m_ref):
    y_ref[...] = solution_of(t_ref[...], basis_ref)
    above, below = sides(lax.axis_index("row"), counts[0], ga_ref[8:24], gb_ref[8:24])
    h = jnp.concatenate([both_ref[TR:], h3_ref[...]], axis=1)
    tall = jnp.concatenate([h, below, above], axis=0)
    m_ref[...] = tall * tall * tall


def columns_kernel(counts, y_ref, ga_ref, gb_ref, *refs):
    i, j = place()
    y = add_columns(y_ref[...], *sides(j, counts[1], ga_ref[:24], gb_ref[:24]))
    strips = pack_rows(y)
    if len(refs) == 5:
        table_ref, out_ref, table_out, a_ref, b_ref = refs
        cols = flat_place(counts)[2]
        table = table_ref[...] + jnp.where(
            cols % 4 == 2, next_table(j, ga_ref[...], gb_ref[...]), 0.0
        )
        table_out[...] = table
        wide = jnp.concatenate([table, jnp.zeros((table.shape[0], FC - 128), jnp.float32)], axis=1)
        strips = [jnp.concatenate([x, wide], axis=0) for x in strips]
    else:
        out_ref, a_ref, b_ref = refs
    out_ref[...] = y
    send(i, a_ref, b_ref, *strips)


def second_kernel(
    counts,
    width,
    y_ref,
    m_ref,
    ga_ref,
    gb_ref,
    table_ref,
    weights_ref,
    basis_ref,
    z_ref,
    w_ref,
    t_ref,
    table_out,
    a_ref,
    b_ref,
):
    i, j = place()
    s = add_rows(y_ref[...], *sides(i, counts[0], ga_ref[:24], gb_ref[:24]))
    mask = grid_mask((FR, FC), counts)
    s = jnp.where(mask, s, 0.0)
    rows = flat_place(counts)[1]
    table = table_ref[...] + row_tables(i, counts[0], rows, ga_ref[...], gb_ref[...])
    table_out[...] = table
    c0 = as_row(table, width)
    coarse = spread(coarse_values(c0, coarse_part(basis_ref, width)), counts)
    mobility = m_ref[...]
    flow = mobility * (lap(s) + lap(coarse))
    z = s + coarse
    w = jnp.where(mask, DAMP * z + lap(flow), 0.0) * SHRINK
    z_ref[...] = z[:128, :256]
    w_ref[...] = w[:128, :256]
    u = column_transform(jnp.concatenate([w[:136], w[152:]], axis=0), basis_ref)
    t = dot(rows_t_part(basis_ref), u) * weights_ref[...]
    t_ref[...] = t
    send(j, a_ref, b_ref, *strips_of(t, basis_ref))


def inverse_stats_kernel(t_ref, basis_ref, both_ref, m_ref, z_ref, w_ref, y_ref, stats_ref):
    y_ref[...] = solution_of(t_ref[...], basis_ref)
    rt, mt, zt, wt = both_ref[:TR], m_ref[:TR, :TC], z_ref[...], w_ref[...]
    lane, row = lanes_of((1, 256)), rows_of((128, 1))
    along = (lane % 128 != 0) & (lane % 128 != 127)
    top, low = mt[:1], mt[127:]
    side = jnp.sum(jnp.where((row > 0) & (row < 127), mt, 0.0), axis=0, keepdims=True)

    def halves(x):
        return [
            jnp.sum(x[:, :128], axis=1, keepdims=True),
            jnp.sum(x[:, 128:], axis=1, keepdims=True),
        ]

    first, last = lane % 128 == 0, lane % 128 == 127
    stats_ref[...] = row_of(
        [
            core_sums(rt * zt),
            core_sums(zt * wt),
            core_sums(wt),
            halves(jnp.where(along, top, 0.0)),
            halves(jnp.where(along, low, 0.0)),
            halves(jnp.where(first, side, 0.0)),
            halves(jnp.where(last, side, 0.0)),
            halves(jnp.where(first, top, 0.0)),
            halves(jnp.where(last, top, 0.0)),
            halves(jnp.where(first, low, 0.0)),
            halves(jnp.where(last, low, 0.0)),
        ]
    )


def dots_kernel(
    counts, y_ref, m_ref, ga_ref, gb_ref, both_ref, w_ref, stats_ref, q_ref, v_ref, stats_out
):
    i, j = place()
    q = add_rows(y_ref[...], *sides(i, counts[0], ga_ref[...], gb_ref[...]))
    q = jnp.where(grid_mask((FR, FC), counts), q, 0.0)
    v = DAMP * q + lap(m_ref[...] * lap(q))
    qt, vt = q[:128, :256], v[:128, :256]
    q_ref[...] = qt
    v_ref[...] = vt
    rest = [
        core_sums(vt),
        core_sums(both_ref[:TR] * qt),
        core_sums(w_ref[...] * qt),
        core_sums(vt * qt),
    ]
    zero = jnp.zeros((1, 1), jnp.float32)
    row = stats_ref[...] + row_of([[zero, zero]] * 11 + rest)
    stats_out[...] = jnp.broadcast_to(row, stats_out.shape)


def end_kernel(
    counts,
    width,
    stats_ref,
    table_ref,
    basis_ref,
    m_ref,
    both_ref,
    z_ref,
    w_ref,
    q_ref,
    v_ref,
    solution_ref,
    residual_ref,
):
    tiles_c = counts[1]
    devices = counts[0] * tiles_c
    table = gathered(stats_ref[...], width)
    st = [table[k : k + 1] for k in range(15)]

    def whole(x):
        return jnp.sum(x, axis=1, keepdims=True)

    rz, zw, rq, wq, qv = (whole(st[k]) for k in (0, 1, 12, 13, 14))
    c0, c1, sums_v = as_row(table_ref[...], width), st[2], st[11]
    g = coarse_values(c1, coarse_part(basis_ref, width))
    lane = lanes_of((1, width))
    cell = lane < 2 * devices
    on_left = lane < devices
    device = lane % devices
    column = device % tiles_c

    def from_lane(distance):
        return pltpu.roll(g, distance % width, 1)

    up = jnp.where(device >= tiles_c, from_lane(tiles_c), 0.0)
    down = jnp.where(device < devices - tiles_c, from_lane(-tiles_c), 0.0)
    left = jnp.where(
        on_left, jnp.where(column > 0, from_lane(1 - devices), 0.0), from_lane(devices)
    )
    right = jnp.where(
        on_left,
        from_lane(-devices),
        jnp.where(column < tiles_c - 1, from_lane(devices - 1), 0.0),
    )
    du, dd, dl, dr = g - up, g - down, g - left, g - right
    energy = DAMP * SUB * SUB * g * g
    energy = energy + st[3] * du * du + st[4] * dd * dd + st[5] * dl * dl + st[6] * dr * dr
    for weight, p, q in ((st[7], du, dl), (st[8], du, dr), (st[9], dd, dl), (st[10], dd, dr)):
        both = p + q
        energy = energy + weight * both * both
    ry = rq + whole(g * c0)
    yw = wq + whole(g * c1)
    yv = qv + whole(jnp.where(cell, 2.0 * g * sums_v + energy, 0.0))
    a = rz / zw
    rz1 = rz - a * ry - a * zw + a * a * yw
    beta1 = 1.0 + rz1 / rz
    dad = (beta1 * beta1 * zw - 2.0 * a * beta1 * yw) * (1.0 / SHRINK) + a * a * yv
    a1 = rz1 / dad
    coarse = spread(g, counts)
    y = q_ref[...] + coarse[:128, :256]
    image = DAMP * coarse + lap(m_ref[...] * lap(coarse))
    v = v_ref[...] + image[:128, :256]
    z, w = z_ref[...], w_ref[...]
    solution_ref[...] = (a * SHRINK) * z + a1 * (beta1 * z - a * y)
    residual_ref[...] = both_ref[:TR] - a * w - a1 * ((beta1 * (1.0 / SHRINK)) * w - a * v)


def call(kernel, outs, *args, flops=10**9):
    shapes = [jax.ShapeDtypeStruct(s, jnp.float32) for s in outs]
    return pl.pallas_call(
        kernel,
        out_shape=shapes,
        compiler_params=pltpu.CompilerParams(vmem_limit_bytes=48 * 1024 * 1024),
        cost_estimate=pl.CostEstimate(flops=flops, bytes_accessed=10**6, transcendentals=0),
    )(*args)


def pairs_from(count, offset):
    found = []
    for k in range(offset, count, 2):
        found += [(k, (k + 1) % count), ((k + 1) % count, k)]
    return found


def body(counts, height, noise):
    nr, nc = counts
    devices = nr * nc
    width = max(128, devices * 2)
    basis = jnp.asarray(constants(nr, 2 * nc, width))
    both_axes = ("row", "col")
    depth = table_shape(counts)[0]

    def swap(a, b, axis):
        count = lax.axis_size(axis)
        gb = lax.ppermute(b, axis, pairs_from(count, 1))
        return lax.ppermute(a, axis, pairs_from(count, 0)), gb

    def row_shift(x, step):
        return lax.ppermute(x, "row", [(k, (k + step) % nr) for k in range(nr)])

    both = jnp.pad(noise, ((0, TR), (0, 0))) + jnp.pad(height, ((TR, 0), (0, 0)))
    a, b = call(functools.partial(begin_kernel, counts), [(32 + depth, 128)] * 2, both)
    ga, gb = swap(a, b, "col")
    r3, h3, table, a, b = call(
        functools.partial(widen_kernel, counts),
        [(128, 128)] * 2 + [(depth, 128)] + [(24 + depth, FC)] * 2,
        both,
        ga,
        gb,
    )
    step = nr // 2
    while step >= 8:
        table = table + row_shift(table, step)
        step //= 2
    if nr > 8:
        a, b = (x.at[24:, :128].set(table) for x in (a, b))
    ga, gb = swap(a, b, "row")
    far = row_shift(table, 4) if nr >= 8 else 0.0
    u, weight = call(forward_kernel, [(TR, 2 * SPEC), (EXT, 2 * SPEC)], both, r3, basis)
    t, a, b = call(
        functools.partial(first_kernel, counts),
        [(EXT, 2 * SPEC)] + [(24, EXT)] * 2,
        ga,
        gb,
        u,
        weight,
        basis,
    )
    table = table + ga[24:, :128] + gb[24:, :128] + far
    step = nc // 2
    while step >= 4:
        table = table + lax.ppermute(table, "col", [(k, (k + step) % nc) for k in range(nc)])
        step //= 2
    wide = jnp.pad(table, ((0, 0), (0, EXT - 128)))
    y, m = call(
        functools.partial(inverse_kernel, counts),
        [(EXT, FC), (FR, FC)],
        t,
        basis,
        both,
        h3,
        ga,
        gb,
    )
    ga, gb = swap(*(jnp.concatenate([x, wide], axis=0) for x in (a, b)), "col")
    y, table, a, b = call(
        functools.partial(columns_kernel, counts),
        [(EXT, FC), (depth, 128)] + [(24 + depth, FC)] * 2,
        y,
        ga,
        gb,
        table,
    )
    ga, gb = swap(a, b, "row")
    z, w, t, table, a, b = call(
        functools.partial(second_kernel, counts, width),
        [(TR, TC)] * 2 + [(EXT, 2 * SPEC), (depth, 128)] + [(24, EXT)] * 2,
        y,
        m,
        ga,
        gb,
        table,
        weight,
        basis,
    )
    ga, gb = swap(a, b, "col")
    y, stats = call(inverse_stats_kernel, [(EXT, FC), (1, 128)], t, basis, both, m, z, w)
    y, a, b = call(
        functools.partial(columns_kernel, counts), [(EXT, FC)] + [(24, FC)] * 2, y, ga, gb
    )
    ga, gb = swap(a, b, "row")
    q, v, stats = call(
        functools.partial(dots_kernel, counts),
        [(TR, TC)] * 2 + [(devices, 128)],
        y,
        m,
        ga,
        gb,
        both,
        w,
        stats,
    )
    stats = lax.all_to_all(stats, both_axes, 0, 0, tiled=True)
    return tuple(
        call(
            functools.partial(end_kernel, counts, width),
            [(TR, TC)] * 2,
            stats,
            table,
            basis,
            m,
            both,
            z,
            w,
            q,
            v,
        )
    )


def solution(mesh):
    counts = (mesh.shape["row"], mesh.shape["col"])
    spec = P("row", "col")
    return jax.shard_map(
        functools.partial(body, counts),
        mesh=mesh,
        in_specs=(spec, spec),
        out_specs=(spec, spec),
        check_vma=False,
    )
```

```python
import functools

import jax
import jax.numpy as jnp
import ml_dtypes
import numpy as np
from jax import lax
from jax.experimental import pallas as pl
from jax.experimental.pallas import tpu as pltpu
from jax.sharding import PartitionSpec as P

SUB = 128
OV = 8
EXT = SUB + 2 * OV
DAMP = 2.0**-28
SHRINK = 2.0**-20

TR, TC = 128, 256
FR, FC = 160, 384
SPEC = 256

highest = lax.Precision.HIGHEST


def sine(count):
    k = np.arange(1, count + 1, dtype=np.float64)
    basis = np.sqrt(2.0 / (count + 1.0)) * np.sin(np.pi * k[:, None] * k[None, :] / (count + 1.0))
    return basis, 2.0 - 2.0 * np.cos(np.pi * k / (count + 1.0))


def block_constants():
    basis, eig = sine(EXT)
    rows = np.roll(basis, -OV, 0)
    cols = np.pad(basis, ((0, SPEC - EXT), (0, SPEC - EXT)))
    scale = np.pad((eig[:, None] + eig[None, :]) ** 2, ((0, 0), (0, SPEC - EXT)))
    wide = lambda x: np.pad(x, ((0, 0), (0, 2 * SPEC - x.shape[1])))
    high = rows.T.astype(ml_dtypes.bfloat16).astype(np.float64)
    low = (rows.T - high).astype(ml_dtypes.bfloat16).astype(np.float64)
    tile = np.concatenate([x[:, :SUB] for x in (high, high, low)], 1)
    halo = np.concatenate([x[:, SUB:] for x in (high, high, low)], 1)
    whole = np.concatenate([high, high, low], 1)
    return [np.tile(scale, (1, 2)), *(wide(x) for x in (rows, rows.T, cols, whole, np.hstack([tile, halo])))]


def rows_part(ref):
    return ref[EXT : 2 * EXT, :EXT]


def rows_t_part(ref):
    return ref[2 * EXT : 3 * EXT, :EXT]


def cols_part(ref):
    return ref[3 * EXT : 3 * EXT + SPEC, :SPEC]


def whole_rows(ref):
    at = 3 * EXT + SPEC
    return ref[at : at + EXT, : 3 * EXT]


def tile_rows(ref):
    at = 4 * EXT + SPEC
    return ref[at : at + EXT, : 3 * SUB]


def halo_rows(ref):
    at = 4 * EXT + SPEC
    return ref[at : at + EXT, 3 * SUB : 3 * EXT]


def coarse_part(ref, width):
    at, lanes = 5 * EXT + SPEC, 2 * SPEC
    parts = [ref[at + k * width : at + (k + 1) * width] for k in range(-(-width // lanes))]
    return (parts[0] if len(parts) == 1 else jnp.concatenate(parts, axis=1))[:, :width]


def constants(nr, nc, width):
    lanes = 2 * SPEC
    inverse = coarse_inverse(nr, nc, -(-width // lanes) * lanes)[:width]
    parts = [*block_constants(), *np.split(inverse, inverse.shape[1] // lanes, 1)]
    return np.concatenate(parts).astype(np.float32)


def coarse_inverse(nr, nc, width):
    br, er = sine(nr)
    bc, ec = sine(nc)
    both = np.kron(br, bc).reshape(nr, nc // 2, 2, nr * nc).transpose(2, 0, 1, 3)
    both = both.reshape(nr * nc, nr * nc)
    scale = (er[:, None] + ec[None, :]) / (SUB * SUB)
    values = (SUB * SUB * (DAMP + scale * scale)).reshape(-1)
    whole = np.zeros((width, width), np.float32)
    whole[: nr * nc, : nr * nc] = (both / values) @ both.T
    return whole


def dot(a, b, side=0):
    return lax.dot_general(
        a, b, (((1,), (side,)), ((), ())), precision=highest, preferred_element_type=jnp.float32
    )


def lap(x):
    rows, lanes = x.shape
    beside = pltpu.roll(x, 1, 0) + pltpu.roll(x, rows - 1, 0)
    beside = beside + (pltpu.roll(x, 1, 1) + pltpu.roll(x, lanes - 1, 1))
    return 4.0 * x - beside


def lanes_of(shape):
    return lax.broadcasted_iota(jnp.int32, shape, 1)


def rows_of(shape):
    return lax.broadcasted_iota(jnp.int32, shape, 0)


def total(x):
    return jnp.sum(jnp.sum(x, axis=0, keepdims=True), axis=1, keepdims=True)


def place():
    return lax.axis_index("row"), lax.axis_index("col")


def is_even(index):
    return lax.rem(index, 2) == 0


def grid_mask(shape, counts):
    i, j = place()
    rr, ll = rows_of(shape), lanes_of(shape)
    below = jnp.where(i < counts[0] - 1, 144, 128)
    above = jnp.where(i > 0, 144, 160)
    right = jnp.where(j < counts[1] - 1, 320, 256)
    left = jnp.where(j > 0, 320, 384)
    return ((rr < below) | (rr >= above)) & ((ll < right) | (ll >= left))


def flat_place(counts):
    i, j = place()
    nr, nc = counts
    shape = table_shape(counts)
    flat = rows_of(shape) * 128 + lanes_of(shape)
    device = flat % (nr * nc)
    return flat, (device // nc + nr - i) % nr, (device % nc + nc - j) % nc


def table_shape(counts):
    return (-(-2 * counts[0] * counts[1] // 1024) * 8, 128)


def table_of(values, counts):
    flat, rows, cols = flat_place(counts)
    devices = counts[0] * counts[1]
    own = jnp.where(flat < devices, values[0], jnp.where(flat < 2 * devices, values[1], 0.0))
    return jnp.where((rows == 0) & (cols == 0), own, 0.0)


def as_row(table, width):
    return jnp.concatenate([table[k : k + 1] for k in range(width // 128)], axis=1)


def row_of(pairs):
    lane = lanes_of((1, 128))
    row = jnp.zeros((1, 128), jnp.float32)
    for k, (left, right) in enumerate(pairs):
        row = jnp.where(lane == k, left, jnp.where(lane == 64 + k, right, row))
    return row


def gathered(rows, width):
    devices = rows.shape[0]
    turned = rows.T
    parts = [turned[:16], turned[64:80]]
    if width > 2 * devices:
        parts.append(jnp.zeros((16, width - 2 * devices), jnp.float32))
    return jnp.concatenate(parts, axis=1)


def coarse_values(c_row, inverse):
    return dot(jnp.broadcast_to(c_row, (8, c_row.shape[1])), inverse)[:1]


def spread(g_row, counts):
    i, j = place()
    nr, nc = counts[0], 2 * counts[1]
    shape = (16, g_row.shape[1])
    which = rows_of(shape)
    r = i - 1 + which // 4
    c = 2 * j - 1 + which % 4
    inside = (r >= 0) & (r < nr) & (c >= 0) & (c < nc) & (which < 12)
    at = lax.rem(c + 2, 2) * (nr * counts[1]) + r * counts[1] + (c + 2) // 2 - 1
    picked = jnp.where(inside & (lanes_of(shape) == at), g_row, 0.0)
    picked = jnp.sum(picked, axis=1, keepdims=True)
    lane = lanes_of((1, 128))
    bands = []
    for d in range(3):
        left, first, second, right = (picked[4 * d + k : 4 * d + k + 1] for k in range(4))
        bands.append(
            jnp.concatenate(
                [
                    jnp.broadcast_to(first, (1, 128)),
                    jnp.broadcast_to(second, (1, 128)),
                    jnp.where(lane < 64, right, left),
                ],
                axis=1,
            )
        )
    return jnp.concatenate(
        [
            jnp.broadcast_to(bands[1], (128, FC)),
            jnp.broadcast_to(bands[2], (16, FC)),
            jnp.broadcast_to(bands[0], (16, FC)),
        ],
        axis=0,
    )


def halves_of(x):
    high = x.astype(jnp.bfloat16)
    return high, (x - high.astype(jnp.float32)).astype(jnp.bfloat16)


def product(a, b):
    return lax.dot_general(a, b, (((1,), (0,)), ((), ())), preferred_element_type=jnp.float32)


def column_transform(w, basis_ref):
    high, low = halves_of(pltpu.roll(w, OV, 1))
    cols, rest = halves_of(cols_part(basis_ref))
    cols = jnp.concatenate([cols, rest, cols], axis=0)

    def block(at):
        part = slice(at, at + SPEC)
        return product(jnp.concatenate([high[:, part], high[:, part], low[:, part]], axis=1), cols)

    return jnp.concatenate([block(0), block(128)], axis=1)


def row_transform(u, basis_ref, part):
    high, low = halves_of(u)
    rows = part(basis_ref).astype(jnp.bfloat16)
    return product(rows, jnp.concatenate([high, low, high], axis=0))


def weights(means, basis_ref):
    lane = lanes_of((1, 2 * SPEC))
    mean = jnp.where(lane < SPEC, means[0], means[1])
    return 1.0 / (DAMP + mean * basis_ref[:EXT])


def strips_of(t, basis_ref, deep):
    cols = cols_part(basis_ref)
    left = dot(cols[:deep], t[:, :SPEC], 1)
    right = dot(cols[EXT - deep : EXT], t[:, SPEC:], 1)
    both = dot(jnp.concatenate([left, right], axis=0), rows_t_part(basis_ref))
    return both[:deep], both[deep:]


def solution_of(t, basis_ref):
    v = dot(rows_part(basis_ref), t)
    cols = cols_part(basis_ref)
    first, second = dot(v[:, :SPEC], cols), dot(v[:, SPEC:], cols)
    y = jnp.concatenate(
        [first[:, :128], first[:, 128:] + second[:, :128], second[:, 128:]], axis=1
    )
    return pltpu.roll(y, FC - OV, 1)


def core_sums(x):
    return [total(x[:, :128]), total(x[:, 128:256])]


def add_columns(y, from_left, from_right):
    far = from_left.shape[0] - OV
    gap = jnp.zeros((56 - far, EXT), jnp.float32)
    turned = jnp.concatenate(
        [from_right[8:], gap, from_right[:8], from_left[far:], gap, from_left[:far]], axis=0
    )
    back = turned.T
    lane = lanes_of((EXT, 128))
    rolled = pltpu.roll(back, 64, 1)
    first = y[:, :128] + jnp.where(lane < 8, rolled, 0.0)
    second = y[:, 128:256] + jnp.where(lane >= 120, rolled, 0.0)
    third = y[:, 256:] + jnp.where((lane < 16) | (lane >= 112), back, 0.0)
    return jnp.concatenate([first, second, third], axis=1)


def pack_rows(y, deep):
    return jnp.concatenate([y[136:], y[: deep - 8]], axis=0), y[136 - deep : 136]


def add_rows(y, from_above, from_below):
    far = from_above.shape[0] - OV
    none = jnp.zeros((8, FC), jnp.float32)
    return jnp.concatenate(
        [
            y[:8] + from_above[far:],
            y[8:120],
            y[120:136] + from_below[:16],
            from_below[16:] if far == 16 else none,
            from_above[:8] if far == 16 else none,
            y[136:] + from_above[far - 8 : far],
        ],
        axis=0,
    )


def sides(index, count, a, b):
    even = is_even(index)
    before = jnp.where(index > 0, jnp.where(even, b, a), 0.0)
    after = jnp.where(index < count - 1, jnp.where(even, a, b), 0.0)
    return before, after


def next_table(index, a, b):
    return jnp.where(is_even(index), a, b)[24:, :128]


def row_tables(index, nr, rows, a, b):
    even = is_even(index)
    after = jnp.where(even, a, b)[24:, :128]
    before = jnp.where(even, b, a)[24:, :128]
    if nr == 4:
        return jnp.where(rows == 2, after, 0.0)
    far = rows % 8
    return jnp.where(
        (far == 2) | (far == 5), after, jnp.where((far == 3) | (far == 6), before, 0.0)
    )


def send(index, a_ref, b_ref, before, after):
    even = is_even(index)
    a_ref[...] = jnp.where(even, after, before)
    b_ref[...] = jnp.where(even, before, after)


def begin_kernel(counts, both_ref, b_ref, a_ref):
    r, h = both_ref[:TR], both_ref[TR:]
    lane = lanes_of((128, 128))
    packed = jnp.where(
        lane < 16,
        r[:, :128],
        jnp.where(
            lane < 64,
            pltpu.roll(h[:, :128], 16, 1),
            jnp.where(lane < 112, pltpu.roll(h[:, 128:], 112, 1), r[:, 128:]),
        ),
    )
    turned = packed.T
    table = table_of(core_sums(r), counts)
    send(
        lax.axis_index("col"),
        a_ref,
        b_ref,
        jnp.concatenate([turned[:32], table], axis=0),
        jnp.concatenate([turned[96:], table], axis=0),
    )


def widen_kernel(counts, both_ref, gb_ref, ga_ref, r3_ref, h3_ref, table_ref, b_ref, a_ref):
    i, j = place()
    from_left, from_right = sides(j, counts[1], ga_ref[:32], gb_ref[:32])
    turned = jnp.concatenate([from_right, jnp.zeros((64, 128), jnp.float32), from_left], axis=0)
    back = turned.T
    lane = lanes_of((128, 128))
    edge = (lane < 16) | (lane >= 112)
    r3 = jnp.where(edge, back, 0.0)
    h3 = jnp.where(
        lane < 16, pltpu.roll(back, 112, 1), jnp.where(lane >= 112, pltpu.roll(back, 16, 1), 0.0)
    )
    r3_ref[...] = r3
    h3_ref[...] = h3
    r, h = both_ref[:TR], both_ref[TR:]
    table = table_of(core_sums(r), counts) + ga_ref[32:] + gb_ref[32:]
    table_ref[...] = table
    wide = jnp.concatenate([table, jnp.zeros((table.shape[0], FC - 128), jnp.float32)], axis=1)

    def strip(r_rows, h_rows):
        return jnp.concatenate(
            [
                jnp.concatenate([r[r_rows], r3[r_rows]], axis=1),
                jnp.concatenate([h[h_rows], h3[h_rows]], axis=1),
                wide,
            ],
            axis=0,
        )

    send(i, a_ref, b_ref, strip(slice(0, 8), slice(0, 16)), strip(slice(120, 128), slice(112, 128)))


def forward_kernel(both_ref, r3_ref, basis_ref, table_ref, t_ref, weights_ref, table_out):
    r, h = both_ref[:TR], both_ref[TR:]
    u = column_transform(jnp.concatenate([r, r3_ref[...]], axis=1), basis_ref)
    t_ref[...] = row_transform(u, basis_ref, tile_rows)
    means = [x / (SUB * SUB) for x in core_sums(h * h * h)]
    weights_ref[...] = weights(means, basis_ref)
    table_out[...] = table_ref[...]


def first_kernel(
    counts,
    gb_ref,
    ga_ref,
    tile_ref,
    weights_ref,
    basis_ref,
    table_ref,
    t_ref,
    table_out,
    b_ref,
    a_ref,
):
    i, j = place()
    above, below = sides(i, counts[0], ga_ref[:8], gb_ref[:8])
    u = column_transform(jnp.concatenate([below, above], axis=0), basis_ref)
    t = (tile_ref[...] + row_transform(u, basis_ref, halo_rows)) * weights_ref[...]
    t_ref[...] = t
    send(j, a_ref, b_ref, *strips_of(t, basis_ref, 24))
    table_out[...] = table_ref[...] + ga_ref[24:, :128] + gb_ref[24:, :128]


def inverse_kernel(counts, t_ref, basis_ref, both_ref, h3_ref, gb_ref, ga_ref, y_ref, m_ref):
    y_ref[...] = solution_of(t_ref[...], basis_ref)
    above, below = sides(lax.axis_index("row"), counts[0], ga_ref[8:24], gb_ref[8:24])
    h = jnp.concatenate([both_ref[TR:], h3_ref[...]], axis=1)
    tall = jnp.concatenate([h, below, above], axis=0)
    m_ref[...] = tall * tall * tall


def columns_kernel(counts, y_ref, *refs):
    i, j = place()
    (ga_ref, gb_ref), refs = (refs[:2] if len(refs) == 7 else refs[1::-1]), refs[2:]
    deep = 24 if len(refs) == 5 else 16
    y = add_columns(y_ref[...], *sides(j, counts[1], ga_ref[:deep], gb_ref[:deep]))
    strips = pack_rows(y, deep)
    if len(refs) == 5:
        table_ref, out_ref, table_out, b_ref, a_ref = refs
        cols = flat_place(counts)[2]
        table = table_ref[...] + jnp.where(
            cols % 4 == 2, next_table(j, ga_ref[...], gb_ref[...]), 0.0
        )
        table_out[...] = table
        wide = jnp.concatenate([table, jnp.zeros((table.shape[0], FC - 128), jnp.float32)], axis=1)
        strips = [jnp.concatenate([x, wide], axis=0) for x in strips]
    else:
        out_ref, b_ref, a_ref = refs
    out_ref[...] = y
    send(i, a_ref, b_ref, *strips)


def second_kernel(
    counts,
    width,
    y_ref,
    m_ref,
    gb_ref,
    ga_ref,
    table_ref,
    weights_ref,
    basis_ref,
    z_ref,
    w_ref,
    t_ref,
    table_out,
    b_ref,
    a_ref,
):
    i, j = place()
    s = add_rows(y_ref[...], *sides(i, counts[0], ga_ref[:24], gb_ref[:24]))
    mask = grid_mask((FR, FC), counts)
    s = jnp.where(mask, s, 0.0)
    rows = flat_place(counts)[1]
    table = table_ref[...] + row_tables(i, counts[0], rows, ga_ref[...], gb_ref[...])
    table_out[...] = table
    c0 = as_row(table, width)
    coarse = spread(coarse_values(c0, coarse_part(basis_ref, width)), counts)
    mobility = m_ref[...]
    flow = mobility * (lap(s) + lap(coarse))
    z = s + coarse
    w = jnp.where(mask, DAMP * z + lap(flow), 0.0) * SHRINK
    z_ref[...] = z[:128, :256]
    w_ref[...] = w[:128, :256]
    u = column_transform(jnp.concatenate([w[:136], w[152:]], axis=0), basis_ref)
    t = row_transform(u, basis_ref, whole_rows) * weights_ref[...]
    t_ref[...] = t
    send(j, a_ref, b_ref, *strips_of(t, basis_ref, 16))


def inverse_stats_kernel(t_ref, basis_ref, both_ref, m_ref, z_ref, w_ref, y_ref, stats_ref):
    y_ref[...] = solution_of(t_ref[...], basis_ref)
    rt, mt, zt, wt = both_ref[:TR], m_ref[:TR, :TC], z_ref[...], w_ref[...]
    lane, row = lanes_of((1, 256)), rows_of((128, 1))
    along = (lane % 128 != 0) & (lane % 128 != 127)
    top, low = mt[:1], mt[127:]
    side = jnp.sum(jnp.where((row > 0) & (row < 127), mt, 0.0), axis=0, keepdims=True)

    def halves(x):
        return [
            jnp.sum(x[:, :128], axis=1, keepdims=True),
            jnp.sum(x[:, 128:], axis=1, keepdims=True),
        ]

    first, last = lane % 128 == 0, lane % 128 == 127
    stats_ref[...] = row_of(
        [
            core_sums(rt * zt),
            core_sums(zt * wt),
            core_sums(wt),
            halves(jnp.where(along, top, 0.0)),
            halves(jnp.where(along, low, 0.0)),
            halves(jnp.where(first, side, 0.0)),
            halves(jnp.where(last, side, 0.0)),
            halves(jnp.where(first, top, 0.0)),
            halves(jnp.where(last, top, 0.0)),
            halves(jnp.where(first, low, 0.0)),
            halves(jnp.where(last, low, 0.0)),
        ]
    )


def dots_kernel(
    counts, y_ref, m_ref, gb_ref, ga_ref, both_ref, w_ref, stats_ref, q_ref, v_ref, stats_out
):
    i, j = place()
    q = add_rows(y_ref[...], *sides(i, counts[0], ga_ref[...], gb_ref[...]))
    q = jnp.where(grid_mask((FR, FC), counts), q, 0.0)
    v = DAMP * q + lap(m_ref[...] * lap(q))
    qt, vt = q[:128, :256], v[:128, :256]
    q_ref[...] = qt
    v_ref[...] = vt
    rest = [
        core_sums(vt),
        core_sums(both_ref[:TR] * qt),
        core_sums(w_ref[...] * qt),
        core_sums(vt * qt),
    ]
    zero = jnp.zeros((1, 1), jnp.float32)
    row = stats_ref[...] + row_of([[zero, zero]] * 11 + rest)
    stats_out[...] = jnp.broadcast_to(row, stats_out.shape)


def end_kernel(
    counts,
    width,
    stats_ref,
    table_ref,
    basis_ref,
    m_ref,
    both_ref,
    z_ref,
    w_ref,
    q_ref,
    v_ref,
    solution_ref,
    residual_ref,
):
    tiles_c = counts[1]
    devices = counts[0] * tiles_c
    table = gathered(stats_ref[...], width)
    st = [table[k : k + 1] for k in range(15)]

    def whole(x):
        return jnp.sum(x, axis=1, keepdims=True)

    rz, zw, rq, wq, qv = (whole(st[k]) for k in (0, 1, 12, 13, 14))
    c0, c1, sums_v = as_row(table_ref[...], width), st[2], st[11]
    g = coarse_values(c1, coarse_part(basis_ref, width))
    lane = lanes_of((1, width))
    cell = lane < 2 * devices
    on_left = lane < devices
    device = lane % devices
    column = device % tiles_c

    def from_lane(distance):
        return pltpu.roll(g, distance % width, 1)

    up = jnp.where(device >= tiles_c, from_lane(tiles_c), 0.0)
    down = jnp.where(device < devices - tiles_c, from_lane(-tiles_c), 0.0)
    left = jnp.where(
        on_left, jnp.where(column > 0, from_lane(1 - devices), 0.0), from_lane(devices)
    )
    right = jnp.where(
        on_left,
        from_lane(-devices),
        jnp.where(column < tiles_c - 1, from_lane(devices - 1), 0.0),
    )
    du, dd, dl, dr = g - up, g - down, g - left, g - right
    energy = DAMP * SUB * SUB * g * g
    energy = energy + st[3] * du * du + st[4] * dd * dd + st[5] * dl * dl + st[6] * dr * dr
    for weight, p, q in ((st[7], du, dl), (st[8], du, dr), (st[9], dd, dl), (st[10], dd, dr)):
        both = p + q
        energy = energy + weight * both * both
    ry = rq + whole(g * c0)
    yw = wq + whole(g * c1)
    yv = qv + whole(jnp.where(cell, 2.0 * g * sums_v + energy, 0.0))
    a = rz / zw
    rz1 = rz - a * ry - a * zw + a * a * yw
    beta1 = 1.0 + rz1 / rz
    dad = (beta1 * beta1 * zw - 2.0 * a * beta1 * yw) * (1.0 / SHRINK) + a * a * yv
    a1 = rz1 / dad
    coarse = spread(g, counts)
    y = q_ref[...] + coarse[:128, :256]
    image = DAMP * coarse + lap(m_ref[...] * lap(coarse))
    v = v_ref[...] + image[:128, :256]
    z, w = z_ref[...], w_ref[...]
    solution_ref[...] = (a * SHRINK) * z + a1 * (beta1 * z - a * y)
    residual_ref[...] = both_ref[:TR] - a * w - a1 * ((beta1 * (1.0 / SHRINK)) * w - a * v)


def call(kernel, outs, *args, flops=10**9):
    shapes = [jax.ShapeDtypeStruct(s, jnp.float32) for s in outs]
    return pl.pallas_call(
        kernel,
        out_shape=shapes,
        compiler_params=pltpu.CompilerParams(vmem_limit_bytes=48 * 1024 * 1024),
        cost_estimate=pl.CostEstimate(flops=flops, bytes_accessed=10**6, transcendentals=0),
    )(*args)


def pairs_from(count, offset):
    found = []
    for k in range(offset, count, 2):
        found += [(k, (k + 1) % count), ((k + 1) % count, k)]
    return found


def body(counts, height, noise):
    nr, nc = counts
    devices = nr * nc
    width = max(128, devices * 2)
    basis = jnp.asarray(constants(nr, 2 * nc, width))
    both_axes = ("row", "col")
    depth = table_shape(counts)[0]

    def swap(a, b, axis):
        count = lax.axis_size(axis)
        gb = lax.ppermute(b, axis, pairs_from(count, 1))
        return lax.ppermute(a, axis, pairs_from(count, 0)), gb

    def row_shift(x, step):
        return lax.ppermute(x, "row", [(k, (k + step) % nr) for k in range(nr)])

    both = jnp.pad(noise, ((0, TR), (0, 0))) + jnp.pad(height, ((TR, 0), (0, 0)))
    b, a = call(functools.partial(begin_kernel, counts), [(32 + depth, 128)] * 2, both)
    ga, gb = swap(a, b, "col")
    r3, h3, table, b, a = call(
        functools.partial(widen_kernel, counts),
        [(128, 128)] * 2 + [(depth, 128)] + [(24 + depth, FC)] * 2,
        both,
        gb,
        ga,
    )
    step = nr // 2
    while step >= 8:
        table = table + row_shift(table, step)
        step //= 2
    if nr > 8:
        a, b = (x.at[24:, :128].set(table) for x in (a, b))
    ga, gb = swap(a, b, "row")
    t, weight, table = call(
        forward_kernel, [(EXT, 2 * SPEC)] * 2 + [(depth, 128)], both, r3, basis, table
    )
    far = row_shift(table, 4) if nr >= 8 else 0.0
    t, table, b, a = call(
        functools.partial(first_kernel, counts),
        [(EXT, 2 * SPEC), (depth, 128)] + [(24, EXT)] * 2,
        gb,
        ga,
        t,
        weight,
        basis,
        table,
    )
    table = table + far
    step = nc // 2
    while step >= 4:
        table = table + lax.ppermute(table, "col", [(k, (k + step) % nc) for k in range(nc)])
        step //= 2
    wide = jnp.pad(table, ((0, 0), (0, EXT - 128)))
    y, m = call(
        functools.partial(inverse_kernel, counts),
        [(EXT, FC), (FR, FC)],
        t,
        basis,
        both,
        h3,
        gb,
        ga,
    )
    ga, gb = swap(*(jnp.concatenate([x, wide], axis=0) for x in (a, b)), "col")
    y, table, b, a = call(
        functools.partial(columns_kernel, counts),
        [(EXT, FC), (depth, 128)] + [(24 + depth, FC)] * 2,
        y,
        ga,
        gb,
        table,
    )
    ga, gb = swap(a, b, "row")
    z, w, t, table, b, a = call(
        functools.partial(second_kernel, counts, width),
        [(TR, TC)] * 2 + [(EXT, 2 * SPEC), (depth, 128)] + [(16, EXT)] * 2,
        y,
        m,
        gb,
        ga,
        table,
        weight,
        basis,
    )
    ga, gb = swap(a, b, "col")
    y, stats = call(inverse_stats_kernel, [(EXT, FC), (1, 128)], t, basis, both, m, z, w)
    y, b, a = call(
        functools.partial(columns_kernel, counts), [(EXT, FC)] + [(16, FC)] * 2, y, gb, ga
    )
    ga, gb = swap(a, b, "row")
    q, v, stats = call(
        functools.partial(dots_kernel, counts),
        [(TR, TC)] * 2 + [(devices, 128)],
        y,
        m,
        gb,
        ga,
        both,
        w,
        stats,
    )
    stats = lax.all_to_all(stats, both_axes, 0, 0, tiled=True)
    return tuple(
        call(
            functools.partial(end_kernel, counts, width),
            [(TR, TC)] * 2,
            stats,
            table,
            basis,
            m,
            both,
            z,
            w,
            q,
            v,
        )
    )


def solution(mesh):
    counts = (mesh.shape["row"], mesh.shape["col"])
    spec = P("row", "col")
    return jax.shard_map(
        functools.partial(body, counts),
        mesh=mesh,
        in_specs=(spec, spec),
        out_specs=(spec, spec),
        check_vma=False,
    )
```

```python
import functools

import jax
import jax.numpy as jnp
import ml_dtypes
import numpy as np
from jax import lax
from jax.experimental import pallas as pl
from jax.experimental.pallas import tpu as pltpu
from jax.sharding import PartitionSpec as P

SUB = 128
OV = 8
EXT = SUB + 2 * OV
DAMP = 2.0**-28
SHRINK = 2.0**-20

TR, TC = 128, 256
FR, FC = 160, 384
SPEC = 256

highest = lax.Precision.HIGHEST


def sine(count):
    k = np.arange(1, count + 1, dtype=np.float64)
    basis = np.sqrt(2.0 / (count + 1.0)) * np.sin(np.pi * k[:, None] * k[None, :] / (count + 1.0))
    return basis, 2.0 - 2.0 * np.cos(np.pi * k / (count + 1.0))


def block_constants():
    basis, eig = sine(EXT)
    rows = np.roll(basis, -OV, 0)
    cols = np.pad(basis, ((0, SPEC - EXT), (0, SPEC - EXT)))
    scale = np.pad((eig[:, None] + eig[None, :]) ** 2, ((0, 0), (0, SPEC - EXT)))
    wide = lambda x: np.pad(x, ((0, 0), (0, 2 * SPEC - x.shape[1])))
    high = rows.T.astype(ml_dtypes.bfloat16).astype(np.float64)
    low = (rows.T - high).astype(ml_dtypes.bfloat16).astype(np.float64)
    tile = np.concatenate([x[:, :SUB] for x in (high, high, low)], 1)
    halo = np.concatenate([x[:, SUB:] for x in (high, high, low)], 1)
    whole = np.concatenate([high, high, low], 1)
    return [np.tile(scale, (1, 2)), *(wide(x) for x in (rows, rows.T, cols, whole, np.hstack([tile, halo])))]


def rows_part(ref):
    return ref[EXT : 2 * EXT, :EXT]


def rows_t_part(ref):
    return ref[2 * EXT : 3 * EXT, :EXT]


def cols_part(ref):
    return ref[3 * EXT : 3 * EXT + SPEC, :SPEC]


def whole_rows(ref):
    at = 3 * EXT + SPEC
    return ref[at : at + EXT, : 3 * EXT]


def tile_rows(ref):
    at = 4 * EXT + SPEC
    return ref[at : at + EXT, : 3 * SUB]


def halo_rows(ref):
    at = 4 * EXT + SPEC
    return ref[at : at + EXT, 3 * SUB : 3 * EXT]


def coarse_part(ref, width):
    at, lanes = 5 * EXT + SPEC, 2 * SPEC
    parts = [ref[at + k * width : at + (k + 1) * width] for k in range(-(-width // lanes))]
    return (parts[0] if len(parts) == 1 else jnp.concatenate(parts, axis=1))[:, :width]


def constants(nr, nc, width):
    lanes = 2 * SPEC
    inverse = coarse_inverse(nr, nc, -(-width // lanes) * lanes)[:width]
    parts = [*block_constants(), *np.split(inverse, inverse.shape[1] // lanes, 1)]
    return np.concatenate(parts).astype(np.float32)


def coarse_inverse(nr, nc, width):
    br, er = sine(nr)
    bc, ec = sine(nc)
    both = np.kron(br, bc).reshape(nr, nc // 2, 2, nr * nc).transpose(2, 0, 1, 3)
    both = both.reshape(nr * nc, nr * nc)
    scale = (er[:, None] + ec[None, :]) / (SUB * SUB)
    values = (SUB * SUB * (DAMP + scale * scale)).reshape(-1)
    whole = np.zeros((width, width), np.float32)
    whole[: nr * nc, : nr * nc] = (both / values) @ both.T
    return whole


def dot(a, b, side=0):
    return lax.dot_general(
        a, b, (((1,), (side,)), ((), ())), precision=highest, preferred_element_type=jnp.float32
    )


def lap(x):
    rows, lanes = x.shape
    beside = pltpu.roll(x, 1, 0) + pltpu.roll(x, rows - 1, 0)
    beside = beside + (pltpu.roll(x, 1, 1) + pltpu.roll(x, lanes - 1, 1))
    return 4.0 * x - beside


def lanes_of(shape):
    return lax.broadcasted_iota(jnp.int32, shape, 1)


def rows_of(shape):
    return lax.broadcasted_iota(jnp.int32, shape, 0)


def total(x):
    return jnp.sum(jnp.sum(x, axis=0, keepdims=True), axis=1, keepdims=True)


def place():
    return lax.axis_index("row"), lax.axis_index("col")


def is_even(index):
    return lax.rem(index, 2) == 0


def grid_mask(shape, counts):
    i, j = place()
    rr, ll = rows_of(shape), lanes_of(shape)
    below = jnp.where(i < counts[0] - 1, 144, 128)
    above = jnp.where(i > 0, 144, 160)
    right = jnp.where(j < counts[1] - 1, 320, 256)
    left = jnp.where(j > 0, 320, 384)
    return ((rr < below) | (rr >= above)) & ((ll < right) | (ll >= left))


def flat_place(counts):
    i, j = place()
    nr, nc = counts
    shape = table_shape(counts)
    flat = rows_of(shape) * 128 + lanes_of(shape)
    device = flat % (nr * nc)
    return flat, (device // nc + nr - i) % nr, (device % nc + nc - j) % nc


def table_shape(counts):
    return (-(-2 * counts[0] * counts[1] // 1024) * 8, 128)


def table_of(values, counts):
    flat, rows, cols = flat_place(counts)
    devices = counts[0] * counts[1]
    own = jnp.where(flat < devices, values[0], jnp.where(flat < 2 * devices, values[1], 0.0))
    return jnp.where((rows == 0) & (cols == 0), own, 0.0)


def as_row(table, width):
    return jnp.concatenate([table[k : k + 1] for k in range(width // 128)], axis=1)


def row_of(pairs):
    lane = lanes_of((1, 128))
    row = jnp.zeros((1, 128), jnp.float32)
    for k, (left, right) in enumerate(pairs):
        row = jnp.where(lane == k, left, jnp.where(lane == 64 + k, right, row))
    return row


def gathered(rows, width):
    devices = rows.shape[0]
    turned = rows.T
    parts = [turned[:16], turned[64:80]]
    if width > 2 * devices:
        parts.append(jnp.zeros((16, width - 2 * devices), jnp.float32))
    return jnp.concatenate(parts, axis=1)


def coarse_values(c_row, inverse):
    return dot(jnp.broadcast_to(c_row, (8, c_row.shape[1])), inverse)[:1]


def spread(g_row, counts):
    i, j = place()
    nr, nc = counts[0], 2 * counts[1]
    shape = (16, g_row.shape[1])
    which = rows_of(shape)
    r = i - 1 + which // 4
    c = 2 * j - 1 + which % 4
    inside = (r >= 0) & (r < nr) & (c >= 0) & (c < nc) & (which < 12)
    at = lax.rem(c + 2, 2) * (nr * counts[1]) + r * counts[1] + (c + 2) // 2 - 1
    picked = jnp.where(inside & (lanes_of(shape) == at), g_row, 0.0)
    picked = jnp.sum(picked, axis=1, keepdims=True)
    lane = lanes_of((1, 128))
    bands = []
    for d in range(3):
        left, first, second, right = (picked[4 * d + k : 4 * d + k + 1] for k in range(4))
        bands.append(
            jnp.concatenate(
                [
                    jnp.broadcast_to(first, (1, 128)),
                    jnp.broadcast_to(second, (1, 128)),
                    jnp.where(lane < 64, right, left),
                ],
                axis=1,
            )
        )
    return jnp.concatenate(
        [
            jnp.broadcast_to(bands[1], (128, FC)),
            jnp.broadcast_to(bands[2], (16, FC)),
            jnp.broadcast_to(bands[0], (16, FC)),
        ],
        axis=0,
    )


def halves_of(x):
    high = x.astype(jnp.bfloat16)
    return high, (x - high.astype(jnp.float32)).astype(jnp.bfloat16)


def product(a, b):
    return lax.dot_general(a, b, (((1,), (0,)), ((), ())), preferred_element_type=jnp.float32)


def column_transform(w, basis_ref):
    high, low = halves_of(pltpu.roll(w, OV, 1))
    cols, rest = halves_of(cols_part(basis_ref))
    cols = jnp.concatenate([cols, rest, cols], axis=0)

    def block(at):
        part = slice(at, at + SPEC)
        return product(jnp.concatenate([high[:, part], high[:, part], low[:, part]], axis=1), cols)

    return jnp.concatenate([block(0), block(128)], axis=1)


def row_transform(u, basis_ref, part):
    high, low = halves_of(u)
    rows = part(basis_ref).astype(jnp.bfloat16)
    return product(rows, jnp.concatenate([high, low, high], axis=0))


def weights(means, basis_ref):
    lane = lanes_of((1, 2 * SPEC))
    mean = jnp.where(lane < SPEC, means[0], means[1])
    return 1.0 / (DAMP + mean * basis_ref[:EXT])


def strips_of(t, basis_ref, deep):
    cols = cols_part(basis_ref)
    left = dot(cols[:deep], t[:, :SPEC], 1)
    right = dot(cols[EXT - deep : EXT], t[:, SPEC:], 1)
    both = dot(jnp.concatenate([left, right], axis=0), rows_t_part(basis_ref))
    return both[:deep], both[deep:]


def solution_of(t, basis_ref):
    v = dot(rows_part(basis_ref), t)
    cols = cols_part(basis_ref)
    first, second = dot(v[:, :SPEC], cols), dot(v[:, SPEC:], cols)
    y = jnp.concatenate(
        [first[:, :128], first[:, 128:] + second[:, :128], second[:, 128:]], axis=1
    )
    return pltpu.roll(y, FC - OV, 1)


def core_sums(x):
    return [total(x[:, :128]), total(x[:, 128:256])]


def add_columns(y, from_left, from_right):
    far = from_left.shape[0] - OV
    gap = jnp.zeros((56 - far, EXT), jnp.float32)
    turned = jnp.concatenate(
        [from_right[8:], gap, from_right[:8], from_left[far:], gap, from_left[:far]], axis=0
    )
    back = turned.T
    lane = lanes_of((EXT, 128))
    rolled = pltpu.roll(back, 64, 1)
    first = y[:, :128] + jnp.where(lane < 8, rolled, 0.0)
    second = y[:, 128:256] + jnp.where(lane >= 120, rolled, 0.0)
    third = y[:, 256:] + jnp.where((lane < 16) | (lane >= 112), back, 0.0)
    return jnp.concatenate([first, second, third], axis=1)


def pack_rows(y, deep):
    return jnp.concatenate([y[136:], y[: deep - 8]], axis=0), y[136 - deep : 136]


def add_rows(y, from_above, from_below):
    far = from_above.shape[0] - OV
    none = jnp.zeros((8, FC), jnp.float32)
    return jnp.concatenate(
        [
            y[:8] + from_above[far:],
            y[8:120],
            y[120:136] + from_below[:16],
            from_below[16:] if far == 16 else none,
            from_above[:8] if far == 16 else none,
            y[136:] + from_above[far - 8 : far],
        ],
        axis=0,
    )


def sides(index, count, a, b):
    even = is_even(index)
    before = jnp.where(index > 0, jnp.where(even, b, a), 0.0)
    after = jnp.where(index < count - 1, jnp.where(even, a, b), 0.0)
    return before, after


def next_table(index, a, b):
    return jnp.where(is_even(index), a, b)[24:, :128]


def row_tables(index, nr, rows, a, b):
    even = is_even(index)
    after = jnp.where(even, a, b)[24:, :128]
    before = jnp.where(even, b, a)[24:, :128]
    if nr == 4:
        return jnp.where(rows == 2, after, 0.0)
    far = rows % 8
    return jnp.where(
        (far == 2) | (far == 5), after, jnp.where((far == 3) | (far == 6), before, 0.0)
    )


def send(index, a_ref, b_ref, before, after):
    even = is_even(index)
    a_ref[...] = jnp.where(even, after, before)
    b_ref[...] = jnp.where(even, before, after)


def begin_kernel(counts, both_ref, b_ref, a_ref):
    r, h = both_ref[:TR], both_ref[TR:]
    lane = lanes_of((128, 128))
    packed = jnp.where(
        lane < 16,
        r[:, :128],
        jnp.where(
            lane < 64,
            pltpu.roll(h[:, :128], 16, 1),
            jnp.where(lane < 112, pltpu.roll(h[:, 128:], 112, 1), r[:, 128:]),
        ),
    )
    turned = packed.T
    table = table_of(core_sums(r), counts)
    send(
        lax.axis_index("col"),
        a_ref,
        b_ref,
        jnp.concatenate([turned[:32], table], axis=0),
        jnp.concatenate([turned[96:], table], axis=0),
    )


def widen_kernel(counts, both_ref, gb_ref, ga_ref, r3_ref, h3_ref, b_ref, a_ref, table_ref):
    i, j = place()
    from_left, from_right = sides(j, counts[1], ga_ref[:32], gb_ref[:32])
    turned = jnp.concatenate([from_right, jnp.zeros((64, 128), jnp.float32), from_left], axis=0)
    back = turned.T
    lane = lanes_of((128, 128))
    edge = (lane < 16) | (lane >= 112)
    r3 = jnp.where(edge, back, 0.0)
    h3 = jnp.where(
        lane < 16, pltpu.roll(back, 112, 1), jnp.where(lane >= 112, pltpu.roll(back, 16, 1), 0.0)
    )
    r3_ref[...] = r3
    h3_ref[...] = h3
    r, h = both_ref[:TR], both_ref[TR:]
    table = table_of(core_sums(r), counts) + ga_ref[32:] + gb_ref[32:]
    table_ref[...] = table
    wide = jnp.concatenate([table, jnp.zeros((table.shape[0], FC - 128), jnp.float32)], axis=1)

    def strip(r_rows, h_rows):
        return jnp.concatenate(
            [
                jnp.concatenate([r[r_rows], r3[r_rows]], axis=1),
                jnp.concatenate([h[h_rows], h3[h_rows]], axis=1),
                wide,
            ],
            axis=0,
        )

    send(i, a_ref, b_ref, strip(slice(0, 8), slice(0, 16)), strip(slice(120, 128), slice(112, 128)))


def weights_kernel(both_ref, table_ref, basis_ref, weights_ref, table_out):
    h = both_ref[TR:]
    means = [x / (SUB * SUB) for x in core_sums(h * h * h)]
    weights_ref[...] = weights(means, basis_ref)
    table_out[...] = table_ref[...]


def forward_kernel(both_ref, r3_ref, basis_ref, t_ref):
    r = both_ref[:TR]
    u = column_transform(jnp.concatenate([r, r3_ref[...]], axis=1), basis_ref)
    t_ref[...] = row_transform(u, basis_ref, tile_rows)


def first_kernel(
    counts,
    gb_ref,
    ga_ref,
    tile_ref,
    weights_ref,
    basis_ref,
    table_ref,
    t_ref,
    table_out,
    b_ref,
    a_ref,
):
    i, j = place()
    above, below = sides(i, counts[0], ga_ref[:8], gb_ref[:8])
    u = column_transform(jnp.concatenate([below, above], axis=0), basis_ref)
    t = (tile_ref[...] + row_transform(u, basis_ref, halo_rows)) * weights_ref[...]
    t_ref[...] = t
    send(j, a_ref, b_ref, *strips_of(t, basis_ref, 24))
    table_out[...] = table_ref[...] + ga_ref[24:, :128] + gb_ref[24:, :128]


def inverse_kernel(counts, t_ref, basis_ref, both_ref, h3_ref, gb_ref, ga_ref, y_ref, m_ref):
    y_ref[...] = solution_of(t_ref[...], basis_ref)
    above, below = sides(lax.axis_index("row"), counts[0], ga_ref[8:24], gb_ref[8:24])
    h = jnp.concatenate([both_ref[TR:], h3_ref[...]], axis=1)
    tall = jnp.concatenate([h, below, above], axis=0)
    m_ref[...] = tall * tall * tall


def columns_kernel(counts, y_ref, *refs):
    i, j = place()
    (ga_ref, gb_ref), refs = (refs[:2] if len(refs) == 7 else refs[1::-1]), refs[2:]
    deep = 24 if len(refs) == 5 else 16
    y = add_columns(y_ref[...], *sides(j, counts[1], ga_ref[:deep], gb_ref[:deep]))
    strips = pack_rows(y, deep)
    if len(refs) == 5:
        table_ref, out_ref, table_out, b_ref, a_ref = refs
        cols = flat_place(counts)[2]
        table = table_ref[...] + jnp.where(
            cols % 4 == 2, next_table(j, ga_ref[...], gb_ref[...]), 0.0
        )
        table_out[...] = table
        wide = jnp.concatenate([table, jnp.zeros((table.shape[0], FC - 128), jnp.float32)], axis=1)
        strips = [jnp.concatenate([x, wide], axis=0) for x in strips]
    else:
        out_ref, b_ref, a_ref = refs
    out_ref[...] = y
    send(i, a_ref, b_ref, *strips)


def second_kernel(
    counts,
    width,
    y_ref,
    m_ref,
    gb_ref,
    ga_ref,
    table_ref,
    weights_ref,
    basis_ref,
    z_ref,
    w_ref,
    t_ref,
    table_out,
    b_ref,
    a_ref,
):
    i, j = place()
    s = add_rows(y_ref[...], *sides(i, counts[0], ga_ref[:24], gb_ref[:24]))
    mask = grid_mask((FR, FC), counts)
    s = jnp.where(mask, s, 0.0)
    rows = flat_place(counts)[1]
    table = table_ref[...] + row_tables(i, counts[0], rows, ga_ref[...], gb_ref[...])
    table_out[...] = table
    c0 = as_row(table, width)
    coarse = spread(coarse_values(c0, coarse_part(basis_ref, width)), counts)
    mobility = m_ref[...]
    flow = mobility * (lap(s) + lap(coarse))
    z = s + coarse
    w = jnp.where(mask, DAMP * z + lap(flow), 0.0) * SHRINK
    z_ref[...] = z[:128, :256]
    w_ref[...] = w[:128, :256]
    u = column_transform(jnp.concatenate([w[:136], w[152:]], axis=0), basis_ref)
    t = row_transform(u, basis_ref, whole_rows) * weights_ref[...]
    t_ref[...] = t
    send(j, a_ref, b_ref, *strips_of(t, basis_ref, 16))


def inverse_stats_kernel(t_ref, basis_ref, both_ref, m_ref, z_ref, w_ref, y_ref, stats_ref):
    y_ref[...] = solution_of(t_ref[...], basis_ref)
    rt, mt, zt, wt = both_ref[:TR], m_ref[:TR, :TC], z_ref[...], w_ref[...]
    lane, row = lanes_of((1, 256)), rows_of((128, 1))
    along = (lane % 128 != 0) & (lane % 128 != 127)
    top, low = mt[:1], mt[127:]
    side = jnp.sum(jnp.where((row > 0) & (row < 127), mt, 0.0), axis=0, keepdims=True)

    def halves(x):
        return [
            jnp.sum(x[:, :128], axis=1, keepdims=True),
            jnp.sum(x[:, 128:], axis=1, keepdims=True),
        ]

    first, last = lane % 128 == 0, lane % 128 == 127
    stats_ref[...] = row_of(
        [
            core_sums(rt * zt),
            core_sums(zt * wt),
            core_sums(wt),
            halves(jnp.where(along, top, 0.0)),
            halves(jnp.where(along, low, 0.0)),
            halves(jnp.where(first, side, 0.0)),
            halves(jnp.where(last, side, 0.0)),
            halves(jnp.where(first, top, 0.0)),
            halves(jnp.where(last, top, 0.0)),
            halves(jnp.where(first, low, 0.0)),
            halves(jnp.where(last, low, 0.0)),
        ]
    )


def dots_kernel(
    counts, y_ref, m_ref, gb_ref, ga_ref, both_ref, w_ref, stats_ref, q_ref, v_ref, stats_out
):
    i, j = place()
    q = add_rows(y_ref[...], *sides(i, counts[0], ga_ref[...], gb_ref[...]))
    q = jnp.where(grid_mask((FR, FC), counts), q, 0.0)
    v = DAMP * q + lap(m_ref[...] * lap(q))
    qt, vt = q[:128, :256], v[:128, :256]
    q_ref[...] = qt
    v_ref[...] = vt
    rest = [
        core_sums(vt),
        core_sums(both_ref[:TR] * qt),
        core_sums(w_ref[...] * qt),
        core_sums(vt * qt),
    ]
    zero = jnp.zeros((1, 1), jnp.float32)
    row = stats_ref[...] + row_of([[zero, zero]] * 11 + rest)
    stats_out[...] = jnp.broadcast_to(row, stats_out.shape)


def end_kernel(
    counts,
    width,
    stats_ref,
    table_ref,
    basis_ref,
    m_ref,
    both_ref,
    z_ref,
    w_ref,
    q_ref,
    v_ref,
    solution_ref,
    residual_ref,
):
    tiles_c = counts[1]
    devices = counts[0] * tiles_c
    table = gathered(stats_ref[...], width)
    st = [table[k : k + 1] for k in range(15)]

    def whole(x):
        return jnp.sum(x, axis=1, keepdims=True)

    rz, zw, rq, wq, qv = (whole(st[k]) for k in (0, 1, 12, 13, 14))
    c0, c1, sums_v = as_row(table_ref[...], width), st[2], st[11]
    g = coarse_values(c1, coarse_part(basis_ref, width))
    lane = lanes_of((1, width))
    cell = lane < 2 * devices
    on_left = lane < devices
    device = lane % devices
    column = device % tiles_c

    def from_lane(distance):
        return pltpu.roll(g, distance % width, 1)

    up = jnp.where(device >= tiles_c, from_lane(tiles_c), 0.0)
    down = jnp.where(device < devices - tiles_c, from_lane(-tiles_c), 0.0)
    left = jnp.where(
        on_left, jnp.where(column > 0, from_lane(1 - devices), 0.0), from_lane(devices)
    )
    right = jnp.where(
        on_left,
        from_lane(-devices),
        jnp.where(column < tiles_c - 1, from_lane(devices - 1), 0.0),
    )
    du, dd, dl, dr = g - up, g - down, g - left, g - right
    energy = DAMP * SUB * SUB * g * g
    energy = energy + st[3] * du * du + st[4] * dd * dd + st[5] * dl * dl + st[6] * dr * dr
    for weight, p, q in ((st[7], du, dl), (st[8], du, dr), (st[9], dd, dl), (st[10], dd, dr)):
        both = p + q
        energy = energy + weight * both * both
    ry = rq + whole(g * c0)
    yw = wq + whole(g * c1)
    yv = qv + whole(jnp.where(cell, 2.0 * g * sums_v + energy, 0.0))
    a = rz / zw
    rz1 = rz - a * ry - a * zw + a * a * yw
    beta1 = 1.0 + rz1 / rz
    dad = (beta1 * beta1 * zw - 2.0 * a * beta1 * yw) * (1.0 / SHRINK) + a * a * yv
    a1 = rz1 / dad
    coarse = spread(g, counts)
    y = q_ref[...] + coarse[:128, :256]
    image = DAMP * coarse + lap(m_ref[...] * lap(coarse))
    v = v_ref[...] + image[:128, :256]
    z, w = z_ref[...], w_ref[...]
    solution_ref[...] = (a * SHRINK) * z + a1 * (beta1 * z - a * y)
    residual_ref[...] = both_ref[:TR] - a * w - a1 * ((beta1 * (1.0 / SHRINK)) * w - a * v)


def call(kernel, outs, *args, flops=10**9):
    shapes = [jax.ShapeDtypeStruct(s, jnp.float32) for s in outs]
    return pl.pallas_call(
        kernel,
        out_shape=shapes,
        compiler_params=pltpu.CompilerParams(vmem_limit_bytes=48 * 1024 * 1024),
        cost_estimate=pl.CostEstimate(flops=flops, bytes_accessed=10**6, transcendentals=0),
    )(*args)


def pairs_from(count, offset, wrap=True):
    found = []
    for k in range(offset, count, 2):
        other = (k + 1) % count
        found += [(k, other), (other, k)] if wrap or other > k else [(k, k), (other, other)]
    return found


def body(counts, height, noise):
    nr, nc = counts
    devices = nr * nc
    width = max(128, devices * 2)
    basis = jnp.asarray(constants(nr, 2 * nc, width))
    both_axes = ("row", "col")
    depth = table_shape(counts)[0]

    def swap(a, b, axis, wrap=True):
        count = lax.axis_size(axis)
        gb = lax.ppermute(b, axis, pairs_from(count, 1, wrap))
        return lax.ppermute(a, axis, pairs_from(count, 0)), gb

    def row_shift(x, step):
        return lax.ppermute(x, "row", [(k, (k + step) % nr) for k in range(nr)])

    both = jnp.pad(noise, ((0, TR), (0, 0))) + jnp.pad(height, ((TR, 0), (0, 0)))
    b, a = call(functools.partial(begin_kernel, counts), [(32 + depth, 128)] * 2, both)
    ga, gb = swap(a, b, "col")
    r3, h3, b, a, table = call(
        functools.partial(widen_kernel, counts),
        [(128, 128)] * 2 + [(24 + depth, FC)] * 2 + [(depth, 128)],
        both,
        gb,
        ga,
    )
    step = nr // 2
    while step >= 8:
        table = table + row_shift(table, step)
        step //= 2
    if nr > 8:
        a, b = (x.at[24:, :128].set(table) for x in (a, b))
    ga, gb = swap(a, b, "row")
    weight, table = call(weights_kernel, [(EXT, 2 * SPEC), (depth, 128)], both, table, basis)
    far = row_shift(table, 4) if nr >= 8 else 0.0
    t = call(forward_kernel, [(EXT, 2 * SPEC)], both, r3, basis)[0]
    t, table, b, a = call(
        functools.partial(first_kernel, counts),
        [(EXT, 2 * SPEC), (depth, 128)] + [(24, EXT)] * 2,
        gb,
        ga,
        t,
        weight,
        basis,
        table,
    )
    table = table + far
    step = nc // 2
    while step >= 4:
        table = table + lax.ppermute(table, "col", [(k, (k + step) % nc) for k in range(nc)])
        step //= 2
    wide = jnp.pad(table, ((0, 0), (0, EXT - 128)))
    y, m = call(
        functools.partial(inverse_kernel, counts),
        [(EXT, FC), (FR, FC)],
        t,
        basis,
        both,
        h3,
        gb,
        ga,
    )
    ga, gb = swap(*(jnp.concatenate([x, wide], axis=0) for x in (a, b)), "col")
    y, table, b, a = call(
        functools.partial(columns_kernel, counts),
        [(EXT, FC), (depth, 128)] + [(24 + depth, FC)] * 2,
        y,
        ga,
        gb,
        table,
    )
    ga, gb = swap(a, b, "row")
    z, w, t, table, b, a = call(
        functools.partial(second_kernel, counts, width),
        [(TR, TC)] * 2 + [(EXT, 2 * SPEC), (depth, 128)] + [(16, EXT)] * 2,
        y,
        m,
        gb,
        ga,
        table,
        weight,
        basis,
    )
    ga, gb = swap(a, b, "col", False)
    y, stats = call(inverse_stats_kernel, [(EXT, FC), (1, 128)], t, basis, both, m, z, w)
    y, b, a = call(
        functools.partial(columns_kernel, counts), [(EXT, FC)] + [(16, FC)] * 2, y, gb, ga
    )
    ga, gb = swap(a, b, "row", False)
    q, v, stats = call(
        functools.partial(dots_kernel, counts),
        [(TR, TC)] * 2 + [(devices, 128)],
        y,
        m,
        gb,
        ga,
        both,
        w,
        stats,
    )
    stats = lax.all_to_all(stats, both_axes, 0, 0, tiled=True)
    return tuple(
        call(
            functools.partial(end_kernel, counts, width),
            [(TR, TC)] * 2,
            stats,
            table,
            basis,
            m,
            both,
            z,
            w,
            q,
            v,
        )
    )


def solution(mesh):
    counts = (mesh.shape["row"], mesh.shape["col"])
    spec = P("row", "col")
    return jax.shard_map(
        functools.partial(body, counts),
        mesh=mesh,
        in_specs=(spec, spec),
        out_specs=(spec, spec),
        check_vma=False,
    )
```

```python
import functools

import jax
import jax.numpy as jnp
import ml_dtypes
import numpy as np
from jax import lax
from jax.experimental import pallas as pl
from jax.experimental.pallas import tpu as pltpu
from jax.sharding import PartitionSpec as P

SUB = 128
OV = 8
EXT = SUB + 2 * OV
DAMP = 2.0**-28
SHRINK = 2.0**-20

TR, TC = 128, 256
FR, FC = 160, 384
SPEC = 256

highest = lax.Precision.HIGHEST


def sine(count):
    k = np.arange(1, count + 1, dtype=np.float64)
    basis = np.sqrt(2.0 / (count + 1.0)) * np.sin(np.pi * k[:, None] * k[None, :] / (count + 1.0))
    return basis, 2.0 - 2.0 * np.cos(np.pi * k / (count + 1.0))


def block_constants():
    basis, eig = sine(EXT)
    rows = np.roll(basis, -OV, 0)
    cols = np.pad(basis, ((0, SPEC - EXT), (0, SPEC - EXT)))
    scale = np.pad((eig[:, None] + eig[None, :]) ** 2, ((0, 0), (0, SPEC - EXT)))
    wide = lambda x: np.pad(x, ((0, 0), (0, 2 * SPEC - x.shape[1])))
    high = rows.T.astype(ml_dtypes.bfloat16).astype(np.float64)
    low = (rows.T - high).astype(ml_dtypes.bfloat16).astype(np.float64)
    tile = np.concatenate([x[:, :SUB] for x in (high, high, low)], 1)
    halo = np.concatenate([x[:, SUB:] for x in (high, high, low)], 1)
    whole = np.concatenate([high, high, low], 1)
    return [np.tile(scale, (1, 2)), *(wide(x) for x in (rows, rows.T, cols, whole, np.hstack([tile, halo])))]


def rows_part(ref):
    return ref[EXT : 2 * EXT, :EXT]


def rows_t_part(ref):
    return ref[2 * EXT : 3 * EXT, :EXT]


def cols_part(ref):
    return ref[3 * EXT : 3 * EXT + SPEC, :SPEC]


def whole_rows(ref):
    at = 3 * EXT + SPEC
    return ref[at : at + EXT, : 3 * EXT]


def tile_rows(ref):
    at = 4 * EXT + SPEC
    return ref[at : at + EXT, : 3 * SUB]


def halo_rows(ref):
    at = 4 * EXT + SPEC
    return ref[at : at + EXT, 3 * SUB : 3 * EXT]


def coarse_part(ref, width):
    at, lanes = 5 * EXT + SPEC, 2 * SPEC
    parts = [ref[at + k * width : at + (k + 1) * width] for k in range(-(-width // lanes))]
    return (parts[0] if len(parts) == 1 else jnp.concatenate(parts, axis=1))[:, :width]


def constants(nr, nc, width):
    lanes = 2 * SPEC
    inverse = coarse_inverse(nr, nc, -(-width // lanes) * lanes)[:width]
    parts = [*block_constants(), *np.split(inverse, inverse.shape[1] // lanes, 1)]
    return np.concatenate(parts).astype(np.float32)


def coarse_inverse(nr, nc, width):
    br, er = sine(nr)
    bc, ec = sine(nc)
    both = np.kron(br, bc).reshape(nr, nc // 2, 2, nr * nc).transpose(2, 0, 1, 3)
    both = both.reshape(nr * nc, nr * nc)
    scale = (er[:, None] + ec[None, :]) / (SUB * SUB)
    values = (SUB * SUB * (DAMP + scale * scale)).reshape(-1)
    whole = np.zeros((width, width), np.float32)
    whole[: nr * nc, : nr * nc] = (both / values) @ both.T
    return whole


def dot(a, b, side=0):
    return lax.dot_general(
        a, b, (((1,), (side,)), ((), ())), precision=highest, preferred_element_type=jnp.float32
    )


def lap(x):
    rows, lanes = x.shape
    beside = pltpu.roll(x, 1, 0) + pltpu.roll(x, rows - 1, 0)
    beside = beside + (pltpu.roll(x, 1, 1) + pltpu.roll(x, lanes - 1, 1))
    return 4.0 * x - beside


def lanes_of(shape):
    return lax.broadcasted_iota(jnp.int32, shape, 1)


def rows_of(shape):
    return lax.broadcasted_iota(jnp.int32, shape, 0)


def total(x):
    return jnp.sum(jnp.sum(x, axis=0, keepdims=True), axis=1, keepdims=True)


def place():
    return lax.axis_index("row"), lax.axis_index("col")


def is_even(index):
    return lax.rem(index, 2) == 0


def grid_mask(shape, counts):
    i, j = place()
    rr, ll = rows_of(shape), lanes_of(shape)
    below = jnp.where(i < counts[0] - 1, 144, 128)
    above = jnp.where(i > 0, 144, 160)
    right = jnp.where(j < counts[1] - 1, 320, 256)
    left = jnp.where(j > 0, 320, 384)
    return ((rr < below) | (rr >= above)) & ((ll < right) | (ll >= left))


def flat_place(counts):
    i, j = place()
    nr, nc = counts
    shape = table_shape(counts)
    flat = rows_of(shape) * 128 + lanes_of(shape)
    device = flat % (nr * nc)
    return flat, (device // nc + nr - i) % nr, (device % nc + nc - j) % nc


def table_shape(counts):
    return (-(-2 * counts[0] * counts[1] // 1024) * 8, 128)


def table_of(values, counts):
    flat, rows, cols = flat_place(counts)
    devices = counts[0] * counts[1]
    own = jnp.where(flat < devices, values[0], jnp.where(flat < 2 * devices, values[1], 0.0))
    return jnp.where((rows == 0) & (cols == 0), own, 0.0)


def as_row(table, width):
    return jnp.concatenate([table[k : k + 1] for k in range(width // 128)], axis=1)


def row_of(pairs):
    lane = lanes_of((1, 128))
    row = jnp.zeros((1, 128), jnp.float32)
    for k, (left, right) in enumerate(pairs):
        row = jnp.where(lane == k, left, jnp.where(lane == 64 + k, right, row))
    return row


def gathered(rows, width):
    devices = rows.shape[0]
    turned = rows.T
    parts = [turned[:16], turned[64:80]]
    if width > 2 * devices:
        parts.append(jnp.zeros((16, width - 2 * devices), jnp.float32))
    return jnp.concatenate(parts, axis=1)


def coarse_values(c_row, inverse):
    return dot(jnp.broadcast_to(c_row, (8, c_row.shape[1])), inverse)[:1]


def spread(g_row, counts):
    i, j = place()
    nr, nc = counts[0], 2 * counts[1]
    shape = (16, g_row.shape[1])
    which = rows_of(shape)
    r = i - 1 + which // 4
    c = 2 * j - 1 + which % 4
    inside = (r >= 0) & (r < nr) & (c >= 0) & (c < nc) & (which < 12)
    at = lax.rem(c + 2, 2) * (nr * counts[1]) + r * counts[1] + (c + 2) // 2 - 1
    picked = jnp.where(inside & (lanes_of(shape) == at), g_row, 0.0)
    picked = jnp.sum(picked, axis=1, keepdims=True)
    lane = lanes_of((1, 128))
    bands = []
    for d in range(3):
        left, first, second, right = (picked[4 * d + k : 4 * d + k + 1] for k in range(4))
        bands.append(
            jnp.concatenate(
                [
                    jnp.broadcast_to(first, (1, 128)),
                    jnp.broadcast_to(second, (1, 128)),
                    jnp.where(lane < 64, right, left),
                ],
                axis=1,
            )
        )
    return jnp.concatenate(
        [
            jnp.broadcast_to(bands[1], (128, FC)),
            jnp.broadcast_to(bands[2], (16, FC)),
            jnp.broadcast_to(bands[0], (16, FC)),
        ],
        axis=0,
    )


def halves_of(x):
    high = x.astype(jnp.bfloat16)
    return high, (x - high.astype(jnp.float32)).astype(jnp.bfloat16)


def product(a, b):
    return lax.dot_general(a, b, (((1,), (0,)), ((), ())), preferred_element_type=jnp.float32)


def column_transform(w, basis_ref):
    high, low = halves_of(pltpu.roll(w, OV, 1))
    cols, rest = halves_of(cols_part(basis_ref))
    cols = jnp.concatenate([cols, rest, cols], axis=0)

    def block(at):
        part = slice(at, at + SPEC)
        return product(jnp.concatenate([high[:, part], high[:, part], low[:, part]], axis=1), cols)

    return jnp.concatenate([block(0), block(128)], axis=1)


def row_transform(u, basis_ref, part):
    high, low = halves_of(u)
    rows = part(basis_ref).astype(jnp.bfloat16)
    return product(rows, jnp.concatenate([high, low, high], axis=0))


def weights(means, basis_ref):
    lane = lanes_of((1, 2 * SPEC))
    mean = jnp.where(lane < SPEC, means[0], means[1])
    return 1.0 / (DAMP + mean * basis_ref[:EXT])


def strips_of(t, basis_ref, deep):
    cols = cols_part(basis_ref)
    left = dot(cols[:deep], t[:, :SPEC], 1)
    right = dot(cols[EXT - deep : EXT], t[:, SPEC:], 1)
    both = dot(jnp.concatenate([left, right], axis=0), rows_t_part(basis_ref))
    return both[:deep], both[deep:]


def solution_of(t, basis_ref):
    v = dot(rows_part(basis_ref), t)
    cols = cols_part(basis_ref)
    first, second = dot(v[:, :SPEC], cols), dot(v[:, SPEC:], cols)
    y = jnp.concatenate(
        [first[:, :128], first[:, 128:] + second[:, :128], second[:, 128:]], axis=1
    )
    return pltpu.roll(y, FC - OV, 1)


def core_sums(x):
    return [total(x[:, :128]), total(x[:, 128:256])]


def add_columns(y, from_left, from_right):
    far = from_left.shape[0] - OV
    gap = jnp.zeros((56 - far, EXT), jnp.float32)
    turned = jnp.concatenate(
        [from_right[8:], gap, from_right[:8], from_left[far:], gap, from_left[:far]], axis=0
    )
    back = turned.T
    lane = lanes_of((EXT, 128))
    rolled = pltpu.roll(back, 64, 1)
    first = y[:, :128] + jnp.where(lane < 8, rolled, 0.0)
    second = y[:, 128:256] + jnp.where(lane >= 120, rolled, 0.0)
    third = y[:, 256:] + jnp.where((lane < 16) | (lane >= 112), back, 0.0)
    return jnp.concatenate([first, second, third], axis=1)


def pack_rows(y, deep):
    return jnp.concatenate([y[136:], y[: deep - 8]], axis=0), y[136 - deep : 136]


def add_rows(y, from_above, from_below):
    far = from_above.shape[0] - OV
    none = jnp.zeros((8, FC), jnp.float32)
    return jnp.concatenate(
        [
            y[:8] + from_above[far:],
            y[8:120],
            y[120:136] + from_below[:16],
            from_below[16:] if far == 16 else none,
            from_above[:8] if far == 16 else none,
            y[136:] + from_above[far - 8 : far],
        ],
        axis=0,
    )


def sides(index, count, a, b):
    even = is_even(index)
    before = jnp.where(index > 0, jnp.where(even, b, a), 0.0)
    after = jnp.where(index < count - 1, jnp.where(even, a, b), 0.0)
    return before, after


def next_table(index, a, b):
    return jnp.where(is_even(index), a, b)[24:, :128]


def row_tables(index, nr, rows, a, b):
    even = is_even(index)
    after = jnp.where(even, a, b)[24:, :128]
    before = jnp.where(even, b, a)[24:, :128]
    if nr == 4:
        return jnp.where(rows == 2, after, 0.0)
    far = rows % 8
    return jnp.where(
        (far == 2) | (far == 5), after, jnp.where((far == 3) | (far == 6), before, 0.0)
    )


def send(index, a_ref, b_ref, before, after):
    even = is_even(index)
    a_ref[...] = jnp.where(even, after, before)
    b_ref[...] = jnp.where(even, before, after)


def begin_kernel(counts, both_ref, b_ref, a_ref):
    r, h = both_ref[:TR], both_ref[TR:]
    lane = lanes_of((128, 128))
    packed = jnp.where(
        lane < 16,
        r[:, :128],
        jnp.where(
            lane < 64,
            pltpu.roll(h[:, :128], 16, 1),
            jnp.where(lane < 112, pltpu.roll(h[:, 128:], 112, 1), r[:, 128:]),
        ),
    )
    turned = packed.T
    table = table_of(core_sums(r), counts)
    send(
        lax.axis_index("col"),
        a_ref,
        b_ref,
        jnp.concatenate([turned[:32], table], axis=0),
        jnp.concatenate([turned[96:], table], axis=0),
    )


def widen_kernel(counts, both_ref, gb_ref, ga_ref, r3_ref, h3_ref, b_ref, a_ref, table_ref):
    i, j = place()
    from_left, from_right = sides(j, counts[1], ga_ref[:32], gb_ref[:32])
    turned = jnp.concatenate([from_right, jnp.zeros((64, 128), jnp.float32), from_left], axis=0)
    back = turned.T
    lane = lanes_of((128, 128))
    edge = (lane < 16) | (lane >= 112)
    r3 = jnp.where(edge, back, 0.0)
    h3 = jnp.where(
        lane < 16, pltpu.roll(back, 112, 1), jnp.where(lane >= 112, pltpu.roll(back, 16, 1), 0.0)
    )
    r3_ref[...] = r3
    h3_ref[...] = h3
    r, h = both_ref[:TR], both_ref[TR:]
    table = table_of(core_sums(r), counts) + ga_ref[32:] + gb_ref[32:]
    table_ref[...] = table
    wide = jnp.concatenate([table, jnp.zeros((table.shape[0], FC - 128), jnp.float32)], axis=1)

    def strip(r_rows, h_rows):
        return jnp.concatenate(
            [
                jnp.concatenate([r[r_rows], r3[r_rows]], axis=1),
                jnp.concatenate([h[h_rows], h3[h_rows]], axis=1),
                wide,
            ],
            axis=0,
        )

    send(i, a_ref, b_ref, strip(slice(0, 8), slice(0, 16)), strip(slice(120, 128), slice(112, 128)))


def weights_kernel(both_ref, table_ref, basis_ref, weights_ref, table_out):
    h = both_ref[TR:]
    means = [x / (SUB * SUB) for x in core_sums(h * h * h)]
    weights_ref[...] = weights(means, basis_ref)
    table_out[...] = table_ref[...]


def forward_kernel(both_ref, r3_ref, basis_ref, t_ref):
    r = both_ref[:TR]
    u = column_transform(jnp.concatenate([r, r3_ref[...]], axis=1), basis_ref)
    t_ref[...] = row_transform(u, basis_ref, tile_rows)


def first_kernel(
    counts,
    gb_ref,
    ga_ref,
    tile_ref,
    weights_ref,
    basis_ref,
    table_ref,
    t_ref,
    table_out,
    b_ref,
    a_ref,
):
    i, j = place()
    above, below = sides(i, counts[0], ga_ref[:8], gb_ref[:8])
    u = column_transform(jnp.concatenate([below, above], axis=0), basis_ref)
    t = (tile_ref[...] + row_transform(u, basis_ref, halo_rows)) * weights_ref[...]
    t_ref[...] = t
    send(j, a_ref, b_ref, *strips_of(t, basis_ref, 24))
    table_out[...] = table_ref[...] + ga_ref[24:, :128] + gb_ref[24:, :128]


def inverse_kernel(counts, t_ref, basis_ref, both_ref, h3_ref, gb_ref, ga_ref, y_ref, m_ref):
    y_ref[...] = solution_of(t_ref[...], basis_ref)
    above, below = sides(lax.axis_index("row"), counts[0], ga_ref[8:24], gb_ref[8:24])
    h = jnp.concatenate([both_ref[TR:], h3_ref[...]], axis=1)
    tall = jnp.concatenate([h, below, above], axis=0)
    m_ref[...] = tall * tall * tall


def columns_kernel(counts, y_ref, *refs):
    i, j = place()
    (ga_ref, gb_ref), refs = (refs[:2] if len(refs) == 7 else refs[1::-1]), refs[2:]
    deep = 24 if len(refs) == 5 else 16
    y = add_columns(y_ref[...], *sides(j, counts[1], ga_ref[:deep], gb_ref[:deep]))
    strips = pack_rows(y, deep)
    if len(refs) == 5:
        table_ref, out_ref, table_out, b_ref, a_ref = refs
        cols = flat_place(counts)[2]
        table = table_ref[...] + jnp.where(
            cols % 4 == 2, next_table(j, ga_ref[...], gb_ref[...]), 0.0
        )
        table_out[...] = table
        wide = jnp.concatenate([table, jnp.zeros((table.shape[0], FC - 128), jnp.float32)], axis=1)
        strips = [jnp.concatenate([x, wide], axis=0) for x in strips]
    else:
        out_ref, b_ref, a_ref = refs
    out_ref[...] = y
    send(i, a_ref, b_ref, *strips)


def second_kernel(
    counts,
    width,
    y_ref,
    m_ref,
    gb_ref,
    ga_ref,
    table_ref,
    weights_ref,
    basis_ref,
    z_ref,
    w_ref,
    t_ref,
    table_out,
    b_ref,
    a_ref,
):
    i, j = place()
    s = add_rows(y_ref[...], *sides(i, counts[0], ga_ref[:24], gb_ref[:24]))
    mask = grid_mask((FR, FC), counts)
    s = jnp.where(mask, s, 0.0)
    rows = flat_place(counts)[1]
    table = table_ref[...] + row_tables(i, counts[0], rows, ga_ref[...], gb_ref[...])
    table_out[...] = table
    c0 = as_row(table, width)
    coarse = spread(coarse_values(c0, coarse_part(basis_ref, width)), counts)
    mobility = m_ref[...]
    flow = mobility * (lap(s) + lap(coarse))
    z = s + coarse
    w = jnp.where(mask, DAMP * z + lap(flow), 0.0) * SHRINK
    z_ref[...] = z[:128, :256]
    w_ref[...] = w[:128, :256]
    u = column_transform(jnp.concatenate([w[:136], w[152:]], axis=0), basis_ref)
    t = row_transform(u, basis_ref, whole_rows) * weights_ref[...]
    t_ref[...] = t
    send(j, a_ref, b_ref, *strips_of(t, basis_ref, 16))


def inverse_stats_kernel(t_ref, basis_ref, both_ref, m_ref, z_ref, w_ref, y_ref, stats_ref):
    y_ref[...] = solution_of(t_ref[...], basis_ref)
    rt, mt, zt, wt = both_ref[:TR], m_ref[:TR, :TC], z_ref[...], w_ref[...]
    lane, row = lanes_of((1, 256)), rows_of((128, 1))
    along = (lane % 128 != 0) & (lane % 128 != 127)
    top, low = mt[:1], mt[127:]
    side = jnp.sum(jnp.where((row > 0) & (row < 127), mt, 0.0), axis=0, keepdims=True)

    def halves(x):
        return [
            jnp.sum(x[:, :128], axis=1, keepdims=True),
            jnp.sum(x[:, 128:], axis=1, keepdims=True),
        ]

    first, last = lane % 128 == 0, lane % 128 == 127
    stats_ref[...] = row_of(
        [
            core_sums(rt * zt),
            core_sums(zt * wt),
            core_sums(wt),
            halves(jnp.where(along, top, 0.0)),
            halves(jnp.where(along, low, 0.0)),
            halves(jnp.where(first, side, 0.0)),
            halves(jnp.where(last, side, 0.0)),
            halves(jnp.where(first, top, 0.0)),
            halves(jnp.where(last, top, 0.0)),
            halves(jnp.where(first, low, 0.0)),
            halves(jnp.where(last, low, 0.0)),
        ]
    )


def dots_kernel(
    counts, y_ref, m_ref, gb_ref, ga_ref, both_ref, w_ref, stats_ref, q_ref, v_ref, stats_out
):
    i, j = place()
    q = add_rows(y_ref[...], *sides(i, counts[0], ga_ref[...], gb_ref[...]))
    q = jnp.where(grid_mask((FR, FC), counts), q, 0.0)
    v = DAMP * q + lap(m_ref[...] * lap(q))
    qt, vt = q[:128, :256], v[:128, :256]
    q_ref[...] = qt
    v_ref[...] = vt
    rest = [
        core_sums(vt),
        core_sums(both_ref[:TR] * qt),
        core_sums(w_ref[...] * qt),
        core_sums(vt * qt),
    ]
    zero = jnp.zeros((1, 1), jnp.float32)
    row = stats_ref[...] + row_of([[zero, zero]] * 11 + rest)
    stats_out[...] = jnp.broadcast_to(row, stats_out.shape)


def end_kernel(
    counts,
    width,
    stats_ref,
    table_ref,
    basis_ref,
    m_ref,
    both_ref,
    z_ref,
    w_ref,
    q_ref,
    v_ref,
    solution_ref,
    residual_ref,
):
    tiles_c = counts[1]
    devices = counts[0] * tiles_c
    table = gathered(stats_ref[...], width)
    st = [table[k : k + 1] for k in range(15)]

    def whole(x):
        return jnp.sum(x, axis=1, keepdims=True)

    rz, zw, rq, wq, qv = (whole(st[k]) for k in (0, 1, 12, 13, 14))
    c0, c1, sums_v = as_row(table_ref[...], width), st[2], st[11]
    g = coarse_values(c1, coarse_part(basis_ref, width))
    lane = lanes_of((1, width))
    cell = lane < 2 * devices
    on_left = lane < devices
    device = lane % devices
    column = device % tiles_c

    def from_lane(distance):
        return pltpu.roll(g, distance % width, 1)

    up = jnp.where(device >= tiles_c, from_lane(tiles_c), 0.0)
    down = jnp.where(device < devices - tiles_c, from_lane(-tiles_c), 0.0)
    left = jnp.where(
        on_left, jnp.where(column > 0, from_lane(1 - devices), 0.0), from_lane(devices)
    )
    right = jnp.where(
        on_left,
        from_lane(-devices),
        jnp.where(column < tiles_c - 1, from_lane(devices - 1), 0.0),
    )
    du, dd, dl, dr = g - up, g - down, g - left, g - right
    energy = DAMP * SUB * SUB * g * g
    energy = energy + st[3] * du * du + st[4] * dd * dd + st[5] * dl * dl + st[6] * dr * dr
    for weight, p, q in ((st[7], du, dl), (st[8], du, dr), (st[9], dd, dl), (st[10], dd, dr)):
        both = p + q
        energy = energy + weight * both * both
    ry = rq + whole(g * c0)
    yw = wq + whole(g * c1)
    yv = qv + whole(jnp.where(cell, 2.0 * g * sums_v + energy, 0.0))
    a = rz / zw
    rz1 = rz - a * ry - a * zw + a * a * yw
    beta1 = 1.0 + rz1 / rz
    dad = (beta1 * beta1 * zw - 2.0 * a * beta1 * yw) * (1.0 / SHRINK) + a * a * yv
    a1 = rz1 / dad
    coarse = spread(g, counts)
    y = q_ref[...] + coarse[:128, :256]
    image = DAMP * coarse + lap(m_ref[...] * lap(coarse))
    v = v_ref[...] + image[:128, :256]
    z, w = z_ref[...], w_ref[...]
    solution_ref[...] = (a * SHRINK) * z + a1 * (beta1 * z - a * y)
    residual_ref[...] = both_ref[:TR] - a * w - a1 * ((beta1 * (1.0 / SHRINK)) * w - a * v)


def call(kernel, outs, *args, flops=10**9):
    shapes = [jax.ShapeDtypeStruct(s, jnp.float32) for s in outs]
    return pl.pallas_call(
        kernel,
        out_shape=shapes,
        compiler_params=pltpu.CompilerParams(vmem_limit_bytes=48 * 1024 * 1024),
        cost_estimate=pl.CostEstimate(flops=flops, bytes_accessed=10**6, transcendentals=0),
    )(*args)


def pairs_from(count, offset):
    found = []
    for k in range(offset, count, 2):
        found += [(k, (k + 1) % count), ((k + 1) % count, k)]
    return found


def near_pairs(counts, axis):
    found = []
    for i in range(counts[0]):
        for j in range(counts[1]):
            at = [i, j]
            if 0 < at[axis] < counts[axis] - 1:
                at[axis] += 1 if at[axis] % 2 else -1
            else:
                at[1 - axis] ^= 1
            found.append((i * counts[1] + j, at[0] * counts[1] + at[1]))
    return found


def body(counts, height, noise):
    nr, nc = counts
    devices = nr * nc
    width = max(128, devices * 2)
    basis = jnp.asarray(constants(nr, 2 * nc, width))
    both_axes = ("row", "col")
    depth = table_shape(counts)[0]

    def swap(a, b, axis, wrap=True):
        count = lax.axis_size(axis)
        if wrap:
            gb = lax.ppermute(b, axis, pairs_from(count, 1))
        else:
            gb = lax.ppermute(b, both_axes, near_pairs(counts, both_axes.index(axis)))
        return lax.ppermute(a, axis, pairs_from(count, 0)), gb

    def row_shift(x, step):
        return lax.ppermute(x, "row", [(k, (k + step) % nr) for k in range(nr)])

    both = jnp.pad(noise, ((0, TR), (0, 0))) + jnp.pad(height, ((TR, 0), (0, 0)))
    b, a = call(functools.partial(begin_kernel, counts), [(32 + depth, 128)] * 2, both)
    ga, gb = swap(a, b, "col")
    r3, h3, b, a, table = call(
        functools.partial(widen_kernel, counts),
        [(128, 128)] * 2 + [(24 + depth, FC)] * 2 + [(depth, 128)],
        both,
        gb,
        ga,
    )
    step = nr // 2
    while step >= 8:
        table = table + row_shift(table, step)
        step //= 2
    if nr > 8:
        a, b = (x.at[24:, :128].set(table) for x in (a, b))
    ga, gb = swap(a, b, "row")
    weight, table = call(weights_kernel, [(EXT, 2 * SPEC), (depth, 128)], both, table, basis)
    far = row_shift(table, 4) if nr >= 8 else 0.0
    t = call(forward_kernel, [(EXT, 2 * SPEC)], both, r3, basis)[0]
    t, table, b, a = call(
        functools.partial(first_kernel, counts),
        [(EXT, 2 * SPEC), (depth, 128)] + [(24, EXT)] * 2,
        gb,
        ga,
        t,
        weight,
        basis,
        table,
    )
    table = table + far
    step = nc // 2
    while step >= 4:
        table = table + lax.ppermute(table, "col", [(k, (k + step) % nc) for k in range(nc)])
        step //= 2
    wide = jnp.pad(table, ((0, 0), (0, EXT - 128)))
    y, m = call(
        functools.partial(inverse_kernel, counts),
        [(EXT, FC), (FR, FC)],
        t,
        basis,
        both,
        h3,
        gb,
        ga,
    )
    ga, gb = swap(*(jnp.concatenate([x, wide], axis=0) for x in (a, b)), "col")
    y, table, b, a = call(
        functools.partial(columns_kernel, counts),
        [(EXT, FC), (depth, 128)] + [(24 + depth, FC)] * 2,
        y,
        ga,
        gb,
        table,
    )
    ga, gb = swap(a, b, "row")
    z, w, t, table, b, a = call(
        functools.partial(second_kernel, counts, width),
        [(TR, TC)] * 2 + [(EXT, 2 * SPEC), (depth, 128)] + [(16, EXT)] * 2,
        y,
        m,
        gb,
        ga,
        table,
        weight,
        basis,
    )
    ga, gb = swap(a, b, "col", False)
    y, stats = call(inverse_stats_kernel, [(EXT, FC), (1, 128)], t, basis, both, m, z, w)
    y, b, a = call(
        functools.partial(columns_kernel, counts), [(EXT, FC)] + [(16, FC)] * 2, y, gb, ga
    )
    ga, gb = swap(a, b, "row", False)
    q, v, stats = call(
        functools.partial(dots_kernel, counts),
        [(TR, TC)] * 2 + [(devices, 128)],
        y,
        m,
        gb,
        ga,
        both,
        w,
        stats,
    )
    stats = lax.all_to_all(stats, both_axes, 0, 0, tiled=True)
    return tuple(
        call(
            functools.partial(end_kernel, counts, width),
            [(TR, TC)] * 2,
            stats,
            table,
            basis,
            m,
            both,
            z,
            w,
            q,
            v,
        )
    )


def solution(mesh):
    counts = (mesh.shape["row"], mesh.shape["col"])
    spec = P("row", "col")
    return jax.shard_map(
        functools.partial(body, counts),
        mesh=mesh,
        in_specs=(spec, spec),
        out_specs=(spec, spec),
        check_vma=False,
    )
```

```python
import functools

import jax
import jax.numpy as jnp
import ml_dtypes
import numpy as np
from jax import lax
from jax.experimental import pallas as pl
from jax.experimental.pallas import tpu as pltpu
from jax.sharding import PartitionSpec as P

SUB = 128
OV = 8
EXT = SUB + 2 * OV
DAMP = 2.0**-28
SHRINK = 2.0**-20

TR, TC = 128, 256
FR, FC = 160, 384
SPEC = 256

highest = lax.Precision.HIGHEST


def sine(count):
    k = np.arange(1, count + 1, dtype=np.float64)
    basis = np.sqrt(2.0 / (count + 1.0)) * np.sin(np.pi * k[:, None] * k[None, :] / (count + 1.0))
    return basis, 2.0 - 2.0 * np.cos(np.pi * k / (count + 1.0))


def block_constants():
    basis, eig = sine(EXT)
    rows = np.roll(basis, -OV, 0)
    cols = np.pad(basis, ((0, SPEC - EXT), (0, SPEC - EXT)))
    scale = np.pad((eig[:, None] + eig[None, :]) ** 2, ((0, 0), (0, SPEC - EXT)))
    wide = lambda x: np.pad(x, ((0, 0), (0, 2 * SPEC - x.shape[1])))
    high = rows.T.astype(ml_dtypes.bfloat16).astype(np.float64)
    low = (rows.T - high).astype(ml_dtypes.bfloat16).astype(np.float64)
    tile = np.concatenate([x[:, :SUB] for x in (high, high, low)], 1)
    halo = np.concatenate([x[:, SUB:] for x in (high, high, low)], 1)
    whole = np.concatenate([high, high, low], 1)
    return [np.tile(scale, (1, 2)), *(wide(x) for x in (rows, rows.T, cols, whole, np.hstack([tile, halo])))]


def rows_part(ref):
    return ref[EXT : 2 * EXT, :EXT]


def rows_t_part(ref):
    return ref[2 * EXT : 3 * EXT, :256]


def cols_part(ref):
    return ref[3 * EXT : 3 * EXT + SPEC, :SPEC]


def whole_rows(ref):
    at = 3 * EXT + SPEC
    return ref[at : at + EXT, : 3 * EXT]


def tile_rows(ref):
    at = 4 * EXT + SPEC
    return ref[at : at + EXT, : 3 * SUB]


def halo_rows(ref):
    at = 4 * EXT + SPEC
    return ref[at : at + EXT, 3 * SUB : 3 * EXT]


def coarse_part(ref, width):
    at, lanes = 5 * EXT + SPEC, 2 * SPEC
    parts = [ref[at + k * width : at + (k + 1) * width] for k in range(-(-width // lanes))]
    return (parts[0] if len(parts) == 1 else jnp.concatenate(parts, axis=1))[:, :width]


def constants(nr, nc, width):
    lanes = 2 * SPEC
    inverse = coarse_inverse(nr, nc, -(-width // lanes) * lanes)[:width]
    parts = [*block_constants(), *np.split(inverse, inverse.shape[1] // lanes, 1)]
    return np.concatenate(parts).astype(np.float32)


def coarse_inverse(nr, nc, width):
    br, er = sine(nr)
    bc, ec = sine(nc)
    both = np.kron(br, bc).reshape(nr, nc // 2, 2, nr * nc).transpose(2, 0, 1, 3)
    both = both.reshape(nr * nc, nr * nc)
    scale = (er[:, None] + ec[None, :]) / (SUB * SUB)
    values = (SUB * SUB * (DAMP + scale * scale)).reshape(-1)
    whole = np.zeros((width, width), np.float32)
    whole[: nr * nc, : nr * nc] = (both / values) @ both.T
    return whole


def dot(a, b, side=0):
    return lax.dot_general(
        a, b, (((1,), (side,)), ((), ())), precision=highest, preferred_element_type=jnp.float32
    )


def lap(x):
    rows, lanes = x.shape
    beside = pltpu.roll(x, 1, 0) + pltpu.roll(x, rows - 1, 0)
    beside = beside + (pltpu.roll(x, 1, 1) + pltpu.roll(x, lanes - 1, 1))
    return 4.0 * x - beside


def lanes_of(shape):
    return lax.broadcasted_iota(jnp.int32, shape, 1)


def rows_of(shape):
    return lax.broadcasted_iota(jnp.int32, shape, 0)


def total(x):
    return jnp.sum(jnp.sum(x, axis=0, keepdims=True), axis=1, keepdims=True)


def place():
    return lax.axis_index("row"), lax.axis_index("col")


def is_even(index):
    return lax.rem(index, 2) == 0


def grid_mask(shape, counts):
    i, j = place()
    rr, ll = rows_of(shape), lanes_of(shape)
    below = jnp.where(i < counts[0] - 1, 144, 128)
    above = jnp.where(i > 0, 144, 160)
    right = jnp.where(j < counts[1] - 1, 320, 256)
    left = jnp.where(j > 0, 320, 384)
    return ((rr < below) | (rr >= above)) & ((ll < right) | (ll >= left))


def flat_place(counts):
    i, j = place()
    nr, nc = counts
    shape = table_shape(counts)
    flat = rows_of(shape) * 128 + lanes_of(shape)
    device = flat % (nr * nc)
    return flat, (device // nc + nr - i) % nr, (device % nc + nc - j) % nc


def table_shape(counts):
    return (-(-2 * counts[0] * counts[1] // 1024) * 8, 128)


def table_of(values, counts):
    flat, rows, cols = flat_place(counts)
    devices = counts[0] * counts[1]
    own = jnp.where(flat < devices, values[0], jnp.where(flat < 2 * devices, values[1], 0.0))
    return jnp.where((rows == 0) & (cols == 0), own, 0.0)


def as_row(table, width):
    return jnp.concatenate([table[k : k + 1] for k in range(width // 128)], axis=1)


def row_of(pairs):
    lane = lanes_of((1, 128))
    row = jnp.zeros((1, 128), jnp.float32)
    for k, (left, right) in enumerate(pairs):
        row = jnp.where(lane == k, left, jnp.where(lane == 64 + k, right, row))
    return row


def gathered(rows, width):
    devices = rows.shape[0]
    turned = rows.T
    parts = [turned[:16], turned[64:80]]
    if width > 2 * devices:
        parts.append(jnp.zeros((16, width - 2 * devices), jnp.float32))
    return jnp.concatenate(parts, axis=1)


def coarse_values(c_row, inverse):
    return dot(jnp.broadcast_to(c_row, (8, c_row.shape[1])), inverse)[:1]


def spread(g_row, counts):
    i, j = place()
    nr, nc = counts[0], 2 * counts[1]
    shape = (16, g_row.shape[1])
    which = rows_of(shape)
    r = i - 1 + which // 4
    c = 2 * j - 1 + which % 4
    inside = (r >= 0) & (r < nr) & (c >= 0) & (c < nc) & (which < 12)
    at = lax.rem(c + 2, 2) * (nr * counts[1]) + r * counts[1] + (c + 2) // 2 - 1
    picked = jnp.where(inside & (lanes_of(shape) == at), g_row, 0.0)
    picked = jnp.sum(picked, axis=1, keepdims=True)
    lane = lanes_of((1, 128))
    bands = []
    for d in range(3):
        left, first, second, right = (picked[4 * d + k : 4 * d + k + 1] for k in range(4))
        bands.append(
            jnp.concatenate(
                [
                    jnp.broadcast_to(first, (1, 128)),
                    jnp.broadcast_to(second, (1, 128)),
                    jnp.where(lane < 64, right, left),
                ],
                axis=1,
            )
        )
    return jnp.concatenate(
        [
            jnp.broadcast_to(bands[1], (128, FC)),
            jnp.broadcast_to(bands[2], (16, FC)),
            jnp.broadcast_to(bands[0], (16, FC)),
        ],
        axis=0,
    )


def halves_of(x):
    high = x.astype(jnp.bfloat16)
    return high, (x - high.astype(jnp.float32)).astype(jnp.bfloat16)


def product(a, b):
    return lax.dot_general(a, b, (((1,), (0,)), ((), ())), preferred_element_type=jnp.float32)


def column_transform(w, basis_ref):
    high, low = halves_of(pltpu.roll(w, OV, 1))
    cols, rest = halves_of(cols_part(basis_ref))
    cols = jnp.concatenate([cols, rest, cols], axis=0)

    def block(at):
        part = slice(at, at + SPEC)
        return product(jnp.concatenate([high[:, part], high[:, part], low[:, part]], axis=1), cols)

    return jnp.concatenate([block(0), block(128)], axis=1)


def row_transform(u, basis_ref, part):
    high, low = halves_of(u)
    rows = part(basis_ref).astype(jnp.bfloat16)
    return product(rows, jnp.concatenate([high, low, high], axis=0))


def weights(means, basis_ref):
    lane = lanes_of((1, 2 * SPEC))
    mean = jnp.where(lane < SPEC, means[0], means[1])
    return 1.0 / (DAMP + mean * basis_ref[:EXT])


def packed(parts, width):
    lane = lanes_of((8, 128))
    out = parts[0]
    for k, part in enumerate(parts[1:], 1):
        out = jnp.where(lane >= k * width, pltpu.roll(part, k * width, 1), out)
    return jnp.where(lane < len(parts) * width, out, 0.0)


def unpacked(block, k, width):
    return pltpu.roll(block, (128 - k * width) % 128, 1)


def pack_strip(strip):
    parts = [strip[at : at + 8, 128:] for at in range(0, strip.shape[0], 8)]
    return jnp.concatenate([strip[:, :128], packed(parts, EXT - SUB)], axis=0)


def unpack_strip(message):
    deep = message.shape[0] - 8
    parts = [unpacked(message[deep:], k, EXT - SUB) for k in range(deep // 8)]
    return message[:deep], jnp.concatenate(parts, axis=0)


def around(tile):
    return pltpu.roll(tile, 16, 1)


def pack_rows_message(rows, table):
    parts = [around(rows[at : at + 8, 256:]) for at in range(0, rows.shape[0], 8)]
    last = jnp.concatenate([packed(parts, 32), table], axis=1)
    return jnp.concatenate([rows[:, :256], last], axis=0)


def unpack_rows(message, start, stop):
    block = message[message.shape[0] - 8 :, :128]
    lane = lanes_of((8, 128))
    thirds = []
    for k in range(start // 8, stop // 8):
        part = pltpu.roll(unpacked(block, k, 32), 112, 1)
        thirds.append(jnp.where((lane < 16) | (lane >= 112), part, 0.0))
    return jnp.concatenate([message[start:stop], jnp.concatenate(thirds, axis=0)], axis=1)


def strips_of(t, basis_ref, deep):
    cols = cols_part(basis_ref)
    left = dot(cols[:deep], t[:, :SPEC], 1)
    right = dot(cols[EXT - deep : EXT], t[:, SPEC:], 1)
    both = dot(jnp.concatenate([left, right], axis=0), rows_t_part(basis_ref))
    return pack_strip(both[:deep]), pack_strip(both[deep:])


def solution_of(t, basis_ref):
    v = dot(rows_part(basis_ref), t)
    cols = cols_part(basis_ref)
    first, second = dot(v[:, :SPEC], cols), dot(v[:, SPEC:], cols)
    y = jnp.concatenate(
        [first[:, :128], first[:, 128:] + second[:, :128], second[:, 128:]], axis=1
    )
    return pltpu.roll(y, FC - OV, 1)


def core_sums(x):
    return [total(x[:, :128]), total(x[:, 128:256])]


def add_columns(y, from_left, from_right):
    left, right = unpack_strip(from_left), unpack_strip(from_right)
    far = left[0].shape[0] - OV
    gap = jnp.zeros((56 - far, 128), jnp.float32)

    def turn(k):
        return jnp.concatenate(
            [right[k][8:], gap, right[k][:8], left[k][far:], gap, left[k][:far]], axis=0
        ).T

    back = jnp.concatenate([turn(0), turn(1)[: EXT - SUB]], axis=0)
    lane = lanes_of((EXT, 128))
    rolled = pltpu.roll(back, 64, 1)
    first = y[:, :128] + jnp.where(lane < 8, rolled, 0.0)
    second = y[:, 128:256] + jnp.where(lane >= 120, rolled, 0.0)
    third = y[:, 256:] + jnp.where((lane < 16) | (lane >= 112), back, 0.0)
    return jnp.concatenate([first, second, third], axis=1)


def pack_rows(y, deep):
    return jnp.concatenate([y[136:], y[: deep - 8]], axis=0), y[136 - deep : 136]


def add_rows(y, from_above, from_below):
    far = from_above.shape[0] - OV
    none = jnp.zeros((8, FC), jnp.float32)
    return jnp.concatenate(
        [
            y[:8] + from_above[far:],
            y[8:120],
            y[120:136] + from_below[:16],
            from_below[16:] if far == 16 else none,
            from_above[:8] if far == 16 else none,
            y[136:] + from_above[far - 8 : far],
        ],
        axis=0,
    )


def sides(index, count, a, b):
    even = is_even(index)
    before = jnp.where(index > 0, jnp.where(even, b, a), 0.0)
    after = jnp.where(index < count - 1, jnp.where(even, a, b), 0.0)
    return before, after


def next_table(index, a, b):
    return jnp.where(is_even(index), a, b)[32:]


def row_tables(index, nr, rows, a, b):
    even = is_even(index)
    after = jnp.where(even, a, b)[24:, 128:]
    before = jnp.where(even, b, a)[24:, 128:]
    if nr == 4:
        return jnp.where(rows == 2, after, 0.0)
    far = rows % 8
    return jnp.where(
        (far == 2) | (far == 5), after, jnp.where((far == 3) | (far == 6), before, 0.0)
    )


def send(index, a_ref, b_ref, before, after):
    even = is_even(index)
    a_ref[...] = jnp.where(even, after, before)
    b_ref[...] = jnp.where(even, before, after)


def begin_kernel(counts, both_ref, b_ref, a_ref):
    r, h = both_ref[:TR], both_ref[TR:]
    lane = lanes_of((128, 128))
    packed = jnp.where(
        lane < 8,
        r[:, :128],
        jnp.where(
            lane < 64,
            pltpu.roll(h[:, :128], 8, 1),
            jnp.where(lane < 120, pltpu.roll(h[:, 128:], 120, 1), r[:, 128:]),
        ),
    )
    turned = packed.T
    table = table_of(core_sums(r), counts)
    send(
        lax.axis_index("col"),
        a_ref,
        b_ref,
        jnp.concatenate([turned[:24], table], axis=0),
        jnp.concatenate([turned[104:], table], axis=0),
    )


def widen_kernel(counts, both_ref, gb_ref, ga_ref, r3_ref, h3_ref, b_ref, a_ref, table_ref):
    i, j = place()
    from_left, from_right = sides(j, counts[1], ga_ref[:24], gb_ref[:24])
    turned = jnp.concatenate([from_right, jnp.zeros((80, 128), jnp.float32), from_left], axis=0)
    back = turned.T
    lane = lanes_of((128, 128))
    r3 = jnp.where((lane < 8) | (lane >= 120), back, 0.0)
    h3 = jnp.where(
        lane < 16, pltpu.roll(back, 120, 1), jnp.where(lane >= 112, pltpu.roll(back, 8, 1), 0.0)
    )
    r3_ref[...] = r3
    h3_ref[...] = h3
    r, h = both_ref[:TR], both_ref[TR:]
    table = table_of(core_sums(r), counts) + ga_ref[24:] + gb_ref[24:]
    table_ref[...] = table

    def strip(r_rows, h_rows):
        rows = jnp.concatenate(
            [
                jnp.concatenate([r[r_rows], r3[r_rows]], axis=1),
                jnp.concatenate([h[h_rows], h3[h_rows]], axis=1),
            ],
            axis=0,
        )
        return pack_rows_message(rows, table)

    send(i, a_ref, b_ref, strip(slice(0, 8), slice(0, 16)), strip(slice(120, 128), slice(112, 128)))


def weights_kernel(both_ref, table_ref, basis_ref, weights_ref, table_out):
    h = both_ref[TR:]
    means = [x / (SUB * SUB) for x in core_sums(h * h * h)]
    weights_ref[...] = weights(means, basis_ref)
    table_out[...] = table_ref[...]


def forward_kernel(both_ref, r3_ref, basis_ref, t_ref):
    r = both_ref[:TR]
    u = column_transform(jnp.concatenate([r, r3_ref[...]], axis=1), basis_ref)
    t_ref[...] = row_transform(u, basis_ref, tile_rows)


def first_kernel(
    counts,
    gb_ref,
    ga_ref,
    tile_ref,
    weights_ref,
    basis_ref,
    table_ref,
    t_ref,
    table_out,
    b_ref,
    a_ref,
):
    i, j = place()
    above, below = sides(i, counts[0], ga_ref[...], gb_ref[...])
    halo = jnp.concatenate([unpack_rows(below, 0, 8), unpack_rows(above, 0, 8)], axis=0)
    u = column_transform(halo, basis_ref)
    t = (tile_ref[...] + row_transform(u, basis_ref, halo_rows)) * weights_ref[...]
    t_ref[...] = t
    send(j, a_ref, b_ref, *strips_of(t, basis_ref, 24))
    table_out[...] = table_ref[...] + ga_ref[24:, 128:] + gb_ref[24:, 128:]


def inverse_kernel(counts, t_ref, basis_ref, both_ref, h3_ref, gb_ref, ga_ref, y_ref, m_ref):
    y_ref[...] = solution_of(t_ref[...], basis_ref)
    above, below = sides(lax.axis_index("row"), counts[0], ga_ref[...], gb_ref[...])
    h = jnp.concatenate([both_ref[TR:], h3_ref[...]], axis=1)
    tall = jnp.concatenate([h, unpack_rows(below, 8, 24), unpack_rows(above, 8, 24)], axis=0)
    m_ref[...] = tall * tall * tall


def columns_kernel(counts, y_ref, *refs):
    i, j = place()
    (ga_ref, gb_ref), refs = (refs[:2] if len(refs) == 7 else refs[1::-1]), refs[2:]
    deep = 24 if len(refs) == 5 else 16
    y = add_columns(y_ref[...], *sides(j, counts[1], ga_ref[: deep + 8], gb_ref[: deep + 8]))
    strips = pack_rows(y, deep)
    if len(refs) == 5:
        table_ref, out_ref, table_out, b_ref, a_ref = refs
        cols = flat_place(counts)[2]
        table = table_ref[...] + jnp.where(
            cols % 4 == 2, next_table(j, ga_ref[...], gb_ref[...]), 0.0
        )
        table_out[...] = table
    else:
        out_ref, b_ref, a_ref = refs
        table = jnp.zeros((8, 128), jnp.float32)
    out_ref[...] = y
    send(i, a_ref, b_ref, *(pack_rows_message(x, table) for x in strips))


def second_kernel(
    counts,
    width,
    y_ref,
    m_ref,
    gb_ref,
    ga_ref,
    table_ref,
    weights_ref,
    basis_ref,
    z_ref,
    w_ref,
    t_ref,
    table_out,
    b_ref,
    a_ref,
):
    i, j = place()
    above, below = sides(i, counts[0], ga_ref[...], gb_ref[...])
    s = add_rows(y_ref[...], unpack_rows(above, 0, 24), unpack_rows(below, 0, 24))
    mask = grid_mask((FR, FC), counts)
    s = jnp.where(mask, s, 0.0)
    rows = flat_place(counts)[1]
    table = table_ref[...] + row_tables(i, counts[0], rows, ga_ref[...], gb_ref[...])
    table_out[...] = table
    c0 = as_row(table, width)
    coarse = spread(coarse_values(c0, coarse_part(basis_ref, width)), counts)
    mobility = m_ref[...]
    flow = mobility * (lap(s) + lap(coarse))
    z = s + coarse
    w = jnp.where(mask, DAMP * z + lap(flow), 0.0) * SHRINK
    z_ref[...] = z[:128, :256]
    w_ref[...] = w[:128, :256]
    u = column_transform(jnp.concatenate([w[:136], w[152:]], axis=0), basis_ref)
    t = row_transform(u, basis_ref, whole_rows) * weights_ref[...]
    t_ref[...] = t
    send(j, a_ref, b_ref, *strips_of(t, basis_ref, 16))


def inverse_stats_kernel(t_ref, basis_ref, both_ref, m_ref, z_ref, w_ref, y_ref, stats_ref):
    y_ref[...] = solution_of(t_ref[...], basis_ref)
    rt, mt, zt, wt = both_ref[:TR], m_ref[:TR, :TC], z_ref[...], w_ref[...]
    lane, row = lanes_of((1, 256)), rows_of((128, 1))
    along = (lane % 128 != 0) & (lane % 128 != 127)
    top, low = mt[:1], mt[127:]
    side = jnp.sum(jnp.where((row > 0) & (row < 127), mt, 0.0), axis=0, keepdims=True)

    def halves(x):
        return [
            jnp.sum(x[:, :128], axis=1, keepdims=True),
            jnp.sum(x[:, 128:], axis=1, keepdims=True),
        ]

    first, last = lane % 128 == 0, lane % 128 == 127
    stats_ref[...] = row_of(
        [
            core_sums(rt * zt),
            core_sums(zt * wt),
            core_sums(wt),
            halves(jnp.where(along, top, 0.0)),
            halves(jnp.where(along, low, 0.0)),
            halves(jnp.where(first, side, 0.0)),
            halves(jnp.where(last, side, 0.0)),
            halves(jnp.where(first, top, 0.0)),
            halves(jnp.where(last, top, 0.0)),
            halves(jnp.where(first, low, 0.0)),
            halves(jnp.where(last, low, 0.0)),
        ]
    )


def dots_kernel(
    counts, y_ref, m_ref, gb_ref, ga_ref, both_ref, w_ref, stats_ref, q_ref, v_ref, stats_out
):
    i, j = place()
    above, below = sides(i, counts[0], ga_ref[...], gb_ref[...])
    q = add_rows(y_ref[...], unpack_rows(above, 0, 16), unpack_rows(below, 0, 16))
    q = jnp.where(grid_mask((FR, FC), counts), q, 0.0)
    v = DAMP * q + lap(m_ref[...] * lap(q))
    qt, vt = q[:128, :256], v[:128, :256]
    q_ref[...] = qt
    v_ref[...] = vt
    rest = [
        core_sums(vt),
        core_sums(both_ref[:TR] * qt),
        core_sums(w_ref[...] * qt),
        core_sums(vt * qt),
    ]
    zero = jnp.zeros((1, 1), jnp.float32)
    row = stats_ref[...] + row_of([[zero, zero]] * 11 + rest)
    stats_out[...] = jnp.broadcast_to(row, stats_out.shape)


def end_kernel(
    counts,
    width,
    stats_ref,
    table_ref,
    basis_ref,
    m_ref,
    both_ref,
    z_ref,
    w_ref,
    q_ref,
    v_ref,
    solution_ref,
    residual_ref,
):
    tiles_c = counts[1]
    devices = counts[0] * tiles_c
    table = gathered(stats_ref[...], width)
    st = [table[k : k + 1] for k in range(15)]

    def whole(x):
        return jnp.sum(x, axis=1, keepdims=True)

    rz, zw, rq, wq, qv = (whole(st[k]) for k in (0, 1, 12, 13, 14))
    c0, c1, sums_v = as_row(table_ref[...], width), st[2], st[11]
    g = coarse_values(c1, coarse_part(basis_ref, width))
    lane = lanes_of((1, width))
    cell = lane < 2 * devices
    on_left = lane < devices
    device = lane % devices
    column = device % tiles_c

    def from_lane(distance):
        return pltpu.roll(g, distance % width, 1)

    up = jnp.where(device >= tiles_c, from_lane(tiles_c), 0.0)
    down = jnp.where(device < devices - tiles_c, from_lane(-tiles_c), 0.0)
    left = jnp.where(
        on_left, jnp.where(column > 0, from_lane(1 - devices), 0.0), from_lane(devices)
    )
    right = jnp.where(
        on_left,
        from_lane(-devices),
        jnp.where(column < tiles_c - 1, from_lane(devices - 1), 0.0),
    )
    du, dd, dl, dr = g - up, g - down, g - left, g - right
    energy = DAMP * SUB * SUB * g * g
    energy = energy + st[3] * du * du + st[4] * dd * dd + st[5] * dl * dl + st[6] * dr * dr
    for weight, p, q in ((st[7], du, dl), (st[8], du, dr), (st[9], dd, dl), (st[10], dd, dr)):
        both = p + q
        energy = energy + weight * both * both
    ry = rq + whole(g * c0)
    yw = wq + whole(g * c1)
    yv = qv + whole(jnp.where(cell, 2.0 * g * sums_v + energy, 0.0))
    a = rz / zw
    rz1 = rz - a * ry - a * zw + a * a * yw
    beta1 = 1.0 + rz1 / rz
    dad = (beta1 * beta1 * zw - 2.0 * a * beta1 * yw) * (1.0 / SHRINK) + a * a * yv
    a1 = rz1 / dad
    coarse = spread(g, counts)
    y = q_ref[...] + coarse[:128, :256]
    image = DAMP * coarse + lap(m_ref[...] * lap(coarse))
    v = v_ref[...] + image[:128, :256]
    z, w = z_ref[...], w_ref[...]
    solution_ref[...] = (a * SHRINK) * z + a1 * (beta1 * z - a * y)
    residual_ref[...] = both_ref[:TR] - a * w - a1 * ((beta1 * (1.0 / SHRINK)) * w - a * v)


def call(kernel, outs, *args, flops=10**9):
    shapes = [jax.ShapeDtypeStruct(s, jnp.float32) for s in outs]
    return pl.pallas_call(
        kernel,
        out_shape=shapes,
        compiler_params=pltpu.CompilerParams(vmem_limit_bytes=48 * 1024 * 1024),
        cost_estimate=pl.CostEstimate(flops=flops, bytes_accessed=10**6, transcendentals=0),
    )(*args)


def pairs_from(count, offset):
    found = []
    for k in range(offset, count, 2):
        found += [(k, (k + 1) % count), ((k + 1) % count, k)]
    return found


def near_pairs(counts, axis):
    found = []
    for i in range(counts[0]):
        for j in range(counts[1]):
            at = [i, j]
            if 0 < at[axis] < counts[axis] - 1:
                at[axis] += 1 if at[axis] % 2 else -1
            else:
                at[1 - axis] ^= 1
            found.append((i * counts[1] + j, at[0] * counts[1] + at[1]))
    return found


def body(counts, height, noise):
    nr, nc = counts
    devices = nr * nc
    width = max(128, devices * 2)
    basis = jnp.asarray(constants(nr, 2 * nc, width))
    both_axes = ("row", "col")
    depth = table_shape(counts)[0]

    def swap(a, b, axis, wrap=True):
        count = lax.axis_size(axis)
        if wrap:
            gb = lax.ppermute(b, axis, pairs_from(count, 1))
        else:
            gb = lax.ppermute(b, both_axes, near_pairs(counts, both_axes.index(axis)))
        return lax.ppermute(a, axis, pairs_from(count, 0)), gb

    def row_shift(x, step):
        return lax.ppermute(x, "row", [(k, (k + step) % nr) for k in range(nr)])

    both = jnp.pad(noise, ((0, TR), (0, 0))) + jnp.pad(height, ((TR, 0), (0, 0)))
    b, a = call(functools.partial(begin_kernel, counts), [(24 + depth, 128)] * 2, both)
    ga, gb = swap(a, b, "col")
    r3, h3, b, a, table = call(
        functools.partial(widen_kernel, counts),
        [(128, 128)] * 2 + [(24 + depth, 256)] * 2 + [(depth, 128)],
        both,
        gb,
        ga,
    )
    step = nr // 2
    while step >= 8:
        table = table + row_shift(table, step)
        step //= 2
    if nr > 8:
        a, b = (x.at[24:, 128:].set(table) for x in (a, b))
    ga, gb = swap(a, b, "row")
    weight, table = call(weights_kernel, [(EXT, 2 * SPEC), (depth, 128)], both, table, basis)
    far = row_shift(table, 4) if nr >= 8 else 0.0
    t = call(forward_kernel, [(EXT, 2 * SPEC)], both, r3, basis)[0]
    t, table, b, a = call(
        functools.partial(first_kernel, counts),
        [(EXT, 2 * SPEC), (depth, 128)] + [(32, 128)] * 2,
        gb,
        ga,
        t,
        weight,
        basis,
        table,
    )
    table = table + far
    step = nc // 2
    while step >= 4:
        table = table + lax.ppermute(table, "col", [(k, (k + step) % nc) for k in range(nc)])
        step //= 2
    y, m = call(
        functools.partial(inverse_kernel, counts),
        [(EXT, FC), (FR, FC)],
        t,
        basis,
        both,
        h3,
        gb,
        ga,
    )
    ga, gb = swap(*(jnp.concatenate([x, table], axis=0) for x in (a, b)), "col")
    y, table, b, a = call(
        functools.partial(columns_kernel, counts),
        [(EXT, FC), (depth, 128)] + [(24 + depth, 256)] * 2,
        y,
        ga,
        gb,
        table,
    )
    ga, gb = swap(a, b, "row")
    z, w, t, table, b, a = call(
        functools.partial(second_kernel, counts, width),
        [(TR, TC)] * 2 + [(EXT, 2 * SPEC), (depth, 128)] + [(24, 128)] * 2,
        y,
        m,
        gb,
        ga,
        table,
        weight,
        basis,
    )
    ga, gb = swap(a, b, "col", False)
    y, stats = call(inverse_stats_kernel, [(EXT, FC), (1, 128)], t, basis, both, m, z, w)
    y, b, a = call(
        functools.partial(columns_kernel, counts), [(EXT, FC)] + [(24, 256)] * 2, y, gb, ga
    )
    ga, gb = swap(a, b, "row", False)
    q, v, stats = call(
        functools.partial(dots_kernel, counts),
        [(TR, TC)] * 2 + [(devices, 128)],
        y,
        m,
        gb,
        ga,
        both,
        w,
        stats,
    )
    stats = lax.all_to_all(stats, both_axes, 0, 0, tiled=True)
    return tuple(
        call(
            functools.partial(end_kernel, counts, width),
            [(TR, TC)] * 2,
            stats,
            table,
            basis,
            m,
            both,
            z,
            w,
            q,
            v,
        )
    )


def solution(mesh):
    counts = (mesh.shape["row"], mesh.shape["col"])
    spec = P("row", "col")
    return jax.shard_map(
        functools.partial(body, counts),
        mesh=mesh,
        in_specs=(spec, spec),
        out_specs=(spec, spec),
        check_vma=False,
    )
```

```python
import functools

import jax
import jax.numpy as jnp
import ml_dtypes
import numpy as np
from jax import lax
from jax.experimental import pallas as pl
from jax.experimental.pallas import tpu as pltpu
from jax.sharding import PartitionSpec as P

SUB = 128
OV = 8
EXT = SUB + 2 * OV
DAMP = 2.0**-28
SHRINK = 2.0**-20

TR, TC = 128, 256
FR, FC = 160, 384
SPEC = 256

highest = lax.Precision.HIGHEST


def sine(count):
    k = np.arange(1, count + 1, dtype=np.float64)
    basis = np.sqrt(2.0 / (count + 1.0)) * np.sin(np.pi * k[:, None] * k[None, :] / (count + 1.0))
    return basis, 2.0 - 2.0 * np.cos(np.pi * k / (count + 1.0))


def block_constants():
    basis, eig = sine(EXT)
    rows = np.roll(basis, -OV, 0)
    cols = np.pad(basis, ((0, SPEC - EXT), (0, SPEC - EXT)))
    scale = np.pad((eig[:, None] + eig[None, :]) ** 2, ((0, 0), (0, SPEC - EXT)))
    wide = lambda x: np.pad(x, ((0, 0), (0, 2 * SPEC - x.shape[1])))
    high = rows.T.astype(ml_dtypes.bfloat16).astype(np.float64)
    low = (rows.T - high).astype(ml_dtypes.bfloat16).astype(np.float64)
    tile = np.concatenate([x[:, :SUB] for x in (high, high, low)], 1)
    halo = np.concatenate([x[:, SUB:] for x in (high, high, low)], 1)
    whole = np.concatenate([high, high, low], 1)
    return [np.tile(scale, (1, 2)), *(wide(x) for x in (rows, rows.T, cols, whole, np.hstack([tile, halo])))]


def rows_part(ref):
    return ref[EXT : 2 * EXT, :EXT]


def rows_t_part(ref):
    return ref[2 * EXT : 3 * EXT, :EXT]


def cols_part(ref):
    return ref[3 * EXT : 3 * EXT + SPEC, :SPEC]


def whole_rows(ref):
    at = 3 * EXT + SPEC
    return ref[at : at + EXT, : 3 * EXT]


def tile_rows(ref):
    at = 4 * EXT + SPEC
    return ref[at : at + EXT, : 3 * SUB]


def halo_rows(ref):
    at = 4 * EXT + SPEC
    return ref[at : at + EXT, 3 * SUB : 3 * EXT]


def coarse_part(ref, width):
    at, lanes = 5 * EXT + SPEC, 2 * SPEC
    parts = [ref[at + k * width : at + (k + 1) * width] for k in range(-(-width // lanes))]
    return (parts[0] if len(parts) == 1 else jnp.concatenate(parts, axis=1))[:, :width]


def constants(nr, nc, width):
    lanes = 2 * SPEC
    inverse = coarse_inverse(nr, nc, -(-width // lanes) * lanes)[:width]
    parts = [*block_constants(), *np.split(inverse, inverse.shape[1] // lanes, 1)]
    return np.concatenate(parts).astype(np.float32)


def coarse_inverse(nr, nc, width):
    br, er = sine(nr)
    bc, ec = sine(nc)
    both = np.kron(br, bc).reshape(nr, nc // 2, 2, nr * nc).transpose(2, 0, 1, 3)
    both = both.reshape(nr * nc, nr * nc)
    scale = (er[:, None] + ec[None, :]) / (SUB * SUB)
    values = (SUB * SUB * (DAMP + scale * scale)).reshape(-1)
    whole = np.zeros((width, width), np.float32)
    whole[: nr * nc, : nr * nc] = (both / values) @ both.T
    return whole


def dot(a, b, side=0):
    return lax.dot_general(
        a, b, (((1,), (side,)), ((), ())), precision=highest, preferred_element_type=jnp.float32
    )


def lap(x):
    rows, lanes = x.shape
    beside = pltpu.roll(x, 1, 0) + pltpu.roll(x, rows - 1, 0)
    beside = beside + (pltpu.roll(x, 1, 1) + pltpu.roll(x, lanes - 1, 1))
    return 4.0 * x - beside


def lanes_of(shape):
    return lax.broadcasted_iota(jnp.int32, shape, 1)


def rows_of(shape):
    return lax.broadcasted_iota(jnp.int32, shape, 0)


def total(x):
    return jnp.sum(jnp.sum(x, axis=0, keepdims=True), axis=1, keepdims=True)


def place():
    return lax.axis_index("row"), lax.axis_index("col")


def is_even(index):
    return lax.rem(index, 2) == 0


def grid_mask(shape, counts):
    i, j = place()
    rr, ll = rows_of(shape), lanes_of(shape)
    below = jnp.where(i < counts[0] - 1, 144, 128)
    above = jnp.where(i > 0, 144, 160)
    right = jnp.where(j < counts[1] - 1, 320, 256)
    left = jnp.where(j > 0, 320, 384)
    return ((rr < below) | (rr >= above)) & ((ll < right) | (ll >= left))


def table_shape(counts):
    return (-(-2 * counts[0] * counts[1] // 1024) * 8, 128)


def table_of(values, counts):
    i, j = place()
    devices = counts[0] * counts[1]
    shape = table_shape(counts)
    at = rows_of(shape) * 128 + lanes_of(shape) - (i * counts[1] + j)
    return jnp.where(at == 0, values[0], jnp.where(at == devices, values[1], 0.0))


def merged(table, *others):
    for other in others:
        table = jnp.where(table != 0.0, table, other)
    return table


def as_row(table, width):
    return jnp.concatenate([table[k : k + 1] for k in range(width // 128)], axis=1)


def row_of(pairs):
    lane = lanes_of((1, 128))
    row = jnp.zeros((1, 128), jnp.float32)
    for k, (left, right) in enumerate(pairs):
        row = jnp.where(lane == k, left, jnp.where(lane == 64 + k, right, row))
    return row


def gathered(rows, width):
    devices = rows.shape[0]
    turned = rows.T
    parts = [turned[:16], turned[64:80]]
    if width > 2 * devices:
        parts.append(jnp.zeros((16, width - 2 * devices), jnp.float32))
    return jnp.concatenate(parts, axis=1)


def coarse_values(c_row, inverse):
    return dot(jnp.broadcast_to(c_row, (8, c_row.shape[1])), inverse)[:1]


def spread(g_row, counts):
    i, j = place()
    nr, nc = counts[0], 2 * counts[1]
    shape = (16, g_row.shape[1])
    which = rows_of(shape)
    r = i - 1 + which // 4
    c = 2 * j - 1 + which % 4
    inside = (r >= 0) & (r < nr) & (c >= 0) & (c < nc) & (which < 12)
    at = lax.rem(c + 2, 2) * (nr * counts[1]) + r * counts[1] + (c + 2) // 2 - 1
    picked = jnp.where(inside & (lanes_of(shape) == at), g_row, 0.0)
    picked = jnp.sum(picked, axis=1, keepdims=True)
    lane = lanes_of((1, 128))
    bands = []
    for d in range(3):
        left, first, second, right = (picked[4 * d + k : 4 * d + k + 1] for k in range(4))
        bands.append(
            jnp.concatenate(
                [
                    jnp.broadcast_to(first, (1, 128)),
                    jnp.broadcast_to(second, (1, 128)),
                    jnp.where(lane < 64, right, left),
                ],
                axis=1,
            )
        )
    return jnp.concatenate(
        [
            jnp.broadcast_to(bands[1], (128, FC)),
            jnp.broadcast_to(bands[2], (16, FC)),
            jnp.broadcast_to(bands[0], (16, FC)),
        ],
        axis=0,
    )


def halves_of(x):
    high = x.astype(jnp.bfloat16)
    return high, (x - high.astype(jnp.float32)).astype(jnp.bfloat16)


def product(a, b):
    return lax.dot_general(a, b, (((1,), (0,)), ((), ())), preferred_element_type=jnp.float32)


def column_transform(w, basis_ref):
    high, low = halves_of(pltpu.roll(w, OV, 1))
    cols, rest = halves_of(cols_part(basis_ref))
    cols = jnp.concatenate([cols, rest, cols], axis=0)

    def block(at):
        part = slice(at, at + SPEC)
        return product(jnp.concatenate([high[:, part], high[:, part], low[:, part]], axis=1), cols)

    return jnp.concatenate([block(0), block(128)], axis=1)


def row_transform(u, basis_ref, part):
    high, low = halves_of(u)
    rows = part(basis_ref).astype(jnp.bfloat16)
    return product(rows, jnp.concatenate([high, low, high], axis=0))


def weights(means, basis_ref):
    lane = lanes_of((1, 2 * SPEC))
    mean = jnp.where(lane < SPEC, means[0], means[1])
    return 1.0 / (DAMP + mean * basis_ref[:EXT])


def strips_of(t, basis_ref, deep):
    cols = cols_part(basis_ref)
    left = dot(cols[:deep], t[:, :SPEC], 1)
    right = dot(cols[EXT - deep : EXT], t[:, SPEC:], 1)
    both = dot(jnp.concatenate([left, right], axis=0), rows_t_part(basis_ref))
    return both[:deep], both[deep:]


def solution_of(t, basis_ref):
    v = dot(rows_part(basis_ref), t)
    cols = cols_part(basis_ref)
    first, second = dot(v[:, :SPEC], cols), dot(v[:, SPEC:], cols)
    y = jnp.concatenate(
        [first[:, :128], first[:, 128:] + second[:, :128], second[:, 128:]], axis=1
    )
    return pltpu.roll(y, FC - OV, 1)


def core_sums(x):
    return [total(x[:, :128]), total(x[:, 128:256])]


def add_columns(y, from_left, from_right):
    far = from_left.shape[0] - OV
    gap = jnp.zeros((56 - far, EXT), jnp.float32)
    turned = jnp.concatenate(
        [from_right[8:], gap, from_right[:8], from_left[far:], gap, from_left[:far]], axis=0
    )
    back = turned.T
    lane = lanes_of((EXT, 128))
    rolled = pltpu.roll(back, 64, 1)
    first = y[:, :128] + jnp.where(lane < 8, rolled, 0.0)
    second = y[:, 128:256] + jnp.where(lane >= 120, rolled, 0.0)
    third = y[:, 256:] + jnp.where((lane < 16) | (lane >= 112), back, 0.0)
    return jnp.concatenate([first, second, third], axis=1)


def pack_rows(y, deep):
    return jnp.concatenate([y[136:], y[: deep - 8]], axis=0), y[136 - deep : 136]


def add_rows(y, from_above, from_below):
    far = from_above.shape[0] - OV
    none = jnp.zeros((8, FC), jnp.float32)
    return jnp.concatenate(
        [
            y[:8] + from_above[far:],
            y[8:120],
            y[120:136] + from_below[:16],
            from_below[16:] if far == 16 else none,
            from_above[:8] if far == 16 else none,
            y[136:] + from_above[far - 8 : far],
        ],
        axis=0,
    )


def sides(index, count, a, b):
    even = is_even(index)
    before = jnp.where(index > 0, jnp.where(even, b, a), 0.0)
    after = jnp.where(index < count - 1, jnp.where(even, a, b), 0.0)
    return before, after


def send(index, a_ref, b_ref, before, after):
    even = is_even(index)
    a_ref[...] = jnp.where(even, after, before)
    b_ref[...] = jnp.where(even, before, after)


def begin_kernel(counts, both_ref, b_ref, a_ref, table_ref):
    r, h = both_ref[:TR], both_ref[TR:]
    lane = lanes_of((128, 128))
    packed = jnp.where(
        lane < 16,
        r[:, :128],
        jnp.where(
            lane < 64,
            pltpu.roll(h[:, :128], 16, 1),
            jnp.where(lane < 112, pltpu.roll(h[:, 128:], 112, 1), r[:, 128:]),
        ),
    )
    turned = packed.T
    table = table_of(core_sums(r), counts)
    table_ref[...] = table
    send(
        lax.axis_index("col"),
        a_ref,
        b_ref,
        jnp.concatenate([turned[:32], table], axis=0),
        jnp.concatenate([turned[96:], table], axis=0),
    )


def widen_kernel(counts, both_ref, own_ref, gb_ref, ga_ref, r3_ref, h3_ref, b_ref, a_ref, table_ref):
    i, j = place()
    from_left, from_right = sides(j, counts[1], ga_ref[:32], gb_ref[:32])
    turned = jnp.concatenate([from_right, jnp.zeros((64, 128), jnp.float32), from_left], axis=0)
    back = turned.T
    lane = lanes_of((128, 128))
    edge = (lane < 16) | (lane >= 112)
    r3 = jnp.where(edge, back, 0.0)
    h3 = jnp.where(
        lane < 16, pltpu.roll(back, 112, 1), jnp.where(lane >= 112, pltpu.roll(back, 16, 1), 0.0)
    )
    r3_ref[...] = r3
    h3_ref[...] = h3
    r, h = both_ref[:TR], both_ref[TR:]
    table = merged(own_ref[...], ga_ref[32:], gb_ref[32:])
    table_ref[...] = table
    wide = jnp.concatenate([table, jnp.zeros((table.shape[0], FC - 128), jnp.float32)], axis=1)

    def strip(r_rows, h_rows):
        return jnp.concatenate(
            [
                jnp.concatenate([r[r_rows], r3[r_rows]], axis=1),
                jnp.concatenate([h[h_rows], h3[h_rows]], axis=1),
                wide,
            ],
            axis=0,
        )

    send(i, a_ref, b_ref, strip(slice(0, 8), slice(0, 16)), strip(slice(120, 128), slice(112, 128)))


def weights_kernel(both_ref, table_ref, basis_ref, weights_ref, table_out):
    h = both_ref[TR:]
    means = [x / (SUB * SUB) for x in core_sums(h * h * h)]
    weights_ref[...] = weights(means, basis_ref)
    table_out[...] = table_ref[...]


def forward_kernel(both_ref, r3_ref, basis_ref, t_ref):
    r = both_ref[:TR]
    u = column_transform(jnp.concatenate([r, r3_ref[...]], axis=1), basis_ref)
    t_ref[...] = row_transform(u, basis_ref, tile_rows)


def first_kernel(
    counts,
    gb_ref,
    ga_ref,
    tile_ref,
    weights_ref,
    basis_ref,
    table_ref,
    t_ref,
    table_out,
    b_ref,
    a_ref,
):
    i, j = place()
    above, below = sides(i, counts[0], ga_ref[:8], gb_ref[:8])
    u = column_transform(jnp.concatenate([below, above], axis=0), basis_ref)
    t = (tile_ref[...] + row_transform(u, basis_ref, halo_rows)) * weights_ref[...]
    t_ref[...] = t
    send(j, a_ref, b_ref, *strips_of(t, basis_ref, 24))
    table_out[...] = merged(table_ref[...], ga_ref[24:, :128], gb_ref[24:, :128])


def mobility_kernel(counts, both_ref, h3_ref, gb_ref, ga_ref, table_ref, m_ref, table_out):
    above, below = sides(lax.axis_index("row"), counts[0], ga_ref[8:24], gb_ref[8:24])
    h = jnp.concatenate([both_ref[TR:], h3_ref[...]], axis=1)
    tall = jnp.concatenate([h, below, above], axis=0)
    m_ref[...] = tall * tall * tall
    table_out[...] = table_ref[...]


def inverse_kernel(t_ref, basis_ref, y_ref):
    y_ref[...] = solution_of(t_ref[...], basis_ref)


def columns_kernel(counts, y_ref, *refs):
    i, j = place()
    (ga_ref, gb_ref), refs = (refs[:2] if len(refs) == 8 else refs[1::-1]), refs[2:]
    deep = 24 if len(refs) == 6 else 16
    y = add_columns(y_ref[...], *sides(j, counts[1], ga_ref[:deep], gb_ref[:deep]))
    strips = pack_rows(y, deep)
    if len(refs) == 6:
        table_ref, far_ref, out_ref, table_out, b_ref, a_ref = refs
        table = merged(table_ref[...], far_ref[...], ga_ref[24:, :128], gb_ref[24:, :128])
        table_out[...] = table
        wide = jnp.concatenate([table, jnp.zeros((table.shape[0], FC - 128), jnp.float32)], axis=1)
        strips = [jnp.concatenate([x, wide], axis=0) for x in strips]
    else:
        out_ref, b_ref, a_ref = refs
    out_ref[...] = y
    send(i, a_ref, b_ref, *strips)


def second_kernel(
    counts,
    width,
    y_ref,
    m_ref,
    gb_ref,
    ga_ref,
    table_ref,
    weights_ref,
    basis_ref,
    z_ref,
    w_ref,
    t_ref,
    table_out,
    b_ref,
    a_ref,
):
    i, j = place()
    s = add_rows(y_ref[...], *sides(i, counts[0], ga_ref[:24], gb_ref[:24]))
    mask = grid_mask((FR, FC), counts)
    s = jnp.where(mask, s, 0.0)
    table = merged(table_ref[...], ga_ref[24:, :128], gb_ref[24:, :128])
    table_out[...] = table
    c0 = as_row(table, width)
    coarse = spread(coarse_values(c0, coarse_part(basis_ref, width)), counts)
    mobility = m_ref[...]
    flow = mobility * (lap(s) + lap(coarse))
    z = s + coarse
    w = jnp.where(mask, DAMP * z + lap(flow), 0.0) * SHRINK
    z_ref[...] = z[:128, :256]
    w_ref[...] = w[:128, :256]
    u = column_transform(jnp.concatenate([w[:136], w[152:]], axis=0), basis_ref)
    t = row_transform(u, basis_ref, whole_rows) * weights_ref[...]
    t_ref[...] = t
    send(j, a_ref, b_ref, *strips_of(t, basis_ref, 16))


def inverse_stats_kernel(t_ref, basis_ref, both_ref, m_ref, z_ref, w_ref, y_ref, stats_ref):
    y_ref[...] = solution_of(t_ref[...], basis_ref)
    rt, mt, zt, wt = both_ref[:TR], m_ref[:TR, :TC], z_ref[...], w_ref[...]
    lane, row = lanes_of((1, 256)), rows_of((128, 1))
    along = (lane % 128 != 0) & (lane % 128 != 127)
    top, low = mt[:1], mt[127:]
    side = jnp.sum(jnp.where((row > 0) & (row < 127), mt, 0.0), axis=0, keepdims=True)

    def halves(x):
        return [
            jnp.sum(x[:, :128], axis=1, keepdims=True),
            jnp.sum(x[:, 128:], axis=1, keepdims=True),
        ]

    first, last = lane % 128 == 0, lane % 128 == 127
    stats_ref[...] = row_of(
        [
            core_sums(rt * zt),
            core_sums(zt * wt),
            core_sums(wt),
            halves(jnp.where(along, top, 0.0)),
            halves(jnp.where(along, low, 0.0)),
            halves(jnp.where(first, side, 0.0)),
            halves(jnp.where(last, side, 0.0)),
            halves(jnp.where(first, top, 0.0)),
            halves(jnp.where(last, top, 0.0)),
            halves(jnp.where(first, low, 0.0)),
            halves(jnp.where(last, low, 0.0)),
        ]
    )


def dots_kernel(
    counts, y_ref, m_ref, gb_ref, ga_ref, both_ref, w_ref, stats_ref, q_ref, v_ref, stats_out
):
    i, j = place()
    q = add_rows(y_ref[...], *sides(i, counts[0], ga_ref[...], gb_ref[...]))
    q = jnp.where(grid_mask((FR, FC), counts), q, 0.0)
    v = DAMP * q + lap(m_ref[...] * lap(q))
    qt, vt = q[:128, :256], v[:128, :256]
    q_ref[...] = qt
    v_ref[...] = vt
    rest = [
        core_sums(vt),
        core_sums(both_ref[:TR] * qt),
        core_sums(w_ref[...] * qt),
        core_sums(vt * qt),
    ]
    zero = jnp.zeros((1, 1), jnp.float32)
    row = stats_ref[...] + row_of([[zero, zero]] * 11 + rest)
    stats_out[...] = jnp.broadcast_to(row, stats_out.shape)


def end_kernel(
    counts,
    width,
    stats_ref,
    table_ref,
    basis_ref,
    m_ref,
    both_ref,
    z_ref,
    w_ref,
    q_ref,
    v_ref,
    solution_ref,
    residual_ref,
):
    tiles_c = counts[1]
    devices = counts[0] * tiles_c
    table = gathered(stats_ref[...], width)
    st = [table[k : k + 1] for k in range(15)]

    def whole(x):
        return jnp.sum(x, axis=1, keepdims=True)

    rz, zw, rq, wq, qv = (whole(st[k]) for k in (0, 1, 12, 13, 14))
    c0, c1, sums_v = as_row(table_ref[...], width), st[2], st[11]
    g = coarse_values(c1, coarse_part(basis_ref, width))
    lane = lanes_of((1, width))
    cell = lane < 2 * devices
    on_left = lane < devices
    device = lane % devices
    column = device % tiles_c

    def from_lane(distance):
        return pltpu.roll(g, distance % width, 1)

    up = jnp.where(device >= tiles_c, from_lane(tiles_c), 0.0)
    down = jnp.where(device < devices - tiles_c, from_lane(-tiles_c), 0.0)
    left = jnp.where(
        on_left, jnp.where(column > 0, from_lane(1 - devices), 0.0), from_lane(devices)
    )
    right = jnp.where(
        on_left,
        from_lane(-devices),
        jnp.where(column < tiles_c - 1, from_lane(devices - 1), 0.0),
    )
    du, dd, dl, dr = g - up, g - down, g - left, g - right
    energy = DAMP * SUB * SUB * g * g
    energy = energy + st[3] * du * du + st[4] * dd * dd + st[5] * dl * dl + st[6] * dr * dr
    for weight, p, q in ((st[7], du, dl), (st[8], du, dr), (st[9], dd, dl), (st[10], dd, dr)):
        both = p + q
        energy = energy + weight * both * both
    ry = rq + whole(g * c0)
    yw = wq + whole(g * c1)
    yv = qv + whole(jnp.where(cell, 2.0 * g * sums_v + energy, 0.0))
    a = rz / zw
    rz1 = rz - a * ry - a * zw + a * a * yw
    beta1 = 1.0 + rz1 / rz
    dad = (beta1 * beta1 * zw - 2.0 * a * beta1 * yw) * (1.0 / SHRINK) + a * a * yv
    a1 = rz1 / dad
    coarse = spread(g, counts)
    y = q_ref[...] + coarse[:128, :256]
    image = DAMP * coarse + lap(m_ref[...] * lap(coarse))
    v = v_ref[...] + image[:128, :256]
    z, w = z_ref[...], w_ref[...]
    solution_ref[...] = (a * SHRINK) * z + a1 * (beta1 * z - a * y)
    residual_ref[...] = both_ref[:TR] - a * w - a1 * ((beta1 * (1.0 / SHRINK)) * w - a * v)


def call(kernel, outs, *args, flops=10**9):
    shapes = [jax.ShapeDtypeStruct(s, jnp.float32) for s in outs]
    return pl.pallas_call(
        kernel,
        out_shape=shapes,
        compiler_params=pltpu.CompilerParams(vmem_limit_bytes=48 * 1024 * 1024),
        cost_estimate=pl.CostEstimate(flops=flops, bytes_accessed=10**6, transcendentals=0),
    )(*args)


def pairs_from(count, offset):
    found = []
    for k in range(offset, count, 2):
        found += [(k, (k + 1) % count), ((k + 1) % count, k)]
    return found


def near_pairs(counts, axis, bit):
    found = []
    for i in range(counts[0]):
        for j in range(counts[1]):
            at = [i, j]
            if 0 < at[axis] < counts[axis] - 1:
                at[axis] += 1 if at[axis] % 2 else -1
            else:
                at[1 - axis] ^= bit
            found.append((i * counts[1] + j, at[0] * counts[1] + at[1]))
    return found


def xor_pairs(counts, rows, cols):
    flat = [(i, j) for i in range(counts[0]) for j in range(counts[1])]
    return [(i * counts[1] + j, (i ^ rows) * counts[1] + (j ^ cols)) for i, j in flat]


def spreads(counts):
    known = np.eye(counts[0] * counts[1], dtype=bool)

    def meet(*swaps):
        return np.logical_or.reduce([known, *(known[[b for _, b in pairs]] for pairs in swaps)])

    even = [xor_pairs(counts, 0, 1), xor_pairs(counts, 1, 0)]
    known = meet(even[0], near_pairs(counts, 1, 1))
    known = meet(even[1], near_pairs(counts, 0, 1), xor_pairs(counts, 4, 0))
    known = meet(even[0], near_pairs(counts, 1, 2), xor_pairs(counts, 2, 3))
    return meet(even[1], near_pairs(counts, 0, 1)).all()


def body(counts, height, noise):
    nr, nc = counts
    devices = nr * nc
    width = max(128, devices * 2)
    basis = jnp.asarray(constants(nr, 2 * nc, width))
    both_axes = ("row", "col")
    depth = table_shape(counts)[0]

    def swap(a, b, axis, bit=1):
        gb = lax.ppermute(b, both_axes, near_pairs(counts, both_axes.index(axis), bit))
        return lax.ppermute(a, axis, pairs_from(lax.axis_size(axis), 0)), gb

    def small_swap(x, rows, cols):
        return lax.ppermute(x, both_axes, xor_pairs(counts, rows, cols))

    both = jnp.pad(noise, ((0, TR), (0, 0))) + jnp.pad(height, ((TR, 0), (0, 0)))
    b, a, table = call(
        functools.partial(begin_kernel, counts), [(32 + depth, 128)] * 2 + [(depth, 128)], both
    )
    if not spreads(counts):
        for axis, count in enumerate(counts):
            bit = 1
            while bit < count:
                table = table + small_swap(table, *((0, bit) if axis else (bit, 0)))
                bit *= 2
    ga, gb = swap(a, b, "col")
    r3, h3, b, a, table = call(
        functools.partial(widen_kernel, counts),
        [(128, 128)] * 2 + [(24 + depth, FC)] * 2 + [(depth, 128)],
        both,
        table,
        gb,
        ga,
    )
    ga, gb = swap(a, b, "row")
    weight, table = call(weights_kernel, [(EXT, 2 * SPEC), (depth, 128)], both, table, basis)
    far = small_swap(table, 4, 0)
    t = call(forward_kernel, [(EXT, 2 * SPEC)], both, r3, basis)[0]
    t, table, b, a = call(
        functools.partial(first_kernel, counts),
        [(EXT, 2 * SPEC), (depth, 128)] + [(24, EXT)] * 2,
        gb,
        ga,
        t,
        weight,
        basis,
        table,
    )
    table = merged(table, far)
    wide = jnp.pad(table, ((0, 0), (0, EXT - 128)))
    m, table_too = call(
        functools.partial(mobility_kernel, counts),
        [(FR, FC), (depth, 128)],
        both,
        h3,
        gb,
        ga,
        table,
    )
    y = call(inverse_kernel, [(EXT, FC)], t, basis)[0]
    ga, gb = swap(*(jnp.concatenate([x, wide], axis=0) for x in (a, b)), "col", 2)
    far = small_swap(table_too, 2, 3)
    y, table, b, a = call(
        functools.partial(columns_kernel, counts),
        [(EXT, FC), (depth, 128)] + [(24 + depth, FC)] * 2,
        y,
        ga,
        gb,
        table,
        far,
    )
    ga, gb = swap(a, b, "row")
    z, w, t, table, b, a = call(
        functools.partial(second_kernel, counts, width),
        [(TR, TC)] * 2 + [(EXT, 2 * SPEC), (depth, 128)] + [(16, EXT)] * 2,
        y,
        m,
        gb,
        ga,
        table,
        weight,
        basis,
    )
    ga, gb = swap(a, b, "col")
    y, stats = call(inverse_stats_kernel, [(EXT, FC), (1, 128)], t, basis, both, m, z, w)
    y, b, a = call(
        functools.partial(columns_kernel, counts), [(EXT, FC)] + [(16, FC)] * 2, y, gb, ga
    )
    ga, gb = swap(a, b, "row")
    q, v, stats = call(
        functools.partial(dots_kernel, counts),
        [(TR, TC)] * 2 + [(devices, 128)],
        y,
        m,
        gb,
        ga,
        both,
        w,
        stats,
    )
    stats = lax.all_to_all(stats, both_axes, 0, 0, tiled=True)
    return tuple(
        call(
            functools.partial(end_kernel, counts, width),
            [(TR, TC)] * 2,
            stats,
            table,
            basis,
            m,
            both,
            z,
            w,
            q,
            v,
        )
    )


def solution(mesh):
    counts = (mesh.shape["row"], mesh.shape["col"])
    spec = P("row", "col")
    return jax.shard_map(
        functools.partial(body, counts),
        mesh=mesh,
        in_specs=(spec, spec),
        out_specs=(spec, spec),
        check_vma=False,
    )
```

```python
import functools

import jax
import jax.numpy as jnp
import ml_dtypes
import numpy as np
from jax import lax
from jax.experimental import pallas as pl
from jax.experimental.pallas import tpu as pltpu
from jax.sharding import PartitionSpec as P

SUB = 128
OV = 8
EXT = SUB + 2 * OV
DAMP = 2.0**-28
SHRINK = 2.0**-20

TR, TC = 128, 256
FR, FC = 160, 384
SPEC = 256

highest = lax.Precision.HIGHEST


def sine(count):
    k = np.arange(1, count + 1, dtype=np.float64)
    basis = np.sqrt(2.0 / (count + 1.0)) * np.sin(np.pi * k[:, None] * k[None, :] / (count + 1.0))
    return basis, 2.0 - 2.0 * np.cos(np.pi * k / (count + 1.0))


def block_constants():
    basis, eig = sine(EXT)
    rows = np.roll(basis, -OV, 0)
    cols = np.pad(basis, ((0, SPEC - EXT), (0, SPEC - EXT)))
    scale = np.pad((eig[:, None] + eig[None, :]) ** 2, ((0, 0), (0, SPEC - EXT)))
    wide = lambda x: np.pad(x, ((0, 0), (0, 2 * SPEC - x.shape[1])))
    high = rows.T.astype(ml_dtypes.bfloat16).astype(np.float64)
    low = (rows.T - high).astype(ml_dtypes.bfloat16).astype(np.float64)
    tile = np.concatenate([x[:, :SUB] for x in (high, high, low)], 1)
    halo = np.concatenate([x[:, SUB:] for x in (high, high, low)], 1)
    inner = np.concatenate([x[:, 16:112] for x in (high, high, low)], 1)
    at = [*range(136, 144), *range(16), *range(112, 136)]
    edge = np.concatenate([x[:, at] for x in (high, high, low)], 1)
    turned = np.hstack([rows.T, np.zeros((EXT, 256 - EXT)), edge])
    return [np.tile(scale, (1, 2)), *(wide(x) for x in (rows, turned, cols, inner, np.hstack([tile, halo])))]


def rows_part(ref):
    return ref[EXT : 2 * EXT, :EXT]


def rows_t_part(ref):
    return ref[2 * EXT : 3 * EXT, :256]


def cols_part(ref):
    return ref[3 * EXT : 3 * EXT + SPEC, :SPEC]


def inner_rows(ref):
    at = 3 * EXT + SPEC
    return ref[at : at + EXT, : 3 * 96]


def edge_rows(ref):
    return ref[2 * EXT : 3 * EXT, 256 : 256 + 3 * 48]


def tile_rows(ref):
    at = 4 * EXT + SPEC
    return ref[at : at + EXT, : 3 * SUB]


def halo_rows(ref):
    at = 4 * EXT + SPEC
    return ref[at : at + EXT, 3 * SUB : 3 * EXT]


def coarse_part(ref, width):
    at, lanes = 5 * EXT + SPEC, 2 * SPEC
    parts = [ref[at + k * width : at + (k + 1) * width] for k in range(-(-width // lanes))]
    return (parts[0] if len(parts) == 1 else jnp.concatenate(parts, axis=1))[:, :width]


def constants(nr, nc, width):
    lanes = 2 * SPEC
    inverse = coarse_inverse(nr, nc, -(-width // lanes) * lanes)[:width]
    parts = [*block_constants(), *np.split(inverse, inverse.shape[1] // lanes, 1)]
    return np.concatenate(parts).astype(np.float32)


def coarse_inverse(nr, nc, width):
    br, er = sine(nr)
    bc, ec = sine(nc)
    both = np.kron(br, bc).reshape(nr, nc // 2, 2, nr * nc).transpose(2, 0, 1, 3)
    both = both.reshape(nr * nc, nr * nc)
    scale = (er[:, None] + ec[None, :]) / (SUB * SUB)
    values = (SUB * SUB * (DAMP + scale * scale)).reshape(-1)
    whole = np.zeros((width, width), np.float32)
    whole[: nr * nc, : nr * nc] = (both / values) @ both.T
    return whole


def dot(a, b, side=0):
    return lax.dot_general(
        a, b, (((1,), (side,)), ((), ())), precision=highest, preferred_element_type=jnp.float32
    )


def lap(x):
    rows, lanes = x.shape
    beside = pltpu.roll(x, 1, 0) + pltpu.roll(x, rows - 1, 0)
    beside = beside + (pltpu.roll(x, 1, 1) + pltpu.roll(x, lanes - 1, 1))
    return 4.0 * x - beside


def lanes_of(shape):
    return lax.broadcasted_iota(jnp.int32, shape, 1)


def rows_of(shape):
    return lax.broadcasted_iota(jnp.int32, shape, 0)


def total(x):
    return jnp.sum(jnp.sum(x, axis=0, keepdims=True), axis=1, keepdims=True)


def place():
    return lax.axis_index("row"), lax.axis_index("col")


def is_even(index):
    return lax.rem(index, 2) == 0


def column_mask(counts):
    j = lax.axis_index("col")
    lane = lanes_of((1, FC))
    right = jnp.where(j < counts[1] - 1, 320, 256)
    left = jnp.where(j > 0, 320, 384)
    return (lane < right) | (lane >= left)


def edge_mask(counts):
    i = lax.axis_index("row")
    row = rows_of((80, 1))
    first = jnp.where(i > 0, 0, 16)
    last = jnp.where(i < counts[0] - 1, 80, 64)
    return (row >= first) & (row < last) & column_mask(counts)


def table_shape(counts):
    return (-(-2 * counts[0] * counts[1] // 1024) * 8, 128)


def table_of(values, counts):
    i, j = place()
    devices = counts[0] * counts[1]
    shape = table_shape(counts)
    at = rows_of(shape) * 128 + lanes_of(shape) - (i * counts[1] + j)
    return jnp.where(at == 0, values[0], jnp.where(at == devices, values[1], 0.0))


def merged(table, *others):
    for other in others:
        table = jnp.where(table != 0.0, table, other)
    return table


def as_row(table, width):
    return jnp.concatenate([table[k : k + 1] for k in range(width // 128)], axis=1)


def row_of(pairs):
    lane = lanes_of((1, 128))
    row = jnp.zeros((1, 128), jnp.float32)
    for k, (left, right) in enumerate(pairs):
        row = jnp.where(lane == k, left, jnp.where(lane == 64 + k, right, row))
    return row


def gathered(rows, width):
    devices = rows.shape[0]
    turned = rows.T
    parts = [turned[:16], turned[64:80]]
    if width > 2 * devices:
        parts.append(jnp.zeros((16, width - 2 * devices), jnp.float32))
    return jnp.concatenate(parts, axis=1)


def coarse_values(c_row, inverse):
    return dot(jnp.broadcast_to(c_row, (8, c_row.shape[1])), inverse)[:1]


def band_rows(g_row, counts):
    i, j = place()
    nr, nc = counts[0], 2 * counts[1]
    shape = (16, g_row.shape[1])
    which = rows_of(shape)
    r = i - 1 + which // 4
    c = 2 * j - 1 + which % 4
    inside = (r >= 0) & (r < nr) & (c >= 0) & (c < nc) & (which < 12)
    at = lax.rem(c + 2, 2) * (nr * counts[1]) + r * counts[1] + (c + 2) // 2 - 1
    picked = jnp.where(inside & (lanes_of(shape) == at), g_row, 0.0)
    picked = jnp.sum(picked, axis=1, keepdims=True)
    lane = lanes_of((1, FC))
    bands = []
    for d in range(3):
        left, first, second, right = (picked[4 * d + k : 4 * d + k + 1] for k in range(4))
        bands.append(
            jnp.where(
                lane < 128,
                first,
                jnp.where(lane < 256, second, jnp.where(lane < 320, right, left)),
            )
        )
    return bands


def edge_bands(bands):
    above, on, below = bands
    return jnp.concatenate(
        [
            jnp.broadcast_to(above, (16, FC)),
            jnp.broadcast_to(on, (48, FC)),
            jnp.broadcast_to(below, (16, FC)),
        ],
        axis=0,
    )


def jumps(row):
    step = row - pltpu.roll(row, 1, 1)
    lane = lanes_of((1, FC))
    at = [jnp.sum(jnp.where(lane == k, step, 0.0), axis=1, keepdims=True) for k in (0, 128, 256)]
    return jnp.where(
        (lane < 64) | (lane >= 320), at[0], jnp.where(lane < 192, at[1], at[2])
    )


def edge_steps():
    lane = lanes_of((1, FC))
    up = (lane == 0) | (lane == 128) | (lane == 256)
    down = (lane == FC - 1) | (lane == 127) | (lane == 255)
    return jnp.where(up, 1.0, jnp.where(down, -1.0, 0.0))


def halves_of(x):
    high = x.astype(jnp.bfloat16)
    return high, (x - high.astype(jnp.float32)).astype(jnp.bfloat16)


def product(a, b):
    return lax.dot_general(a, b, (((1,), (0,)), ((), ())), preferred_element_type=jnp.float32)


def column_transform(w, basis_ref):
    high, low = halves_of(pltpu.roll(w, OV, 1))
    cols, rest = halves_of(cols_part(basis_ref))
    cols = jnp.concatenate([cols, rest, cols], axis=0)

    def block(at):
        part = slice(at, at + SPEC)
        return product(jnp.concatenate([high[:, part], high[:, part], low[:, part]], axis=1), cols)

    return jnp.concatenate([block(0), block(128)], axis=1)


def row_transform(u, basis_ref, part):
    high, low = halves_of(u)
    rows = part(basis_ref).astype(jnp.bfloat16)
    return product(rows, jnp.concatenate([high, low, high], axis=0))


def weights(means, basis_ref):
    lane = lanes_of((1, 2 * SPEC))
    mean = jnp.where(lane < SPEC, means[0], means[1])
    return 1.0 / (DAMP + mean * basis_ref[:EXT])


def strips_of(t, basis_ref, deep):
    cols = cols_part(basis_ref)
    left = dot(cols[:deep], t[:, :SPEC], 1)
    right = dot(cols[EXT - deep : EXT], t[:, SPEC:], 1)
    both = dot(jnp.concatenate([left, right], axis=0), rows_t_part(basis_ref)[:, :EXT])
    return both[:deep], both[deep:]


def solution_of(t, basis_ref):
    v = dot(rows_part(basis_ref), t)
    cols = cols_part(basis_ref)
    first, second = dot(v[:, :SPEC], cols), dot(v[:, SPEC:], cols)
    y = jnp.concatenate(
        [first[:, :128], first[:, 128:] + second[:, :128], second[:, 128:]], axis=1
    )
    return pltpu.roll(y, FC - OV, 1)


def core_sums(x):
    return [total(x[:, :128]), total(x[:, 128:256])]


def add_columns(y, from_left, from_right):
    far = from_left.shape[0] - OV
    gap = jnp.zeros((56 - far, EXT), jnp.float32)
    turned = jnp.concatenate(
        [from_right[8:], gap, from_right[:8], from_left[far:], gap, from_left[:far]], axis=0
    )
    back = turned.T
    lane = lanes_of((EXT, 128))
    rolled = pltpu.roll(back, 64, 1)
    first = y[:, :128] + jnp.where(lane < 8, rolled, 0.0)
    second = y[:, 128:256] + jnp.where(lane >= 120, rolled, 0.0)
    third = y[:, 256:] + jnp.where((lane < 16) | (lane >= 112), back, 0.0)
    return jnp.concatenate([first, second, third], axis=1)


def pack_rows(y, deep):
    return jnp.concatenate([y[136:], y[: deep - 8]], axis=0), y[136 - deep : 136]


def edges(y, from_above, from_below):
    far = from_above.shape[0] - OV
    none = jnp.zeros((8, FC), jnp.float32)
    return jnp.concatenate(
        [
            from_above[:8] if far == 16 else none,
            y[136:] + from_above[far - 8 : far],
            y[:8] + from_above[far:],
            y[8:24],
            y[104:120],
            y[120:136] + from_below[:16],
            from_below[16:] if far == 16 else none,
        ],
        axis=0,
    )


def edge_part(frame):
    return jnp.concatenate([frame[144:], frame[:24], frame[104:144]], axis=0)


def with_edges(edge, inner):
    return jnp.concatenate([edge[16:32, :TC], inner, edge[48:64, :TC]], axis=0)


def sides(index, count, a, b):
    even = is_even(index)
    before = jnp.where(index > 0, jnp.where(even, b, a), 0.0)
    after = jnp.where(index < count - 1, jnp.where(even, a, b), 0.0)
    return before, after


def send(index, a_ref, b_ref, before, after):
    even = is_even(index)
    a_ref[...] = jnp.where(even, after, before)
    b_ref[...] = jnp.where(even, before, after)


def begin_kernel(counts, both_ref, b_ref, a_ref, table_ref):
    r, h = both_ref[:TR], both_ref[TR:]
    lane = lanes_of((128, 128))
    packed = jnp.where(
        lane < 16,
        r[:, :128],
        jnp.where(
            lane < 64,
            pltpu.roll(h[:, :128], 16, 1),
            jnp.where(lane < 112, pltpu.roll(h[:, 128:], 112, 1), r[:, 128:]),
        ),
    )
    turned = packed.T
    table = table_of(core_sums(r), counts)
    table_ref[...] = table
    send(
        lax.axis_index("col"),
        a_ref,
        b_ref,
        jnp.concatenate([turned[:32], table], axis=0),
        jnp.concatenate([turned[96:], table], axis=0),
    )


def widen_kernel(counts, both_ref, own_ref, gb_ref, ga_ref, r3_ref, h3_ref, b_ref, a_ref, table_ref):
    i, j = place()
    from_left, from_right = sides(j, counts[1], ga_ref[:32], gb_ref[:32])
    turned = jnp.concatenate([from_right, jnp.zeros((64, 128), jnp.float32), from_left], axis=0)
    back = turned.T
    lane = lanes_of((128, 128))
    edge = (lane < 16) | (lane >= 112)
    r3 = jnp.where(edge, back, 0.0)
    h3 = jnp.where(
        lane < 16, pltpu.roll(back, 112, 1), jnp.where(lane >= 112, pltpu.roll(back, 16, 1), 0.0)
    )
    r3_ref[...] = r3
    h3_ref[...] = h3
    r, h = both_ref[:TR], both_ref[TR:]
    table = merged(own_ref[...], ga_ref[32:], gb_ref[32:])
    table_ref[...] = table
    wide = jnp.concatenate([table, jnp.zeros((table.shape[0], FC - 128), jnp.float32)], axis=1)

    def strip(r_rows, h_rows):
        return jnp.concatenate(
            [
                jnp.concatenate([r[r_rows], r3[r_rows]], axis=1),
                jnp.concatenate([h[h_rows], h3[h_rows]], axis=1),
                wide,
            ],
            axis=0,
        )

    send(i, a_ref, b_ref, strip(slice(0, 8), slice(0, 16)), strip(slice(120, 128), slice(112, 128)))


def weights_kernel(both_ref, table_ref, basis_ref, weights_ref, table_out):
    h = both_ref[TR:]
    means = [x / (SUB * SUB) for x in core_sums(h * h * h)]
    weights_ref[...] = weights(means, basis_ref)
    table_out[...] = table_ref[...]


def forward_kernel(both_ref, r3_ref, basis_ref, t_ref):
    r = both_ref[:TR]
    u = column_transform(jnp.concatenate([r, r3_ref[...]], axis=1), basis_ref)
    t_ref[...] = row_transform(u, basis_ref, tile_rows)


def first_kernel(
    counts,
    gb_ref,
    ga_ref,
    tile_ref,
    weights_ref,
    basis_ref,
    table_ref,
    t_ref,
    table_out,
    b_ref,
    a_ref,
):
    i, j = place()
    above, below = sides(i, counts[0], ga_ref[:8], gb_ref[:8])
    u = column_transform(jnp.concatenate([below, above], axis=0), basis_ref)
    t = (tile_ref[...] + row_transform(u, basis_ref, halo_rows)) * weights_ref[...]
    t_ref[...] = t
    send(j, a_ref, b_ref, *strips_of(t, basis_ref, 24))
    table_out[...] = merged(table_ref[...], ga_ref[24:, :128], gb_ref[24:, :128])


def mobility_kernel(counts, both_ref, h3_ref, gb_ref, ga_ref, m_ref):
    above, below = sides(lax.axis_index("row"), counts[0], ga_ref[8:24], gb_ref[8:24])
    h = jnp.concatenate([both_ref[TR:], h3_ref[...]], axis=1)
    tall = jnp.concatenate([h, below, above], axis=0)
    m_ref[...] = tall * tall * tall


def inverse_kernel(t_ref, basis_ref, table_ref, y_ref):
    y_ref[...] = solution_of(t_ref[...], basis_ref)


def columns_kernel(counts, y_ref, *refs):
    i, j = place()
    (ga_ref, gb_ref), refs = (refs[:2] if len(refs) == 7 else refs[1::-1]), refs[2:]
    deep = 24 if len(refs) == 5 else 16
    y = add_columns(y_ref[...], *sides(j, counts[1], ga_ref[:deep], gb_ref[:deep]))
    strips = pack_rows(y, deep)
    if len(refs) == 5:
        table_ref, out_ref, table_out, b_ref, a_ref = refs
        table = merged(table_ref[...], ga_ref[24:, :128], gb_ref[24:, :128])
        table_out[...] = table
        wide = jnp.concatenate([table, jnp.zeros((table.shape[0], FC - 128), jnp.float32)], axis=1)
        strips = [jnp.concatenate([x, wide], axis=0) for x in strips]
    else:
        out_ref, b_ref, a_ref = refs
    out_ref[...] = y
    send(i, a_ref, b_ref, *strips)


def inner_kernel(
    counts, y_ref, m_ref, basis_ref, table_ref, w_ref, f_ref, gw_ref, gf_ref, table_out
):
    mask = column_mask(counts)
    s = jnp.where(mask, y_ref[8:120], 0.0)
    m = m_ref[8:120]
    w = DAMP * s + lap(m * lap(s))
    w = jnp.where(mask, w[8:104], 0.0) * SHRINK
    f = lap(m * edge_steps())
    f = jnp.where(mask, f[8:104], 0.0) * SHRINK
    w_ref[...] = w[:, :TC]
    f_ref[...] = f[:, :TC]
    gw_ref[...] = row_transform(w, basis_ref, inner_rows)
    gf_ref[...] = row_transform(f, basis_ref, inner_rows)
    table_out[...] = table_ref[...]


def second_kernel(
    counts,
    width,
    y_ref,
    m_ref,
    gb_ref,
    ga_ref,
    table_ref,
    far_ref,
    inner_w_ref,
    f_ref,
    gw_ref,
    gf_ref,
    weights_ref,
    basis_ref,
    z_ref,
    w_ref,
    t_ref,
    table_out,
    b_ref,
    a_ref,
):
    i, j = place()
    y = y_ref[...]
    mask = edge_mask(counts)
    s = edges(y, *sides(i, counts[0], ga_ref[:24], gb_ref[:24]))
    s = jnp.where(mask, s, 0.0)
    table = merged(table_ref[...], far_ref[...], ga_ref[24:, :128], gb_ref[24:, :128])
    table_out[...] = table
    g = coarse_values(as_row(table, width), coarse_part(basis_ref, width))
    bands = band_rows(g, counts)
    coarse = edge_bands(bands)
    m = edge_part(m_ref)
    flow = m * (lap(s) + lap(coarse))
    z = s + coarse
    w = jnp.where(mask, DAMP * z + lap(flow), 0.0) * SHRINK
    step = jumps(bands[1])
    damped = (DAMP * SHRINK) * bands[1]
    z_ref[...] = with_edges(z, y[16:112, :TC] + bands[1][:, :TC])
    w_ref[...] = with_edges(w, inner_w_ref[...] + step[:, :TC] * f_ref[...] + damped[:, :TC])
    lane = lanes_of((EXT, 256))
    ones = jnp.where((lane >= 16) & (lane < 112), rows_t_part(basis_ref), 0.0)
    ones = jnp.sum(ones, axis=1, keepdims=True)
    u = gw_ref[...] + step * gf_ref[...] + ones * damped
    u = u + row_transform(jnp.concatenate([w[8:32], w[48:72]], axis=0), basis_ref, edge_rows)
    t = column_transform(u, basis_ref) * weights_ref[...]
    t_ref[...] = t
    send(j, a_ref, b_ref, *strips_of(t, basis_ref, 16))


def inverse_stats_kernel(t_ref, basis_ref, both_ref, m_ref, z_ref, w_ref, y_ref, stats_ref):
    y_ref[...] = solution_of(t_ref[...], basis_ref)
    rt, mt, zt, wt = both_ref[:TR], m_ref[:TR, :TC], z_ref[...], w_ref[...]
    lane, row = lanes_of((1, 256)), rows_of((128, 1))
    along = (lane % 128 != 0) & (lane % 128 != 127)
    top, low = mt[:1], mt[127:]
    side = jnp.sum(jnp.where((row > 0) & (row < 127), mt, 0.0), axis=0, keepdims=True)

    def halves(x):
        return [
            jnp.sum(x[:, :128], axis=1, keepdims=True),
            jnp.sum(x[:, 128:], axis=1, keepdims=True),
        ]

    first, last = lane % 128 == 0, lane % 128 == 127
    stats_ref[...] = row_of(
        [
            core_sums(rt * zt),
            core_sums(zt * wt),
            core_sums(wt),
            halves(jnp.where(along, top, 0.0)),
            halves(jnp.where(along, low, 0.0)),
            halves(jnp.where(first, side, 0.0)),
            halves(jnp.where(last, side, 0.0)),
            halves(jnp.where(first, top, 0.0)),
            halves(jnp.where(last, top, 0.0)),
            halves(jnp.where(first, low, 0.0)),
            halves(jnp.where(last, low, 0.0)),
        ]
    )


def inner_dots_kernel(counts, y_ref, m_ref, both_ref, w_ref, stats_ref, v_ref, stats_out):
    q = jnp.where(column_mask(counts), y_ref[8:120], 0.0)
    v = (DAMP * q + lap(m_ref[8:120] * lap(q)))[8:104, :TC]
    q = q[8:104, :TC]
    v_ref[...] = v
    rest = [
        core_sums(v),
        core_sums(both_ref[16:112] * q),
        core_sums(w_ref[16:112] * q),
        core_sums(v * q),
    ]
    zero = jnp.zeros((1, 1), jnp.float32)
    stats_out[...] = stats_ref[...] + row_of([[zero, zero]] * 11 + rest)


def dots_kernel(
    counts, y_ref, m_ref, gb_ref, ga_ref, both_ref, w_ref, stats_ref, inner_v_ref, q_ref, v_ref, stats_out
):
    i, j = place()
    y = y_ref[...]
    q = edges(y, *sides(i, counts[0], ga_ref[...], gb_ref[...]))
    q = jnp.where(edge_mask(counts), q, 0.0)
    v = DAMP * q + lap(edge_part(m_ref) * lap(q))
    q_ref[...] = with_edges(q, y[16:112, :TC])
    v_ref[...] = with_edges(v, inner_v_ref[...])
    qe, ve = (jnp.concatenate([x[16:32, :TC], x[48:64, :TC]], axis=0) for x in (q, v))
    re = jnp.concatenate([both_ref[:16], both_ref[112:128]], axis=0)
    we = jnp.concatenate([w_ref[:16], w_ref[112:]], axis=0)
    rest = [core_sums(ve), core_sums(re * qe), core_sums(we * qe), core_sums(ve * qe)]
    zero = jnp.zeros((1, 1), jnp.float32)
    row = stats_ref[...] + row_of([[zero, zero]] * 11 + rest)
    stats_out[...] = jnp.broadcast_to(row, stats_out.shape)


def end_kernel(
    counts,
    width,
    stats_ref,
    table_ref,
    basis_ref,
    m_ref,
    both_ref,
    z_ref,
    w_ref,
    q_ref,
    v_ref,
    solution_ref,
    residual_ref,
):
    tiles_c = counts[1]
    devices = counts[0] * tiles_c
    table = gathered(stats_ref[...], width)
    st = [table[k : k + 1] for k in range(15)]

    def whole(x):
        return jnp.sum(x, axis=1, keepdims=True)

    rz, zw, rq, wq, qv = (whole(st[k]) for k in (0, 1, 12, 13, 14))
    c0, c1, sums_v = as_row(table_ref[...], width), st[2], st[11]
    g = coarse_values(c1, coarse_part(basis_ref, width))
    lane = lanes_of((1, width))
    cell = lane < 2 * devices
    on_left = lane < devices
    device = lane % devices
    column = device % tiles_c

    def from_lane(distance):
        return pltpu.roll(g, distance % width, 1)

    up = jnp.where(device >= tiles_c, from_lane(tiles_c), 0.0)
    down = jnp.where(device < devices - tiles_c, from_lane(-tiles_c), 0.0)
    left = jnp.where(
        on_left, jnp.where(column > 0, from_lane(1 - devices), 0.0), from_lane(devices)
    )
    right = jnp.where(
        on_left,
        from_lane(-devices),
        jnp.where(column < tiles_c - 1, from_lane(devices - 1), 0.0),
    )
    du, dd, dl, dr = g - up, g - down, g - left, g - right
    energy = DAMP * SUB * SUB * g * g
    energy = energy + st[3] * du * du + st[4] * dd * dd + st[5] * dl * dl + st[6] * dr * dr
    for weight, p, q in ((st[7], du, dl), (st[8], du, dr), (st[9], dd, dl), (st[10], dd, dr)):
        both = p + q
        energy = energy + weight * both * both
    ry = rq + whole(g * c0)
    yw = wq + whole(g * c1)
    yv = qv + whole(jnp.where(cell, 2.0 * g * sums_v + energy, 0.0))
    a = rz / zw
    rz1 = rz - a * ry - a * zw + a * a * yw
    beta1 = 1.0 + rz1 / rz
    dad = (beta1 * beta1 * zw - 2.0 * a * beta1 * yw) * (1.0 / SHRINK) + a * a * yv
    a1 = rz1 / dad
    above, on, below = band_rows(g, counts)
    coarse = jnp.concatenate(
        [
            jnp.broadcast_to(on, (128, FC)),
            jnp.broadcast_to(below, (16, FC)),
            jnp.broadcast_to(above, (16, FC)),
        ],
        axis=0,
    )
    y = q_ref[...] + coarse[:128, :256]
    image = DAMP * coarse + lap(m_ref[...] * lap(coarse))
    v = v_ref[...] + image[:128, :256]
    z, w = z_ref[...], w_ref[...]
    solution_ref[...] = (a * SHRINK) * z + a1 * (beta1 * z - a * y)
    residual_ref[...] = both_ref[:TR] - a * w - a1 * ((beta1 * (1.0 / SHRINK)) * w - a * v)


def call(kernel, outs, *args, flops=10**9):
    shapes = [jax.ShapeDtypeStruct(s, jnp.float32) for s in outs]
    return pl.pallas_call(
        kernel,
        out_shape=shapes,
        compiler_params=pltpu.CompilerParams(vmem_limit_bytes=48 * 1024 * 1024),
        cost_estimate=pl.CostEstimate(flops=flops, bytes_accessed=10**6, transcendentals=0),
    )(*args)


def pairs_from(count, offset):
    found = []
    for k in range(offset, count, 2):
        found += [(k, (k + 1) % count), ((k + 1) % count, k)]
    return found


def near_pairs(counts, axis, bit):
    found = []
    for i in range(counts[0]):
        for j in range(counts[1]):
            at = [i, j]
            if 0 < at[axis] < counts[axis] - 1:
                at[axis] += 1 if at[axis] % 2 else -1
            else:
                at[1 - axis] ^= bit
            found.append((i * counts[1] + j, at[0] * counts[1] + at[1]))
    return found


def xor_pairs(counts, rows, cols):
    flat = [(i, j) for i in range(counts[0]) for j in range(counts[1])]
    return [(i * counts[1] + j, (i ^ rows) * counts[1] + (j ^ cols)) for i, j in flat]


def spreads(counts):
    known = np.eye(counts[0] * counts[1], dtype=bool)

    def meet(*swaps):
        return np.logical_or.reduce([known, *(known[[b for _, b in pairs]] for pairs in swaps)])

    even = [xor_pairs(counts, 0, 1), xor_pairs(counts, 1, 0)]
    known = meet(even[0], near_pairs(counts, 1, 4))
    known = meet(even[1], near_pairs(counts, 0, 1), xor_pairs(counts, 4, 2))
    known = meet(even[0], near_pairs(counts, 1, 3))
    return meet(even[1], near_pairs(counts, 0, 1), xor_pairs(counts, 2, 2)).all()


def body(counts, height, noise):
    nr, nc = counts
    devices = nr * nc
    width = max(128, devices * 2)
    basis = jnp.asarray(constants(nr, 2 * nc, width))
    both_axes = ("row", "col")
    depth = table_shape(counts)[0]

    def swap(a, b, axis, bit=1):
        gb = lax.ppermute(b, both_axes, near_pairs(counts, both_axes.index(axis), bit))
        return lax.ppermute(a, axis, pairs_from(lax.axis_size(axis), 0)), gb

    def small_swap(x, rows, cols):
        return lax.ppermute(x, both_axes, xor_pairs(counts, rows, cols))

    both = jnp.pad(noise, ((0, TR), (0, 0))) + jnp.pad(height, ((TR, 0), (0, 0)))
    b, a, table = call(
        functools.partial(begin_kernel, counts), [(32 + depth, 128)] * 2 + [(depth, 128)], both
    )
    if not spreads(counts):
        for axis, count in enumerate(counts):
            bit = 1
            while bit < count:
                table = table + small_swap(table, *((0, bit) if axis else (bit, 0)))
                bit *= 2
    ga, gb = swap(a, b, "col", 4)
    r3, h3, b, a, table = call(
        functools.partial(widen_kernel, counts),
        [(128, 128)] * 2 + [(24 + depth, FC)] * 2 + [(depth, 128)],
        both,
        table,
        gb,
        ga,
    )
    ga, gb = swap(a, b, "row")
    weight, table = call(weights_kernel, [(EXT, 2 * SPEC), (depth, 128)], both, table, basis)
    far = small_swap(table, 4, 2)
    t = call(forward_kernel, [(EXT, 2 * SPEC)], both, r3, basis)[0]
    t, table, b, a = call(
        functools.partial(first_kernel, counts),
        [(EXT, 2 * SPEC), (depth, 128)] + [(24, EXT)] * 2,
        gb,
        ga,
        t,
        weight,
        basis,
        table,
    )
    table = merged(table, far)
    wide = jnp.pad(table, ((0, 0), (0, EXT - 128)))
    m = call(functools.partial(mobility_kernel, counts), [(FR, FC)], both, h3, gb, ga)[0]
    y = call(inverse_kernel, [(EXT, FC)], t, basis, table)[0]
    ga, gb = swap(*(jnp.concatenate([x, wide], axis=0) for x in (a, b)), "col", 3)
    y, table, b, a = call(
        functools.partial(columns_kernel, counts),
        [(EXT, FC), (depth, 128)] + [(24 + depth, FC)] * 2,
        y,
        ga,
        gb,
        table,
    )
    ga, gb = swap(a, b, "row")
    inner_w, f, gw, gf, table_too = call(
        functools.partial(inner_kernel, counts),
        [(96, TC)] * 2 + [(EXT, FC)] * 2 + [(depth, 128)],
        y,
        m,
        basis,
        table,
    )
    far = small_swap(table_too, 2, 2)
    z, w, t, table, b, a = call(
        functools.partial(second_kernel, counts, width),
        [(TR, TC)] * 2 + [(EXT, 2 * SPEC), (depth, 128)] + [(16, EXT)] * 2,
        y,
        m,
        gb,
        ga,
        table,
        far,
        inner_w,
        f,
        gw,
        gf,
        weight,
        basis,
    )
    ga, gb = swap(a, b, "col")
    y, stats = call(inverse_stats_kernel, [(EXT, FC), (1, 128)], t, basis, both, m, z, w)
    y, b, a = call(
        functools.partial(columns_kernel, counts), [(EXT, FC)] + [(16, FC)] * 2, y, gb, ga
    )
    ga, gb = swap(a, b, "row")
    inner_v, stats = call(
        functools.partial(inner_dots_kernel, counts),
        [(96, TC), (1, 128)],
        y,
        m,
        both,
        w,
        stats,
    )
    q, v, stats = call(
        functools.partial(dots_kernel, counts),
        [(TR, TC)] * 2 + [(devices, 128)],
        y,
        m,
        gb,
        ga,
        both,
        w,
        stats,
        inner_v,
    )
    stats = lax.all_to_all(stats, both_axes, 0, 0, tiled=True)
    return tuple(
        call(
            functools.partial(end_kernel, counts, width),
            [(TR, TC)] * 2,
            stats,
            table,
            basis,
            m,
            both,
            z,
            w,
            q,
            v,
        )
    )


def solution(mesh):
    counts = (mesh.shape["row"], mesh.shape["col"])
    spec = P("row", "col")
    return jax.shard_map(
        functools.partial(body, counts),
        mesh=mesh,
        in_specs=(spec, spec),
        out_specs=(spec, spec),
        check_vma=False,
    )
```

```python
import functools

import jax
import jax.numpy as jnp
import ml_dtypes
import numpy as np
from jax import lax
from jax.experimental import pallas as pl
from jax.experimental.pallas import tpu as pltpu
from jax.sharding import PartitionSpec as P

SUB = 128
OV = 8
EXT = SUB + 2 * OV
DAMP = 2.0**-28
SHRINK = 2.0**-20

TR, TC = 128, 256
FR, FC = 160, 384
SPEC = 256

highest = lax.Precision.HIGHEST


def sine(count):
    k = np.arange(1, count + 1, dtype=np.float64)
    basis = np.sqrt(2.0 / (count + 1.0)) * np.sin(np.pi * k[:, None] * k[None, :] / (count + 1.0))
    return basis, 2.0 - 2.0 * np.cos(np.pi * k / (count + 1.0))


def block_constants():
    basis, eig = sine(EXT)
    rows = np.roll(basis, -OV, 0)
    cols = np.pad(basis, ((0, SPEC - EXT), (0, SPEC - EXT)))
    scale = np.pad((eig[:, None] + eig[None, :]) ** 2, ((0, 0), (0, SPEC - EXT)))
    wide = lambda x: np.pad(x, ((0, 0), (0, 2 * SPEC - x.shape[1])))
    high = rows.T.astype(ml_dtypes.bfloat16).astype(np.float64)
    low = (rows.T - high).astype(ml_dtypes.bfloat16).astype(np.float64)
    tile = np.concatenate([x[:, :SUB] for x in (high, high, low)], 1)
    halo = np.concatenate([x[:, SUB:] for x in (high, high, low)], 1)
    inner = np.concatenate([x[:, 16:112] for x in (high, high, low)], 1)
    at = [*range(136, 144), *range(16), *range(112, 136)]
    edge = np.concatenate([x[:, at] for x in (high, high, low)], 1)
    turned = np.hstack([rows.T, np.zeros((EXT, 256 - EXT)), edge])
    return [np.tile(scale, (1, 2)), *(wide(x) for x in (rows, turned, cols, inner, np.hstack([tile, halo])))]


def rows_part(ref):
    return ref[EXT : 2 * EXT, :EXT]


def rows_t_part(ref):
    return ref[2 * EXT : 3 * EXT, :256]


def cols_part(ref):
    return ref[3 * EXT : 3 * EXT + SPEC, :SPEC]


def inner_rows(ref):
    at = 3 * EXT + SPEC
    return ref[at : at + EXT, : 3 * 96]


def edge_rows(ref):
    return ref[2 * EXT : 3 * EXT, 256 : 256 + 3 * 48]


def tile_rows(ref):
    at = 4 * EXT + SPEC
    return ref[at : at + EXT, : 3 * SUB]


def halo_rows(ref):
    at = 4 * EXT + SPEC
    return ref[at : at + EXT, 3 * SUB : 3 * EXT]


def coarse_part(ref, width):
    at, lanes = 5 * EXT + SPEC, 2 * SPEC
    parts = [ref[at + k * width : at + (k + 1) * width] for k in range(-(-width // lanes))]
    return (parts[0] if len(parts) == 1 else jnp.concatenate(parts, axis=1))[:, :width]


def constants(nr, nc, width):
    lanes = 2 * SPEC
    inverse = coarse_inverse(nr, nc, -(-width // lanes) * lanes)[:width]
    parts = [*block_constants(), *np.split(inverse, inverse.shape[1] // lanes, 1)]
    return np.concatenate(parts).astype(np.float32)


def coarse_inverse(nr, nc, width):
    br, er = sine(nr)
    bc, ec = sine(nc)
    both = np.kron(br, bc).reshape(nr, nc // 2, 2, nr * nc).transpose(2, 0, 1, 3)
    both = both.reshape(nr * nc, nr * nc)
    scale = (er[:, None] + ec[None, :]) / (SUB * SUB)
    values = (SUB * SUB * (DAMP + scale * scale)).reshape(-1)
    whole = np.zeros((width, width), np.float32)
    whole[: nr * nc, : nr * nc] = (both / values) @ both.T
    return whole


def dot(a, b, side=0):
    return lax.dot_general(
        a, b, (((1,), (side,)), ((), ())), precision=highest, preferred_element_type=jnp.float32
    )


def lap(x):
    rows, lanes = x.shape
    beside = pltpu.roll(x, 1, 0) + pltpu.roll(x, rows - 1, 0)
    beside = beside + (pltpu.roll(x, 1, 1) + pltpu.roll(x, lanes - 1, 1))
    return 4.0 * x - beside


def lanes_of(shape):
    return lax.broadcasted_iota(jnp.int32, shape, 1)


def rows_of(shape):
    return lax.broadcasted_iota(jnp.int32, shape, 0)


def total(x):
    return jnp.sum(jnp.sum(x, axis=0, keepdims=True), axis=1, keepdims=True)


def place():
    return lax.axis_index("row"), lax.axis_index("col")


def is_even(index):
    return lax.rem(index, 2) == 0


def column_mask(counts):
    j = lax.axis_index("col")
    lane = lanes_of((1, FC))
    right = jnp.where(j < counts[1] - 1, 320, 256)
    left = jnp.where(j > 0, 320, 384)
    return (lane < right) | (lane >= left)


def edge_mask(counts):
    i = lax.axis_index("row")
    row = rows_of((80, 1))
    first = jnp.where(i > 0, 0, 16)
    last = jnp.where(i < counts[0] - 1, 80, 64)
    return (row >= first) & (row < last) & column_mask(counts)


def table_shape(counts):
    return (-(-2 * counts[0] * counts[1] // 1024) * 8, 128)


def table_of(values, counts):
    i, j = place()
    devices = counts[0] * counts[1]
    shape = table_shape(counts)
    at = rows_of(shape) * 128 + lanes_of(shape) - (i * counts[1] + j)
    return jnp.where(at == 0, values[0], jnp.where(at == devices, values[1], 0.0))


def merged(table, *others):
    for other in others:
        table = jnp.where(table != 0.0, table, other)
    return table


def as_row(table, width):
    return jnp.concatenate([table[k : k + 1] for k in range(width // 128)], axis=1)


def row_of(pairs):
    lane = lanes_of((1, 128))
    row = jnp.zeros((1, 128), jnp.float32)
    for k, (left, right) in enumerate(pairs):
        row = jnp.where(lane == k, left, jnp.where(lane == 64 + k, right, row))
    return row


def coarse_values(c_row, inverse):
    return dot(jnp.broadcast_to(c_row, (8, c_row.shape[1])), inverse)[:1]


def band_rows(g_row, counts):
    i, j = place()
    nr, nc = counts[0], 2 * counts[1]
    shape = (16, g_row.shape[1])
    which = rows_of(shape)
    r = i - 1 + which // 4
    c = 2 * j - 1 + which % 4
    inside = (r >= 0) & (r < nr) & (c >= 0) & (c < nc) & (which < 12)
    at = lax.rem(c + 2, 2) * (nr * counts[1]) + r * counts[1] + (c + 2) // 2 - 1
    picked = jnp.where(inside & (lanes_of(shape) == at), g_row, 0.0)
    picked = jnp.sum(picked, axis=1, keepdims=True)
    return as_bands([picked[k : k + 1] for k in range(12)])


def as_bands(values):
    lane = lanes_of((1, FC))
    bands = []
    for d in range(3):
        left, first, second, right = values[4 * d : 4 * d + 4]
        bands.append(
            jnp.where(
                lane < 128,
                first,
                jnp.where(lane < 256, second, jnp.where(lane < 320, right, left)),
            )
        )
    return bands


def edge_bands(bands):
    above, on, below = bands
    return jnp.concatenate(
        [
            jnp.broadcast_to(above, (16, FC)),
            jnp.broadcast_to(on, (48, FC)),
            jnp.broadcast_to(below, (16, FC)),
        ],
        axis=0,
    )


def jumps(row):
    step = row - pltpu.roll(row, 1, 1)
    lane = lanes_of((1, FC))
    at = [jnp.sum(jnp.where(lane == k, step, 0.0), axis=1, keepdims=True) for k in (0, 128, 256)]
    return jnp.where(
        (lane < 64) | (lane >= 320), at[0], jnp.where(lane < 192, at[1], at[2])
    )


def edge_steps():
    lane = lanes_of((1, FC))
    up = (lane == 0) | (lane == 128) | (lane == 256)
    down = (lane == FC - 1) | (lane == 127) | (lane == 255)
    return jnp.where(up, 1.0, jnp.where(down, -1.0, 0.0))


def halves_of(x):
    high = x.astype(jnp.bfloat16)
    return high, (x - high.astype(jnp.float32)).astype(jnp.bfloat16)


def product(a, b):
    return lax.dot_general(a, b, (((1,), (0,)), ((), ())), preferred_element_type=jnp.float32)


def column_transform(w, basis_ref):
    high, low = halves_of(pltpu.roll(w, OV, 1))
    cols, rest = halves_of(cols_part(basis_ref))
    cols = jnp.concatenate([cols, rest, cols], axis=0)

    def block(at):
        part = slice(at, at + SPEC)
        return product(jnp.concatenate([high[:, part], high[:, part], low[:, part]], axis=1), cols)

    return jnp.concatenate([block(0), block(128)], axis=1)


def row_transform(u, basis_ref, part):
    high, low = halves_of(u)
    rows = part(basis_ref).astype(jnp.bfloat16)
    return product(rows, jnp.concatenate([high, low, high], axis=0))


def weights(means, basis_ref):
    lane = lanes_of((1, 2 * SPEC))
    mean = jnp.where(lane < SPEC, means[0], means[1])
    return 1.0 / (DAMP + mean * basis_ref[:EXT])


def strips_of(t, basis_ref, deep):
    cols = cols_part(basis_ref)
    left = dot(cols[:deep], t[:, :SPEC], 1)
    right = dot(cols[EXT - deep : EXT], t[:, SPEC:], 1)
    both = dot(jnp.concatenate([left, right], axis=0), rows_t_part(basis_ref)[:, :EXT])
    return both[:deep], both[deep:]


def solution_of(t, basis_ref):
    v = dot(rows_part(basis_ref), t)
    cols = cols_part(basis_ref)
    first, second = dot(v[:, :SPEC], cols), dot(v[:, SPEC:], cols)
    y = jnp.concatenate(
        [first[:, :128], first[:, 128:] + second[:, :128], second[:, 128:]], axis=1
    )
    return pltpu.roll(y, FC - OV, 1)


def core_sums(x):
    return [total(x[:, :128]), total(x[:, 128:256])]


def add_columns(y, from_left, from_right):
    far = from_left.shape[0] - OV
    gap = jnp.zeros((56 - far, EXT), jnp.float32)
    turned = jnp.concatenate(
        [from_right[8:], gap, from_right[:8], from_left[far:], gap, from_left[:far]], axis=0
    )
    back = turned.T
    lane = lanes_of((EXT, 128))
    rolled = pltpu.roll(back, 64, 1)
    first = y[:, :128] + jnp.where(lane < 8, rolled, 0.0)
    second = y[:, 128:256] + jnp.where(lane >= 120, rolled, 0.0)
    third = y[:, 256:] + jnp.where((lane < 16) | (lane >= 112), back, 0.0)
    return jnp.concatenate([first, second, third], axis=1)


def pack_rows(y, deep):
    return jnp.concatenate([y[136:], y[: deep - 8]], axis=0), y[136 - deep : 136]


def edges(y, from_above, from_below):
    far = from_above.shape[0] - OV
    none = jnp.zeros((8, FC), jnp.float32)
    return jnp.concatenate(
        [
            from_above[:8] if far == 16 else none,
            y[136:] + from_above[far - 8 : far],
            y[:8] + from_above[far:],
            y[8:24],
            y[104:120],
            y[120:136] + from_below[:16],
            from_below[16:] if far == 16 else none,
        ],
        axis=0,
    )


def edge_part(frame):
    return jnp.concatenate([frame[144:], frame[:24], frame[104:144]], axis=0)


def with_edges(edge, inner):
    return jnp.concatenate([edge[16:32, :TC], inner, edge[48:64, :TC]], axis=0)


def sides(index, count, a, b):
    even = is_even(index)
    before = jnp.where(index > 0, jnp.where(even, b, a), 0.0)
    after = jnp.where(index < count - 1, jnp.where(even, a, b), 0.0)
    return before, after


def send(index, a_ref, b_ref, before, after):
    even = is_even(index)
    a_ref[...] = jnp.where(even, after, before)
    b_ref[...] = jnp.where(even, before, after)


def begin_kernel(counts, both_ref, b_ref, a_ref, table_ref):
    r, h = both_ref[:TR], both_ref[TR:]
    lane = lanes_of((128, 128))
    packed = jnp.where(
        lane < 16,
        r[:, :128],
        jnp.where(
            lane < 64,
            pltpu.roll(h[:, :128], 16, 1),
            jnp.where(lane < 112, pltpu.roll(h[:, 128:], 112, 1), r[:, 128:]),
        ),
    )
    turned = packed.T
    table = table_of(core_sums(r), counts)
    table_ref[...] = table
    send(
        lax.axis_index("col"),
        a_ref,
        b_ref,
        jnp.concatenate([turned[:32], table], axis=0),
        jnp.concatenate([turned[96:], table], axis=0),
    )


def widen_kernel(counts, both_ref, own_ref, gb_ref, ga_ref, r3_ref, h3_ref, b_ref, a_ref, table_ref):
    i, j = place()
    from_left, from_right = sides(j, counts[1], ga_ref[:32], gb_ref[:32])
    turned = jnp.concatenate([from_right, jnp.zeros((64, 128), jnp.float32), from_left], axis=0)
    back = turned.T
    lane = lanes_of((128, 128))
    edge = (lane < 16) | (lane >= 112)
    r3 = jnp.where(edge, back, 0.0)
    h3 = jnp.where(
        lane < 16, pltpu.roll(back, 112, 1), jnp.where(lane >= 112, pltpu.roll(back, 16, 1), 0.0)
    )
    r3_ref[...] = r3
    h3_ref[...] = h3
    r, h = both_ref[:TR], both_ref[TR:]
    table = merged(own_ref[...], ga_ref[32:], gb_ref[32:])
    table_ref[...] = table
    wide = jnp.concatenate([table, jnp.zeros((table.shape[0], FC - 128), jnp.float32)], axis=1)

    def strip(r_rows, h_rows):
        return jnp.concatenate(
            [
                jnp.concatenate([r[r_rows], r3[r_rows]], axis=1),
                jnp.concatenate([h[h_rows], h3[h_rows]], axis=1),
                wide,
            ],
            axis=0,
        )

    send(i, a_ref, b_ref, strip(slice(0, 8), slice(0, 16)), strip(slice(120, 128), slice(112, 128)))


def weights_kernel(both_ref, table_ref, basis_ref, weights_ref, table_out):
    h = both_ref[TR:]
    means = [x / (SUB * SUB) for x in core_sums(h * h * h)]
    weights_ref[...] = weights(means, basis_ref)
    table_out[...] = table_ref[...]


def forward_kernel(both_ref, r3_ref, basis_ref, t_ref):
    r = both_ref[:TR]
    u = column_transform(jnp.concatenate([r, r3_ref[...]], axis=1), basis_ref)
    t_ref[...] = row_transform(u, basis_ref, tile_rows)


def first_kernel(
    counts,
    gb_ref,
    ga_ref,
    tile_ref,
    weights_ref,
    basis_ref,
    table_ref,
    t_ref,
    table_out,
    b_ref,
    a_ref,
):
    i, j = place()
    above, below = sides(i, counts[0], ga_ref[:8], gb_ref[:8])
    u = column_transform(jnp.concatenate([below, above], axis=0), basis_ref)
    t = (tile_ref[...] + row_transform(u, basis_ref, halo_rows)) * weights_ref[...]
    t_ref[...] = t
    send(j, a_ref, b_ref, *strips_of(t, basis_ref, 24))
    table_out[...] = merged(table_ref[...], ga_ref[24:, :128], gb_ref[24:, :128])


def inverse_kernel(counts, t_ref, basis_ref, both_ref, h3_ref, gb_ref, ga_ref, y_ref, m_ref):
    y_ref[...] = solution_of(t_ref[...], basis_ref)
    above, below = sides(lax.axis_index("row"), counts[0], ga_ref[8:24], gb_ref[8:24])
    h = jnp.concatenate([both_ref[TR:], h3_ref[...]], axis=1)
    tall = jnp.concatenate([h, below, above], axis=0)
    m_ref[...] = tall * tall * tall


def columns_kernel(counts, y_ref, *refs):
    i, j = place()
    (ga_ref, gb_ref), refs = (refs[:2] if len(refs) == 7 else refs[1::-1]), refs[2:]
    deep = 24 if len(refs) == 5 else 16
    y = add_columns(y_ref[...], *sides(j, counts[1], ga_ref[:deep], gb_ref[:deep]))
    strips = pack_rows(y, deep)
    if len(refs) == 5:
        table_ref, out_ref, table_out, b_ref, a_ref = refs
        table = merged(table_ref[...], ga_ref[24:, :128], gb_ref[24:, :128])
        table_out[...] = table
        wide = jnp.concatenate([table, jnp.zeros((table.shape[0], FC - 128), jnp.float32)], axis=1)
        strips = [jnp.concatenate([x, wide], axis=0) for x in strips]
    else:
        out_ref, b_ref, a_ref = refs
    out_ref[...] = y
    send(i, a_ref, b_ref, *strips)


def inner_kernel(counts, y_ref, m_ref, basis_ref, w_ref, f_ref, gw_ref, gf_ref):
    mask = column_mask(counts)
    s = jnp.where(mask, y_ref[8:120], 0.0)
    m = m_ref[8:120]
    w = DAMP * s + lap(m * lap(s))
    w = jnp.where(mask, w[8:104], 0.0) * SHRINK
    f = lap(m * edge_steps())
    f = jnp.where(mask, f[8:104], 0.0) * SHRINK
    w_ref[...] = w[:, :TC]
    f_ref[...] = f[:, :TC]
    gw_ref[...] = row_transform(w, basis_ref, inner_rows)
    gf_ref[...] = row_transform(f, basis_ref, inner_rows)


def second_kernel(
    counts,
    width,
    y_ref,
    m_ref,
    gb_ref,
    ga_ref,
    table_ref,
    inner_w_ref,
    f_ref,
    gw_ref,
    gf_ref,
    weights_ref,
    basis_ref,
    z_ref,
    w_ref,
    t_ref,
    b_ref,
    a_ref,
):
    i, j = place()
    y = y_ref[...]
    mask = edge_mask(counts)
    s = edges(y, *sides(i, counts[0], ga_ref[:24], gb_ref[:24]))
    s = jnp.where(mask, s, 0.0)
    table = merged(table_ref[...], ga_ref[24:, :128], gb_ref[24:, :128])
    g = coarse_values(as_row(table, width), coarse_part(basis_ref, width))
    bands = band_rows(g, counts)
    coarse = edge_bands(bands)
    m = edge_part(m_ref)
    flow = m * (lap(s) + lap(coarse))
    z = s + coarse
    w = jnp.where(mask, DAMP * z + lap(flow), 0.0) * SHRINK
    step = jumps(bands[1])
    damped = (DAMP * SHRINK) * bands[1]
    z_ref[...] = with_edges(z, y[16:112, :TC] + bands[1][:, :TC])
    w_ref[...] = with_edges(w, inner_w_ref[...] + step[:, :TC] * f_ref[...] + damped[:, :TC])
    lane = lanes_of((EXT, 256))
    ones = jnp.where((lane >= 16) & (lane < 112), rows_t_part(basis_ref), 0.0)
    ones = jnp.sum(ones, axis=1, keepdims=True)
    u = gw_ref[...] + step * gf_ref[...] + ones * damped
    u = u + row_transform(jnp.concatenate([w[8:32], w[48:72]], axis=0), basis_ref, edge_rows)
    t = column_transform(u, basis_ref) * weights_ref[...]
    t_ref[...] = t
    send(j, a_ref, b_ref, *strips_of(t, basis_ref, 16))


def inverse_stats_kernel(t_ref, basis_ref, both_ref, m_ref, z_ref, w_ref, y_ref, stats_ref):
    y_ref[...] = solution_of(t_ref[...], basis_ref)
    rt, mt, zt, wt = both_ref[:TR], m_ref[:TR, :TC], z_ref[...], w_ref[...]
    lane, row = lanes_of((1, 256)), rows_of((128, 1))
    along = (lane % 128 != 0) & (lane % 128 != 127)
    top, low = mt[:1], mt[127:]
    side = jnp.sum(jnp.where((row > 0) & (row < 127), mt, 0.0), axis=0, keepdims=True)

    def halves(x):
        return [
            jnp.sum(x[:, :128], axis=1, keepdims=True),
            jnp.sum(x[:, 128:], axis=1, keepdims=True),
        ]

    first, last = lane % 128 == 0, lane % 128 == 127
    zero = jnp.zeros((1, 1), jnp.float32)
    stats_ref[...] = row_of(
        [
            core_sums(rt * zt),
            core_sums(zt * wt),
            core_sums(wt),
            halves(jnp.where(along, top, 0.0)),
            halves(jnp.where(along, low, 0.0)),
            halves(jnp.where(first, side, 0.0)),
            halves(jnp.where(last, side, 0.0)),
            halves(jnp.where(first, top, 0.0)),
            halves(jnp.where(last, top, 0.0)),
            halves(jnp.where(first, low, 0.0)),
            halves(jnp.where(last, low, 0.0)),
            *[[zero, zero]] * 4,
            core_sums(rt),
        ]
    )


def inner_dots_kernel(counts, y_ref, m_ref, both_ref, w_ref, stats_ref, v_ref, stats_out):
    q = jnp.where(column_mask(counts), y_ref[8:120], 0.0)
    v = (DAMP * q + lap(m_ref[8:120] * lap(q)))[8:104, :TC]
    q = q[8:104, :TC]
    v_ref[...] = v
    rest = [
        core_sums(v),
        core_sums(both_ref[16:112] * q),
        core_sums(w_ref[16:112] * q),
        core_sums(v * q),
    ]
    zero = jnp.zeros((1, 1), jnp.float32)
    stats_out[...] = stats_ref[...] + row_of([[zero, zero]] * 11 + rest)


def dots_kernel(
    counts, y_ref, m_ref, gb_ref, ga_ref, both_ref, w_ref, stats_ref, inner_v_ref, q_ref, v_ref, stats_out
):
    i, j = place()
    y = y_ref[...]
    q = edges(y, *sides(i, counts[0], ga_ref[...], gb_ref[...]))
    q = jnp.where(edge_mask(counts), q, 0.0)
    v = DAMP * q + lap(edge_part(m_ref) * lap(q))
    q_ref[...] = with_edges(q, y[16:112, :TC])
    v_ref[...] = with_edges(v, inner_v_ref[...])
    qe, ve = (jnp.concatenate([x[16:32, :TC], x[48:64, :TC]], axis=0) for x in (q, v))
    re = jnp.concatenate([both_ref[:16], both_ref[112:128]], axis=0)
    we = jnp.concatenate([w_ref[:16], w_ref[112:]], axis=0)
    rest = [core_sums(ve), core_sums(re * qe), core_sums(we * qe), core_sums(ve * qe)]
    zero = jnp.zeros((1, 1), jnp.float32)
    row = stats_ref[...] + row_of([[zero, zero]] * 11 + rest)
    stats_out[...] = jnp.broadcast_to(row, stats_out.shape)


def end_kernel(
    counts,
    width,
    stats_ref,
    basis_ref,
    m_ref,
    f_ref,
    both_ref,
    z_ref,
    w_ref,
    q_ref,
    v_ref,
    solution_ref,
    residual_ref,
):
    i, j = place()
    tiles_c = counts[1]
    devices = counts[0] * tiles_c
    rows = stats_ref[...]
    st = jnp.concatenate([rows, pltpu.roll(rows, 64, 1)], axis=0)
    inverse = coarse_part(basis_ref, width)[: 2 * devices, : 2 * devices]
    g = jnp.broadcast_to(dot(inverse, st)[:, 2:3], st.shape)
    lane, row = lanes_of(st.shape), rows_of(st.shape)
    device = row % devices
    column = device % tiles_c
    on_left = row < devices

    def from_row(distance):
        return pltpu.roll(g, distance % (2 * devices), 0)

    up = jnp.where(device >= tiles_c, from_row(tiles_c), 0.0)
    down = jnp.where(device < devices - tiles_c, from_row(-tiles_c), 0.0)
    left = jnp.where(on_left, jnp.where(column > 0, from_row(1 - devices), 0.0), from_row(devices))
    right = jnp.where(
        on_left, from_row(-devices), jnp.where(column < tiles_c - 1, from_row(devices - 1), 0.0)
    )
    du, dd, dl, dr = g - up, g - down, g - left, g - right
    across = jnp.where(
        (lane == 3) | (lane == 7) | (lane == 8),
        du,
        jnp.where((lane == 4) | (lane == 9) | (lane == 10), dd, 0.0),
    )
    across = across + jnp.where(
        (lane == 5) | (lane == 7) | (lane == 9),
        dl,
        jnp.where((lane == 6) | (lane == 8) | (lane == 10), dr, 0.0),
    )
    factor = jnp.where((lane == 2) | (lane == 15), g, across * across)
    factor = jnp.where(lane == 11, 2.0 * g, factor)
    factor = jnp.where((lane < 2) | ((lane >= 12) & (lane < 15)), 1.0, factor)
    terms = jnp.where(lane == 16, (DAMP * SUB * SUB) * g * g, st * factor)
    sums = jnp.sum(terms, axis=0, keepdims=True)

    def whole(wanted):
        return jnp.sum(jnp.where(wanted, sums, 0.0), axis=1, keepdims=True)

    at = lanes_of((1, 128))
    rz, zw = whole(at == 0), whole(at == 1)
    ry = whole((at == 12) | (at == 15))
    yw = whole((at == 13) | (at == 2))
    yv = whole(((at >= 3) & (at < 12)) | (at == 14) | (at == 16))
    a = rz / zw
    rz1 = rz - a * ry - a * zw + a * a * yw
    beta1 = 1.0 + rz1 / rz
    dad = (beta1 * beta1 * zw - 2.0 * a * beta1 * yw) * (1.0 / SHRINK) + a * a * yv
    a1 = rz1 / dad
    r = i - 1 + lane // 4
    c = 2 * j - 1 + lane % 4
    inside = (r >= 0) & (r < counts[0]) & (c >= 0) & (c < 2 * tiles_c) & (lane < 12)
    where = lax.rem(c + 2, 2) * devices + r * tiles_c + (c + 2) // 2 - 1
    picked = jnp.sum(jnp.where(inside & (row == where), g, 0.0), axis=0, keepdims=True)
    bands = as_bands([picked[:, k : k + 1] for k in range(12)])
    on = bands[1][:, :TC]
    coarse = edge_bands(bands)
    image = DAMP * coarse + lap(edge_part(m_ref) * lap(coarse))
    image = with_edges(image, (jumps(bands[1]) * (1.0 / SHRINK))[:, :TC] * f_ref[...] + DAMP * on)
    y = q_ref[...] + on
    v = v_ref[...] + image
    z, w = z_ref[...], w_ref[...]
    solution_ref[...] = (a * SHRINK) * z + a1 * (beta1 * z - a * y)
    residual_ref[...] = both_ref[:TR] - a * w - a1 * ((beta1 * (1.0 / SHRINK)) * w - a * v)


def call(kernel, outs, *args, flops=10**9):
    shapes = [jax.ShapeDtypeStruct(s, jnp.float32) for s in outs]
    return pl.pallas_call(
        kernel,
        out_shape=shapes,
        compiler_params=pltpu.CompilerParams(vmem_limit_bytes=48 * 1024 * 1024),
        cost_estimate=pl.CostEstimate(flops=flops, bytes_accessed=10**6, transcendentals=0),
    )(*args)


def pairs_from(count, offset):
    found = []
    for k in range(offset, count, 2):
        found += [(k, (k + 1) % count), ((k + 1) % count, k)]
    return found


def odd_pairs(counts, axis, bit):
    found = []
    for i in range(counts[0]):
        for j in range(counts[1]):
            at = [i, j]
            if bit and at[axis] in (0, counts[axis] - 1):
                at[1 - axis] ^= bit
            else:
                at[axis] = (at[axis] + (1 if at[axis] % 2 else -1)) % counts[axis]
            found.append((i * counts[1] + j, at[0] * counts[1] + at[1]))
    return found


def xor_pairs(counts, rows, cols):
    flat = [(i, j) for i in range(counts[0]) for j in range(counts[1])]
    return [(i * counts[1] + j, (i ^ rows) * counts[1] + (j ^ cols)) for i, j in flat]


def spreads(counts):
    known = np.eye(counts[0] * counts[1], dtype=bool)

    def meet(*swaps):
        return np.logical_or.reduce([known, *(known[[b for _, b in pairs]] for pairs in swaps)])

    even = [xor_pairs(counts, 0, 1), xor_pairs(counts, 1, 0)]
    known = meet(even[0], odd_pairs(counts, 1, 0))
    known = meet(even[1], odd_pairs(counts, 0, 0), xor_pairs(counts, 4, 0))
    known = meet(even[0], odd_pairs(counts, 1, 1))
    return meet(even[1], odd_pairs(counts, 0, 0)).all()


def body(counts, height, noise):
    nr, nc = counts
    devices = nr * nc
    width = max(128, devices * 2)
    basis = jnp.asarray(constants(nr, 2 * nc, width))
    both_axes = ("row", "col")
    depth = table_shape(counts)[0]

    def swap(a, b, axis, bit=0):
        gb = lax.ppermute(b, both_axes, odd_pairs(counts, both_axes.index(axis), bit))
        return lax.ppermute(a, axis, pairs_from(lax.axis_size(axis), 0)), gb

    def small_swap(x, rows, cols):
        return lax.ppermute(x, both_axes, xor_pairs(counts, rows, cols))

    both = jnp.pad(noise, ((0, TR), (0, 0))) + jnp.pad(height, ((TR, 0), (0, 0)))
    b, a, table = call(
        functools.partial(begin_kernel, counts), [(32 + depth, 128)] * 2 + [(depth, 128)], both
    )
    if not spreads(counts):
        for axis, count in enumerate(counts):
            bit = 1
            while bit < count:
                table = table + small_swap(table, *((0, bit) if axis else (bit, 0)))
                bit *= 2
    ga, gb = swap(a, b, "col")
    r3, h3, b, a, table = call(
        functools.partial(widen_kernel, counts),
        [(128, 128)] * 2 + [(24 + depth, FC)] * 2 + [(depth, 128)],
        both,
        table,
        gb,
        ga,
    )
    ga, gb = swap(a, b, "row")
    weight, table = call(weights_kernel, [(EXT, 2 * SPEC), (depth, 128)], both, table, basis)
    far = small_swap(table, 4, 0)
    t = call(forward_kernel, [(EXT, 2 * SPEC)], both, r3, basis)[0]
    t, table, b, a = call(
        functools.partial(first_kernel, counts),
        [(EXT, 2 * SPEC), (depth, 128)] + [(24, EXT)] * 2,
        gb,
        ga,
        t,
        weight,
        basis,
        table,
    )
    table = merged(table, far)
    wide = jnp.pad(table, ((0, 0), (0, EXT - 128)))
    y, m = call(
        functools.partial(inverse_kernel, counts),
        [(EXT, FC), (FR, FC)],
        t,
        basis,
        both,
        h3,
        gb,
        ga,
    )
    ga, gb = swap(*(jnp.concatenate([x, wide], axis=0) for x in (a, b)), "col", 1)
    y, table, b, a = call(
        functools.partial(columns_kernel, counts),
        [(EXT, FC), (depth, 128)] + [(24 + depth, FC)] * 2,
        y,
        ga,
        gb,
        table,
    )
    ga, gb = swap(a, b, "row")
    inner_w, f, gw, gf = call(
        functools.partial(inner_kernel, counts),
        [(96, TC)] * 2 + [(EXT, FC)] * 2,
        y,
        m,
        basis,
    )
    z, w, t, b, a = call(
        functools.partial(second_kernel, counts, width),
        [(TR, TC)] * 2 + [(EXT, 2 * SPEC)] + [(16, EXT)] * 2,
        y,
        m,
        gb,
        ga,
        table,
        inner_w,
        f,
        gw,
        gf,
        weight,
        basis,
    )
    ga, gb = swap(a, b, "col", 1)
    y, stats = call(inverse_stats_kernel, [(EXT, FC), (1, 128)], t, basis, both, m, z, w)
    y, b, a = call(
        functools.partial(columns_kernel, counts), [(EXT, FC)] + [(16, FC)] * 2, y, gb, ga
    )
    ga, gb = swap(a, b, "row", 1)
    inner_v, stats = call(
        functools.partial(inner_dots_kernel, counts),
        [(96, TC), (1, 128)],
        y,
        m,
        both,
        w,
        stats,
    )
    q, v, stats = call(
        functools.partial(dots_kernel, counts),
        [(TR, TC)] * 2 + [(devices, 128)],
        y,
        m,
        gb,
        ga,
        both,
        w,
        stats,
        inner_v,
    )
    stats = lax.all_to_all(stats, both_axes, 0, 0, tiled=True)
    return tuple(
        call(
            functools.partial(end_kernel, counts, width),
            [(TR, TC)] * 2,
            stats,
            basis,
            m,
            f,
            both,
            z,
            w,
            q,
            v,
        )
    )


def solution(mesh):
    counts = (mesh.shape["row"], mesh.shape["col"])
    spec = P("row", "col")
    return jax.shard_map(
        functools.partial(body, counts),
        mesh=mesh,
        in_specs=(spec, spec),
        out_specs=(spec, spec),
        check_vma=False,
    )
```

```python
import functools

import jax
import jax.numpy as jnp
import ml_dtypes
import numpy as np
from jax import lax
from jax.experimental import pallas as pl
from jax.experimental.pallas import tpu as pltpu
from jax.sharding import PartitionSpec as P

SUB = 128
OV = 8
EXT = SUB + 2 * OV
DAMP = 2.0**-28
SHRINK = 2.0**-20

TR, TC = 128, 256
FR, FC = 160, 384
SPEC = 256

highest = lax.Precision.HIGHEST


def sine(count):
    k = np.arange(1, count + 1, dtype=np.float64)
    basis = np.sqrt(2.0 / (count + 1.0)) * np.sin(np.pi * k[:, None] * k[None, :] / (count + 1.0))
    return basis, 2.0 - 2.0 * np.cos(np.pi * k / (count + 1.0))


def block_constants():
    basis, eig = sine(EXT)
    rows = np.roll(basis, -OV, 0)
    cols = np.pad(basis, ((0, SPEC - EXT), (0, SPEC - EXT)))
    scale = np.pad((eig[:, None] + eig[None, :]) ** 2, ((0, 0), (0, SPEC - EXT)))
    wide = lambda x: np.pad(x, ((0, 0), (0, 2 * SPEC - x.shape[1])))
    high = rows.T.astype(ml_dtypes.bfloat16).astype(np.float64)
    low = (rows.T - high).astype(ml_dtypes.bfloat16).astype(np.float64)
    tile = np.concatenate([x[:, :SUB] for x in (high, high, low)], 1)
    halo = np.concatenate([x[:, SUB:] for x in (high, high, low)], 1)
    inner = np.concatenate([x[:, 16:112] for x in (high, high, low)], 1)
    at = [*range(136, 144), *range(16), *range(112, 136)]
    edge = np.concatenate([x[:, at] for x in (high, high, low)], 1)
    turned = np.hstack([rows.T, np.zeros((EXT, 256 - EXT)), edge])
    return [np.tile(scale, (1, 2)), *(wide(x) for x in (rows, turned, cols, inner, np.hstack([tile, halo])))]


def rows_part(ref):
    return ref[EXT : 2 * EXT, :EXT]


def rows_t_part(ref):
    return ref[2 * EXT : 3 * EXT, :256]


def cols_part(ref):
    return ref[3 * EXT : 3 * EXT + SPEC, :SPEC]


def inner_rows(ref):
    at = 3 * EXT + SPEC
    return ref[at : at + EXT, : 3 * 96]


def edge_rows(ref):
    return ref[2 * EXT : 3 * EXT, 256 : 256 + 3 * 48]


def tile_rows(ref):
    at = 4 * EXT + SPEC
    return ref[at : at + EXT, : 3 * SUB]


def halo_rows(ref):
    at = 4 * EXT + SPEC
    return ref[at : at + EXT, 3 * SUB : 3 * EXT]


def coarse_part(ref, width):
    at, lanes = 5 * EXT + SPEC, 2 * SPEC
    parts = [ref[at + k * width : at + (k + 1) * width] for k in range(-(-width // lanes))]
    return (parts[0] if len(parts) == 1 else jnp.concatenate(parts, axis=1))[:, :width]


def constants(nr, nc, width):
    lanes = 2 * SPEC
    inverse = coarse_inverse(nr, nc, -(-width // lanes) * lanes)[:width]
    parts = [*block_constants(), *np.split(inverse, inverse.shape[1] // lanes, 1)]
    return np.concatenate(parts).astype(np.float32)


def coarse_inverse(nr, nc, width):
    br, er = sine(nr)
    bc, ec = sine(nc)
    both = np.kron(br, bc).reshape(nr, nc // 2, 2, nr * nc).transpose(2, 0, 1, 3)
    both = both.reshape(nr * nc, nr * nc)
    scale = (er[:, None] + ec[None, :]) / (SUB * SUB)
    values = (SUB * SUB * (DAMP + scale * scale)).reshape(-1)
    whole = np.zeros((width, width), np.float32)
    whole[: nr * nc, : nr * nc] = (both / values) @ both.T
    return whole


def dot(a, b, side=0):
    return lax.dot_general(
        a, b, (((1,), (side,)), ((), ())), precision=highest, preferred_element_type=jnp.float32
    )


def lap(x):
    rows, lanes = x.shape
    beside = pltpu.roll(x, 1, 0) + pltpu.roll(x, rows - 1, 0)
    beside = beside + (pltpu.roll(x, 1, 1) + pltpu.roll(x, lanes - 1, 1))
    return 4.0 * x - beside


def lanes_of(shape):
    return lax.broadcasted_iota(jnp.int32, shape, 1)


def rows_of(shape):
    return lax.broadcasted_iota(jnp.int32, shape, 0)


def total(x):
    return jnp.sum(jnp.sum(x, axis=0, keepdims=True), axis=1, keepdims=True)


def place():
    return lax.axis_index("row"), lax.axis_index("col")


def is_even(index):
    return lax.rem(index, 2) == 0


def column_mask(counts):
    j = lax.axis_index("col")
    lane = lanes_of((1, FC))
    right = jnp.where(j < counts[1] - 1, 320, 256)
    left = jnp.where(j > 0, 320, 384)
    return (lane < right) | (lane >= left)


def edge_mask(counts):
    i = lax.axis_index("row")
    row = rows_of((80, 1))
    first = jnp.where(i > 0, 0, 16)
    last = jnp.where(i < counts[0] - 1, 80, 64)
    return (row >= first) & (row < last) & column_mask(counts)


def table_shape(counts):
    return (-(-2 * counts[0] * counts[1] // 1024) * 8, 128)


def table_of(values, counts):
    i, j = place()
    devices = counts[0] * counts[1]
    shape = table_shape(counts)
    at = rows_of(shape) * 128 + lanes_of(shape) - (i * counts[1] + j)
    return jnp.where(at == 0, values[0], jnp.where(at == devices, values[1], 0.0))


def merged(table, *others):
    for other in others:
        table = jnp.where(table != 0.0, table, other)
    return table


def as_row(table, width):
    return jnp.concatenate([table[k : k + 1] for k in range(width // 128)], axis=1)


def row_of(pairs):
    lane = lanes_of((1, 128))
    row = jnp.zeros((1, 128), jnp.float32)
    for k, (left, right) in enumerate(pairs):
        row = jnp.where(lane == k, left, jnp.where(lane == 64 + k, right, row))
    return row


def near_inverse(counts, inverse):
    i, j = place()
    nr, nc = counts[0], 2 * counts[1]
    shape = (16, inverse.shape[0])
    which = rows_of(shape)
    r = i - 1 + which // 4
    c = 2 * j - 1 + which % 4
    inside = (r >= 0) & (r < nr) & (c >= 0) & (c < nc) & (which < 12)
    at = lax.rem(c + 2, 2) * (nr * counts[1]) + r * counts[1] + (c + 2) // 2 - 1
    return dot(jnp.where(inside & (lanes_of(shape) == at), 1.0, 0.0), inverse)


def as_bands(values):
    lane = lanes_of((1, FC))
    bands = []
    for d in range(3):
        left, first, second, right = values[4 * d : 4 * d + 4]
        bands.append(
            jnp.where(
                lane < 128,
                first,
                jnp.where(lane < 256, second, jnp.where(lane < 320, right, left)),
            )
        )
    return bands


def edge_bands(bands):
    above, on, below = bands
    return jnp.concatenate(
        [
            jnp.broadcast_to(above, (16, FC)),
            jnp.broadcast_to(on, (48, FC)),
            jnp.broadcast_to(below, (16, FC)),
        ],
        axis=0,
    )


def jumps(row):
    step = row - pltpu.roll(row, 1, 1)
    lane = lanes_of((1, FC))
    at = [jnp.sum(jnp.where(lane == k, step, 0.0), axis=1, keepdims=True) for k in (0, 128, 256)]
    return jnp.where(
        (lane < 64) | (lane >= 320), at[0], jnp.where(lane < 192, at[1], at[2])
    )


def edge_steps():
    lane = lanes_of((1, FC))
    up = (lane == 0) | (lane == 128) | (lane == 256)
    down = (lane == FC - 1) | (lane == 127) | (lane == 255)
    return jnp.where(up, 1.0, jnp.where(down, -1.0, 0.0))


def halves_of(x):
    high = x.astype(jnp.bfloat16)
    return high, (x - high.astype(jnp.float32)).astype(jnp.bfloat16)


def product(a, b):
    return lax.dot_general(a, b, (((1,), (0,)), ((), ())), preferred_element_type=jnp.float32)


def column_transform(w, basis_ref):
    high, low = halves_of(pltpu.roll(w, OV, 1))
    cols, rest = halves_of(cols_part(basis_ref))
    cols = jnp.concatenate([cols, rest, cols], axis=0)

    def block(at):
        part = slice(at, at + SPEC)
        return product(jnp.concatenate([high[:, part], high[:, part], low[:, part]], axis=1), cols)

    return jnp.concatenate([block(0), block(128)], axis=1)


def row_transform(u, basis_ref, part):
    high, low = halves_of(u)
    rows = part(basis_ref).astype(jnp.bfloat16)
    return product(rows, jnp.concatenate([high, low, high], axis=0))


def strips_of(t, basis_ref, deep):
    cols = cols_part(basis_ref)
    left = dot(cols[:deep], t[:, :SPEC], 1)
    right = dot(cols[EXT - deep : EXT], t[:, SPEC:], 1)
    both = dot(jnp.concatenate([left, right], axis=0), rows_t_part(basis_ref)[:, :EXT])
    return both[:deep], both[deep:]


def solution_of(t, basis_ref):
    v = dot(rows_part(basis_ref), t)
    cols = cols_part(basis_ref)
    first, second = dot(v[:, :SPEC], cols), dot(v[:, SPEC:], cols)
    y = jnp.concatenate(
        [first[:, :128], first[:, 128:] + second[:, :128], second[:, 128:]], axis=1
    )
    return pltpu.roll(y, FC - OV, 1)


def core_sums(x):
    return [total(x[:, :128]), total(x[:, 128:256])]


def add_columns(y, from_left, from_right):
    far = from_left.shape[0] - OV
    gap = jnp.zeros((56 - far, EXT), jnp.float32)
    turned = jnp.concatenate(
        [from_right[8:], gap, from_right[:8], from_left[far:], gap, from_left[:far]], axis=0
    )
    back = turned.T
    lane = lanes_of((EXT, 128))
    rolled = pltpu.roll(back, 64, 1)
    first = y[:, :128] + jnp.where(lane < 8, rolled, 0.0)
    second = y[:, 128:256] + jnp.where(lane >= 120, rolled, 0.0)
    third = y[:, 256:] + jnp.where((lane < 16) | (lane >= 112), back, 0.0)
    return jnp.concatenate([first, second, third], axis=1)


def pack_rows(y, deep):
    return jnp.concatenate([y[136:], y[: deep - 8]], axis=0), y[136 - deep : 136]


def edges(y, from_above, from_below):
    far = from_above.shape[0] - OV
    none = jnp.zeros((8, FC), jnp.float32)
    return jnp.concatenate(
        [
            from_above[:8] if far == 16 else none,
            y[136:] + from_above[far - 8 : far],
            y[:8] + from_above[far:],
            y[8:24],
            y[104:120],
            y[120:136] + from_below[:16],
            from_below[16:] if far == 16 else none,
        ],
        axis=0,
    )


def edge_part(frame):
    return jnp.concatenate([frame[144:], frame[:24], frame[104:144]], axis=0)


def with_edges(edge, inner):
    return jnp.concatenate([edge[16:32, :TC], inner, edge[48:64, :TC]], axis=0)


def sides(index, count, a, b):
    even = is_even(index)
    before = jnp.where(index > 0, jnp.where(even, b, a), 0.0)
    after = jnp.where(index < count - 1, jnp.where(even, a, b), 0.0)
    return before, after


def send(index, a_ref, b_ref, before, after):
    even = is_even(index)
    a_ref[...] = jnp.where(even, after, before)
    b_ref[...] = jnp.where(even, before, after)


def begin_kernel(counts, both_ref, b_ref, a_ref, table_ref):
    r, h = both_ref[:TR], both_ref[TR:]
    lane = lanes_of((128, 128))
    packed = jnp.where(
        lane < 16,
        r[:, :128],
        jnp.where(
            lane < 64,
            pltpu.roll(h[:, :128], 16, 1),
            jnp.where(lane < 112, pltpu.roll(h[:, 128:], 112, 1), r[:, 128:]),
        ),
    )
    turned = packed.T
    table = table_of(core_sums(r), counts)
    table_ref[...] = table
    send(
        lax.axis_index("col"),
        a_ref,
        b_ref,
        jnp.concatenate([turned[:32], table], axis=0),
        jnp.concatenate([turned[96:], table], axis=0),
    )


def widen_kernel(counts, both_ref, own_ref, gb_ref, ga_ref, r3_ref, h3_ref, b_ref, a_ref, table_ref):
    i, j = place()
    from_left, from_right = sides(j, counts[1], ga_ref[:32], gb_ref[:32])
    turned = jnp.concatenate([from_right, jnp.zeros((64, 128), jnp.float32), from_left], axis=0)
    back = turned.T
    lane = lanes_of((128, 128))
    edge = (lane < 16) | (lane >= 112)
    r3 = jnp.where(edge, back, 0.0)
    h3 = jnp.where(
        lane < 16, pltpu.roll(back, 112, 1), jnp.where(lane >= 112, pltpu.roll(back, 16, 1), 0.0)
    )
    r3_ref[...] = r3
    h3_ref[...] = h3
    r, h = both_ref[:TR], both_ref[TR:]
    table = merged(own_ref[...], ga_ref[32:], gb_ref[32:])
    table_ref[...] = table
    wide = jnp.concatenate([table, jnp.zeros((table.shape[0], FC - 128), jnp.float32)], axis=1)

    def strip(r_rows, h_rows):
        return jnp.concatenate(
            [
                jnp.concatenate([r[r_rows], r3[r_rows]], axis=1),
                jnp.concatenate([h[h_rows], h3[h_rows]], axis=1),
                wide,
            ],
            axis=0,
        )

    send(i, a_ref, b_ref, strip(slice(0, 8), slice(0, 16)), strip(slice(120, 128), slice(112, 128)))


def means_kernel(both_ref, table_ref, basis_ref, means_ref, table_out):
    h = both_ref[TR:]
    lane = lanes_of((1, 2 * SPEC))
    left, right = (x / (SUB * SUB) for x in core_sums(h * h * h))
    means_ref[...] = jnp.where(lane < SPEC, left, right)
    table_out[...] = table_ref[...]


def forward_kernel(both_ref, r3_ref, means_ref, basis_ref, t_ref, weights_ref):
    r = both_ref[:TR]
    u = column_transform(jnp.concatenate([r, r3_ref[...]], axis=1), basis_ref)
    t_ref[...] = row_transform(u, basis_ref, tile_rows)
    weights_ref[...] = 1.0 / (DAMP + means_ref[...] * basis_ref[:EXT])


def first_kernel(
    counts,
    gb_ref,
    ga_ref,
    tile_ref,
    weights_ref,
    basis_ref,
    table_ref,
    t_ref,
    table_out,
    b_ref,
    a_ref,
):
    i, j = place()
    above, below = sides(i, counts[0], ga_ref[:8], gb_ref[:8])
    u = column_transform(jnp.concatenate([below, above], axis=0), basis_ref)
    t = (tile_ref[...] + row_transform(u, basis_ref, halo_rows)) * weights_ref[...]
    t_ref[...] = t
    send(j, a_ref, b_ref, *strips_of(t, basis_ref, 24))
    table_out[...] = merged(table_ref[...], ga_ref[24:, :128], gb_ref[24:, :128])


def inverse_kernel(counts, t_ref, basis_ref, both_ref, h3_ref, gb_ref, ga_ref, y_ref, m_ref):
    y_ref[...] = solution_of(t_ref[...], basis_ref)
    above, below = sides(lax.axis_index("row"), counts[0], ga_ref[8:24], gb_ref[8:24])
    h = jnp.concatenate([both_ref[TR:], h3_ref[...]], axis=1)
    tall = jnp.concatenate([h, below, above], axis=0)
    m_ref[...] = tall * tall * tall


def columns_kernel(counts, y_ref, *refs):
    i, j = place()
    (ga_ref, gb_ref), refs = (refs[:2] if len(refs) == 7 else refs[1::-1]), refs[2:]
    deep = 24 if len(refs) == 5 else 16
    y = add_columns(y_ref[...], *sides(j, counts[1], ga_ref[:deep], gb_ref[:deep]))
    strips = pack_rows(y, deep)
    if len(refs) == 5:
        table_ref, out_ref, table_out, b_ref, a_ref = refs
        table = merged(table_ref[...], ga_ref[24:, :128], gb_ref[24:, :128])
        table_out[...] = table
        wide = jnp.concatenate([table, jnp.zeros((table.shape[0], FC - 128), jnp.float32)], axis=1)
        strips = [jnp.concatenate([x, wide], axis=0) for x in strips]
    else:
        out_ref, b_ref, a_ref = refs
    out_ref[...] = y
    send(i, a_ref, b_ref, *strips)


def inner_kernel(counts, width, y_ref, m_ref, basis_ref, w_ref, f_ref, gw_ref, gf_ref, near_ref):
    mask = column_mask(counts)
    s = jnp.where(mask, y_ref[8:120], 0.0)
    m = m_ref[8:120]
    w = DAMP * s + lap(m * lap(s))
    w = jnp.where(mask, w[8:104], 0.0) * SHRINK
    f = lap(m * edge_steps())
    f = jnp.where(mask, f[8:104], 0.0) * SHRINK
    w_ref[...] = w[:, :TC]
    f_ref[...] = f[:, :TC]
    gw_ref[...] = row_transform(w, basis_ref, inner_rows)
    gf_ref[...] = row_transform(f, basis_ref, inner_rows)
    near_ref[...] = near_inverse(counts, coarse_part(basis_ref, width))


def second_kernel(
    counts,
    width,
    y_ref,
    m_ref,
    gb_ref,
    ga_ref,
    table_ref,
    inner_w_ref,
    f_ref,
    gw_ref,
    gf_ref,
    near_ref,
    weights_ref,
    basis_ref,
    z_ref,
    w_ref,
    t_ref,
    b_ref,
    a_ref,
):
    i, j = place()
    y = y_ref[...]
    mask = edge_mask(counts)
    s = edges(y, *sides(i, counts[0], ga_ref[:24], gb_ref[:24]))
    s = jnp.where(mask, s, 0.0)
    table = merged(table_ref[...], ga_ref[24:, :128], gb_ref[24:, :128])
    picked = jnp.sum(near_ref[...] * as_row(table, width), axis=1, keepdims=True)
    bands = as_bands([picked[k : k + 1] for k in range(12)])
    coarse = edge_bands(bands)
    m = edge_part(m_ref)
    flow = m * (lap(s) + lap(coarse))
    z = s + coarse
    w = jnp.where(mask, DAMP * z + lap(flow), 0.0) * SHRINK
    step = jumps(bands[1])
    damped = (DAMP * SHRINK) * bands[1]
    z_ref[...] = with_edges(z, y[16:112, :TC] + bands[1][:, :TC])
    w_ref[...] = with_edges(w, inner_w_ref[...] + step[:, :TC] * f_ref[...] + damped[:, :TC])
    lane = lanes_of((EXT, 256))
    ones = jnp.where((lane >= 16) & (lane < 112), rows_t_part(basis_ref), 0.0)
    ones = jnp.sum(ones, axis=1, keepdims=True)
    u = gw_ref[...] + step * gf_ref[...] + ones * damped
    u = u + row_transform(jnp.concatenate([w[8:32], w[48:72]], axis=0), basis_ref, edge_rows)
    t = column_transform(u, basis_ref) * weights_ref[...]
    t_ref[...] = t
    send(j, a_ref, b_ref, *strips_of(t, basis_ref, 16))


def inverse_stats_kernel(t_ref, basis_ref, both_ref, m_ref, z_ref, w_ref, y_ref, stats_ref):
    y_ref[...] = solution_of(t_ref[...], basis_ref)
    rt, mt, zt, wt = both_ref[:TR], m_ref[:TR, :TC], z_ref[...], w_ref[...]
    lane, row = lanes_of((1, 256)), rows_of((128, 1))
    along = (lane % 128 != 0) & (lane % 128 != 127)
    top, low = mt[:1], mt[127:]
    side = jnp.sum(jnp.where((row > 0) & (row < 127), mt, 0.0), axis=0, keepdims=True)

    def halves(x):
        return [
            jnp.sum(x[:, :128], axis=1, keepdims=True),
            jnp.sum(x[:, 128:], axis=1, keepdims=True),
        ]

    first, last = lane % 128 == 0, lane % 128 == 127
    zero = jnp.zeros((1, 1), jnp.float32)
    stats_ref[...] = row_of(
        [
            core_sums(rt * zt),
            core_sums(zt * wt),
            core_sums(wt),
            halves(jnp.where(along, top, 0.0)),
            halves(jnp.where(along, low, 0.0)),
            halves(jnp.where(first, side, 0.0)),
            halves(jnp.where(last, side, 0.0)),
            halves(jnp.where(first, top, 0.0)),
            halves(jnp.where(last, top, 0.0)),
            halves(jnp.where(first, low, 0.0)),
            halves(jnp.where(last, low, 0.0)),
            *[[zero, zero]] * 4,
            core_sums(rt),
        ]
    )


def inner_dots_kernel(counts, y_ref, m_ref, both_ref, w_ref, stats_ref, v_ref, stats_out):
    q = jnp.where(column_mask(counts), y_ref[8:120], 0.0)
    v = (DAMP * q + lap(m_ref[8:120] * lap(q)))[8:104, :TC]
    q = q[8:104, :TC]
    v_ref[...] = v
    rest = [
        core_sums(v),
        core_sums(both_ref[16:112] * q),
        core_sums(w_ref[16:112] * q),
        core_sums(v * q),
    ]
    zero = jnp.zeros((1, 1), jnp.float32)
    stats_out[...] = stats_ref[...] + row_of([[zero, zero]] * 11 + rest)


def dots_kernel(
    counts, y_ref, m_ref, gb_ref, ga_ref, both_ref, w_ref, stats_ref, inner_v_ref, q_ref, v_ref, stats_out
):
    i, j = place()
    y = y_ref[...]
    q = edges(y, *sides(i, counts[0], ga_ref[...], gb_ref[...]))
    q = jnp.where(edge_mask(counts), q, 0.0)
    v = DAMP * q + lap(edge_part(m_ref) * lap(q))
    q_ref[...] = with_edges(q, y[16:112, :TC])
    v_ref[...] = with_edges(v, inner_v_ref[...])
    qe, ve = (jnp.concatenate([x[16:32, :TC], x[48:64, :TC]], axis=0) for x in (q, v))
    re = jnp.concatenate([both_ref[:16], both_ref[112:128]], axis=0)
    we = jnp.concatenate([w_ref[:16], w_ref[112:]], axis=0)
    rest = [core_sums(ve), core_sums(re * qe), core_sums(we * qe), core_sums(ve * qe)]
    zero = jnp.zeros((1, 1), jnp.float32)
    row = stats_ref[...] + row_of([[zero, zero]] * 11 + rest)
    stats_out[...] = jnp.broadcast_to(row, stats_out.shape)


def end_kernel(
    counts,
    width,
    stats_ref,
    basis_ref,
    m_ref,
    f_ref,
    both_ref,
    z_ref,
    w_ref,
    q_ref,
    v_ref,
    solution_ref,
    residual_ref,
    solution_vmem,
    residual_vmem,
    sems,
):
    i, j = place()
    tiles_c = counts[1]
    devices = counts[0] * tiles_c
    rows = stats_ref[...]
    st = jnp.concatenate([rows, pltpu.roll(rows, 64, 1)], axis=0)
    inverse = coarse_part(basis_ref, width)[: 2 * devices, : 2 * devices]
    g = jnp.broadcast_to(dot(inverse, st)[:, 2:3], st.shape)
    lane, row = lanes_of(st.shape), rows_of(st.shape)
    device = row % devices
    column = device % tiles_c
    on_left = row < devices

    def from_row(distance):
        return pltpu.roll(g, distance % (2 * devices), 0)

    up = jnp.where(device >= tiles_c, from_row(tiles_c), 0.0)
    down = jnp.where(device < devices - tiles_c, from_row(-tiles_c), 0.0)
    left = jnp.where(on_left, jnp.where(column > 0, from_row(1 - devices), 0.0), from_row(devices))
    right = jnp.where(
        on_left, from_row(-devices), jnp.where(column < tiles_c - 1, from_row(devices - 1), 0.0)
    )
    du, dd, dl, dr = g - up, g - down, g - left, g - right
    across = jnp.where(
        (lane == 3) | (lane == 7) | (lane == 8),
        du,
        jnp.where((lane == 4) | (lane == 9) | (lane == 10), dd, 0.0),
    )
    across = across + jnp.where(
        (lane == 5) | (lane == 7) | (lane == 9),
        dl,
        jnp.where((lane == 6) | (lane == 8) | (lane == 10), dr, 0.0),
    )
    factor = jnp.where((lane == 2) | (lane == 15), g, across * across)
    factor = jnp.where(lane == 11, 2.0 * g, factor)
    factor = jnp.where((lane < 2) | ((lane >= 12) & (lane < 15)), 1.0, factor)
    terms = jnp.where(lane == 16, (DAMP * SUB * SUB) * g * g, st * factor)
    sums = jnp.sum(terms, axis=0, keepdims=True)

    def whole(wanted):
        return jnp.sum(jnp.where(wanted, sums, 0.0), axis=1, keepdims=True)

    at = lanes_of((1, 128))
    rz, zw = whole(at == 0), whole(at == 1)
    ry = whole((at == 12) | (at == 15))
    yw = whole((at == 13) | (at == 2))
    yv = whole(((at >= 3) & (at < 12)) | (at == 14) | (at == 16))
    a = rz / zw
    rz1 = rz - a * ry - a * zw + a * a * yw
    beta1 = 1.0 + rz1 / rz
    dad = (beta1 * beta1 * zw - 2.0 * a * beta1 * yw) * (1.0 / SHRINK) + a * a * yv
    a1 = rz1 / dad
    r = i - 1 + lane // 4
    c = 2 * j - 1 + lane % 4
    inside = (r >= 0) & (r < counts[0]) & (c >= 0) & (c < 2 * tiles_c) & (lane < 12)
    where = lax.rem(c + 2, 2) * devices + r * tiles_c + (c + 2) // 2 - 1
    picked = jnp.sum(jnp.where(inside & (row == where), g, 0.0), axis=0, keepdims=True)
    bands = as_bands([picked[:, k : k + 1] for k in range(12)])
    on = bands[1][:, :TC]
    coarse = edge_bands(bands)
    image = DAMP * coarse + lap(edge_part(m_ref) * lap(coarse))
    image = with_edges(image, (jumps(bands[1]) * (1.0 / SHRINK))[:, :TC] * f_ref[...] + DAMP * on)
    y = q_ref[...] + on
    v = v_ref[...] + image
    z, w = z_ref[...], w_ref[...]
    first = pltpu.make_async_copy(solution_vmem, solution_ref, sems.at[0])
    second = pltpu.make_async_copy(residual_vmem, residual_ref, sems.at[1])
    solution_vmem[...] = (a * SHRINK) * z + a1 * (beta1 * z - a * y)
    first.start()
    residual_vmem[...] = both_ref[:TR] - a * w - a1 * ((beta1 * (1.0 / SHRINK)) * w - a * v)
    second.start()
    first.wait()
    second.wait()


def call(kernel, outs, *args, flops=10**9, **options):
    shapes = [jax.ShapeDtypeStruct(s, jnp.float32) for s in outs]
    return pl.pallas_call(
        kernel,
        out_shape=shapes,
        compiler_params=pltpu.CompilerParams(vmem_limit_bytes=48 * 1024 * 1024),
        cost_estimate=pl.CostEstimate(flops=flops, bytes_accessed=10**6, transcendentals=0),
        **options,
    )(*args)


def pairs_from(count, offset):
    found = []
    for k in range(offset, count, 2):
        found += [(k, (k + 1) % count), ((k + 1) % count, k)]
    return found


def odd_pairs(counts, axis, bit):
    found = []
    for i in range(counts[0]):
        for j in range(counts[1]):
            at = [i, j]
            if bit and at[axis] in (0, counts[axis] - 1):
                at[1 - axis] ^= bit
            else:
                at[axis] = (at[axis] + (1 if at[axis] % 2 else -1)) % counts[axis]
            found.append((i * counts[1] + j, at[0] * counts[1] + at[1]))
    return found


def xor_pairs(counts, rows, cols):
    flat = [(i, j) for i in range(counts[0]) for j in range(counts[1])]
    return [(i * counts[1] + j, (i ^ rows) * counts[1] + (j ^ cols)) for i, j in flat]


def spreads(counts):
    known = np.eye(counts[0] * counts[1], dtype=bool)

    def meet(*swaps):
        return np.logical_or.reduce([known, *(known[[b for _, b in pairs]] for pairs in swaps)])

    even = [xor_pairs(counts, 0, 1), xor_pairs(counts, 1, 0)]
    known = meet(even[0], odd_pairs(counts, 1, 1))
    known = meet(even[1], odd_pairs(counts, 0, 0), xor_pairs(counts, 4, 0))
    known = meet(even[0], odd_pairs(counts, 1, 0))
    return meet(even[1], odd_pairs(counts, 0, 0)).all()


def body(counts, height, noise):
    nr, nc = counts
    devices = nr * nc
    width = max(128, devices * 2)
    basis = jnp.asarray(constants(nr, 2 * nc, width))
    both_axes = ("row", "col")
    depth = table_shape(counts)[0]

    def swap(a, b, axis, bit=0):
        gb = lax.ppermute(b, both_axes, odd_pairs(counts, both_axes.index(axis), bit))
        return lax.ppermute(a, axis, pairs_from(lax.axis_size(axis), 0)), gb

    def small_swap(x, rows, cols):
        return lax.ppermute(x, both_axes, xor_pairs(counts, rows, cols))

    both = jnp.pad(noise, ((0, TR), (0, 0))) + jnp.pad(height, ((TR, 0), (0, 0)))
    b, a, table = call(
        functools.partial(begin_kernel, counts), [(32 + depth, 128)] * 2 + [(depth, 128)], both
    )
    if not spreads(counts):
        for axis, count in enumerate(counts):
            bit = 1
            while bit < count:
                table = table + small_swap(table, *((0, bit) if axis else (bit, 0)))
                bit *= 2
    ga, gb = swap(a, b, "col", 1)
    r3, h3, b, a, table = call(
        functools.partial(widen_kernel, counts),
        [(128, 128)] * 2 + [(24 + depth, FC)] * 2 + [(depth, 128)],
        both,
        table,
        gb,
        ga,
    )
    ga, gb = swap(a, b, "row")
    means, table = call(means_kernel, [(1, 2 * SPEC), (depth, 128)], both, table, basis)
    far = small_swap(table, 4, 0)
    t, weight = call(forward_kernel, [(EXT, 2 * SPEC)] * 2, both, r3, means, basis)
    t, table, b, a = call(
        functools.partial(first_kernel, counts),
        [(EXT, 2 * SPEC), (depth, 128)] + [(24, EXT)] * 2,
        gb,
        ga,
        t,
        weight,
        basis,
        table,
    )
    table = merged(table, far)
    wide = jnp.pad(table, ((0, 0), (0, EXT - 128)))
    y, m = call(
        functools.partial(inverse_kernel, counts),
        [(EXT, FC), (FR, FC)],
        t,
        basis,
        both,
        h3,
        gb,
        ga,
    )
    ga, gb = swap(*(jnp.concatenate([x, wide], axis=0) for x in (a, b)), "col")
    y, table, b, a = call(
        functools.partial(columns_kernel, counts),
        [(EXT, FC), (depth, 128)] + [(24 + depth, FC)] * 2,
        y,
        ga,
        gb,
        table,
    )
    ga, gb = swap(a, b, "row")
    inner_w, f, gw, gf, near = call(
        functools.partial(inner_kernel, counts, width),
        [(96, TC)] * 2 + [(EXT, FC)] * 2 + [(16, width)],
        y,
        m,
        basis,
    )
    z, w, t, b, a = call(
        functools.partial(second_kernel, counts, width),
        [(TR, TC)] * 2 + [(EXT, 2 * SPEC)] + [(16, EXT)] * 2,
        y,
        m,
        gb,
        ga,
        table,
        inner_w,
        f,
        gw,
        gf,
        near,
        weight,
        basis,
    )
    ga, gb = swap(a, b, "col", 1)
    y, stats = call(inverse_stats_kernel, [(EXT, FC), (1, 128)], t, basis, both, m, z, w)
    y, b, a = call(
        functools.partial(columns_kernel, counts), [(EXT, FC)] + [(16, FC)] * 2, y, gb, ga
    )
    ga, gb = swap(a, b, "row", 1)
    inner_v, stats = call(
        functools.partial(inner_dots_kernel, counts),
        [(96, TC), (1, 128)],
        y,
        m,
        both,
        w,
        stats,
    )
    q, v, stats = call(
        functools.partial(dots_kernel, counts),
        [(TR, TC)] * 2 + [(devices, 128)],
        y,
        m,
        gb,
        ga,
        both,
        w,
        stats,
        inner_v,
    )
    stats = lax.all_to_all(stats, both_axes, 0, 0, tiled=True)
    return tuple(
        call(
            functools.partial(end_kernel, counts, width),
            [(TR, TC)] * 2,
            stats,
            basis,
            m,
            f,
            both,
            z,
            w,
            q,
            v,
            out_specs=[pl.BlockSpec(memory_space=pl.ANY)] * 2,
            scratch_shapes=[pltpu.VMEM((TR, TC), jnp.float32)] * 2 + [pltpu.SemaphoreType.DMA((2,))],
        )
    )


def solution(mesh):
    counts = (mesh.shape["row"], mesh.shape["col"])
    spec = P("row", "col")
    return jax.shard_map(
        functools.partial(body, counts),
        mesh=mesh,
        in_specs=(spec, spec),
        out_specs=(spec, spec),
        check_vma=False,
    )
```

```python
import functools

import jax
import jax.numpy as jnp
import ml_dtypes
import numpy as np
from jax import lax
from jax.experimental import pallas as pl
from jax.experimental.pallas import tpu as pltpu
from jax.sharding import PartitionSpec as P

SUB = 128
OV = 8
EXT = SUB + 2 * OV
DAMP = 2.0**-28
SHRINK = 2.0**-20

TR, TC = 128, 256
FR, FC = 160, 384
SPEC = 256

highest = lax.Precision.HIGHEST


def sine(count):
    k = np.arange(1, count + 1, dtype=np.float64)
    basis = np.sqrt(2.0 / (count + 1.0)) * np.sin(np.pi * k[:, None] * k[None, :] / (count + 1.0))
    return basis, 2.0 - 2.0 * np.cos(np.pi * k / (count + 1.0))


def block_constants():
    basis, eig = sine(EXT)
    rows = np.roll(basis, -OV, 0)
    cols = np.pad(basis, ((0, SPEC - EXT), (0, SPEC - EXT)))
    scale = np.pad((eig[:, None] + eig[None, :]) ** 2, ((0, 0), (0, SPEC - EXT)))
    wide = lambda x: np.pad(x, ((0, 0), (0, 2 * SPEC - x.shape[1])))
    high = rows.T.astype(ml_dtypes.bfloat16).astype(np.float64)
    low = (rows.T - high).astype(ml_dtypes.bfloat16).astype(np.float64)
    tile = np.concatenate([x[:, :SUB] for x in (high, high, low)], 1)
    halo = np.concatenate([x[:, SUB:] for x in (high, high, low)], 1)
    inner = np.concatenate([x[:, 16:112] for x in (high, high, low)], 1)
    at = [*range(136, 144), *range(16), *range(112, 136)]
    edge = np.concatenate([x[:, at] for x in (high, high, low)], 1)
    turned = np.hstack([rows.T, np.zeros((EXT, 256 - EXT)), edge])
    return [np.tile(scale, (1, 2)), *(wide(x) for x in (rows, turned, cols, inner, np.hstack([tile, halo])))]


def rows_part(ref):
    return ref[EXT : 2 * EXT, :EXT]


def rows_t_part(ref):
    return ref[2 * EXT : 3 * EXT, :256]


def cols_part(ref):
    return ref[3 * EXT : 3 * EXT + SPEC, :SPEC]


def inner_rows(ref):
    at = 3 * EXT + SPEC
    return ref[at : at + EXT, : 3 * 96]


def edge_rows(ref):
    return ref[2 * EXT : 3 * EXT, 256 : 256 + 3 * 48]


def tile_rows(ref):
    at = 4 * EXT + SPEC
    return ref[at : at + EXT, : 3 * SUB]


def halo_rows(ref):
    at = 4 * EXT + SPEC
    return ref[at : at + EXT, 3 * SUB : 3 * EXT]


def coarse_part(ref, width):
    at, lanes = 5 * EXT + SPEC, 2 * SPEC
    parts = [ref[at + k * width : at + (k + 1) * width] for k in range(-(-width // lanes))]
    return (parts[0] if len(parts) == 1 else jnp.concatenate(parts, axis=1))[:, :width]


def constants(nr, nc, width):
    lanes = 2 * SPEC
    inverse = coarse_inverse(nr, nc, -(-width // lanes) * lanes)[:width]
    parts = [*block_constants(), *np.split(inverse, inverse.shape[1] // lanes, 1)]
    return np.concatenate(parts).astype(np.float32)


def coarse_inverse(nr, nc, width):
    br, er = sine(nr)
    bc, ec = sine(nc)
    both = np.kron(br, bc).reshape(nr, nc // 2, 2, nr * nc).transpose(2, 0, 1, 3)
    both = both.reshape(nr * nc, nr * nc)
    scale = (er[:, None] + ec[None, :]) / (SUB * SUB)
    values = (SUB * SUB * (DAMP + scale * scale)).reshape(-1)
    whole = np.zeros((width, width), np.float32)
    whole[: nr * nc, : nr * nc] = (both / values) @ both.T
    return whole


def dot(a, b, side=0):
    return lax.dot_general(
        a, b, (((1,), (side,)), ((), ())), precision=highest, preferred_element_type=jnp.float32
    )


def lap(x):
    rows, lanes = x.shape
    beside = pltpu.roll(x, 1, 0) + pltpu.roll(x, rows - 1, 0)
    beside = beside + (pltpu.roll(x, 1, 1) + pltpu.roll(x, lanes - 1, 1))
    return 4.0 * x - beside


def lanes_of(shape):
    return lax.broadcasted_iota(jnp.int32, shape, 1)


def rows_of(shape):
    return lax.broadcasted_iota(jnp.int32, shape, 0)


def total(x):
    return jnp.sum(jnp.sum(x, axis=0, keepdims=True), axis=1, keepdims=True)


def place():
    return lax.axis_index("row"), lax.axis_index("col")


def is_even(index):
    return lax.rem(index, 2) == 0


def column_mask(counts):
    j = lax.axis_index("col")
    lane = lanes_of((1, FC))
    right = jnp.where(j < counts[1] - 1, 320, 256)
    left = jnp.where(j > 0, 320, 384)
    return (lane < right) | (lane >= left)


def edge_mask(counts):
    i = lax.axis_index("row")
    row = rows_of((80, 1))
    first = jnp.where(i > 0, 0, 16)
    last = jnp.where(i < counts[0] - 1, 80, 64)
    return (row >= first) & (row < last) & column_mask(counts)


def table_shape(counts):
    return (-(-2 * counts[0] * counts[1] // 1024) * 8, 128)


def table_of(values, counts):
    i, j = place()
    devices = counts[0] * counts[1]
    shape = table_shape(counts)
    at = rows_of(shape) * 128 + lanes_of(shape) - (i * counts[1] + j)
    return jnp.where(at == 0, values[0], jnp.where(at == devices, values[1], 0.0))


def merged(table, *others):
    for other in others:
        table = jnp.where(table != 0.0, table, other)
    return table


def as_row(table, width):
    return jnp.concatenate([table[k : k + 1] for k in range(width // 128)], axis=1)


def row_of(pairs):
    lane = lanes_of((1, 128))
    row = jnp.zeros((1, 128), jnp.float32)
    for k, (left, right) in enumerate(pairs):
        row = jnp.where(lane == k, left, jnp.where(lane == 64 + k, right, row))
    return row


def near_inverse(counts, inverse):
    i, j = place()
    nr, nc = counts[0], 2 * counts[1]
    shape = (16, inverse.shape[0])
    which = rows_of(shape)
    r = i - 1 + which // 4
    c = 2 * j - 1 + which % 4
    inside = (r >= 0) & (r < nr) & (c >= 0) & (c < nc) & (which < 12)
    at = lax.rem(c + 2, 2) * (nr * counts[1]) + r * counts[1] + (c + 2) // 2 - 1
    return dot(jnp.where(inside & (lanes_of(shape) == at), 1.0, 0.0), inverse)


def as_bands(values):
    lane = lanes_of((1, FC))
    bands = []
    for d in range(3):
        left, first, second, right = values[4 * d : 4 * d + 4]
        bands.append(
            jnp.where(
                lane < 128,
                first,
                jnp.where(lane < 256, second, jnp.where(lane < 320, right, left)),
            )
        )
    return bands


def edge_bands(bands):
    above, on, below = bands
    return jnp.concatenate(
        [
            jnp.broadcast_to(above, (16, FC)),
            jnp.broadcast_to(on, (48, FC)),
            jnp.broadcast_to(below, (16, FC)),
        ],
        axis=0,
    )


def jumps(row):
    step = row - pltpu.roll(row, 1, 1)
    lane = lanes_of((1, FC))
    at = [jnp.sum(jnp.where(lane == k, step, 0.0), axis=1, keepdims=True) for k in (0, 128, 256)]
    return jnp.where(
        (lane < 64) | (lane >= 320), at[0], jnp.where(lane < 192, at[1], at[2])
    )


def edge_steps():
    lane = lanes_of((1, FC))
    up = (lane == 0) | (lane == 128) | (lane == 256)
    down = (lane == FC - 1) | (lane == 127) | (lane == 255)
    return jnp.where(up, 1.0, jnp.where(down, -1.0, 0.0))


def halves_of(x):
    high = x.astype(jnp.bfloat16)
    return high, (x - high.astype(jnp.float32)).astype(jnp.bfloat16)


def product(a, b):
    return lax.dot_general(a, b, (((1,), (0,)), ((), ())), preferred_element_type=jnp.float32)


def column_transform(w, basis_ref):
    high, low = halves_of(pltpu.roll(w, OV, 1))
    cols, rest = halves_of(cols_part(basis_ref))
    cols = jnp.concatenate([cols, rest, cols], axis=0)

    def block(at):
        part = slice(at, at + SPEC)
        return product(jnp.concatenate([high[:, part], high[:, part], low[:, part]], axis=1), cols)

    return jnp.concatenate([block(0), block(128)], axis=1)


def row_transform(u, basis_ref, part):
    high, low = halves_of(u)
    rows = part(basis_ref).astype(jnp.bfloat16)
    return product(rows, jnp.concatenate([high, low, high], axis=0))


def weights(means, basis_ref):
    lane = lanes_of((1, 2 * SPEC))
    mean = jnp.where(lane < SPEC, means[0], means[1])
    return 1.0 / (DAMP + mean * basis_ref[:EXT])


def strips_of(t, basis_ref, deep):
    cols = cols_part(basis_ref)
    left = dot(cols[:deep], t[:, :SPEC], 1)
    right = dot(cols[EXT - deep : EXT], t[:, SPEC:], 1)
    both = dot(jnp.concatenate([left, right], axis=0), rows_t_part(basis_ref)[:, :EXT])
    return both[:deep], both[deep:]


def solution_of(t, basis_ref):
    v = dot(rows_part(basis_ref), t)
    cols = cols_part(basis_ref)
    first, second = dot(v[:, :SPEC], cols), dot(v[:, SPEC:], cols)
    y = jnp.concatenate(
        [first[:, :128], first[:, 128:] + second[:, :128], second[:, 128:]], axis=1
    )
    return pltpu.roll(y, FC - OV, 1)


def core_sums(x):
    return [total(x[:, :128]), total(x[:, 128:256])]


def add_columns(y, from_left, from_right):
    far = from_left.shape[0] - OV
    gap = jnp.zeros((56 - far, EXT), jnp.float32)
    turned = jnp.concatenate(
        [from_right[8:], gap, from_right[:8], from_left[far:], gap, from_left[:far]], axis=0
    )
    back = turned.T
    lane = lanes_of((EXT, 128))
    rolled = pltpu.roll(back, 64, 1)
    first = y[:, :128] + jnp.where(lane < 8, rolled, 0.0)
    second = y[:, 128:256] + jnp.where(lane >= 120, rolled, 0.0)
    third = y[:, 256:] + jnp.where((lane < 16) | (lane >= 112), back, 0.0)
    return jnp.concatenate([first, second, third], axis=1)


def pack_rows(y, deep):
    return jnp.concatenate([y[136:], y[: deep - 8]], axis=0), y[136 - deep : 136]


def edges(y, from_above, from_below):
    far = from_above.shape[0] - OV
    none = jnp.zeros((8, FC), jnp.float32)
    return jnp.concatenate(
        [
            from_above[:8] if far == 16 else none,
            y[136:] + from_above[far - 8 : far],
            y[:8] + from_above[far:],
            y[8:24],
            y[104:120],
            y[120:136] + from_below[:16],
            from_below[16:] if far == 16 else none,
        ],
        axis=0,
    )


def edge_part(frame):
    return jnp.concatenate([frame[144:], frame[:24], frame[104:144]], axis=0)


def with_edges(edge, inner):
    return jnp.concatenate([edge[16:32, :TC], inner, edge[48:64, :TC]], axis=0)


def sides(index, count, a, b):
    even = is_even(index)
    before = jnp.where(index > 0, jnp.where(even, b, a), 0.0)
    after = jnp.where(index < count - 1, jnp.where(even, a, b), 0.0)
    return before, after


def send(index, a_ref, b_ref, before, after):
    even = is_even(index)
    a_ref[...] = jnp.where(even, after, before)
    b_ref[...] = jnp.where(even, before, after)


def begin_kernel(counts, both_ref, b_ref, a_ref, table_ref):
    r, h = both_ref[:TR], both_ref[TR:]
    lane = lanes_of((128, 128))
    packed = jnp.where(
        lane < 16,
        r[:, :128],
        jnp.where(
            lane < 64,
            pltpu.roll(h[:, :128], 16, 1),
            jnp.where(lane < 112, pltpu.roll(h[:, 128:], 112, 1), r[:, 128:]),
        ),
    )
    turned = packed.T
    table = table_of(core_sums(r), counts)
    table_ref[...] = table
    send(
        lax.axis_index("col"),
        a_ref,
        b_ref,
        jnp.concatenate([turned[:32], table], axis=0),
        jnp.concatenate([turned[96:], table], axis=0),
    )


def widen_kernel(counts, both_ref, own_ref, gb_ref, ga_ref, r3_ref, h3_ref, b_ref, a_ref, table_ref):
    i, j = place()
    from_left, from_right = sides(j, counts[1], ga_ref[:32], gb_ref[:32])
    turned = jnp.concatenate([from_right, jnp.zeros((64, 128), jnp.float32), from_left], axis=0)
    back = turned.T
    lane = lanes_of((128, 128))
    edge = (lane < 16) | (lane >= 112)
    r3 = jnp.where(edge, back, 0.0)
    h3 = jnp.where(
        lane < 16, pltpu.roll(back, 112, 1), jnp.where(lane >= 112, pltpu.roll(back, 16, 1), 0.0)
    )
    r3_ref[...] = r3
    h3_ref[...] = h3
    r, h = both_ref[:TR], both_ref[TR:]
    table = merged(own_ref[...], ga_ref[32:], gb_ref[32:])
    table_ref[...] = table
    wide = jnp.concatenate([table, jnp.zeros((table.shape[0], FC - 128), jnp.float32)], axis=1)

    def strip(r_rows, h_rows):
        return jnp.concatenate(
            [
                jnp.concatenate([r[r_rows], r3[r_rows]], axis=1),
                jnp.concatenate([h[h_rows], h3[h_rows]], axis=1),
                wide,
            ],
            axis=0,
        )

    send(i, a_ref, b_ref, strip(slice(0, 8), slice(0, 16)), strip(slice(120, 128), slice(112, 128)))


def weights_kernel(both_ref, table_ref, basis_ref, weights_ref, table_out):
    h = both_ref[TR:]
    means = [x / (SUB * SUB) for x in core_sums(h * h * h)]
    weights_ref[...] = weights(means, basis_ref)
    table_out[...] = table_ref[...]


def forward_kernel(both_ref, r3_ref, basis_ref, t_ref):
    r = both_ref[:TR]
    u = column_transform(jnp.concatenate([r, r3_ref[...]], axis=1), basis_ref)
    t_ref[...] = row_transform(u, basis_ref, tile_rows)


def first_kernel(
    counts,
    gb_ref,
    ga_ref,
    tile_ref,
    weights_ref,
    basis_ref,
    table_ref,
    t_ref,
    table_out,
    b_ref,
    a_ref,
):
    i, j = place()
    above, below = sides(i, counts[0], ga_ref[:8], gb_ref[:8])
    u = column_transform(jnp.concatenate([below, above], axis=0), basis_ref)
    t = (tile_ref[...] + row_transform(u, basis_ref, halo_rows)) * weights_ref[...]
    t_ref[...] = t
    send(j, a_ref, b_ref, *strips_of(t, basis_ref, 24))
    table_out[...] = merged(table_ref[...], ga_ref[24:, :128], gb_ref[24:, :128])


def inverse_kernel(counts, t_ref, basis_ref, both_ref, h3_ref, gb_ref, ga_ref, y_ref, m_ref):
    y_ref[...] = solution_of(t_ref[...], basis_ref)
    above, below = sides(lax.axis_index("row"), counts[0], ga_ref[8:24], gb_ref[8:24])
    h = jnp.concatenate([both_ref[TR:], h3_ref[...]], axis=1)
    tall = jnp.concatenate([h, below, above], axis=0)
    m_ref[...] = tall * tall * tall


def columns_kernel(counts, y_ref, *refs):
    i, j = place()
    (ga_ref, gb_ref), refs = (refs[:2] if len(refs) == 7 else refs[1::-1]), refs[2:]
    deep = 24 if len(refs) == 5 else 16
    y = add_columns(y_ref[...], *sides(j, counts[1], ga_ref[:deep], gb_ref[:deep]))
    strips = pack_rows(y, deep)
    if len(refs) == 5:
        table_ref, out_ref, table_out, b_ref, a_ref = refs
        table = merged(table_ref[...], ga_ref[24:, :128], gb_ref[24:, :128])
        table_out[...] = table
        wide = jnp.concatenate([table, jnp.zeros((table.shape[0], FC - 128), jnp.float32)], axis=1)
        strips = [jnp.concatenate([x, wide], axis=0) for x in strips]
    else:
        out_ref, b_ref, a_ref = refs
    out_ref[...] = y
    send(i, a_ref, b_ref, *strips)


def inner_kernel(counts, width, y_ref, m_ref, basis_ref, w_ref, f_ref, gw_ref, gf_ref, near_ref):
    mask = column_mask(counts)
    s = jnp.where(mask, y_ref[8:120], 0.0)
    m = m_ref[8:120]
    w = DAMP * s + lap(m * lap(s))
    w = jnp.where(mask, w[8:104], 0.0) * SHRINK
    f = lap(m * edge_steps())
    f = jnp.where(mask, f[8:104], 0.0) * SHRINK
    w_ref[...] = w[:, :TC]
    f_ref[...] = f[:, :TC]
    gw_ref[...] = row_transform(w, basis_ref, inner_rows)
    gf_ref[...] = row_transform(f, basis_ref, inner_rows)
    near_ref[...] = near_inverse(counts, coarse_part(basis_ref, width))


def second_kernel(
    counts,
    width,
    y_ref,
    m_ref,
    gb_ref,
    ga_ref,
    table_ref,
    inner_w_ref,
    f_ref,
    gw_ref,
    gf_ref,
    near_ref,
    weights_ref,
    basis_ref,
    z_ref,
    w_ref,
    t_ref,
    b_ref,
    a_ref,
):
    i, j = place()
    y = y_ref[...]
    mask = edge_mask(counts)
    s = edges(y, *sides(i, counts[0], ga_ref[:24], gb_ref[:24]))
    s = jnp.where(mask, s, 0.0)
    table = merged(table_ref[...], ga_ref[24:, :128], gb_ref[24:, :128])
    picked = jnp.sum(near_ref[...] * as_row(table, width), axis=1, keepdims=True)
    bands = as_bands([picked[k : k + 1] for k in range(12)])
    coarse = edge_bands(bands)
    m = edge_part(m_ref)
    flow = m * (lap(s) + lap(coarse))
    z = s + coarse
    w = jnp.where(mask, DAMP * z + lap(flow), 0.0) * SHRINK
    step = jumps(bands[1])
    damped = (DAMP * SHRINK) * bands[1]
    z_ref[...] = with_edges(z, y[16:112, :TC] + bands[1][:, :TC])
    w_ref[...] = with_edges(w, inner_w_ref[...] + step[:, :TC] * f_ref[...] + damped[:, :TC])
    lane = lanes_of((EXT, 256))
    ones = jnp.where((lane >= 16) & (lane < 112), rows_t_part(basis_ref), 0.0)
    ones = jnp.sum(ones, axis=1, keepdims=True)
    u = gw_ref[...] + step * gf_ref[...] + ones * damped
    u = u + row_transform(jnp.concatenate([w[8:32], w[48:72]], axis=0), basis_ref, edge_rows)
    t = column_transform(u, basis_ref) * weights_ref[...]
    t_ref[...] = t
    send(j, a_ref, b_ref, *strips_of(t, basis_ref, 16))


def inverse_stats_kernel(t_ref, basis_ref, both_ref, m_ref, z_ref, w_ref, y_ref, stats_ref):
    y_ref[...] = solution_of(t_ref[...], basis_ref)
    rt, mt, zt, wt = both_ref[:TR], m_ref[:TR, :TC], z_ref[...], w_ref[...]
    lane, row = lanes_of((1, 256)), rows_of((128, 1))
    along = (lane % 128 != 0) & (lane % 128 != 127)
    top, low = mt[:1], mt[127:]
    side = jnp.sum(jnp.where((row > 0) & (row < 127), mt, 0.0), axis=0, keepdims=True)

    def halves(x):
        return [
            jnp.sum(x[:, :128], axis=1, keepdims=True),
            jnp.sum(x[:, 128:], axis=1, keepdims=True),
        ]

    first, last = lane % 128 == 0, lane % 128 == 127
    zero = jnp.zeros((1, 1), jnp.float32)
    stats_ref[...] = row_of(
        [
            core_sums(rt * zt),
            core_sums(zt * wt),
            core_sums(wt),
            halves(jnp.where(along, top, 0.0)),
            halves(jnp.where(along, low, 0.0)),
            halves(jnp.where(first, side, 0.0)),
            halves(jnp.where(last, side, 0.0)),
            halves(jnp.where(first, top, 0.0)),
            halves(jnp.where(last, top, 0.0)),
            halves(jnp.where(first, low, 0.0)),
            halves(jnp.where(last, low, 0.0)),
            *[[zero, zero]] * 4,
            core_sums(rt),
        ]
    )


def inner_dots_kernel(counts, y_ref, m_ref, both_ref, w_ref, stats_ref, v_ref, stats_out):
    q = jnp.where(column_mask(counts), y_ref[8:120], 0.0)
    v = (DAMP * q + lap(m_ref[8:120] * lap(q)))[8:104, :TC]
    q = q[8:104, :TC]
    v_ref[...] = v
    rest = [
        core_sums(v),
        core_sums(both_ref[16:112] * q),
        core_sums(w_ref[16:112] * q),
        core_sums(v * q),
    ]
    zero = jnp.zeros((1, 1), jnp.float32)
    stats_out[...] = stats_ref[...] + row_of([[zero, zero]] * 11 + rest)


def dots_kernel(
    counts, y_ref, m_ref, gb_ref, ga_ref, both_ref, w_ref, stats_ref, inner_v_ref, q_ref, v_ref, stats_out
):
    i, j = place()
    y = y_ref[...]
    q = edges(y, *sides(i, counts[0], ga_ref[...], gb_ref[...]))
    q = jnp.where(edge_mask(counts), q, 0.0)
    v = DAMP * q + lap(edge_part(m_ref) * lap(q))
    q_ref[...] = with_edges(q, y[16:112, :TC])
    v_ref[...] = with_edges(v, inner_v_ref[...])
    qe, ve = (jnp.concatenate([x[16:32, :TC], x[48:64, :TC]], axis=0) for x in (q, v))
    re = jnp.concatenate([both_ref[:16], both_ref[112:128]], axis=0)
    we = jnp.concatenate([w_ref[:16], w_ref[112:]], axis=0)
    rest = [core_sums(ve), core_sums(re * qe), core_sums(we * qe), core_sums(ve * qe)]
    zero = jnp.zeros((1, 1), jnp.float32)
    row = stats_ref[...] + row_of([[zero, zero]] * 11 + rest)
    stats_out[...] = jnp.broadcast_to(row, stats_out.shape)


def end_kernel(
    counts,
    width,
    stats_ref,
    basis_ref,
    m_ref,
    f_ref,
    both_ref,
    z_ref,
    w_ref,
    q_ref,
    v_ref,
    solution_ref,
    residual_ref,
):
    i, j = place()
    tiles_c = counts[1]
    devices = counts[0] * tiles_c
    rows = stats_ref[...]
    st = jnp.concatenate([rows, pltpu.roll(rows, 64, 1)], axis=0)
    inverse = coarse_part(basis_ref, width)[: 2 * devices, : 2 * devices]
    g = jnp.broadcast_to(dot(inverse, st)[:, 2:3], st.shape)
    lane, row = lanes_of(st.shape), rows_of(st.shape)
    device = row % devices
    column = device % tiles_c
    on_left = row < devices

    def from_row(distance):
        return pltpu.roll(g, distance % (2 * devices), 0)

    up = jnp.where(device >= tiles_c, from_row(tiles_c), 0.0)
    down = jnp.where(device < devices - tiles_c, from_row(-tiles_c), 0.0)
    left = jnp.where(on_left, jnp.where(column > 0, from_row(1 - devices), 0.0), from_row(devices))
    right = jnp.where(
        on_left, from_row(-devices), jnp.where(column < tiles_c - 1, from_row(devices - 1), 0.0)
    )
    du, dd, dl, dr = g - up, g - down, g - left, g - right
    across = jnp.where(
        (lane == 3) | (lane == 7) | (lane == 8),
        du,
        jnp.where((lane == 4) | (lane == 9) | (lane == 10), dd, 0.0),
    )
    across = across + jnp.where(
        (lane == 5) | (lane == 7) | (lane == 9),
        dl,
        jnp.where((lane == 6) | (lane == 8) | (lane == 10), dr, 0.0),
    )
    factor = jnp.where((lane == 2) | (lane == 15), g, across * across)
    factor = jnp.where(lane == 11, 2.0 * g, factor)
    factor = jnp.where((lane < 2) | ((lane >= 12) & (lane < 15)), 1.0, factor)
    terms = jnp.where(lane == 16, (DAMP * SUB * SUB) * g * g, st * factor)
    sums = jnp.sum(terms, axis=0, keepdims=True)

    def whole(wanted):
        return jnp.sum(jnp.where(wanted, sums, 0.0), axis=1, keepdims=True)

    at = lanes_of((1, 128))
    rz, zw = whole(at == 0), whole(at == 1)
    ry = whole((at == 12) | (at == 15))
    yw = whole((at == 13) | (at == 2))
    yv = whole(((at >= 3) & (at < 12)) | (at == 14) | (at == 16))
    a = rz / zw
    rz1 = rz - a * ry - a * zw + a * a * yw
    beta1 = 1.0 + rz1 / rz
    dad = (beta1 * beta1 * zw - 2.0 * a * beta1 * yw) * (1.0 / SHRINK) + a * a * yv
    a1 = rz1 / dad
    r = i - 1 + lane // 4
    c = 2 * j - 1 + lane % 4
    inside = (r >= 0) & (r < counts[0]) & (c >= 0) & (c < 2 * tiles_c) & (lane < 12)
    where = lax.rem(c + 2, 2) * devices + r * tiles_c + (c + 2) // 2 - 1
    picked = jnp.sum(jnp.where(inside & (row == where), g, 0.0), axis=0, keepdims=True)
    bands = as_bands([picked[:, k : k + 1] for k in range(12)])
    on = bands[1][:, :TC]
    coarse = edge_bands(bands)
    image = DAMP * coarse + lap(edge_part(m_ref) * lap(coarse))
    image = with_edges(image, (jumps(bands[1]) * (1.0 / SHRINK))[:, :TC] * f_ref[...] + DAMP * on)
    y = q_ref[...] + on
    v = v_ref[...] + image
    z, w = z_ref[...], w_ref[...]
    solution_ref[...] = (a * SHRINK) * z + a1 * (beta1 * z - a * y)
    residual_ref[...] = both_ref[:TR] - a * w - a1 * ((beta1 * (1.0 / SHRINK)) * w - a * v)


def call(kernel, outs, *args, flops=10**9):
    shapes = [jax.ShapeDtypeStruct(s, jnp.float32) for s in outs]
    return pl.pallas_call(
        kernel,
        out_shape=shapes,
        compiler_params=pltpu.CompilerParams(vmem_limit_bytes=48 * 1024 * 1024),
        cost_estimate=pl.CostEstimate(flops=flops, bytes_accessed=10**6, transcendentals=0),
    )(*args)


def pairs_from(count, offset):
    found = []
    for k in range(offset, count, 2):
        found += [(k, (k + 1) % count), ((k + 1) % count, k)]
    return found


def odd_pairs(counts, axis, bit):
    found = []
    for i in range(counts[0]):
        for j in range(counts[1]):
            at = [i, j]
            if bit and at[axis] in (0, counts[axis] - 1):
                at[1 - axis] ^= bit
            else:
                at[axis] = (at[axis] + (1 if at[axis] % 2 else -1)) % counts[axis]
            found.append((i * counts[1] + j, at[0] * counts[1] + at[1]))
    return found


def xor_pairs(counts, rows, cols):
    flat = [(i, j) for i in range(counts[0]) for j in range(counts[1])]
    return [(i * counts[1] + j, (i ^ rows) * counts[1] + (j ^ cols)) for i, j in flat]


def spreads(counts):
    known = np.eye(counts[0] * counts[1], dtype=bool)

    def meet(*swaps):
        return np.logical_or.reduce([known, *(known[[b for _, b in pairs]] for pairs in swaps)])

    even = [xor_pairs(counts, 0, 1), xor_pairs(counts, 1, 0)]
    known = meet(even[0], odd_pairs(counts, 1, 0))
    known = meet(even[1], odd_pairs(counts, 0, 0), xor_pairs(counts, 4, 0))
    known = meet(even[0], odd_pairs(counts, 1, 1))
    return meet(even[1], odd_pairs(counts, 0, 0)).all()


def body(counts, height, noise):
    nr, nc = counts
    devices = nr * nc
    width = max(128, devices * 2)
    basis = jnp.asarray(constants(nr, 2 * nc, width))
    both_axes = ("row", "col")
    depth = table_shape(counts)[0]

    def swap(a, b, axis, bit=0):
        gb = lax.ppermute(b, both_axes, odd_pairs(counts, both_axes.index(axis), bit))
        return lax.ppermute(a, axis, pairs_from(lax.axis_size(axis), 0)), gb

    def small_swap(x, rows, cols):
        return lax.ppermute(x, both_axes, xor_pairs(counts, rows, cols))

    both = jnp.pad(noise, ((0, TR), (0, 0))) + jnp.pad(height, ((TR, 0), (0, 0)))
    b, a, table = call(
        functools.partial(begin_kernel, counts), [(32 + depth, 128)] * 2 + [(depth, 128)], both
    )
    if not spreads(counts):
        for axis, count in enumerate(counts):
            bit = 1
            while bit < count:
                table = table + small_swap(table, *((0, bit) if axis else (bit, 0)))
                bit *= 2
    ga, gb = swap(a, b, "col")
    r3, h3, b, a, table = call(
        functools.partial(widen_kernel, counts),
        [(128, 128)] * 2 + [(24 + depth, FC)] * 2 + [(depth, 128)],
        both,
        table,
        gb,
        ga,
    )
    ga, gb = swap(a, b, "row")
    weight, table = call(weights_kernel, [(EXT, 2 * SPEC), (depth, 128)], both, table, basis)
    far = small_swap(table, 4, 0)
    t = call(forward_kernel, [(EXT, 2 * SPEC)], both, r3, basis)[0]
    t, table, b, a = call(
        functools.partial(first_kernel, counts),
        [(EXT, 2 * SPEC), (depth, 128)] + [(24, EXT)] * 2,
        gb,
        ga,
        t,
        weight,
        basis,
        table,
    )
    table = merged(table, far)
    wide = jnp.pad(table, ((0, 0), (0, EXT - 128)))
    y, m = call(
        functools.partial(inverse_kernel, counts),
        [(EXT, FC), (FR, FC)],
        t,
        basis,
        both,
        h3,
        gb,
        ga,
    )
    ga, gb = swap(*(jnp.concatenate([x, wide], axis=0) for x in (a, b)), "col", 1)
    y, table, b, a = call(
        functools.partial(columns_kernel, counts),
        [(EXT, FC), (depth, 128)] + [(24 + depth, FC)] * 2,
        y,
        ga,
        gb,
        table,
    )
    ga, gb = swap(a, b, "row")
    inner_w, f, gw, gf, near = call(
        functools.partial(inner_kernel, counts, width),
        [(96, TC)] * 2 + [(EXT, FC)] * 2 + [(16, width)],
        y,
        m,
        basis,
    )
    z, w, t, b, a = call(
        functools.partial(second_kernel, counts, width),
        [(TR, TC)] * 2 + [(EXT, 2 * SPEC)] + [(16, EXT)] * 2,
        y,
        m,
        gb,
        ga,
        table,
        inner_w,
        f,
        gw,
        gf,
        near,
        weight,
        basis,
    )
    ga, gb = swap(a, b, "col", 1)
    y, stats = call(inverse_stats_kernel, [(EXT, FC), (1, 128)], t, basis, both, m, z, w)
    y, b, a = call(
        functools.partial(columns_kernel, counts), [(EXT, FC)] + [(16, FC)] * 2, y, gb, ga
    )
    ga, gb = swap(a, b, "row", 1)
    inner_v, stats = call(
        functools.partial(inner_dots_kernel, counts),
        [(96, TC), (1, 128)],
        y,
        m,
        both,
        w,
        stats,
    )
    q, v, stats = call(
        functools.partial(dots_kernel, counts),
        [(TR, TC)] * 2 + [(devices, 128)],
        y,
        m,
        gb,
        ga,
        both,
        w,
        stats,
        inner_v,
    )
    stats = lax.all_to_all(stats, both_axes, 0, 0, tiled=True)
    return tuple(
        call(
            functools.partial(end_kernel, counts, width),
            [(TR, TC)] * 2,
            stats,
            basis,
            m,
            f,
            both,
            z,
            w,
            q,
            v,
        )
    )


def solution(mesh):
    counts = (mesh.shape["row"], mesh.shape["col"])
    spec = P("row", "col")
    return jax.shard_map(
        functools.partial(body, counts),
        mesh=mesh,
        in_specs=(spec, spec),
        out_specs=(spec, spec),
        check_vma=False,
    )
```

```python
import functools

import jax
import jax.numpy as jnp
import ml_dtypes
import numpy as np
from jax import lax
from jax.experimental import pallas as pl
from jax.experimental.pallas import tpu as pltpu
from jax.sharding import PartitionSpec as P

SUB = 128
OV = 8
EXT = SUB + 2 * OV
DAMP = 2.0**-28
SHRINK = 2.0**-20

TR, TC = 128, 256
FR, FC = 160, 384
SPEC = 256

highest = lax.Precision.HIGHEST


def sine(count):
    k = np.arange(1, count + 1, dtype=np.float64)
    basis = np.sqrt(2.0 / (count + 1.0)) * np.sin(np.pi * k[:, None] * k[None, :] / (count + 1.0))
    return basis, 2.0 - 2.0 * np.cos(np.pi * k / (count + 1.0))


def block_constants():
    basis, eig = sine(EXT)
    rows = np.roll(basis, -OV, 0)
    cols = np.pad(basis, ((0, SPEC - EXT), (0, SPEC - EXT)))
    scale = np.pad((eig[:, None] + eig[None, :]) ** 2, ((0, 0), (0, SPEC - EXT)))
    wide = lambda x: np.pad(x, ((0, 0), (0, 2 * SPEC - x.shape[1])))
    high = rows.T.astype(ml_dtypes.bfloat16).astype(np.float64)
    low = (rows.T - high).astype(ml_dtypes.bfloat16).astype(np.float64)
    tile = np.concatenate([x[:, :SUB] for x in (high, high, low)], 1)
    halo = np.concatenate([x[:, SUB:] for x in (high, high, low)], 1)
    inner = np.concatenate([x[:, 16:112] for x in (high, high, low)], 1)
    at = [*range(136, 144), *range(16), *range(112, 136)]
    edge = np.concatenate([x[:, at] for x in (high, high, low)], 1)
    turned = np.hstack([rows.T, np.zeros((EXT, 256 - EXT)), edge])
    return [np.tile(scale, (1, 2)), *(wide(x) for x in (rows, turned, cols, inner, np.hstack([tile, halo])))]


def rows_part(ref):
    return ref[EXT : 2 * EXT, :EXT]


def rows_t_part(ref):
    return ref[2 * EXT : 3 * EXT, :256]


def cols_part(ref):
    return ref[3 * EXT : 3 * EXT + SPEC, :SPEC]


def inner_rows(ref):
    at = 3 * EXT + SPEC
    return ref[at : at + EXT, : 3 * 96]


def edge_rows(ref):
    return ref[2 * EXT : 3 * EXT, 256 : 256 + 3 * 48]


def tile_rows(ref):
    at = 4 * EXT + SPEC
    return ref[at : at + EXT, : 3 * SUB]


def halo_rows(ref):
    at = 4 * EXT + SPEC
    return ref[at : at + EXT, 3 * SUB : 3 * EXT]


def coarse_part(ref, width):
    at, lanes = 5 * EXT + SPEC, 2 * SPEC
    parts = [ref[at + k * width : at + (k + 1) * width] for k in range(-(-width // lanes))]
    return (parts[0] if len(parts) == 1 else jnp.concatenate(parts, axis=1))[:, :width]


def constants(nr, nc, width):
    lanes = 2 * SPEC
    inverse = coarse_inverse(nr, nc, -(-width // lanes) * lanes)[:width]
    parts = [*block_constants(), *np.split(inverse, inverse.shape[1] // lanes, 1)]
    return np.concatenate(parts).astype(np.float32)


def coarse_inverse(nr, nc, width):
    br, er = sine(nr)
    bc, ec = sine(nc)
    both = np.kron(br, bc).reshape(nr, nc // 2, 2, nr * nc).transpose(2, 0, 1, 3)
    both = both.reshape(nr * nc, nr * nc)
    scale = (er[:, None] + ec[None, :]) / (SUB * SUB)
    values = (SUB * SUB * (DAMP + scale * scale)).reshape(-1)
    whole = np.zeros((width, width), np.float32)
    whole[: nr * nc, : nr * nc] = (both / values) @ both.T
    return whole


def dot(a, b, side=0):
    return lax.dot_general(
        a, b, (((1,), (side,)), ((), ())), precision=highest, preferred_element_type=jnp.float32
    )


def lap(x):
    rows, lanes = x.shape
    beside = pltpu.roll(x, 1, 0) + pltpu.roll(x, rows - 1, 0)
    beside = beside + (pltpu.roll(x, 1, 1) + pltpu.roll(x, lanes - 1, 1))
    return 4.0 * x - beside


def lanes_of(shape):
    return lax.broadcasted_iota(jnp.int32, shape, 1)


def rows_of(shape):
    return lax.broadcasted_iota(jnp.int32, shape, 0)


def total(x):
    return jnp.sum(jnp.sum(x, axis=0, keepdims=True), axis=1, keepdims=True)


def place():
    return lax.axis_index("row"), lax.axis_index("col")


def is_even(index):
    return lax.rem(index, 2) == 0


def column_mask(counts):
    j = lax.axis_index("col")
    lane = lanes_of((1, FC))
    right = jnp.where(j < counts[1] - 1, 320, 256)
    left = jnp.where(j > 0, 320, 384)
    return (lane < right) | (lane >= left)


def edge_mask(counts):
    i = lax.axis_index("row")
    row = rows_of((80, 1))
    first = jnp.where(i > 0, 0, 16)
    last = jnp.where(i < counts[0] - 1, 80, 64)
    return (row >= first) & (row < last) & column_mask(counts)


def table_shape(counts):
    return (-(-2 * counts[0] * counts[1] // 1024) * 8, 128)


def table_of(values, counts):
    i, j = place()
    devices = counts[0] * counts[1]
    shape = table_shape(counts)
    at = rows_of(shape) * 128 + lanes_of(shape) - (i * counts[1] + j)
    return jnp.where(at == 0, values[0], jnp.where(at == devices, values[1], 0.0))


def merged(table, *others):
    for other in others:
        table = jnp.where(table != 0.0, table, other)
    return table


def as_row(table, width):
    return jnp.concatenate([table[k : k + 1] for k in range(width // 128)], axis=1)


def row_of(pairs):
    lane = lanes_of((1, 128))
    row = jnp.zeros((1, 128), jnp.float32)
    for k, (left, right) in enumerate(pairs):
        row = jnp.where(lane == k, left, jnp.where(lane == 64 + k, right, row))
    return row


def near_inverse(counts, inverse):
    i, j = place()
    nr, nc = counts[0], 2 * counts[1]
    shape = (16, inverse.shape[0])
    which = rows_of(shape)
    r = i - 1 + which // 4
    c = 2 * j - 1 + which % 4
    inside = (r >= 0) & (r < nr) & (c >= 0) & (c < nc) & (which < 12)
    at = lax.rem(c + 2, 2) * (nr * counts[1]) + r * counts[1] + (c + 2) // 2 - 1
    return dot(jnp.where(inside & (lanes_of(shape) == at), 1.0, 0.0), inverse)


def as_bands(values):
    lane = lanes_of((1, FC))
    bands = []
    for d in range(3):
        left, first, second, right = values[4 * d : 4 * d + 4]
        bands.append(
            jnp.where(
                lane < 128,
                first,
                jnp.where(lane < 256, second, jnp.where(lane < 320, right, left)),
            )
        )
    return bands


def edge_bands(bands):
    above, on, below = bands
    return jnp.concatenate(
        [
            jnp.broadcast_to(above, (16, FC)),
            jnp.broadcast_to(on, (48, FC)),
            jnp.broadcast_to(below, (16, FC)),
        ],
        axis=0,
    )


def jumps(row):
    step = row - pltpu.roll(row, 1, 1)
    lane = lanes_of((1, FC))
    at = [jnp.sum(jnp.where(lane == k, step, 0.0), axis=1, keepdims=True) for k in (0, 128, 256)]
    return jnp.where(
        (lane < 64) | (lane >= 320), at[0], jnp.where(lane < 192, at[1], at[2])
    )


def edge_steps():
    lane = lanes_of((1, FC))
    up = (lane == 0) | (lane == 128) | (lane == 256)
    down = (lane == FC - 1) | (lane == 127) | (lane == 255)
    return jnp.where(up, 1.0, jnp.where(down, -1.0, 0.0))


def halves_of(x):
    high = x.astype(jnp.bfloat16)
    return high, (x - high.astype(jnp.float32)).astype(jnp.bfloat16)


def product(a, b):
    return lax.dot_general(a, b, (((1,), (0,)), ((), ())), preferred_element_type=jnp.float32)


def column_transform(w, basis_ref):
    high, low = halves_of(pltpu.roll(w, OV, 1))
    cols, rest = halves_of(cols_part(basis_ref))
    cols = jnp.concatenate([cols, rest, cols], axis=0)

    def block(at):
        part = slice(at, at + SPEC)
        return product(jnp.concatenate([high[:, part], high[:, part], low[:, part]], axis=1), cols)

    return jnp.concatenate([block(0), block(128)], axis=1)


def row_transform(u, basis_ref, part):
    high, low = halves_of(u)
    rows = part(basis_ref).astype(jnp.bfloat16)
    return product(rows, jnp.concatenate([high, low, high], axis=0))


def weights(means, basis_ref):
    lane = lanes_of((1, 2 * SPEC))
    mean = jnp.where(lane < SPEC, means[0], means[1])
    return 1.0 / (DAMP + mean * basis_ref[:EXT])


def strips_of(t, basis_ref, deep):
    cols = cols_part(basis_ref)
    left = dot(cols[:deep], t[:, :SPEC], 1)
    right = dot(cols[EXT - deep : EXT], t[:, SPEC:], 1)
    both = dot(jnp.concatenate([left, right], axis=0), rows_t_part(basis_ref)[:, :EXT])
    return both[:deep], both[deep:]


def solution_of(t, basis_ref):
    v = dot(rows_part(basis_ref), t)
    cols = cols_part(basis_ref)
    first, second = dot(v[:, :SPEC], cols), dot(v[:, SPEC:], cols)
    y = jnp.concatenate(
        [first[:, :128], first[:, 128:] + second[:, :128], second[:, 128:]], axis=1
    )
    return pltpu.roll(y, FC - OV, 1)


def core_sums(x):
    return [total(x[:, :128]), total(x[:, 128:256])]


def add_columns(y, from_left, from_right):
    far = from_left.shape[0] - OV
    gap = jnp.zeros((56 - far, EXT), jnp.float32)
    turned = jnp.concatenate(
        [from_right[8:], gap, from_right[:8], from_left[far:], gap, from_left[:far]], axis=0
    )
    back = turned.T
    lane = lanes_of((EXT, 128))
    rolled = pltpu.roll(back, 64, 1)
    first = y[:, :128] + jnp.where(lane < 8, rolled, 0.0)
    second = y[:, 128:256] + jnp.where(lane >= 120, rolled, 0.0)
    third = y[:, 256:] + jnp.where((lane < 16) | (lane >= 112), back, 0.0)
    return jnp.concatenate([first, second, third], axis=1)


def pack_rows(y, deep):
    return jnp.concatenate([y[136:], y[: deep - 8]], axis=0), y[136 - deep : 136]


def edges(y, from_above, from_below):
    far = from_above.shape[0] - OV
    none = jnp.zeros((8, FC), jnp.float32)
    return jnp.concatenate(
        [
            from_above[:8] if far == 16 else none,
            y[136:] + from_above[far - 8 : far],
            y[:8] + from_above[far:],
            y[8:24],
            y[104:120],
            y[120:136] + from_below[:16],
            from_below[16:] if far == 16 else none,
        ],
        axis=0,
    )


def edge_part(frame):
    return jnp.concatenate([frame[144:], frame[:24], frame[104:144]], axis=0)


def with_edges(edge, inner):
    return jnp.concatenate([edge[16:32, :TC], inner, edge[48:64, :TC]], axis=0)


def sides(index, count, a, b):
    even = is_even(index)
    before = jnp.where(index > 0, jnp.where(even, b, a), 0.0)
    after = jnp.where(index < count - 1, jnp.where(even, a, b), 0.0)
    return before, after


def send(index, a_ref, b_ref, before, after):
    even = is_even(index)
    a_ref[...] = jnp.where(even, after, before)
    b_ref[...] = jnp.where(even, before, after)


def begin_kernel(counts, both_ref, b_ref, a_ref, table_ref):
    r, h = both_ref[:TR], both_ref[TR:]
    lane = lanes_of((128, 128))
    packed = jnp.where(
        lane < 16,
        r[:, :128],
        jnp.where(
            lane < 64,
            pltpu.roll(h[:, :128], 16, 1),
            jnp.where(lane < 112, pltpu.roll(h[:, 128:], 112, 1), r[:, 128:]),
        ),
    )
    turned = packed.T
    table = table_of(core_sums(r), counts)
    table_ref[...] = table
    send(
        lax.axis_index("col"),
        a_ref,
        b_ref,
        jnp.concatenate([turned[:32], table], axis=0),
        jnp.concatenate([turned[96:], table], axis=0),
    )


def widen_kernel(counts, both_ref, own_ref, gb_ref, ga_ref, r3_ref, h3_ref, b_ref, a_ref, table_ref):
    i, j = place()
    from_left, from_right = sides(j, counts[1], ga_ref[:32], gb_ref[:32])
    turned = jnp.concatenate([from_right, jnp.zeros((64, 128), jnp.float32), from_left], axis=0)
    back = turned.T
    lane = lanes_of((128, 128))
    edge = (lane < 16) | (lane >= 112)
    r3 = jnp.where(edge, back, 0.0)
    h3 = jnp.where(
        lane < 16, pltpu.roll(back, 112, 1), jnp.where(lane >= 112, pltpu.roll(back, 16, 1), 0.0)
    )
    r3_ref[...] = r3
    h3_ref[...] = h3
    r, h = both_ref[:TR], both_ref[TR:]
    table = merged(own_ref[...], ga_ref[32:], gb_ref[32:])
    table_ref[...] = table
    wide = jnp.concatenate([table, jnp.zeros((table.shape[0], FC - 128), jnp.float32)], axis=1)

    def strip(r_rows, h_rows):
        return jnp.concatenate(
            [
                jnp.concatenate([r[r_rows], r3[r_rows]], axis=1),
                jnp.concatenate([h[h_rows], h3[h_rows]], axis=1),
                wide,
            ],
            axis=0,
        )

    send(i, a_ref, b_ref, strip(slice(0, 8), slice(0, 16)), strip(slice(120, 128), slice(112, 128)))


def weights_kernel(both_ref, table_ref, basis_ref, weights_ref, table_out):
    h = both_ref[TR:]
    means = [x / (SUB * SUB) for x in core_sums(h * h * h)]
    weights_ref[...] = weights(means, basis_ref)
    table_out[...] = table_ref[...]


def forward_kernel(both_ref, r3_ref, basis_ref, t_ref):
    r = both_ref[:TR]
    u = column_transform(jnp.concatenate([r, r3_ref[...]], axis=1), basis_ref)
    t_ref[...] = row_transform(u, basis_ref, tile_rows)


def first_kernel(
    counts,
    gb_ref,
    ga_ref,
    tile_ref,
    weights_ref,
    basis_ref,
    table_ref,
    t_ref,
    table_out,
    b_ref,
    a_ref,
):
    i, j = place()
    above, below = sides(i, counts[0], ga_ref[:8], gb_ref[:8])
    u = column_transform(jnp.concatenate([below, above], axis=0), basis_ref)
    t = (tile_ref[...] + row_transform(u, basis_ref, halo_rows)) * weights_ref[...]
    t_ref[...] = t
    send(j, a_ref, b_ref, *strips_of(t, basis_ref, 24))
    table_out[...] = merged(table_ref[...], ga_ref[24:, :128], gb_ref[24:, :128])


def inverse_kernel(counts, t_ref, basis_ref, both_ref, h3_ref, gb_ref, ga_ref, y_ref, m_ref):
    y_ref[...] = solution_of(t_ref[...], basis_ref)
    above, below = sides(lax.axis_index("row"), counts[0], ga_ref[8:24], gb_ref[8:24])
    h = jnp.concatenate([both_ref[TR:], h3_ref[...]], axis=1)
    tall = jnp.concatenate([h, below, above], axis=0)
    m_ref[...] = tall * tall * tall


def columns_kernel(counts, y_ref, *refs):
    i, j = place()
    (ga_ref, gb_ref), refs = (refs[:2] if len(refs) == 7 else refs[1::-1]), refs[2:]
    deep = 24 if len(refs) == 5 else 16
    y = add_columns(y_ref[...], *sides(j, counts[1], ga_ref[:deep], gb_ref[:deep]))
    strips = pack_rows(y, deep)
    if len(refs) == 5:
        table_ref, out_ref, table_out, b_ref, a_ref = refs
        table = merged(table_ref[...], ga_ref[24:, :128], gb_ref[24:, :128])
        table_out[...] = table
        wide = jnp.concatenate([table, jnp.zeros((table.shape[0], FC - 128), jnp.float32)], axis=1)
        strips = [jnp.concatenate([x, wide], axis=0) for x in strips]
    else:
        out_ref, b_ref, a_ref = refs
    out_ref[...] = y
    send(i, a_ref, b_ref, *strips)


def inner_kernel(counts, width, y_ref, m_ref, basis_ref, w_ref, f_ref, gw_ref, gf_ref, near_ref):
    mask = column_mask(counts)
    s = jnp.where(mask, y_ref[8:120], 0.0)
    m = m_ref[8:120]
    w = DAMP * s + lap(m * lap(s))
    w = jnp.where(mask, w[8:104], 0.0) * SHRINK
    f = lap(m * edge_steps())
    f = jnp.where(mask, f[8:104], 0.0) * SHRINK
    w_ref[...] = w[:, :TC]
    f_ref[...] = f[:, :TC]
    gw_ref[...] = row_transform(w, basis_ref, inner_rows)
    gf_ref[...] = row_transform(f, basis_ref, inner_rows)
    near_ref[...] = near_inverse(counts, coarse_part(basis_ref, width))


def second_kernel(
    counts,
    width,
    y_ref,
    m_ref,
    gb_ref,
    ga_ref,
    table_ref,
    inner_w_ref,
    f_ref,
    gw_ref,
    gf_ref,
    near_ref,
    weights_ref,
    basis_ref,
    z_ref,
    w_ref,
    t_ref,
    b_ref,
    a_ref,
):
    i, j = place()
    y = y_ref[...]
    mask = edge_mask(counts)
    s = edges(y, *sides(i, counts[0], ga_ref[:24], gb_ref[:24]))
    s = jnp.where(mask, s, 0.0)
    table = merged(table_ref[...], ga_ref[24:, :128], gb_ref[24:, :128])
    picked = jnp.sum(near_ref[...] * as_row(table, width), axis=1, keepdims=True)
    bands = as_bands([picked[k : k + 1] for k in range(12)])
    coarse = edge_bands(bands)
    m = edge_part(m_ref)
    flow = m * (lap(s) + lap(coarse))
    z = s + coarse
    w = jnp.where(mask, DAMP * z + lap(flow), 0.0) * SHRINK
    step = jumps(bands[1])
    damped = (DAMP * SHRINK) * bands[1]
    z_ref[...] = with_edges(z, y[16:112, :TC] + bands[1][:, :TC])
    w_ref[...] = with_edges(w, inner_w_ref[...] + step[:, :TC] * f_ref[...] + damped[:, :TC])
    lane = lanes_of((EXT, 256))
    ones = jnp.where((lane >= 16) & (lane < 112), rows_t_part(basis_ref), 0.0)
    ones = jnp.sum(ones, axis=1, keepdims=True)
    u = gw_ref[...] + step * gf_ref[...] + ones * damped
    u = u + row_transform(jnp.concatenate([w[8:32], w[48:72]], axis=0), basis_ref, edge_rows)
    t = column_transform(u, basis_ref) * weights_ref[...]
    t_ref[...] = t
    send(j, a_ref, b_ref, *strips_of(t, basis_ref, 16))


def inverse_stats_kernel(t_ref, basis_ref, both_ref, m_ref, z_ref, w_ref, y_ref, stats_ref):
    y_ref[...] = solution_of(t_ref[...], basis_ref)
    rt, mt, zt, wt = both_ref[:TR], m_ref[:TR, :TC], z_ref[...], w_ref[...]
    lane, row = lanes_of((1, 256)), rows_of((128, 1))
    along = (lane % 128 != 0) & (lane % 128 != 127)
    top, low = mt[:1], mt[127:]
    side = jnp.sum(jnp.where((row > 0) & (row < 127), mt, 0.0), axis=0, keepdims=True)

    def halves(x):
        return [
            jnp.sum(x[:, :128], axis=1, keepdims=True),
            jnp.sum(x[:, 128:], axis=1, keepdims=True),
        ]

    first, last = lane % 128 == 0, lane % 128 == 127
    zero = jnp.zeros((1, 1), jnp.float32)
    stats_ref[...] = row_of(
        [
            core_sums(rt * zt),
            core_sums(zt * wt),
            core_sums(wt),
            halves(jnp.where(along, top, 0.0)),
            halves(jnp.where(along, low, 0.0)),
            halves(jnp.where(first, side, 0.0)),
            halves(jnp.where(last, side, 0.0)),
            halves(jnp.where(first, top, 0.0)),
            halves(jnp.where(last, top, 0.0)),
            halves(jnp.where(first, low, 0.0)),
            halves(jnp.where(last, low, 0.0)),
            *[[zero, zero]] * 4,
            core_sums(rt),
        ]
    )


def inner_dots_kernel(counts, y_ref, m_ref, both_ref, w_ref, stats_ref, v_ref, stats_out):
    q = jnp.where(column_mask(counts), y_ref[8:120], 0.0)
    v = (DAMP * q + lap(m_ref[8:120] * lap(q)))[8:104, :TC]
    q = q[8:104, :TC]
    v_ref[...] = v
    rest = [
        core_sums(v),
        core_sums(both_ref[16:112] * q),
        core_sums(w_ref[16:112] * q),
        core_sums(v * q),
    ]
    zero = jnp.zeros((1, 1), jnp.float32)
    stats_out[...] = stats_ref[...] + row_of([[zero, zero]] * 11 + rest)


def dots_kernel(
    counts, y_ref, m_ref, gb_ref, ga_ref, both_ref, w_ref, stats_ref, inner_v_ref, q_ref, v_ref, stats_out
):
    i, j = place()
    y = y_ref[...]
    q = edges(y, *sides(i, counts[0], ga_ref[...], gb_ref[...]))
    q = jnp.where(edge_mask(counts), q, 0.0)
    v = DAMP * q + lap(edge_part(m_ref) * lap(q))
    q_ref[...] = with_edges(q, y[16:112, :TC])
    v_ref[...] = with_edges(v, inner_v_ref[...])
    qe, ve = (jnp.concatenate([x[16:32, :TC], x[48:64, :TC]], axis=0) for x in (q, v))
    re = jnp.concatenate([both_ref[:16], both_ref[112:128]], axis=0)
    we = jnp.concatenate([w_ref[:16], w_ref[112:]], axis=0)
    rest = [core_sums(ve), core_sums(re * qe), core_sums(we * qe), core_sums(ve * qe)]
    zero = jnp.zeros((1, 1), jnp.float32)
    row = stats_ref[...] + row_of([[zero, zero]] * 11 + rest)
    stats_out[...] = jnp.broadcast_to(row, stats_out.shape)


def end_kernel(
    counts,
    width,
    stats_ref,
    basis_ref,
    m_ref,
    f_ref,
    both_ref,
    z_ref,
    w_ref,
    q_ref,
    v_ref,
    solution_ref,
    residual_ref,
):
    i, j = place()
    tiles_c = counts[1]
    devices = counts[0] * tiles_c
    rows = stats_ref[...]
    st = jnp.concatenate([rows, pltpu.roll(rows, 64, 1)], axis=0)
    inverse = coarse_part(basis_ref, width)[: 2 * devices, : 2 * devices]
    g = jnp.broadcast_to(dot(inverse, st)[:, 2:3], st.shape)
    lane, row = lanes_of(st.shape), rows_of(st.shape)
    device = row % devices
    column = device % tiles_c
    on_left = row < devices

    def from_row(distance):
        return pltpu.roll(g, distance % (2 * devices), 0)

    up = jnp.where(device >= tiles_c, from_row(tiles_c), 0.0)
    down = jnp.where(device < devices - tiles_c, from_row(-tiles_c), 0.0)
    left = jnp.where(on_left, jnp.where(column > 0, from_row(1 - devices), 0.0), from_row(devices))
    right = jnp.where(
        on_left, from_row(-devices), jnp.where(column < tiles_c - 1, from_row(devices - 1), 0.0)
    )
    du, dd, dl, dr = g - up, g - down, g - left, g - right
    across = jnp.where(
        (lane == 3) | (lane == 7) | (lane == 8),
        du,
        jnp.where((lane == 4) | (lane == 9) | (lane == 10), dd, 0.0),
    )
    across = across + jnp.where(
        (lane == 5) | (lane == 7) | (lane == 9),
        dl,
        jnp.where((lane == 6) | (lane == 8) | (lane == 10), dr, 0.0),
    )
    factor = jnp.where((lane == 2) | (lane == 15), g, across * across)
    factor = jnp.where(lane == 11, 2.0 * g, factor)
    factor = jnp.where((lane < 2) | ((lane >= 12) & (lane < 15)), 1.0, factor)
    terms = jnp.where(lane == 16, (DAMP * SUB * SUB) * g * g, st * factor)
    sums = jnp.sum(terms, axis=0, keepdims=True)

    def whole(wanted):
        return jnp.sum(jnp.where(wanted, sums, 0.0), axis=1, keepdims=True)

    at = lanes_of((1, 128))
    rz, zw = whole(at == 0), whole(at == 1)
    ry = whole((at == 12) | (at == 15))
    yw = whole((at == 13) | (at == 2))
    yv = whole(((at >= 3) & (at < 12)) | (at == 14) | (at == 16))
    a = rz / zw
    rz1 = rz - a * ry - a * zw + a * a * yw
    beta1 = 1.0 + rz1 / rz
    dad = (beta1 * beta1 * zw - 2.0 * a * beta1 * yw) * (1.0 / SHRINK) + a * a * yv
    a1 = rz1 / dad
    r = i - 1 + lane // 4
    c = 2 * j - 1 + lane % 4
    inside = (r >= 0) & (r < counts[0]) & (c >= 0) & (c < 2 * tiles_c) & (lane < 12)
    where = lax.rem(c + 2, 2) * devices + r * tiles_c + (c + 2) // 2 - 1
    picked = jnp.sum(jnp.where(inside & (row == where), g, 0.0), axis=0, keepdims=True)
    bands = as_bands([picked[:, k : k + 1] for k in range(12)])
    on = bands[1][:, :TC]
    coarse = edge_bands(bands)
    image = DAMP * coarse + lap(edge_part(m_ref) * lap(coarse))
    image = with_edges(image, (jumps(bands[1]) * (1.0 / SHRINK))[:, :TC] * f_ref[...] + DAMP * on)
    y = q_ref[...] + on
    v = v_ref[...] + image
    z, w = z_ref[...], w_ref[...]
    solution_ref[...] = (a * SHRINK) * z + a1 * (beta1 * z - a * y)
    residual_ref[...] = both_ref[:TR] - a * w - a1 * ((beta1 * (1.0 / SHRINK)) * w - a * v)


def call(kernel, outs, *args, flops=10**9):
    shapes = [jax.ShapeDtypeStruct(s, jnp.float32) for s in outs]
    return pl.pallas_call(
        kernel,
        out_shape=shapes,
        compiler_params=pltpu.CompilerParams(vmem_limit_bytes=48 * 1024 * 1024),
        cost_estimate=pl.CostEstimate(flops=flops, bytes_accessed=10**6, transcendentals=0),
    )(*args)


def pairs_from(count, offset):
    found = []
    for k in range(offset, count, 2):
        found += [(k, (k + 1) % count), ((k + 1) % count, k)]
    return found


def odd_pairs(counts, axis, bit):
    found = []
    for i in range(counts[0]):
        for j in range(counts[1]):
            at = [i, j]
            if bit and at[axis] in (0, counts[axis] - 1):
                at[1 - axis] ^= bit
            else:
                at[axis] = (at[axis] + (1 if at[axis] % 2 else -1)) % counts[axis]
            found.append((i * counts[1] + j, at[0] * counts[1] + at[1]))
    return found


def xor_pairs(counts, rows, cols):
    flat = [(i, j) for i in range(counts[0]) for j in range(counts[1])]
    return [(i * counts[1] + j, (i ^ rows) * counts[1] + (j ^ cols)) for i, j in flat]


def spreads(counts):
    known = np.eye(counts[0] * counts[1], dtype=bool)

    def meet(*swaps):
        return np.logical_or.reduce([known, *(known[[b for _, b in pairs]] for pairs in swaps)])

    even = [xor_pairs(counts, 0, 1), xor_pairs(counts, 1, 0)]
    own = meet(xor_pairs(counts, 4, 0), xor_pairs(counts, 4, 2))
    known = meet(even[0], odd_pairs(counts, 1, 0))
    known = meet(even[1], odd_pairs(counts, 0, 0)) | own
    known = meet(even[0], odd_pairs(counts, 1, 1))
    return meet(even[1], odd_pairs(counts, 0, 0)).all()


def body(counts, height, noise):
    nr, nc = counts
    devices = nr * nc
    width = max(128, devices * 2)
    basis = jnp.asarray(constants(nr, 2 * nc, width))
    both_axes = ("row", "col")
    depth = table_shape(counts)[0]

    def swap(a, b, axis, bit=0):
        gb = lax.ppermute(b, both_axes, odd_pairs(counts, both_axes.index(axis), bit))
        return lax.ppermute(a, axis, pairs_from(lax.axis_size(axis), 0)), gb

    def small_swap(x, rows, cols):
        return lax.ppermute(x, both_axes, xor_pairs(counts, rows, cols))

    both = jnp.pad(noise, ((0, TR), (0, 0))) + jnp.pad(height, ((TR, 0), (0, 0)))
    b, a, table = call(
        functools.partial(begin_kernel, counts), [(32 + depth, 128)] * 2 + [(depth, 128)], both
    )
    if not spreads(counts):
        for axis, count in enumerate(counts):
            bit = 1
            while bit < count:
                table = table + small_swap(table, *((0, bit) if axis else (bit, 0)))
                bit *= 2
    ga, gb = swap(a, b, "col")
    weight, own = call(weights_kernel, [(EXT, 2 * SPEC), (depth, 128)], both, table, basis)
    far = [small_swap(own, 4, 0), small_swap(own, 4, 2)]
    r3, h3, b, a, table = call(
        functools.partial(widen_kernel, counts),
        [(128, 128)] * 2 + [(24 + depth, FC)] * 2 + [(depth, 128)],
        both,
        table,
        gb,
        ga,
    )
    ga, gb = swap(a, b, "row")
    t = call(forward_kernel, [(EXT, 2 * SPEC)], both, r3, basis)[0]
    t, table, b, a = call(
        functools.partial(first_kernel, counts),
        [(EXT, 2 * SPEC), (depth, 128)] + [(24, EXT)] * 2,
        gb,
        ga,
        t,
        weight,
        basis,
        table,
    )
    table = merged(table, *far)
    wide = jnp.pad(table, ((0, 0), (0, EXT - 128)))
    y, m = call(
        functools.partial(inverse_kernel, counts),
        [(EXT, FC), (FR, FC)],
        t,
        basis,
        both,
        h3,
        gb,
        ga,
    )
    ga, gb = swap(*(jnp.concatenate([x, wide], axis=0) for x in (a, b)), "col", 1)
    y, table, b, a = call(
        functools.partial(columns_kernel, counts),
        [(EXT, FC), (depth, 128)] + [(24 + depth, FC)] * 2,
        y,
        ga,
        gb,
        table,
    )
    ga, gb = swap(a, b, "row")
    inner_w, f, gw, gf, near = call(
        functools.partial(inner_kernel, counts, width),
        [(96, TC)] * 2 + [(EXT, FC)] * 2 + [(16, width)],
        y,
        m,
        basis,
    )
    z, w, t, b, a = call(
        functools.partial(second_kernel, counts, width),
        [(TR, TC)] * 2 + [(EXT, 2 * SPEC)] + [(16, EXT)] * 2,
        y,
        m,
        gb,
        ga,
        table,
        inner_w,
        f,
        gw,
        gf,
        near,
        weight,
        basis,
    )
    ga, gb = swap(a, b, "col", 1)
    y, stats = call(inverse_stats_kernel, [(EXT, FC), (1, 128)], t, basis, both, m, z, w)
    y, b, a = call(
        functools.partial(columns_kernel, counts), [(EXT, FC)] + [(16, FC)] * 2, y, gb, ga
    )
    ga, gb = swap(a, b, "row", 1)
    inner_v, stats = call(
        functools.partial(inner_dots_kernel, counts),
        [(96, TC), (1, 128)],
        y,
        m,
        both,
        w,
        stats,
    )
    q, v, stats = call(
        functools.partial(dots_kernel, counts),
        [(TR, TC)] * 2 + [(devices, 128)],
        y,
        m,
        gb,
        ga,
        both,
        w,
        stats,
        inner_v,
    )
    stats = lax.all_to_all(stats, both_axes, 0, 0, tiled=True)
    return tuple(
        call(
            functools.partial(end_kernel, counts, width),
            [(TR, TC)] * 2,
            stats,
            basis,
            m,
            f,
            both,
            z,
            w,
            q,
            v,
        )
    )


def solution(mesh):
    counts = (mesh.shape["row"], mesh.shape["col"])
    spec = P("row", "col")
    return jax.shard_map(
        functools.partial(body, counts),
        mesh=mesh,
        in_specs=(spec, spec),
        out_specs=(spec, spec),
        check_vma=False,
    )
```

```python
import functools

import jax
import jax.numpy as jnp
import ml_dtypes
import numpy as np
from jax import lax
from jax.experimental import pallas as pl
from jax.experimental.pallas import tpu as pltpu
from jax.sharding import PartitionSpec as P

SUB = 128
OV = 8
EXT = SUB + 2 * OV
DAMP = 2.0**-28
SHRINK = 2.0**-20

TR, TC = 128, 256
FR, FC = 160, 384
SPEC = 256

highest = lax.Precision.HIGHEST


def sine(count):
    k = np.arange(1, count + 1, dtype=np.float64)
    basis = np.sqrt(2.0 / (count + 1.0)) * np.sin(np.pi * k[:, None] * k[None, :] / (count + 1.0))
    return basis, 2.0 - 2.0 * np.cos(np.pi * k / (count + 1.0))


def block_constants():
    basis, eig = sine(EXT)
    rows = np.roll(basis, -OV, 0)
    cols = np.pad(basis, ((0, SPEC - EXT), (0, SPEC - EXT)))
    scale = np.pad((eig[:, None] + eig[None, :]) ** 2, ((0, 0), (0, SPEC - EXT)))
    wide = lambda x: np.pad(x, ((0, 0), (0, 2 * SPEC - x.shape[1])))
    high = rows.T.astype(ml_dtypes.bfloat16).astype(np.float64)
    low = (rows.T - high).astype(ml_dtypes.bfloat16).astype(np.float64)
    tile = np.concatenate([x[:, :SUB] for x in (high, high, low)], 1)
    halo = np.concatenate([x[:, SUB:] for x in (high, high, low)], 1)
    inner = np.concatenate([x[:, 16:112] for x in (high, high, low)], 1)
    at = [*range(136, 144), *range(16), *range(112, 136)]
    edge = np.concatenate([x[:, at] for x in (high, high, low)], 1)
    turned = np.hstack([rows.T, np.zeros((EXT, 256 - EXT)), edge])
    return [np.tile(scale, (1, 2)), *(wide(x) for x in (rows, turned, cols, inner, np.hstack([tile, halo])))]


def rows_part(ref):
    return ref[EXT : 2 * EXT, :EXT]


def rows_t_part(ref):
    return ref[2 * EXT : 3 * EXT, :256]


def cols_part(ref):
    return ref[3 * EXT : 3 * EXT + SPEC, :SPEC]


def inner_rows(ref):
    at = 3 * EXT + SPEC
    return ref[at : at + EXT, : 3 * 96]


def edge_rows(ref):
    return ref[2 * EXT : 3 * EXT, 256 : 256 + 3 * 48]


def tile_rows(ref):
    at = 4 * EXT + SPEC
    return ref[at : at + EXT, : 3 * SUB]


def halo_rows(ref):
    at = 4 * EXT + SPEC
    return ref[at : at + EXT, 3 * SUB : 3 * EXT]


def coarse_part(ref, width):
    at, lanes = 5 * EXT + SPEC, 2 * SPEC
    parts = [ref[at + k * width : at + (k + 1) * width] for k in range(-(-width // lanes))]
    return (parts[0] if len(parts) == 1 else jnp.concatenate(parts, axis=1))[:, :width]


def constants(nr, nc, width):
    lanes = 2 * SPEC
    inverse = coarse_inverse(nr, nc, -(-width // lanes) * lanes)[:width]
    parts = [*block_constants(), *np.split(inverse, inverse.shape[1] // lanes, 1)]
    return np.concatenate(parts).astype(np.float32)


def coarse_inverse(nr, nc, width):
    br, er = sine(nr)
    bc, ec = sine(nc)
    both = np.kron(br, bc).reshape(nr, nc // 2, 2, nr * nc).transpose(2, 0, 1, 3)
    both = both.reshape(nr * nc, nr * nc)
    scale = (er[:, None] + ec[None, :]) / (SUB * SUB)
    values = (SUB * SUB * (DAMP + scale * scale)).reshape(-1)
    whole = np.zeros((width, width), np.float32)
    whole[: nr * nc, : nr * nc] = (both / values) @ both.T
    return whole


def dot(a, b, side=0):
    return lax.dot_general(
        a, b, (((1,), (side,)), ((), ())), precision=highest, preferred_element_type=jnp.float32
    )


def lap(x):
    rows, lanes = x.shape
    beside = pltpu.roll(x, 1, 0) + pltpu.roll(x, rows - 1, 0)
    beside = beside + (pltpu.roll(x, 1, 1) + pltpu.roll(x, lanes - 1, 1))
    return 4.0 * x - beside


def lanes_of(shape):
    return lax.broadcasted_iota(jnp.int32, shape, 1)


def rows_of(shape):
    return lax.broadcasted_iota(jnp.int32, shape, 0)


def total(x):
    return jnp.sum(jnp.sum(x, axis=0, keepdims=True), axis=1, keepdims=True)


def place():
    return lax.axis_index("row"), lax.axis_index("col")


def is_even(index):
    return lax.rem(index, 2) == 0


def column_mask(counts):
    j = lax.axis_index("col")
    lane = lanes_of((1, FC))
    right = jnp.where(j < counts[1] - 1, 320, 256)
    left = jnp.where(j > 0, 320, 384)
    return (lane < right) | (lane >= left)


def edge_mask(counts):
    i = lax.axis_index("row")
    row = rows_of((80, 1))
    first = jnp.where(i > 0, 0, 16)
    last = jnp.where(i < counts[0] - 1, 80, 64)
    return (row >= first) & (row < last) & column_mask(counts)


def table_shape(counts):
    return (-(-2 * counts[0] * counts[1] // 1024) * 8, 128)


def table_of(values, counts):
    i, j = place()
    devices = counts[0] * counts[1]
    shape = table_shape(counts)
    at = rows_of(shape) * 128 + lanes_of(shape) - (i * counts[1] + j)
    return jnp.where(at == 0, values[0], jnp.where(at == devices, values[1], 0.0))


def merged(table, *others):
    for other in others:
        table = jnp.where(table != 0.0, table, other)
    return table


def as_row(table, width):
    return jnp.concatenate([table[k : k + 1] for k in range(width // 128)], axis=1)


def row_of(pairs):
    lane = lanes_of((1, 128))
    row = jnp.zeros((1, 128), jnp.float32)
    for k, (left, right) in enumerate(pairs):
        row = jnp.where(lane == k, left, jnp.where(lane == 64 + k, right, row))
    return row


def near_inverse(counts, inverse):
    i, j = place()
    nr, nc = counts[0], 2 * counts[1]
    shape = (16, inverse.shape[0])
    which = rows_of(shape)
    r = i - 1 + which // 4
    c = 2 * j - 1 + which % 4
    inside = (r >= 0) & (r < nr) & (c >= 0) & (c < nc) & (which < 12)
    at = lax.rem(c + 2, 2) * (nr * counts[1]) + r * counts[1] + (c + 2) // 2 - 1
    return dot(jnp.where(inside & (lanes_of(shape) == at), 1.0, 0.0), inverse)


def as_bands(values):
    lane = lanes_of((1, FC))
    bands = []
    for d in range(3):
        left, first, second, right = values[4 * d : 4 * d + 4]
        bands.append(
            jnp.where(
                lane < 128,
                first,
                jnp.where(lane < 256, second, jnp.where(lane < 320, right, left)),
            )
        )
    return bands


def edge_bands(bands):
    above, on, below = bands
    return jnp.concatenate(
        [
            jnp.broadcast_to(above, (16, FC)),
            jnp.broadcast_to(on, (48, FC)),
            jnp.broadcast_to(below, (16, FC)),
        ],
        axis=0,
    )


def jumps(row):
    step = row - pltpu.roll(row, 1, 1)
    lane = lanes_of((1, FC))
    at = [jnp.sum(jnp.where(lane == k, step, 0.0), axis=1, keepdims=True) for k in (0, 128, 256)]
    return jnp.where(
        (lane < 64) | (lane >= 320), at[0], jnp.where(lane < 192, at[1], at[2])
    )


def edge_steps():
    lane = lanes_of((1, FC))
    up = (lane == 0) | (lane == 128) | (lane == 256)
    down = (lane == FC - 1) | (lane == 127) | (lane == 255)
    return jnp.where(up, 1.0, jnp.where(down, -1.0, 0.0))


def halves_of(x):
    high = x.astype(jnp.bfloat16)
    return high, (x - high.astype(jnp.float32)).astype(jnp.bfloat16)


def product(a, b):
    return lax.dot_general(a, b, (((1,), (0,)), ((), ())), preferred_element_type=jnp.float32)


def column_transform(w, basis_ref):
    high, low = halves_of(pltpu.roll(w, OV, 1))
    cols, rest = halves_of(cols_part(basis_ref))
    cols = jnp.concatenate([cols, rest, cols], axis=0)

    def block(at):
        part = slice(at, at + SPEC)
        return product(jnp.concatenate([high[:, part], high[:, part], low[:, part]], axis=1), cols)

    return jnp.concatenate([block(0), block(128)], axis=1)


def row_transform(u, basis_ref, part):
    high, low = halves_of(u)
    rows = part(basis_ref).astype(jnp.bfloat16)
    return product(rows, jnp.concatenate([high, low, high], axis=0))


def weights(means, basis_ref):
    lane = lanes_of((1, 2 * SPEC))
    mean = jnp.where(lane < SPEC, means[0], means[1])
    return 1.0 / (DAMP + mean * basis_ref[:EXT])


def strips_of(t, basis_ref, deep):
    cols = cols_part(basis_ref)
    left = dot(cols[:deep], t[:, :SPEC], 1)
    right = dot(cols[EXT - deep : EXT], t[:, SPEC:], 1)
    both = dot(jnp.concatenate([left, right], axis=0), rows_t_part(basis_ref)[:, :EXT])
    return both[:deep], both[deep:]


def solution_of(t, basis_ref):
    v = dot(rows_part(basis_ref), t)
    cols = cols_part(basis_ref)
    first, second = dot(v[:, :SPEC], cols), dot(v[:, SPEC:], cols)
    y = jnp.concatenate(
        [first[:, :128], first[:, 128:] + second[:, :128], second[:, 128:]], axis=1
    )
    return pltpu.roll(y, FC - OV, 1)


def core_sums(x):
    return [total(x[:, :128]), total(x[:, 128:256])]


def add_columns(y, from_left, from_right):
    far = from_left.shape[0] - OV
    gap = jnp.zeros((56 - far, EXT), jnp.float32)
    turned = jnp.concatenate(
        [from_right[8:], gap, from_right[:8], from_left[far:], gap, from_left[:far]], axis=0
    )
    back = turned.T
    lane = lanes_of((EXT, 128))
    rolled = pltpu.roll(back, 64, 1)
    first = y[:, :128] + jnp.where(lane < 8, rolled, 0.0)
    second = y[:, 128:256] + jnp.where(lane >= 120, rolled, 0.0)
    third = y[:, 256:] + jnp.where((lane < 16) | (lane >= 112), back, 0.0)
    return jnp.concatenate([first, second, third], axis=1)


def pack_rows(y, deep):
    return jnp.concatenate([y[136:], y[: deep - 8]], axis=0), y[136 - deep : 136]


def edges(y, from_above, from_below):
    far = from_above.shape[0] - OV
    none = jnp.zeros((8, FC), jnp.float32)
    return jnp.concatenate(
        [
            from_above[:8] if far == 16 else none,
            y[136:] + from_above[far - 8 : far],
            y[:8] + from_above[far:],
            y[8:24],
            y[104:120],
            y[120:136] + from_below[:16],
            from_below[16:] if far == 16 else none,
        ],
        axis=0,
    )


def edge_part(frame):
    return jnp.concatenate([frame[144:], frame[:24], frame[104:144]], axis=0)


def with_edges(edge, inner):
    return jnp.concatenate([edge[16:32, :TC], inner, edge[48:64, :TC]], axis=0)


def sides(index, count, a, b):
    even = is_even(index)
    before = jnp.where(index > 0, jnp.where(even, b, a), 0.0)
    after = jnp.where(index < count - 1, jnp.where(even, a, b), 0.0)
    return before, after


def send(index, a_ref, b_ref, before, after):
    even = is_even(index)
    a_ref[...] = jnp.where(even, after, before)
    b_ref[...] = jnp.where(even, before, after)


def begin_kernel(counts, both_ref, b_ref, a_ref, table_ref):
    r, h = both_ref[:TR], both_ref[TR:]
    lane = lanes_of((128, 128))
    packed = jnp.where(
        lane < 16,
        r[:, :128],
        jnp.where(
            lane < 64,
            pltpu.roll(h[:, :128], 16, 1),
            jnp.where(lane < 112, pltpu.roll(h[:, 128:], 112, 1), r[:, 128:]),
        ),
    )
    turned = packed.T
    table = table_of(core_sums(r), counts)
    table_ref[...] = table
    send(
        lax.axis_index("col"),
        a_ref,
        b_ref,
        jnp.concatenate([turned[:32], table], axis=0),
        jnp.concatenate([turned[96:], table], axis=0),
    )


def statistics_kernel(both_ref, table_ref, stats_ref, table_out):
    h = both_ref[TR:]
    mt = h * h * h
    lane, row = lanes_of((1, 256)), rows_of((128, 1))
    along = (lane % 128 != 0) & (lane % 128 != 127)
    top, low = mt[:1], mt[127:]
    side = jnp.sum(jnp.where((row > 0) & (row < 127), mt, 0.0), axis=0, keepdims=True)

    def halves(x):
        return [
            jnp.sum(x[:, :128], axis=1, keepdims=True),
            jnp.sum(x[:, 128:], axis=1, keepdims=True),
        ]

    first, last = lane % 128 == 0, lane % 128 == 127
    zero = jnp.zeros((1, 1), jnp.float32)
    stats_ref[...] = row_of(
        [
            *[[zero, zero]] * 3,
            halves(jnp.where(along, top, 0.0)),
            halves(jnp.where(along, low, 0.0)),
            halves(jnp.where(first, side, 0.0)),
            halves(jnp.where(last, side, 0.0)),
            halves(jnp.where(first, top, 0.0)),
            halves(jnp.where(last, top, 0.0)),
            halves(jnp.where(first, low, 0.0)),
            halves(jnp.where(last, low, 0.0)),
        ]
    )
    table_out[...] = table_ref[...]


def widen_kernel(counts, both_ref, own_ref, gb_ref, ga_ref, r3_ref, h3_ref, b_ref, a_ref, table_ref):
    i, j = place()
    from_left, from_right = sides(j, counts[1], ga_ref[:32], gb_ref[:32])
    turned = jnp.concatenate([from_right, jnp.zeros((64, 128), jnp.float32), from_left], axis=0)
    back = turned.T
    lane = lanes_of((128, 128))
    edge = (lane < 16) | (lane >= 112)
    r3 = jnp.where(edge, back, 0.0)
    h3 = jnp.where(
        lane < 16, pltpu.roll(back, 112, 1), jnp.where(lane >= 112, pltpu.roll(back, 16, 1), 0.0)
    )
    r3_ref[...] = r3
    h3_ref[...] = h3
    r, h = both_ref[:TR], both_ref[TR:]
    table = merged(own_ref[...], ga_ref[32:], gb_ref[32:])
    table_ref[...] = table
    wide = jnp.concatenate([table, jnp.zeros((table.shape[0], FC - 128), jnp.float32)], axis=1)

    def strip(r_rows, h_rows):
        return jnp.concatenate(
            [
                jnp.concatenate([r[r_rows], r3[r_rows]], axis=1),
                jnp.concatenate([h[h_rows], h3[h_rows]], axis=1),
                wide,
            ],
            axis=0,
        )

    send(i, a_ref, b_ref, strip(slice(0, 8), slice(0, 16)), strip(slice(120, 128), slice(112, 128)))


def weights_kernel(both_ref, table_ref, basis_ref, weights_ref, table_out):
    h = both_ref[TR:]
    means = [x / (SUB * SUB) for x in core_sums(h * h * h)]
    weights_ref[...] = weights(means, basis_ref)
    table_out[...] = table_ref[...]


def forward_kernel(both_ref, r3_ref, basis_ref, t_ref):
    r = both_ref[:TR]
    u = column_transform(jnp.concatenate([r, r3_ref[...]], axis=1), basis_ref)
    t_ref[...] = row_transform(u, basis_ref, tile_rows)


def first_kernel(
    counts,
    gb_ref,
    ga_ref,
    tile_ref,
    weights_ref,
    basis_ref,
    table_ref,
    t_ref,
    table_out,
    b_ref,
    a_ref,
):
    i, j = place()
    above, below = sides(i, counts[0], ga_ref[:8], gb_ref[:8])
    u = column_transform(jnp.concatenate([below, above], axis=0), basis_ref)
    t = (tile_ref[...] + row_transform(u, basis_ref, halo_rows)) * weights_ref[...]
    t_ref[...] = t
    send(j, a_ref, b_ref, *strips_of(t, basis_ref, 24))
    table_out[...] = merged(table_ref[...], ga_ref[24:, :128], gb_ref[24:, :128])


def inverse_kernel(counts, t_ref, basis_ref, both_ref, h3_ref, gb_ref, ga_ref, y_ref, m_ref):
    y_ref[...] = solution_of(t_ref[...], basis_ref)
    above, below = sides(lax.axis_index("row"), counts[0], ga_ref[8:24], gb_ref[8:24])
    h = jnp.concatenate([both_ref[TR:], h3_ref[...]], axis=1)
    tall = jnp.concatenate([h, below, above], axis=0)
    m_ref[...] = tall * tall * tall


def columns_kernel(counts, y_ref, *refs):
    i, j = place()
    (ga_ref, gb_ref), refs = (refs[:2] if len(refs) == 7 else refs[1::-1]), refs[2:]
    deep = 24 if len(refs) == 5 else 16
    y = add_columns(y_ref[...], *sides(j, counts[1], ga_ref[:deep], gb_ref[:deep]))
    strips = pack_rows(y, deep)
    if len(refs) == 5:
        table_ref, out_ref, table_out, b_ref, a_ref = refs
        table = merged(table_ref[...], ga_ref[24:, :128], gb_ref[24:, :128])
        table_out[...] = table
        wide = jnp.concatenate([table, jnp.zeros((table.shape[0], FC - 128), jnp.float32)], axis=1)
        strips = [jnp.concatenate([x, wide], axis=0) for x in strips]
    else:
        out_ref, b_ref, a_ref = refs
    out_ref[...] = y
    send(i, a_ref, b_ref, *strips)


def inner_kernel(counts, width, y_ref, m_ref, basis_ref, w_ref, f_ref, gw_ref, gf_ref, near_ref):
    mask = column_mask(counts)
    s = jnp.where(mask, y_ref[8:120], 0.0)
    m = m_ref[8:120]
    w = DAMP * s + lap(m * lap(s))
    w = jnp.where(mask, w[8:104], 0.0) * SHRINK
    f = lap(m * edge_steps())
    f = jnp.where(mask, f[8:104], 0.0) * SHRINK
    w_ref[...] = w[:, :TC]
    f_ref[...] = f[:, :TC]
    gw_ref[...] = row_transform(w, basis_ref, inner_rows)
    gf_ref[...] = row_transform(f, basis_ref, inner_rows)
    near_ref[...] = near_inverse(counts, coarse_part(basis_ref, width))


def second_kernel(
    counts,
    width,
    y_ref,
    m_ref,
    gb_ref,
    ga_ref,
    table_ref,
    inner_w_ref,
    f_ref,
    gw_ref,
    gf_ref,
    near_ref,
    weights_ref,
    basis_ref,
    z_ref,
    w_ref,
    t_ref,
    b_ref,
    a_ref,
):
    i, j = place()
    y = y_ref[...]
    mask = edge_mask(counts)
    s = edges(y, *sides(i, counts[0], ga_ref[:24], gb_ref[:24]))
    s = jnp.where(mask, s, 0.0)
    table = merged(table_ref[...], ga_ref[24:, :128], gb_ref[24:, :128])
    picked = jnp.sum(near_ref[...] * as_row(table, width), axis=1, keepdims=True)
    bands = as_bands([picked[k : k + 1] for k in range(12)])
    coarse = edge_bands(bands)
    m = edge_part(m_ref)
    flow = m * (lap(s) + lap(coarse))
    z = s + coarse
    w = jnp.where(mask, DAMP * z + lap(flow), 0.0) * SHRINK
    step = jumps(bands[1])
    damped = (DAMP * SHRINK) * bands[1]
    z_ref[...] = with_edges(z, y[16:112, :TC] + bands[1][:, :TC])
    w_ref[...] = with_edges(w, inner_w_ref[...] + step[:, :TC] * f_ref[...] + damped[:, :TC])
    lane = lanes_of((EXT, 256))
    ones = jnp.where((lane >= 16) & (lane < 112), rows_t_part(basis_ref), 0.0)
    ones = jnp.sum(ones, axis=1, keepdims=True)
    u = gw_ref[...] + step * gf_ref[...] + ones * damped
    u = u + row_transform(jnp.concatenate([w[8:32], w[48:72]], axis=0), basis_ref, edge_rows)
    t = column_transform(u, basis_ref) * weights_ref[...]
    t_ref[...] = t
    send(j, a_ref, b_ref, *strips_of(t, basis_ref, 16))


def inverse_stats_kernel(t_ref, basis_ref, both_ref, z_ref, w_ref, edge_stats_ref, y_ref, stats_ref):
    y_ref[...] = solution_of(t_ref[...], basis_ref)
    rt, zt, wt = both_ref[:TR], z_ref[...], w_ref[...]
    zero = jnp.zeros((1, 1), jnp.float32)
    sums = [core_sums(rt * zt), core_sums(zt * wt), core_sums(wt), *[[zero, zero]] * 12, core_sums(rt)]
    stats_ref[...] = edge_stats_ref[...] + row_of(sums)


def inner_dots_kernel(counts, y_ref, m_ref, both_ref, w_ref, stats_ref, v_ref, stats_out):
    q = jnp.where(column_mask(counts), y_ref[8:120], 0.0)
    v = (DAMP * q + lap(m_ref[8:120] * lap(q)))[8:104, :TC]
    q = q[8:104, :TC]
    v_ref[...] = v
    rest = [
        core_sums(v),
        core_sums(both_ref[16:112] * q),
        core_sums(w_ref[16:112] * q),
        core_sums(v * q),
    ]
    zero = jnp.zeros((1, 1), jnp.float32)
    stats_out[...] = stats_ref[...] + row_of([[zero, zero]] * 11 + rest)


def dots_kernel(
    counts, y_ref, m_ref, gb_ref, ga_ref, both_ref, w_ref, stats_ref, inner_v_ref, q_ref, v_ref, stats_out
):
    i, j = place()
    y = y_ref[...]
    q = edges(y, *sides(i, counts[0], ga_ref[...], gb_ref[...]))
    q = jnp.where(edge_mask(counts), q, 0.0)
    v = DAMP * q + lap(edge_part(m_ref) * lap(q))
    q_ref[...] = with_edges(q, y[16:112, :TC])
    v_ref[...] = with_edges(v, inner_v_ref[...])
    qe, ve = (jnp.concatenate([x[16:32, :TC], x[48:64, :TC]], axis=0) for x in (q, v))
    re = jnp.concatenate([both_ref[:16], both_ref[112:128]], axis=0)
    we = jnp.concatenate([w_ref[:16], w_ref[112:]], axis=0)
    rest = [core_sums(ve), core_sums(re * qe), core_sums(we * qe), core_sums(ve * qe)]
    zero = jnp.zeros((1, 1), jnp.float32)
    row = stats_ref[...] + row_of([[zero, zero]] * 11 + rest)
    stats_out[...] = jnp.broadcast_to(row, stats_out.shape)


def end_kernel(
    counts,
    width,
    stats_ref,
    basis_ref,
    m_ref,
    f_ref,
    both_ref,
    z_ref,
    w_ref,
    q_ref,
    v_ref,
    solution_ref,
    residual_ref,
):
    i, j = place()
    tiles_c = counts[1]
    devices = counts[0] * tiles_c
    rows = stats_ref[...]
    st = jnp.concatenate([rows, pltpu.roll(rows, 64, 1)], axis=0)
    inverse = coarse_part(basis_ref, width)[: 2 * devices, : 2 * devices]
    g = jnp.broadcast_to(dot(inverse, st)[:, 2:3], st.shape)
    lane, row = lanes_of(st.shape), rows_of(st.shape)
    device = row % devices
    column = device % tiles_c
    on_left = row < devices

    def from_row(distance):
        return pltpu.roll(g, distance % (2 * devices), 0)

    up = jnp.where(device >= tiles_c, from_row(tiles_c), 0.0)
    down = jnp.where(device < devices - tiles_c, from_row(-tiles_c), 0.0)
    left = jnp.where(on_left, jnp.where(column > 0, from_row(1 - devices), 0.0), from_row(devices))
    right = jnp.where(
        on_left, from_row(-devices), jnp.where(column < tiles_c - 1, from_row(devices - 1), 0.0)
    )
    du, dd, dl, dr = g - up, g - down, g - left, g - right
    across = jnp.where(
        (lane == 3) | (lane == 7) | (lane == 8),
        du,
        jnp.where((lane == 4) | (lane == 9) | (lane == 10), dd, 0.0),
    )
    across = across + jnp.where(
        (lane == 5) | (lane == 7) | (lane == 9),
        dl,
        jnp.where((lane == 6) | (lane == 8) | (lane == 10), dr, 0.0),
    )
    factor = jnp.where((lane == 2) | (lane == 15), g, across * across)
    factor = jnp.where(lane == 11, 2.0 * g, factor)
    factor = jnp.where((lane < 2) | ((lane >= 12) & (lane < 15)), 1.0, factor)
    terms = jnp.where(lane == 16, (DAMP * SUB * SUB) * g * g, st * factor)
    sums = jnp.sum(terms, axis=0, keepdims=True)

    def whole(wanted):
        return jnp.sum(jnp.where(wanted, sums, 0.0), axis=1, keepdims=True)

    at = lanes_of((1, 128))
    rz, zw = whole(at == 0), whole(at == 1)
    ry = whole((at == 12) | (at == 15))
    yw = whole((at == 13) | (at == 2))
    yv = whole(((at >= 3) & (at < 12)) | (at == 14) | (at == 16))
    a = rz / zw
    rz1 = rz - a * ry - a * zw + a * a * yw
    beta1 = 1.0 + rz1 / rz
    dad = (beta1 * beta1 * zw - 2.0 * a * beta1 * yw) * (1.0 / SHRINK) + a * a * yv
    a1 = rz1 / dad
    r = i - 1 + lane // 4
    c = 2 * j - 1 + lane % 4
    inside = (r >= 0) & (r < counts[0]) & (c >= 0) & (c < 2 * tiles_c) & (lane < 12)
    where = lax.rem(c + 2, 2) * devices + r * tiles_c + (c + 2) // 2 - 1
    picked = jnp.sum(jnp.where(inside & (row == where), g, 0.0), axis=0, keepdims=True)
    bands = as_bands([picked[:, k : k + 1] for k in range(12)])
    on = bands[1][:, :TC]
    coarse = edge_bands(bands)
    image = DAMP * coarse + lap(edge_part(m_ref) * lap(coarse))
    image = with_edges(image, (jumps(bands[1]) * (1.0 / SHRINK))[:, :TC] * f_ref[...] + DAMP * on)
    y = q_ref[...] + on
    v = v_ref[...] + image
    z, w = z_ref[...], w_ref[...]
    solution_ref[...] = (a * SHRINK) * z + a1 * (beta1 * z - a * y)
    residual_ref[...] = both_ref[:TR] - a * w - a1 * ((beta1 * (1.0 / SHRINK)) * w - a * v)


def call(kernel, outs, *args, flops=10**9):
    shapes = [jax.ShapeDtypeStruct(s, jnp.float32) for s in outs]
    return pl.pallas_call(
        kernel,
        out_shape=shapes,
        compiler_params=pltpu.CompilerParams(vmem_limit_bytes=48 * 1024 * 1024),
        cost_estimate=pl.CostEstimate(flops=flops, bytes_accessed=10**6, transcendentals=0),
    )(*args)


def pairs_from(count, offset):
    found = []
    for k in range(offset, count, 2):
        found += [(k, (k + 1) % count), ((k + 1) % count, k)]
    return found


def odd_pairs(counts, axis, bit):
    found = []
    for i in range(counts[0]):
        for j in range(counts[1]):
            at = [i, j]
            if at[axis] in (0, counts[axis] - 1):
                at[1 - axis] ^= bit
            else:
                at[axis] += 1 if at[axis] % 2 else -1
            found.append((i * counts[1] + j, at[0] * counts[1] + at[1]))
    return found


def xor_pairs(counts, rows, cols):
    flat = [(i, j) for i in range(counts[0]) for j in range(counts[1])]
    return [(i * counts[1] + j, (i ^ rows) * counts[1] + (j ^ cols)) for i, j in flat]


def spreads(counts):
    known = np.eye(counts[0] * counts[1], dtype=bool)

    def meet(*swaps):
        return np.logical_or.reduce([known, *(known[[b for _, b in pairs]] for pairs in swaps)])

    even = [xor_pairs(counts, 0, 1), xor_pairs(counts, 1, 0)]
    own = meet(xor_pairs(counts, 2, 3), xor_pairs(counts, 6, 3))
    known = meet(even[0], odd_pairs(counts, 1, 1))
    known = meet(even[1], odd_pairs(counts, 0, 1), xor_pairs(counts, 4, 0)) | own
    known = meet(even[0], odd_pairs(counts, 1, 2))
    return meet(even[1], odd_pairs(counts, 0, 1)).all()


def body(counts, height, noise):
    nr, nc = counts
    devices = nr * nc
    width = max(128, devices * 2)
    basis = jnp.asarray(constants(nr, 2 * nc, width))
    both_axes = ("row", "col")
    depth = table_shape(counts)[0]

    def swap(a, b, axis, bit=1):
        gb = lax.ppermute(b, both_axes, odd_pairs(counts, both_axes.index(axis), bit))
        return lax.ppermute(a, axis, pairs_from(lax.axis_size(axis), 0)), gb

    def small_swap(x, rows, cols):
        return lax.ppermute(x, both_axes, xor_pairs(counts, rows, cols))

    both = jnp.pad(noise, ((0, TR), (0, 0))) + jnp.pad(height, ((TR, 0), (0, 0)))
    b, a, table = call(
        functools.partial(begin_kernel, counts), [(32 + depth, 128)] * 2 + [(depth, 128)], both
    )
    if not spreads(counts):
        for axis, count in enumerate(counts):
            bit = 1
            while bit < count:
                table = table + small_swap(table, *((0, bit) if axis else (bit, 0)))
                bit *= 2
    ga, gb = swap(a, b, "col")
    edge_stats, own = call(statistics_kernel, [(1, 128), (depth, 128)], both, table)
    far = [small_swap(own, 2, 3), small_swap(own, 6, 3)]
    r3, h3, b, a, table = call(
        functools.partial(widen_kernel, counts),
        [(128, 128)] * 2 + [(24 + depth, FC)] * 2 + [(depth, 128)],
        both,
        table,
        gb,
        ga,
    )
    ga, gb = swap(a, b, "row")
    weight, table = call(weights_kernel, [(EXT, 2 * SPEC), (depth, 128)], both, table, basis)
    far.append(small_swap(table, 4, 0))
    t = call(forward_kernel, [(EXT, 2 * SPEC)], both, r3, basis)[0]
    t, table, b, a = call(
        functools.partial(first_kernel, counts),
        [(EXT, 2 * SPEC), (depth, 128)] + [(24, EXT)] * 2,
        gb,
        ga,
        t,
        weight,
        basis,
        table,
    )
    table = merged(table, *far)
    wide = jnp.pad(table, ((0, 0), (0, EXT - 128)))
    y, m = call(
        functools.partial(inverse_kernel, counts),
        [(EXT, FC), (FR, FC)],
        t,
        basis,
        both,
        h3,
        gb,
        ga,
    )
    ga, gb = swap(*(jnp.concatenate([x, wide], axis=0) for x in (a, b)), "col", 2)
    y, table, b, a = call(
        functools.partial(columns_kernel, counts),
        [(EXT, FC), (depth, 128)] + [(24 + depth, FC)] * 2,
        y,
        ga,
        gb,
        table,
    )
    ga, gb = swap(a, b, "row")
    inner_w, f, gw, gf, near = call(
        functools.partial(inner_kernel, counts, width),
        [(96, TC)] * 2 + [(EXT, FC)] * 2 + [(16, width)],
        y,
        m,
        basis,
    )
    z, w, t, b, a = call(
        functools.partial(second_kernel, counts, width),
        [(TR, TC)] * 2 + [(EXT, 2 * SPEC)] + [(16, EXT)] * 2,
        y,
        m,
        gb,
        ga,
        table,
        inner_w,
        f,
        gw,
        gf,
        near,
        weight,
        basis,
    )
    ga, gb = swap(a, b, "col")
    y, stats = call(inverse_stats_kernel, [(EXT, FC), (1, 128)], t, basis, both, z, w, edge_stats)
    y, b, a = call(
        functools.partial(columns_kernel, counts), [(EXT, FC)] + [(16, FC)] * 2, y, gb, ga
    )
    ga, gb = swap(a, b, "row")
    inner_v, stats = call(
        functools.partial(inner_dots_kernel, counts),
        [(96, TC), (1, 128)],
        y,
        m,
        both,
        w,
        stats,
    )
    q, v, stats = call(
        functools.partial(dots_kernel, counts),
        [(TR, TC)] * 2 + [(devices, 128)],
        y,
        m,
        gb,
        ga,
        both,
        w,
        stats,
        inner_v,
    )
    stats = lax.all_to_all(stats, both_axes, 0, 0, tiled=True)
    return tuple(
        call(
            functools.partial(end_kernel, counts, width),
            [(TR, TC)] * 2,
            stats,
            basis,
            m,
            f,
            both,
            z,
            w,
            q,
            v,
        )
    )


def solution(mesh):
    counts = (mesh.shape["row"], mesh.shape["col"])
    spec = P("row", "col")
    return jax.shard_map(
        functools.partial(body, counts),
        mesh=mesh,
        in_specs=(spec, spec),
        out_specs=(spec, spec),
        check_vma=False,
    )
```

```python
import functools

import jax
import jax.numpy as jnp
import ml_dtypes
import numpy as np
from jax import lax
from jax.experimental import pallas as pl
from jax.experimental.pallas import tpu as pltpu
from jax.sharding import PartitionSpec as P

SUB = 128
OV = 8
EXT = SUB + 2 * OV
DAMP = 2.0**-28
SHRINK = 2.0**-20

TR, TC = 128, 256
FR, FC = 160, 384
SPEC = 256

highest = lax.Precision.HIGHEST


def sine(count):
    k = np.arange(1, count + 1, dtype=np.float64)
    basis = np.sqrt(2.0 / (count + 1.0)) * np.sin(np.pi * k[:, None] * k[None, :] / (count + 1.0))
    return basis, 2.0 - 2.0 * np.cos(np.pi * k / (count + 1.0))


def block_constants():
    basis, eig = sine(EXT)
    rows = np.roll(basis, -OV, 0)
    cols = np.pad(basis, ((0, SPEC - EXT), (0, SPEC - EXT)))
    scale = np.pad((eig[:, None] + eig[None, :]) ** 2, ((0, 0), (0, SPEC - EXT)))
    wide = lambda x: np.pad(x, ((0, 0), (0, 2 * SPEC - x.shape[1])))
    high = rows.T.astype(ml_dtypes.bfloat16).astype(np.float64)
    low = (rows.T - high).astype(ml_dtypes.bfloat16).astype(np.float64)
    tile = np.concatenate([x[:, :SUB] for x in (high, high, low)], 1)
    halo = np.concatenate([x[:, SUB:] for x in (high, high, low)], 1)
    inner = np.concatenate([x[:, 16:112] for x in (high, high, low)], 1)
    at = [*range(136, 144), *range(16), *range(112, 136)]
    edge = np.concatenate([x[:, at] for x in (high, high, low)], 1)
    turned = np.hstack([rows.T, np.zeros((EXT, 256 - EXT)), edge])
    return [np.tile(scale, (1, 2)), *(wide(x) for x in (rows, turned, cols, inner, np.hstack([tile, halo])))]


def rows_part(ref):
    return ref[EXT : 2 * EXT, :EXT]


def rows_t_part(ref):
    return ref[2 * EXT : 3 * EXT, :256]


def cols_part(ref):
    return ref[3 * EXT : 3 * EXT + SPEC, :SPEC]


def inner_rows(ref):
    at = 3 * EXT + SPEC
    return ref[at : at + EXT, : 3 * 96]


def edge_rows(ref):
    return ref[2 * EXT : 3 * EXT, 256 : 256 + 3 * 48]


def tile_rows(ref):
    at = 4 * EXT + SPEC
    return ref[at : at + EXT, : 3 * SUB]


def halo_rows(ref):
    at = 4 * EXT + SPEC
    return ref[at : at + EXT, 3 * SUB : 3 * EXT]


def coarse_part(ref, width):
    at, lanes = 5 * EXT + SPEC, 2 * SPEC
    parts = [ref[at + k * width : at + (k + 1) * width] for k in range(-(-width // lanes))]
    return (parts[0] if len(parts) == 1 else jnp.concatenate(parts, axis=1))[:, :width]


def constants(nr, nc, width):
    lanes = 2 * SPEC
    inverse = coarse_inverse(nr, nc, -(-width // lanes) * lanes)[:width]
    parts = [*block_constants(), *np.split(inverse, inverse.shape[1] // lanes, 1)]
    return np.concatenate(parts).astype(np.float32)


def coarse_inverse(nr, nc, width):
    br, er = sine(nr)
    bc, ec = sine(nc)
    both = np.kron(br, bc).reshape(nr, nc // 2, 2, nr * nc).transpose(2, 0, 1, 3)
    both = both.reshape(nr * nc, nr * nc)
    scale = (er[:, None] + ec[None, :]) / (SUB * SUB)
    values = (SUB * SUB * (DAMP + scale * scale)).reshape(-1)
    whole = np.zeros((width, width), np.float32)
    whole[: nr * nc, : nr * nc] = (both / values) @ both.T
    return whole


def dot(a, b, side=0):
    return lax.dot_general(
        a, b, (((1,), (side,)), ((), ())), precision=highest, preferred_element_type=jnp.float32
    )


def lap(x):
    rows, lanes = x.shape
    beside = pltpu.roll(x, 1, 0) + pltpu.roll(x, rows - 1, 0)
    beside = beside + (pltpu.roll(x, 1, 1) + pltpu.roll(x, lanes - 1, 1))
    return 4.0 * x - beside


def lanes_of(shape):
    return lax.broadcasted_iota(jnp.int32, shape, 1)


def rows_of(shape):
    return lax.broadcasted_iota(jnp.int32, shape, 0)


def total(x):
    return jnp.sum(jnp.sum(x, axis=0, keepdims=True), axis=1, keepdims=True)


def place():
    return lax.axis_index("row"), lax.axis_index("col")


def is_even(index):
    return lax.rem(index, 2) == 0


def column_mask(counts):
    j = lax.axis_index("col")
    lane = lanes_of((1, FC))
    right = jnp.where(j < counts[1] - 1, 320, 256)
    left = jnp.where(j > 0, 320, 384)
    return (lane < right) | (lane >= left)


def edge_mask(counts):
    i = lax.axis_index("row")
    row = rows_of((80, 1))
    first = jnp.where(i > 0, 0, 16)
    last = jnp.where(i < counts[0] - 1, 80, 64)
    return (row >= first) & (row < last) & column_mask(counts)


def table_shape(counts):
    return (-(-2 * counts[0] * counts[1] // 1024) * 8, 128)


def table_of(values, counts):
    i, j = place()
    devices = counts[0] * counts[1]
    shape = table_shape(counts)
    at = rows_of(shape) * 128 + lanes_of(shape) - (i * counts[1] + j)
    return jnp.where(at == 0, values[0], jnp.where(at == devices, values[1], 0.0))


def merged(table, *others):
    for other in others:
        table = jnp.where(table != 0.0, table, other)
    return table


def as_row(table, width):
    return jnp.concatenate([table[k : k + 1] for k in range(width // 128)], axis=1)


def row_of(pairs):
    lane = lanes_of((1, 128))
    row = jnp.zeros((1, 128), jnp.float32)
    for k, (left, right) in enumerate(pairs):
        row = jnp.where(lane == k, left, jnp.where(lane == 64 + k, right, row))
    return row


def near_inverse(counts, inverse):
    i, j = place()
    nr, nc = counts[0], 2 * counts[1]
    shape = (16, inverse.shape[0])
    which = rows_of(shape)
    r = i - 1 + which // 4
    c = 2 * j - 1 + which % 4
    inside = (r >= 0) & (r < nr) & (c >= 0) & (c < nc) & (which < 12)
    at = lax.rem(c + 2, 2) * (nr * counts[1]) + r * counts[1] + (c + 2) // 2 - 1
    return dot(jnp.where(inside & (lanes_of(shape) == at), 1.0, 0.0), inverse)


def as_bands(values):
    lane = lanes_of((1, FC))
    bands = []
    for d in range(3):
        left, first, second, right = values[4 * d : 4 * d + 4]
        bands.append(
            jnp.where(
                lane < 128,
                first,
                jnp.where(lane < 256, second, jnp.where(lane < 320, right, left)),
            )
        )
    return bands


def edge_bands(bands):
    above, on, below = bands
    return jnp.concatenate(
        [
            jnp.broadcast_to(above, (16, FC)),
            jnp.broadcast_to(on, (48, FC)),
            jnp.broadcast_to(below, (16, FC)),
        ],
        axis=0,
    )


def jumps(row):
    step = row - pltpu.roll(row, 1, 1)
    lane = lanes_of((1, FC))
    at = [jnp.sum(jnp.where(lane == k, step, 0.0), axis=1, keepdims=True) for k in (0, 128, 256)]
    return jnp.where(
        (lane < 64) | (lane >= 320), at[0], jnp.where(lane < 192, at[1], at[2])
    )


def edge_steps():
    lane = lanes_of((1, FC))
    up = (lane == 0) | (lane == 128) | (lane == 256)
    down = (lane == FC - 1) | (lane == 127) | (lane == 255)
    return jnp.where(up, 1.0, jnp.where(down, -1.0, 0.0))


def halves_of(x):
    high = x.astype(jnp.bfloat16)
    return high, (x - high.astype(jnp.float32)).astype(jnp.bfloat16)


def product(a, b):
    return lax.dot_general(a, b, (((1,), (0,)), ((), ())), preferred_element_type=jnp.float32)


def column_transform(w, basis_ref):
    high, low = halves_of(pltpu.roll(w, OV, 1))
    cols, rest = halves_of(cols_part(basis_ref))
    cols = jnp.concatenate([cols, rest, cols], axis=0)

    def block(at):
        part = slice(at, at + SPEC)
        return product(jnp.concatenate([high[:, part], high[:, part], low[:, part]], axis=1), cols)

    return jnp.concatenate([block(0), block(128)], axis=1)


def row_transform(u, basis_ref, part):
    high, low = halves_of(u)
    rows = part(basis_ref).astype(jnp.bfloat16)
    return product(rows, jnp.concatenate([high, low, high], axis=0))


def weights(means, basis_ref):
    lane = lanes_of((1, 2 * SPEC))
    mean = jnp.where(lane < SPEC, means[0], means[1])
    return 1.0 / (DAMP + mean * basis_ref[:EXT])


def strips_of(t, basis_ref, deep):
    cols = cols_part(basis_ref)
    left = dot(cols[:deep], t[:, :SPEC], 1)
    right = dot(cols[EXT - deep : EXT], t[:, SPEC:], 1)
    both = dot(jnp.concatenate([left, right], axis=0), rows_t_part(basis_ref)[:, :EXT])
    return both[:deep], both[deep:]


def solution_of(t, basis_ref):
    v = dot(rows_part(basis_ref), t)
    cols = cols_part(basis_ref)
    first, second = dot(v[:, :SPEC], cols), dot(v[:, SPEC:], cols)
    y = jnp.concatenate(
        [first[:, :128], first[:, 128:] + second[:, :128], second[:, 128:]], axis=1
    )
    return pltpu.roll(y, FC - OV, 1)


def core_sums(x):
    return [total(x[:, :128]), total(x[:, 128:256])]


def add_columns(y, from_left, from_right):
    far = from_left.shape[0] - OV
    gap = jnp.zeros((56 - far, EXT), jnp.float32)
    turned = jnp.concatenate(
        [from_right[8:], gap, from_right[:8], from_left[far:], gap, from_left[:far]], axis=0
    )
    back = turned.T
    lane = lanes_of((EXT, 128))
    rolled = pltpu.roll(back, 64, 1)
    first = y[:, :128] + jnp.where(lane < 8, rolled, 0.0)
    second = y[:, 128:256] + jnp.where(lane >= 120, rolled, 0.0)
    third = y[:, 256:] + jnp.where((lane < 16) | (lane >= 112), back, 0.0)
    return jnp.concatenate([first, second, third], axis=1)


def pack_rows(y, deep):
    return jnp.concatenate([y[136:], y[: deep - 8]], axis=0), y[136 - deep : 136]


def edges(y, from_above, from_below):
    far = from_above.shape[0] - OV
    none = jnp.zeros((8, FC), jnp.float32)
    return jnp.concatenate(
        [
            from_above[:8] if far == 16 else none,
            y[136:] + from_above[far - 8 : far],
            y[:8] + from_above[far:],
            y[8:24],
            y[104:120],
            y[120:136] + from_below[:16],
            from_below[16:] if far == 16 else none,
        ],
        axis=0,
    )


def edge_part(frame):
    return jnp.concatenate([frame[144:], frame[:24], frame[104:144]], axis=0)


def with_edges(edge, inner):
    return jnp.concatenate([edge[16:32, :TC], inner, edge[48:64, :TC]], axis=0)


def sides(index, count, a, b):
    even = is_even(index)
    before = jnp.where(index > 0, jnp.where(even, b, a), 0.0)
    after = jnp.where(index < count - 1, jnp.where(even, a, b), 0.0)
    return before, after


def send(index, a_ref, b_ref, before, after):
    even = is_even(index)
    a_ref[...] = jnp.where(even, after, before)
    b_ref[...] = jnp.where(even, before, after)


def begin_kernel(counts, both_ref, b_ref, a_ref, table_ref):
    r, h = both_ref[:TR], both_ref[TR:]
    lane = lanes_of((128, 128))
    packed = jnp.where(
        lane < 16,
        r[:, :128],
        jnp.where(
            lane < 64,
            pltpu.roll(h[:, :128], 16, 1),
            jnp.where(lane < 112, pltpu.roll(h[:, 128:], 112, 1), r[:, 128:]),
        ),
    )
    turned = packed.T
    table = table_of(core_sums(r), counts)
    table_ref[...] = table
    send(
        lax.axis_index("col"),
        a_ref,
        b_ref,
        jnp.concatenate([turned[:32], table], axis=0),
        jnp.concatenate([turned[96:], table], axis=0),
    )


def statistics_kernel(both_ref, table_ref, stats_ref, table_out):
    h = both_ref[TR:]
    mt = h * h * h
    lane, row = lanes_of((1, 256)), rows_of((128, 1))
    along = (lane % 128 != 0) & (lane % 128 != 127)
    top, low = mt[:1], mt[127:]
    side = jnp.sum(jnp.where((row > 0) & (row < 127), mt, 0.0), axis=0, keepdims=True)

    def halves(x):
        return [
            jnp.sum(x[:, :128], axis=1, keepdims=True),
            jnp.sum(x[:, 128:], axis=1, keepdims=True),
        ]

    first, last = lane % 128 == 0, lane % 128 == 127
    zero = jnp.zeros((1, 1), jnp.float32)
    stats_ref[...] = row_of(
        [
            *[[zero, zero]] * 3,
            halves(jnp.where(along, top, 0.0)),
            halves(jnp.where(along, low, 0.0)),
            halves(jnp.where(first, side, 0.0)),
            halves(jnp.where(last, side, 0.0)),
            halves(jnp.where(first, top, 0.0)),
            halves(jnp.where(last, top, 0.0)),
            halves(jnp.where(first, low, 0.0)),
            halves(jnp.where(last, low, 0.0)),
        ]
    )
    table_out[...] = table_ref[...]


def widen_kernel(counts, both_ref, own_ref, gb_ref, ga_ref, r3_ref, h3_ref, b_ref, a_ref, table_ref):
    i, j = place()
    from_left, from_right = sides(j, counts[1], ga_ref[:32], gb_ref[:32])
    turned = jnp.concatenate([from_right, jnp.zeros((64, 128), jnp.float32), from_left], axis=0)
    back = turned.T
    lane = lanes_of((128, 128))
    edge = (lane < 16) | (lane >= 112)
    r3 = jnp.where(edge, back, 0.0)
    h3 = jnp.where(
        lane < 16, pltpu.roll(back, 112, 1), jnp.where(lane >= 112, pltpu.roll(back, 16, 1), 0.0)
    )
    r3_ref[...] = r3
    h3_ref[...] = h3
    r, h = both_ref[:TR], both_ref[TR:]
    table = merged(own_ref[...], ga_ref[32:], gb_ref[32:])
    table_ref[...] = table
    wide = jnp.concatenate([table, jnp.zeros((table.shape[0], FC - 128), jnp.float32)], axis=1)

    def strip(r_rows, h_rows):
        return jnp.concatenate(
            [
                jnp.concatenate([r[r_rows], r3[r_rows]], axis=1),
                jnp.concatenate([h[h_rows], h3[h_rows]], axis=1),
                wide,
            ],
            axis=0,
        )

    send(i, a_ref, b_ref, strip(slice(0, 8), slice(0, 16)), strip(slice(120, 128), slice(112, 128)))


def weights_kernel(both_ref, table_ref, basis_ref, weights_ref, table_out):
    h = both_ref[TR:]
    means = [x / (SUB * SUB) for x in core_sums(h * h * h)]
    weights_ref[...] = weights(means, basis_ref)
    table_out[...] = table_ref[...]


def forward_kernel(both_ref, r3_ref, basis_ref, t_ref):
    r = both_ref[:TR]
    u = column_transform(jnp.concatenate([r, r3_ref[...]], axis=1), basis_ref)
    t_ref[...] = row_transform(u, basis_ref, tile_rows)


def first_kernel(
    counts,
    gb_ref,
    ga_ref,
    tile_ref,
    weights_ref,
    basis_ref,
    table_ref,
    t_ref,
    table_out,
    b_ref,
    a_ref,
):
    i, j = place()
    above, below = sides(i, counts[0], ga_ref[:8], gb_ref[:8])
    u = column_transform(jnp.concatenate([below, above], axis=0), basis_ref)
    t = (tile_ref[...] + row_transform(u, basis_ref, halo_rows)) * weights_ref[...]
    t_ref[...] = t
    send(j, a_ref, b_ref, *strips_of(t, basis_ref, 24))
    table_out[...] = merged(table_ref[...], ga_ref[24:, :128], gb_ref[24:, :128])


def inverse_kernel(counts, t_ref, basis_ref, both_ref, h3_ref, gb_ref, ga_ref, y_ref, m_ref):
    y_ref[...] = solution_of(t_ref[...], basis_ref)
    above, below = sides(lax.axis_index("row"), counts[0], ga_ref[8:24], gb_ref[8:24])
    h = jnp.concatenate([both_ref[TR:], h3_ref[...]], axis=1)
    tall = jnp.concatenate([h, below, above], axis=0)
    m_ref[...] = tall * tall * tall


def columns_kernel(counts, y_ref, *refs):
    i, j = place()
    (ga_ref, gb_ref), refs = (refs[:2] if len(refs) == 7 else refs[1::-1]), refs[2:]
    deep = 24 if len(refs) == 5 else 16
    y = add_columns(y_ref[...], *sides(j, counts[1], ga_ref[:deep], gb_ref[:deep]))
    strips = pack_rows(y, deep)
    if len(refs) == 5:
        table_ref, out_ref, table_out, b_ref, a_ref = refs
        table = merged(table_ref[...], ga_ref[24:, :128], gb_ref[24:, :128])
        table_out[...] = table
        wide = jnp.concatenate([table, jnp.zeros((table.shape[0], FC - 128), jnp.float32)], axis=1)
        strips = [jnp.concatenate([x, wide], axis=0) for x in strips]
    else:
        out_ref, b_ref, a_ref = refs
    out_ref[...] = y
    send(i, a_ref, b_ref, *strips)


def inner_kernel(counts, width, y_ref, m_ref, basis_ref, w_ref, f_ref, gw_ref, gf_ref, near_ref):
    mask = column_mask(counts)
    s = jnp.where(mask, y_ref[8:120], 0.0)
    m = m_ref[8:120]
    w = DAMP * s + lap(m * lap(s))
    w = jnp.where(mask, w[8:104], 0.0) * SHRINK
    f = lap(m * edge_steps())
    f = jnp.where(mask, f[8:104], 0.0) * SHRINK
    w_ref[...] = w[:, :TC]
    f_ref[...] = f[:, :TC]
    gw_ref[...] = row_transform(w, basis_ref, inner_rows)
    gf_ref[...] = row_transform(f, basis_ref, inner_rows)
    near_ref[...] = near_inverse(counts, coarse_part(basis_ref, width))


def second_kernel(
    counts,
    width,
    y_ref,
    m_ref,
    gb_ref,
    ga_ref,
    table_ref,
    inner_w_ref,
    f_ref,
    gw_ref,
    gf_ref,
    near_ref,
    weights_ref,
    basis_ref,
    z_ref,
    w_ref,
    t_ref,
    b_ref,
    a_ref,
):
    i, j = place()
    y = y_ref[...]
    mask = edge_mask(counts)
    s = edges(y, *sides(i, counts[0], ga_ref[:24], gb_ref[:24]))
    s = jnp.where(mask, s, 0.0)
    table = merged(table_ref[...], ga_ref[24:, :128], gb_ref[24:, :128])
    picked = jnp.sum(near_ref[...] * as_row(table, width), axis=1, keepdims=True)
    bands = as_bands([picked[k : k + 1] for k in range(12)])
    coarse = edge_bands(bands)
    m = edge_part(m_ref)
    flow = m * (lap(s) + lap(coarse))
    z = s + coarse
    w = jnp.where(mask, DAMP * z + lap(flow), 0.0) * SHRINK
    step = jumps(bands[1])
    damped = (DAMP * SHRINK) * bands[1]
    z_ref[...] = with_edges(z, y[16:112, :TC] + bands[1][:, :TC])
    w_ref[...] = with_edges(w, inner_w_ref[...] + step[:, :TC] * f_ref[...] + damped[:, :TC])
    lane = lanes_of((EXT, 256))
    ones = jnp.where((lane >= 16) & (lane < 112), rows_t_part(basis_ref), 0.0)
    ones = jnp.sum(ones, axis=1, keepdims=True)
    u = gw_ref[...] + step * gf_ref[...] + ones * damped
    u = u + row_transform(jnp.concatenate([w[8:32], w[48:72]], axis=0), basis_ref, edge_rows)
    t = column_transform(u, basis_ref) * weights_ref[...]
    t_ref[...] = t
    send(j, a_ref, b_ref, *strips_of(t, basis_ref, 16))


def inverse_stats_kernel(t_ref, basis_ref, both_ref, z_ref, w_ref, edge_stats_ref, y_ref, stats_ref):
    y_ref[...] = solution_of(t_ref[...], basis_ref)
    rt, zt, wt = both_ref[:TR], z_ref[...], w_ref[...]
    zero = jnp.zeros((1, 1), jnp.float32)
    sums = [core_sums(rt * zt), core_sums(zt * wt), core_sums(wt), *[[zero, zero]] * 12, core_sums(rt)]
    stats_ref[...] = edge_stats_ref[...] + row_of(sums)


def inner_dots_kernel(counts, y_ref, m_ref, both_ref, w_ref, stats_ref, v_ref, stats_out):
    q = jnp.where(column_mask(counts), y_ref[8:120], 0.0)
    v = (DAMP * q + lap(m_ref[8:120] * lap(q)))[8:104, :TC]
    q = q[8:104, :TC]
    v_ref[...] = v
    rest = [
        core_sums(v),
        core_sums(both_ref[16:112] * q),
        core_sums(w_ref[16:112] * q),
        core_sums(v * q),
    ]
    zero = jnp.zeros((1, 1), jnp.float32)
    stats_out[...] = stats_ref[...] + row_of([[zero, zero]] * 11 + rest)


def dots_kernel(
    counts, y_ref, m_ref, gb_ref, ga_ref, both_ref, w_ref, stats_ref, inner_v_ref, q_ref, v_ref, stats_out
):
    i, j = place()
    y = y_ref[...]
    q = edges(y, *sides(i, counts[0], ga_ref[...], gb_ref[...]))
    q = jnp.where(edge_mask(counts), q, 0.0)
    v = DAMP * q + lap(edge_part(m_ref) * lap(q))
    q_ref[...] = with_edges(q, y[16:112, :TC])
    v_ref[...] = with_edges(v, inner_v_ref[...])
    qe, ve = (jnp.concatenate([x[16:32, :TC], x[48:64, :TC]], axis=0) for x in (q, v))
    re = jnp.concatenate([both_ref[:16], both_ref[112:128]], axis=0)
    we = jnp.concatenate([w_ref[:16], w_ref[112:]], axis=0)
    rest = [core_sums(ve), core_sums(re * qe), core_sums(we * qe), core_sums(ve * qe)]
    zero = jnp.zeros((1, 1), jnp.float32)
    row = stats_ref[...] + row_of([[zero, zero]] * 11 + rest)
    stats_out[...] = jnp.broadcast_to(row, stats_out.shape)


def end_kernel(
    counts,
    width,
    stats_ref,
    basis_ref,
    m_ref,
    f_ref,
    both_ref,
    z_ref,
    w_ref,
    q_ref,
    v_ref,
    solution_ref,
    residual_ref,
):
    i, j = place()
    tiles_c = counts[1]
    devices = counts[0] * tiles_c
    rows = stats_ref[...]
    st = jnp.concatenate([rows, pltpu.roll(rows, 64, 1)], axis=0)
    inverse = coarse_part(basis_ref, width)[: 2 * devices, : 2 * devices]
    g = jnp.broadcast_to(dot(inverse, st)[:, 2:3], st.shape)
    lane, row = lanes_of(st.shape), rows_of(st.shape)
    device = row % devices
    column = device % tiles_c
    on_left = row < devices

    def from_row(distance):
        return pltpu.roll(g, distance % (2 * devices), 0)

    up = jnp.where(device >= tiles_c, from_row(tiles_c), 0.0)
    down = jnp.where(device < devices - tiles_c, from_row(-tiles_c), 0.0)
    left = jnp.where(on_left, jnp.where(column > 0, from_row(1 - devices), 0.0), from_row(devices))
    right = jnp.where(
        on_left, from_row(-devices), jnp.where(column < tiles_c - 1, from_row(devices - 1), 0.0)
    )
    du, dd, dl, dr = g - up, g - down, g - left, g - right
    across = jnp.where(
        (lane == 3) | (lane == 7) | (lane == 8),
        du,
        jnp.where((lane == 4) | (lane == 9) | (lane == 10), dd, 0.0),
    )
    across = across + jnp.where(
        (lane == 5) | (lane == 7) | (lane == 9),
        dl,
        jnp.where((lane == 6) | (lane == 8) | (lane == 10), dr, 0.0),
    )
    factor = jnp.where((lane == 2) | (lane == 15), g, across * across)
    factor = jnp.where(lane == 11, 2.0 * g, factor)
    factor = jnp.where((lane < 2) | ((lane >= 12) & (lane < 15)), 1.0, factor)
    terms = jnp.where(lane == 16, (DAMP * SUB * SUB) * g * g, st * factor)
    sums = jnp.sum(terms, axis=0, keepdims=True)

    def whole(wanted):
        return jnp.sum(jnp.where(wanted, sums, 0.0), axis=1, keepdims=True)

    at = lanes_of((1, 128))
    rz, zw = whole(at == 0), whole(at == 1)
    ry = whole((at == 12) | (at == 15))
    yw = whole((at == 13) | (at == 2))
    yv = whole(((at >= 3) & (at < 12)) | (at == 14) | (at == 16))
    a = rz / zw
    rz1 = rz - a * ry - a * zw + a * a * yw
    beta1 = 1.0 + rz1 / rz
    dad = (beta1 * beta1 * zw - 2.0 * a * beta1 * yw) * (1.0 / SHRINK) + a * a * yv
    a1 = rz1 / dad
    r = i - 1 + lane // 4
    c = 2 * j - 1 + lane % 4
    inside = (r >= 0) & (r < counts[0]) & (c >= 0) & (c < 2 * tiles_c) & (lane < 12)
    where = lax.rem(c + 2, 2) * devices + r * tiles_c + (c + 2) // 2 - 1
    picked = jnp.sum(jnp.where(inside & (row == where), g, 0.0), axis=0, keepdims=True)
    bands = as_bands([picked[:, k : k + 1] for k in range(12)])
    on = bands[1][:, :TC]
    coarse = edge_bands(bands)
    image = DAMP * coarse + lap(edge_part(m_ref) * lap(coarse))
    image = with_edges(image, (jumps(bands[1]) * (1.0 / SHRINK))[:, :TC] * f_ref[...] + DAMP * on)
    y = q_ref[...] + on
    v = v_ref[...] + image
    z, w = z_ref[...], w_ref[...]
    solution_ref[...] = (a * SHRINK) * z + a1 * (beta1 * z - a * y)
    residual_ref[...] = both_ref[:TR] - a * w - a1 * ((beta1 * (1.0 / SHRINK)) * w - a * v)


def call(kernel, outs, *args, flops=10**9):
    shapes = [jax.ShapeDtypeStruct(s, jnp.float32) for s in outs]
    return pl.pallas_call(
        kernel,
        out_shape=shapes,
        compiler_params=pltpu.CompilerParams(vmem_limit_bytes=48 * 1024 * 1024),
        cost_estimate=pl.CostEstimate(flops=flops, bytes_accessed=10**6, transcendentals=0),
    )(*args)


def pairs_from(count, offset):
    found = []
    for k in range(offset, count, 2):
        found += [(k, (k + 1) % count), ((k + 1) % count, k)]
    return found


def odd_pairs(counts, axis, bit):
    found = []
    for i in range(counts[0]):
        for j in range(counts[1]):
            at = [i, j]
            if bit and at[axis] in (0, counts[axis] - 1):
                at[1 - axis] ^= bit
            else:
                at[axis] = (at[axis] + (1 if at[axis] % 2 else -1)) % counts[axis]
            found.append((i * counts[1] + j, at[0] * counts[1] + at[1]))
    return found


def xor_pairs(counts, rows, cols):
    flat = [(i, j) for i in range(counts[0]) for j in range(counts[1])]
    return [(i * counts[1] + j, (i ^ rows) * counts[1] + (j ^ cols)) for i, j in flat]


def spreads(counts):
    known = np.eye(counts[0] * counts[1], dtype=bool)

    def meet(*swaps):
        return np.logical_or.reduce([known, *(known[[b for _, b in pairs]] for pairs in swaps)])

    even = [xor_pairs(counts, 0, 1), xor_pairs(counts, 1, 0)]
    own = meet(xor_pairs(counts, 2, 3))
    known = meet(even[0], odd_pairs(counts, 1, 1))
    known = meet(even[1], odd_pairs(counts, 0, 0), xor_pairs(counts, 4, 2)) | own
    known = meet(even[0], odd_pairs(counts, 1, 2))
    return meet(even[1], odd_pairs(counts, 0, 1)).all()


def body(counts, height, noise):
    nr, nc = counts
    devices = nr * nc
    width = max(128, devices * 2)
    basis = jnp.asarray(constants(nr, 2 * nc, width))
    both_axes = ("row", "col")
    depth = table_shape(counts)[0]

    def swap(a, b, axis, bit=1):
        gb = lax.ppermute(b, both_axes, odd_pairs(counts, both_axes.index(axis), bit))
        return lax.ppermute(a, axis, pairs_from(lax.axis_size(axis), 0)), gb

    def small_swap(x, rows, cols):
        return lax.ppermute(x, both_axes, xor_pairs(counts, rows, cols))

    both = jnp.pad(noise, ((0, TR), (0, 0))) + jnp.pad(height, ((TR, 0), (0, 0)))
    b, a, table = call(
        functools.partial(begin_kernel, counts), [(32 + depth, 128)] * 2 + [(depth, 128)], both
    )
    if not spreads(counts):
        for axis, count in enumerate(counts):
            bit = 1
            while bit < count:
                table = table + small_swap(table, *((0, bit) if axis else (bit, 0)))
                bit *= 2
    ga, gb = swap(a, b, "col")
    edge_stats, own = call(statistics_kernel, [(1, 128), (depth, 128)], both, table)
    far = [small_swap(own, 2, 3)]
    r3, h3, b, a, table = call(
        functools.partial(widen_kernel, counts),
        [(128, 128)] * 2 + [(24 + depth, FC)] * 2 + [(depth, 128)],
        both,
        table,
        gb,
        ga,
    )
    ga, gb = swap(a, b, "row", 0)
    weight, table = call(weights_kernel, [(EXT, 2 * SPEC), (depth, 128)], both, table, basis)
    far.append(small_swap(table, 4, 2))
    t = call(forward_kernel, [(EXT, 2 * SPEC)], both, r3, basis)[0]
    t, table, b, a = call(
        functools.partial(first_kernel, counts),
        [(EXT, 2 * SPEC), (depth, 128)] + [(24, EXT)] * 2,
        gb,
        ga,
        t,
        weight,
        basis,
        table,
    )
    table = merged(table, *far)
    wide = jnp.pad(table, ((0, 0), (0, EXT - 128)))
    y, m = call(
        functools.partial(inverse_kernel, counts),
        [(EXT, FC), (FR, FC)],
        t,
        basis,
        both,
        h3,
        gb,
        ga,
    )
    ga, gb = swap(*(jnp.concatenate([x, wide], axis=0) for x in (a, b)), "col", 2)
    y, table, b, a = call(
        functools.partial(columns_kernel, counts),
        [(EXT, FC), (depth, 128)] + [(24 + depth, FC)] * 2,
        y,
        ga,
        gb,
        table,
    )
    ga, gb = swap(a, b, "row")
    inner_w, f, gw, gf, near = call(
        functools.partial(inner_kernel, counts, width),
        [(96, TC)] * 2 + [(EXT, FC)] * 2 + [(16, width)],
        y,
        m,
        basis,
    )
    z, w, t, b, a = call(
        functools.partial(second_kernel, counts, width),
        [(TR, TC)] * 2 + [(EXT, 2 * SPEC)] + [(16, EXT)] * 2,
        y,
        m,
        gb,
        ga,
        table,
        inner_w,
        f,
        gw,
        gf,
        near,
        weight,
        basis,
    )
    ga, gb = swap(a, b, "col")
    y, stats = call(inverse_stats_kernel, [(EXT, FC), (1, 128)], t, basis, both, z, w, edge_stats)
    y, b, a = call(
        functools.partial(columns_kernel, counts), [(EXT, FC)] + [(16, FC)] * 2, y, gb, ga
    )
    ga, gb = swap(a, b, "row")
    inner_v, stats = call(
        functools.partial(inner_dots_kernel, counts),
        [(96, TC), (1, 128)],
        y,
        m,
        both,
        w,
        stats,
    )
    q, v, stats = call(
        functools.partial(dots_kernel, counts),
        [(TR, TC)] * 2 + [(devices, 128)],
        y,
        m,
        gb,
        ga,
        both,
        w,
        stats,
        inner_v,
    )
    stats = lax.all_to_all(stats, both_axes, 0, 0, tiled=True)
    return tuple(
        call(
            functools.partial(end_kernel, counts, width),
            [(TR, TC)] * 2,
            stats,
            basis,
            m,
            f,
            both,
            z,
            w,
            q,
            v,
        )
    )


def solution(mesh):
    counts = (mesh.shape["row"], mesh.shape["col"])
    spec = P("row", "col")
    return jax.shard_map(
        functools.partial(body, counts),
        mesh=mesh,
        in_specs=(spec, spec),
        out_specs=(spec, spec),
        check_vma=False,
    )
```

```python
import functools

import jax
import jax.numpy as jnp
import ml_dtypes
import numpy as np
from jax import lax
from jax.experimental import pallas as pl
from jax.experimental.pallas import tpu as pltpu
from jax.sharding import PartitionSpec as P

SUB = 128
OV = 8
EXT = SUB + 2 * OV
DAMP = 2.0**-28
SHRINK = 2.0**-20

TR, TC = 128, 256
FR, FC = 160, 384
SPEC = 256

highest = lax.Precision.HIGHEST


def sine(count):
    k = np.arange(1, count + 1, dtype=np.float64)
    basis = np.sqrt(2.0 / (count + 1.0)) * np.sin(np.pi * k[:, None] * k[None, :] / (count + 1.0))
    return basis, 2.0 - 2.0 * np.cos(np.pi * k / (count + 1.0))


def block_constants():
    basis, eig = sine(EXT)
    rows = np.roll(basis, -OV, 0)
    cols = np.pad(basis, ((0, SPEC - EXT), (0, SPEC - EXT)))
    scale = np.pad((eig[:, None] + eig[None, :]) ** 2, ((0, 0), (0, SPEC - EXT)))
    wide = lambda x: np.pad(x, ((0, 0), (0, 2 * SPEC - x.shape[1])))
    high = rows.T.astype(ml_dtypes.bfloat16).astype(np.float64)
    low = (rows.T - high).astype(ml_dtypes.bfloat16).astype(np.float64)
    tile = np.concatenate([x[:, :SUB] for x in (high, high, low)], 1)
    halo = np.concatenate([x[:, SUB:] for x in (high, high, low)], 1)
    inner = np.concatenate([x[:, 16:112] for x in (high, high, low)], 1)
    at = [*range(136, 144), *range(16), *range(112, 136)]
    edge = np.concatenate([x[:, at] for x in (high, high, low)], 1)
    turned = np.hstack([rows.T, np.zeros((EXT, 256 - EXT)), edge])
    return [np.tile(scale, (1, 2)), *(wide(x) for x in (rows, turned, cols, inner, np.hstack([tile, halo])))]


def rows_part(ref):
    return ref[EXT : 2 * EXT, :EXT]


def rows_t_part(ref):
    return ref[2 * EXT : 3 * EXT, :256]


def cols_part(ref):
    return ref[3 * EXT : 3 * EXT + SPEC, :SPEC]


def inner_rows(ref):
    at = 3 * EXT + SPEC
    return ref[at : at + EXT, : 3 * 96]


def edge_rows(ref):
    return ref[2 * EXT : 3 * EXT, 256 : 256 + 3 * 48]


def tile_rows(ref):
    at = 4 * EXT + SPEC
    return ref[at : at + EXT, : 3 * SUB]


def halo_rows(ref):
    at = 4 * EXT + SPEC
    return ref[at : at + EXT, 3 * SUB : 3 * EXT]


def coarse_part(ref, width):
    at, lanes = 5 * EXT + SPEC, 2 * SPEC
    parts = [ref[at + k * width : at + (k + 1) * width] for k in range(-(-width // lanes))]
    return (parts[0] if len(parts) == 1 else jnp.concatenate(parts, axis=1))[:, :width]


def constants(nr, nc, width):
    lanes = 2 * SPEC
    inverse = coarse_inverse(nr, nc, -(-width // lanes) * lanes)[:width]
    parts = [*block_constants(), *np.split(inverse, inverse.shape[1] // lanes, 1)]
    return np.concatenate(parts).astype(np.float32)


def coarse_inverse(nr, nc, width):
    br, er = sine(nr)
    bc, ec = sine(nc)
    both = np.kron(br, bc).reshape(nr, nc // 2, 2, nr * nc).transpose(2, 0, 1, 3)
    both = both.reshape(nr * nc, nr * nc)
    scale = (er[:, None] + ec[None, :]) / (SUB * SUB)
    values = (SUB * SUB * (DAMP + scale * scale)).reshape(-1)
    whole = np.zeros((width, width), np.float32)
    whole[: nr * nc, : nr * nc] = (both / values) @ both.T
    return whole


def dot(a, b, side=0):
    return lax.dot_general(
        a, b, (((1,), (side,)), ((), ())), precision=highest, preferred_element_type=jnp.float32
    )


def lap(x):
    rows, lanes = x.shape
    beside = pltpu.roll(x, 1, 0) + pltpu.roll(x, rows - 1, 0)
    beside = beside + (pltpu.roll(x, 1, 1) + pltpu.roll(x, lanes - 1, 1))
    return 4.0 * x - beside


def lanes_of(shape):
    return lax.broadcasted_iota(jnp.int32, shape, 1)


def rows_of(shape):
    return lax.broadcasted_iota(jnp.int32, shape, 0)


def total(x):
    return jnp.sum(jnp.sum(x, axis=0, keepdims=True), axis=1, keepdims=True)


def place():
    return lax.axis_index("row"), lax.axis_index("col")


def is_even(index):
    return lax.rem(index, 2) == 0


def column_mask(counts):
    j = lax.axis_index("col")
    lane = lanes_of((1, FC))
    right = jnp.where(j < counts[1] - 1, 320, 256)
    left = jnp.where(j > 0, 320, 384)
    return (lane < right) | (lane >= left)


def edge_mask(counts):
    i = lax.axis_index("row")
    row = rows_of((80, 1))
    first = jnp.where(i > 0, 0, 16)
    last = jnp.where(i < counts[0] - 1, 80, 64)
    return (row >= first) & (row < last) & column_mask(counts)


def table_shape(counts):
    return (-(-2 * counts[0] * counts[1] // 1024) * 8, 128)


def table_of(values, counts):
    i, j = place()
    devices = counts[0] * counts[1]
    shape = table_shape(counts)
    at = rows_of(shape) * 128 + lanes_of(shape) - (i * counts[1] + j)
    return jnp.where(at == 0, values[0], jnp.where(at == devices, values[1], 0.0))


def merged(table, *others):
    for other in others:
        table = jnp.where(table != 0.0, table, other)
    return table


def as_row(table, width):
    return jnp.concatenate([table[k : k + 1] for k in range(width // 128)], axis=1)


def row_of(pairs):
    lane = lanes_of((1, 128))
    row = jnp.zeros((1, 128), jnp.float32)
    for k, (left, right) in enumerate(pairs):
        row = jnp.where(lane == k, left, jnp.where(lane == 64 + k, right, row))
    return row


def near_inverse(counts, inverse):
    i, j = place()
    nr, nc = counts[0], 2 * counts[1]
    shape = (16, inverse.shape[0])
    which = rows_of(shape)
    r = i - 1 + which // 4
    c = 2 * j - 1 + which % 4
    inside = (r >= 0) & (r < nr) & (c >= 0) & (c < nc) & (which < 12)
    at = lax.rem(c + 2, 2) * (nr * counts[1]) + r * counts[1] + (c + 2) // 2 - 1
    return dot(jnp.where(inside & (lanes_of(shape) == at), 1.0, 0.0), inverse)


def as_bands(values):
    lane = lanes_of((1, FC))
    bands = []
    for d in range(3):
        left, first, second, right = values[4 * d : 4 * d + 4]
        bands.append(
            jnp.where(
                lane < 128,
                first,
                jnp.where(lane < 256, second, jnp.where(lane < 320, right, left)),
            )
        )
    return bands


def edge_bands(bands):
    above, on, below = bands
    return jnp.concatenate(
        [
            jnp.broadcast_to(above, (16, FC)),
            jnp.broadcast_to(on, (48, FC)),
            jnp.broadcast_to(below, (16, FC)),
        ],
        axis=0,
    )


def jumps(row):
    step = row - pltpu.roll(row, 1, 1)
    lane = lanes_of((1, FC))
    at = [jnp.sum(jnp.where(lane == k, step, 0.0), axis=1, keepdims=True) for k in (0, 128, 256)]
    return jnp.where(
        (lane < 64) | (lane >= 320), at[0], jnp.where(lane < 192, at[1], at[2])
    )


def edge_steps():
    lane = lanes_of((1, FC))
    up = (lane == 0) | (lane == 128) | (lane == 256)
    down = (lane == FC - 1) | (lane == 127) | (lane == 255)
    return jnp.where(up, 1.0, jnp.where(down, -1.0, 0.0))


def halves_of(x):
    high = x.astype(jnp.bfloat16)
    return high, (x - high.astype(jnp.float32)).astype(jnp.bfloat16)


def product(a, b):
    return lax.dot_general(a, b, (((1,), (0,)), ((), ())), preferred_element_type=jnp.float32)


def column_transform(w, basis_ref):
    high, low = halves_of(pltpu.roll(w, OV, 1))
    cols, rest = halves_of(cols_part(basis_ref))
    cols = jnp.concatenate([cols, rest, cols], axis=0)

    def block(at):
        part = slice(at, at + SPEC)
        return product(jnp.concatenate([high[:, part], high[:, part], low[:, part]], axis=1), cols)

    return jnp.concatenate([block(0), block(128)], axis=1)


def row_transform(u, basis_ref, part):
    high, low = halves_of(u)
    rows = part(basis_ref).astype(jnp.bfloat16)
    return product(rows, jnp.concatenate([high, low, high], axis=0))


def weights(means, basis_ref):
    lane = lanes_of((1, 2 * SPEC))
    mean = jnp.where(lane < SPEC, means[0], means[1])
    return 1.0 / (DAMP + mean * basis_ref[:EXT])


def strips_of(t, basis_ref, deep):
    cols = cols_part(basis_ref)
    left = dot(cols[:deep], t[:, :SPEC], 1)
    right = dot(cols[EXT - deep : EXT], t[:, SPEC:], 1)
    both = dot(jnp.concatenate([left, right], axis=0), rows_t_part(basis_ref)[:, :EXT])
    return both[:deep], both[deep:]


def solution_of(t, basis_ref):
    v = dot(rows_part(basis_ref), t)
    cols = cols_part(basis_ref)
    first, second = dot(v[:, :SPEC], cols), dot(v[:, SPEC:], cols)
    y = jnp.concatenate(
        [first[:, :128], first[:, 128:] + second[:, :128], second[:, 128:]], axis=1
    )
    return pltpu.roll(y, FC - OV, 1)


def core_sums(x):
    return [total(x[:, :128]), total(x[:, 128:256])]


def add_columns(y, from_left, from_right):
    far = from_left.shape[0] - OV
    gap = jnp.zeros((56 - far, EXT), jnp.float32)
    turned = jnp.concatenate(
        [from_right[8:], gap, from_right[:8], from_left[far:], gap, from_left[:far]], axis=0
    )
    back = turned.T
    lane = lanes_of((EXT, 128))
    rolled = pltpu.roll(back, 64, 1)
    first = y[:, :128] + jnp.where(lane < 8, rolled, 0.0)
    second = y[:, 128:256] + jnp.where(lane >= 120, rolled, 0.0)
    third = y[:, 256:] + jnp.where((lane < 16) | (lane >= 112), back, 0.0)
    return jnp.concatenate([first, second, third], axis=1)


def pack_rows(y, deep):
    return jnp.concatenate([y[136:], y[: deep - 8]], axis=0), y[136 - deep : 136]


def edges(y, from_above, from_below):
    far = from_above.shape[0] - OV
    none = jnp.zeros((8, FC), jnp.float32)
    return jnp.concatenate(
        [
            from_above[:8] if far == 16 else none,
            y[136:] + from_above[far - 8 : far],
            y[:8] + from_above[far:],
            y[8:24],
            y[104:120],
            y[120:136] + from_below[:16],
            from_below[16:] if far == 16 else none,
        ],
        axis=0,
    )


def edge_part(frame):
    return jnp.concatenate([frame[144:], frame[:24], frame[104:144]], axis=0)


def with_edges(edge, inner):
    return jnp.concatenate([edge[16:32, :TC], inner, edge[48:64, :TC]], axis=0)


def sides(index, count, a, b):
    even = is_even(index)
    before = jnp.where(index > 0, jnp.where(even, b, a), 0.0)
    after = jnp.where(index < count - 1, jnp.where(even, a, b), 0.0)
    return before, after


def fold(rows, table):
    lane = lanes_of((8, 128))
    free = (lane >= 32) & (lane < 96)
    third = jnp.concatenate(
        [
            jnp.where(free, pltpu.roll(table, 32, 1), rows[:8, 256:]),
            jnp.where(free, pltpu.roll(table, 96, 1), rows[8:16, 256:]),
            rows[16:, 256:],
        ],
        axis=0,
    )
    return jnp.concatenate([rows[:, :256], third], axis=1)


def unfold(ref):
    low, high = ref[:8, 256:], ref[8:16, 256:]
    return jnp.where(lanes_of((8, 128)) < 64, pltpu.roll(low, 96, 1), pltpu.roll(high, 32, 1))


def row_sides(index, count, ga_ref, gb_ref, rows):
    lane = lanes_of((1, FC))
    used = (lane < 288) | (lane >= 352)
    return [jnp.where(used, x, 0.0) for x in sides(index, count, ga_ref[rows], gb_ref[rows])]


def send(index, a_ref, b_ref, before, after):
    even = is_even(index)
    a_ref[...] = jnp.where(even, after, before)
    b_ref[...] = jnp.where(even, before, after)


def begin_kernel(counts, both_ref, b_ref, a_ref, table_ref):
    r, h = both_ref[:TR], both_ref[TR:]
    lane = lanes_of((128, 128))
    packed = jnp.where(
        lane < 16,
        r[:, :128],
        jnp.where(
            lane < 64,
            pltpu.roll(h[:, :128], 16, 1),
            jnp.where(lane < 112, pltpu.roll(h[:, 128:], 112, 1), r[:, 128:]),
        ),
    )
    turned = packed.T
    table = table_of(core_sums(r), counts)
    table_ref[...] = table
    send(
        lax.axis_index("col"),
        a_ref,
        b_ref,
        jnp.concatenate([turned[:32], table], axis=0),
        jnp.concatenate([turned[96:], table], axis=0),
    )


def widen_kernel(counts, both_ref, own_ref, gb_ref, ga_ref, r3_ref, h3_ref, b_ref, a_ref, table_ref):
    i, j = place()
    from_left, from_right = sides(j, counts[1], ga_ref[:32], gb_ref[:32])
    turned = jnp.concatenate([from_right, jnp.zeros((64, 128), jnp.float32), from_left], axis=0)
    back = turned.T
    lane = lanes_of((128, 128))
    edge = (lane < 16) | (lane >= 112)
    r3 = jnp.where(edge, back, 0.0)
    h3 = jnp.where(
        lane < 16, pltpu.roll(back, 112, 1), jnp.where(lane >= 112, pltpu.roll(back, 16, 1), 0.0)
    )
    r3_ref[...] = r3
    h3_ref[...] = h3
    r, h = both_ref[:TR], both_ref[TR:]
    table = merged(own_ref[...], ga_ref[32:], gb_ref[32:])
    table_ref[...] = table

    def strip(r_rows, h_rows):
        rows = jnp.concatenate(
            [
                jnp.concatenate([r[r_rows], r3[r_rows]], axis=1),
                jnp.concatenate([h[h_rows], h3[h_rows]], axis=1),
            ],
            axis=0,
        )
        return fold(rows, table)

    send(i, a_ref, b_ref, strip(slice(0, 8), slice(0, 16)), strip(slice(120, 128), slice(112, 128)))


def weights_kernel(both_ref, table_ref, basis_ref, weights_ref, table_out):
    h = both_ref[TR:]
    means = [x / (SUB * SUB) for x in core_sums(h * h * h)]
    weights_ref[...] = weights(means, basis_ref)
    table_out[...] = table_ref[...]


def forward_kernel(both_ref, r3_ref, basis_ref, t_ref):
    r = both_ref[:TR]
    u = column_transform(jnp.concatenate([r, r3_ref[...]], axis=1), basis_ref)
    t_ref[...] = row_transform(u, basis_ref, tile_rows)


def first_kernel(
    counts,
    gb_ref,
    ga_ref,
    tile_ref,
    weights_ref,
    basis_ref,
    table_ref,
    t_ref,
    table_out,
    b_ref,
    a_ref,
):
    i, j = place()
    above, below = row_sides(i, counts[0], ga_ref, gb_ref, slice(0, 8))
    u = column_transform(jnp.concatenate([below, above], axis=0), basis_ref)
    t = (tile_ref[...] + row_transform(u, basis_ref, halo_rows)) * weights_ref[...]
    t_ref[...] = t
    send(j, a_ref, b_ref, *strips_of(t, basis_ref, 24))
    table_out[...] = merged(table_ref[...], unfold(ga_ref), unfold(gb_ref))


def inverse_kernel(counts, t_ref, basis_ref, both_ref, h3_ref, gb_ref, ga_ref, y_ref, m_ref):
    y_ref[...] = solution_of(t_ref[...], basis_ref)
    above, below = row_sides(lax.axis_index("row"), counts[0], ga_ref, gb_ref, slice(8, 24))
    h = jnp.concatenate([both_ref[TR:], h3_ref[...]], axis=1)
    tall = jnp.concatenate([h, below, above], axis=0)
    m_ref[...] = tall * tall * tall


def columns_kernel(counts, y_ref, *refs):
    i, j = place()
    (ga_ref, gb_ref), refs = (refs[:2] if len(refs) == 7 else refs[1::-1]), refs[2:]
    deep = 24 if len(refs) == 5 else 16
    y = add_columns(y_ref[...], *sides(j, counts[1], ga_ref[:deep], gb_ref[:deep]))
    strips = pack_rows(y, deep)
    if len(refs) == 5:
        table_ref, out_ref, table_out, b_ref, a_ref = refs
        table = merged(table_ref[...], ga_ref[24:, :128], gb_ref[24:, :128])
        table_out[...] = table
        strips = [fold(x, table) for x in strips]
    else:
        out_ref, b_ref, a_ref = refs
    out_ref[...] = y
    send(i, a_ref, b_ref, *strips)


def inner_kernel(counts, width, y_ref, m_ref, basis_ref, w_ref, f_ref, gw_ref, gf_ref, near_ref):
    mask = column_mask(counts)
    s = jnp.where(mask, y_ref[8:120], 0.0)
    m = m_ref[8:120]
    w = DAMP * s + lap(m * lap(s))
    w = jnp.where(mask, w[8:104], 0.0) * SHRINK
    f = lap(m * edge_steps())
    f = jnp.where(mask, f[8:104], 0.0) * SHRINK
    w_ref[...] = w[:, :TC]
    f_ref[...] = f[:, :TC]
    gw_ref[...] = row_transform(w, basis_ref, inner_rows)
    gf_ref[...] = row_transform(f, basis_ref, inner_rows)
    near_ref[...] = near_inverse(counts, coarse_part(basis_ref, width))


def second_kernel(
    counts,
    width,
    y_ref,
    m_ref,
    gb_ref,
    ga_ref,
    table_ref,
    inner_w_ref,
    f_ref,
    gw_ref,
    gf_ref,
    near_ref,
    weights_ref,
    basis_ref,
    z_ref,
    w_ref,
    t_ref,
    b_ref,
    a_ref,
):
    i, j = place()
    y = y_ref[...]
    mask = edge_mask(counts)
    s = edges(y, *row_sides(i, counts[0], ga_ref, gb_ref, slice(0, 24)))
    s = jnp.where(mask, s, 0.0)
    table = merged(table_ref[...], unfold(ga_ref), unfold(gb_ref))
    picked = jnp.sum(near_ref[...] * as_row(table, width), axis=1, keepdims=True)
    bands = as_bands([picked[k : k + 1] for k in range(12)])
    coarse = edge_bands(bands)
    m = edge_part(m_ref)
    flow = m * (lap(s) + lap(coarse))
    z = s + coarse
    w = jnp.where(mask, DAMP * z + lap(flow), 0.0) * SHRINK
    step = jumps(bands[1])
    damped = (DAMP * SHRINK) * bands[1]
    z_ref[...] = with_edges(z, y[16:112, :TC] + bands[1][:, :TC])
    w_ref[...] = with_edges(w, inner_w_ref[...] + step[:, :TC] * f_ref[...] + damped[:, :TC])
    lane = lanes_of((EXT, 256))
    ones = jnp.where((lane >= 16) & (lane < 112), rows_t_part(basis_ref), 0.0)
    ones = jnp.sum(ones, axis=1, keepdims=True)
    u = gw_ref[...] + step * gf_ref[...] + ones * damped
    u = u + row_transform(jnp.concatenate([w[8:32], w[48:72]], axis=0), basis_ref, edge_rows)
    t = column_transform(u, basis_ref) * weights_ref[...]
    t_ref[...] = t
    send(j, a_ref, b_ref, *strips_of(t, basis_ref, 16))


def inverse_stats_kernel(t_ref, basis_ref, both_ref, m_ref, z_ref, w_ref, y_ref, stats_ref):
    y_ref[...] = solution_of(t_ref[...], basis_ref)
    rt, mt, zt, wt = both_ref[:TR], m_ref[:TR, :TC], z_ref[...], w_ref[...]
    lane, row = lanes_of((1, 256)), rows_of((128, 1))
    along = (lane % 128 != 0) & (lane % 128 != 127)
    top, low = mt[:1], mt[127:]
    side = jnp.sum(jnp.where((row > 0) & (row < 127), mt, 0.0), axis=0, keepdims=True)

    def halves(x):
        return [
            jnp.sum(x[:, :128], axis=1, keepdims=True),
            jnp.sum(x[:, 128:], axis=1, keepdims=True),
        ]

    first, last = lane % 128 == 0, lane % 128 == 127
    zero = jnp.zeros((1, 1), jnp.float32)
    stats_ref[...] = row_of(
        [
            core_sums(rt * zt),
            core_sums(zt * wt),
            core_sums(wt),
            halves(jnp.where(along, top, 0.0)),
            halves(jnp.where(along, low, 0.0)),
            halves(jnp.where(first, side, 0.0)),
            halves(jnp.where(last, side, 0.0)),
            halves(jnp.where(first, top, 0.0)),
            halves(jnp.where(last, top, 0.0)),
            halves(jnp.where(first, low, 0.0)),
            halves(jnp.where(last, low, 0.0)),
            *[[zero, zero]] * 4,
            core_sums(rt),
        ]
    )


def inner_dots_kernel(counts, y_ref, m_ref, both_ref, w_ref, stats_ref, v_ref, stats_out):
    q = jnp.where(column_mask(counts), y_ref[8:120], 0.0)
    v = (DAMP * q + lap(m_ref[8:120] * lap(q)))[8:104, :TC]
    q = q[8:104, :TC]
    v_ref[...] = v
    rest = [
        core_sums(v),
        core_sums(both_ref[16:112] * q),
        core_sums(w_ref[16:112] * q),
        core_sums(v * q),
    ]
    zero = jnp.zeros((1, 1), jnp.float32)
    stats_out[...] = stats_ref[...] + row_of([[zero, zero]] * 11 + rest)


def dots_kernel(
    counts, y_ref, m_ref, gb_ref, ga_ref, both_ref, w_ref, stats_ref, inner_v_ref, q_ref, v_ref, stats_out
):
    i, j = place()
    y = y_ref[...]
    q = edges(y, *sides(i, counts[0], ga_ref[...], gb_ref[...]))
    q = jnp.where(edge_mask(counts), q, 0.0)
    v = DAMP * q + lap(edge_part(m_ref) * lap(q))
    q_ref[...] = with_edges(q, y[16:112, :TC])
    v_ref[...] = with_edges(v, inner_v_ref[...])
    qe, ve = (jnp.concatenate([x[16:32, :TC], x[48:64, :TC]], axis=0) for x in (q, v))
    re = jnp.concatenate([both_ref[:16], both_ref[112:128]], axis=0)
    we = jnp.concatenate([w_ref[:16], w_ref[112:]], axis=0)
    rest = [core_sums(ve), core_sums(re * qe), core_sums(we * qe), core_sums(ve * qe)]
    zero = jnp.zeros((1, 1), jnp.float32)
    row = stats_ref[...] + row_of([[zero, zero]] * 11 + rest)
    stats_out[...] = jnp.broadcast_to(row, stats_out.shape)


def end_kernel(
    counts,
    width,
    stats_ref,
    basis_ref,
    m_ref,
    f_ref,
    both_ref,
    z_ref,
    w_ref,
    q_ref,
    v_ref,
    solution_ref,
    residual_ref,
):
    i, j = place()
    tiles_c = counts[1]
    devices = counts[0] * tiles_c
    rows = stats_ref[...]
    st = jnp.concatenate([rows, pltpu.roll(rows, 64, 1)], axis=0)
    inverse = coarse_part(basis_ref, width)[: 2 * devices, : 2 * devices]
    g = jnp.broadcast_to(dot(inverse, st)[:, 2:3], st.shape)
    lane, row = lanes_of(st.shape), rows_of(st.shape)
    device = row % devices
    column = device % tiles_c
    on_left = row < devices

    def from_row(distance):
        return pltpu.roll(g, distance % (2 * devices), 0)

    up = jnp.where(device >= tiles_c, from_row(tiles_c), 0.0)
    down = jnp.where(device < devices - tiles_c, from_row(-tiles_c), 0.0)
    left = jnp.where(on_left, jnp.where(column > 0, from_row(1 - devices), 0.0), from_row(devices))
    right = jnp.where(
        on_left, from_row(-devices), jnp.where(column < tiles_c - 1, from_row(devices - 1), 0.0)
    )
    du, dd, dl, dr = g - up, g - down, g - left, g - right
    across = jnp.where(
        (lane == 3) | (lane == 7) | (lane == 8),
        du,
        jnp.where((lane == 4) | (lane == 9) | (lane == 10), dd, 0.0),
    )
    across = across + jnp.where(
        (lane == 5) | (lane == 7) | (lane == 9),
        dl,
        jnp.where((lane == 6) | (lane == 8) | (lane == 10), dr, 0.0),
    )
    factor = jnp.where((lane == 2) | (lane == 15), g, across * across)
    factor = jnp.where(lane == 11, 2.0 * g, factor)
    factor = jnp.where((lane < 2) | ((lane >= 12) & (lane < 15)), 1.0, factor)
    terms = jnp.where(lane == 16, (DAMP * SUB * SUB) * g * g, st * factor)
    sums = jnp.sum(terms, axis=0, keepdims=True)

    def whole(wanted):
        return jnp.sum(jnp.where(wanted, sums, 0.0), axis=1, keepdims=True)

    at = lanes_of((1, 128))
    rz, zw = whole(at == 0), whole(at == 1)
    ry = whole((at == 12) | (at == 15))
    yw = whole((at == 13) | (at == 2))
    yv = whole(((at >= 3) & (at < 12)) | (at == 14) | (at == 16))
    a = rz / zw
    rz1 = rz - a * ry - a * zw + a * a * yw
    beta1 = 1.0 + rz1 / rz
    dad = (beta1 * beta1 * zw - 2.0 * a * beta1 * yw) * (1.0 / SHRINK) + a * a * yv
    a1 = rz1 / dad
    r = i - 1 + lane // 4
    c = 2 * j - 1 + lane % 4
    inside = (r >= 0) & (r < counts[0]) & (c >= 0) & (c < 2 * tiles_c) & (lane < 12)
    where = lax.rem(c + 2, 2) * devices + r * tiles_c + (c + 2) // 2 - 1
    picked = jnp.sum(jnp.where(inside & (row == where), g, 0.0), axis=0, keepdims=True)
    bands = as_bands([picked[:, k : k + 1] for k in range(12)])
    on = bands[1][:, :TC]
    coarse = edge_bands(bands)
    image = DAMP * coarse + lap(edge_part(m_ref) * lap(coarse))
    image = with_edges(image, (jumps(bands[1]) * (1.0 / SHRINK))[:, :TC] * f_ref[...] + DAMP * on)
    y = q_ref[...] + on
    v = v_ref[...] + image
    z, w = z_ref[...], w_ref[...]
    solution_ref[...] = (a * SHRINK) * z + a1 * (beta1 * z - a * y)
    residual_ref[...] = both_ref[:TR] - a * w - a1 * ((beta1 * (1.0 / SHRINK)) * w - a * v)


def call(kernel, outs, *args, flops=10**9):
    shapes = [jax.ShapeDtypeStruct(s, jnp.float32) for s in outs]
    return pl.pallas_call(
        kernel,
        out_shape=shapes,
        compiler_params=pltpu.CompilerParams(vmem_limit_bytes=48 * 1024 * 1024),
        cost_estimate=pl.CostEstimate(flops=flops, bytes_accessed=10**6, transcendentals=0),
    )(*args)


def pairs_from(count, offset):
    found = []
    for k in range(offset, count, 2):
        found += [(k, (k + 1) % count), ((k + 1) % count, k)]
    return found


def odd_pairs(counts, axis, bit):
    found = []
    for i in range(counts[0]):
        for j in range(counts[1]):
            at = [i, j]
            if bit and at[axis] in (0, counts[axis] - 1):
                at[1 - axis] ^= bit
            else:
                at[axis] = (at[axis] + (1 if at[axis] % 2 else -1)) % counts[axis]
            found.append((i * counts[1] + j, at[0] * counts[1] + at[1]))
    return found


def xor_pairs(counts, rows, cols):
    flat = [(i, j) for i in range(counts[0]) for j in range(counts[1])]
    return [(i * counts[1] + j, (i ^ rows) * counts[1] + (j ^ cols)) for i, j in flat]


def spreads(counts):
    known = np.eye(counts[0] * counts[1], dtype=bool)

    def meet(*swaps):
        return np.logical_or.reduce([known, *(known[[b for _, b in pairs]] for pairs in swaps)])

    even = [xor_pairs(counts, 0, 1), xor_pairs(counts, 1, 0)]
    known = meet(even[0], odd_pairs(counts, 1, 0))
    known = meet(even[1], odd_pairs(counts, 0, 0), xor_pairs(counts, 4, 0))
    known = meet(even[0], odd_pairs(counts, 1, 1))
    return meet(even[1], odd_pairs(counts, 0, 0)).all()


def body(counts, height, noise):
    nr, nc = counts
    devices = nr * nc
    width = max(128, devices * 2)
    basis = jnp.asarray(constants(nr, 2 * nc, width))
    both_axes = ("row", "col")
    depth = table_shape(counts)[0]

    def swap(a, b, axis, bit=0):
        gb = lax.ppermute(b, both_axes, odd_pairs(counts, both_axes.index(axis), bit))
        return lax.ppermute(a, axis, pairs_from(lax.axis_size(axis), 0)), gb

    def small_swap(x, rows, cols):
        return lax.ppermute(x, both_axes, xor_pairs(counts, rows, cols))

    both = jnp.pad(noise, ((0, TR), (0, 0))) + jnp.pad(height, ((TR, 0), (0, 0)))
    b, a, table = call(
        functools.partial(begin_kernel, counts), [(32 + depth, 128)] * 2 + [(depth, 128)], both
    )
    if not spreads(counts):
        for axis, count in enumerate(counts):
            bit = 1
            while bit < count:
                table = table + small_swap(table, *((0, bit) if axis else (bit, 0)))
                bit *= 2
    ga, gb = swap(a, b, "col")
    r3, h3, b, a, table = call(
        functools.partial(widen_kernel, counts),
        [(128, 128)] * 2 + [(24, FC)] * 2 + [(depth, 128)],
        both,
        table,
        gb,
        ga,
    )
    ga, gb = swap(a, b, "row")
    weight, table = call(weights_kernel, [(EXT, 2 * SPEC), (depth, 128)], both, table, basis)
    far = small_swap(table, 4, 0)
    t = call(forward_kernel, [(EXT, 2 * SPEC)], both, r3, basis, flops=5 * 10**8)[0]
    t, table, b, a = call(
        functools.partial(first_kernel, counts),
        [(EXT, 2 * SPEC), (depth, 128)] + [(24, EXT)] * 2,
        gb,
        ga,
        t,
        weight,
        basis,
        table,
    )
    table = merged(table, far)
    wide = jnp.pad(table, ((0, 0), (0, EXT - 128)))
    y, m = call(
        functools.partial(inverse_kernel, counts),
        [(EXT, FC), (FR, FC)],
        t,
        basis,
        both,
        h3,
        gb,
        ga,
    )
    ga, gb = swap(*(jnp.concatenate([x, wide], axis=0) for x in (a, b)), "col", 1)
    y, table, b, a = call(
        functools.partial(columns_kernel, counts),
        [(EXT, FC), (depth, 128)] + [(24, FC)] * 2,
        y,
        ga,
        gb,
        table,
    )
    ga, gb = swap(a, b, "row")
    inner_w, f, gw, gf, near = call(
        functools.partial(inner_kernel, counts, width),
        [(96, TC)] * 2 + [(EXT, FC)] * 2 + [(16, width)],
        y,
        m,
        basis,
    )
    z, w, t, b, a = call(
        functools.partial(second_kernel, counts, width),
        [(TR, TC)] * 2 + [(EXT, 2 * SPEC)] + [(16, EXT)] * 2,
        y,
        m,
        gb,
        ga,
        table,
        inner_w,
        f,
        gw,
        gf,
        near,
        weight,
        basis,
    )
    ga, gb = swap(a, b, "col", 1)
    y, stats = call(inverse_stats_kernel, [(EXT, FC), (1, 128)], t, basis, both, m, z, w)
    y, b, a = call(
        functools.partial(columns_kernel, counts), [(EXT, FC)] + [(16, FC)] * 2, y, gb, ga
    )
    ga, gb = swap(a, b, "row", 1)
    inner_v, stats = call(
        functools.partial(inner_dots_kernel, counts),
        [(96, TC), (1, 128)],
        y,
        m,
        both,
        w,
        stats,
    )
    q, v, stats = call(
        functools.partial(dots_kernel, counts),
        [(TR, TC)] * 2 + [(devices, 128)],
        y,
        m,
        gb,
        ga,
        both,
        w,
        stats,
        inner_v,
    )
    stats = lax.all_to_all(stats, both_axes, 0, 0, tiled=True)
    return tuple(
        call(
            functools.partial(end_kernel, counts, width),
            [(TR, TC)] * 2,
            stats,
            basis,
            m,
            f,
            both,
            z,
            w,
            q,
            v,
        )
    )


def solution(mesh):
    counts = (mesh.shape["row"], mesh.shape["col"])
    spec = P("row", "col")
    return jax.shard_map(
        functools.partial(body, counts),
        mesh=mesh,
        in_specs=(spec, spec),
        out_specs=(spec, spec),
        check_vma=False,
    )
```

```python
import functools

import jax
import jax.numpy as jnp
import ml_dtypes
import numpy as np
from jax import lax
from jax.experimental import pallas as pl
from jax.experimental.pallas import tpu as pltpu
from jax.sharding import PartitionSpec as P

SUB = 128
OV = 8
EXT = SUB + 2 * OV
DAMP = 2.0**-28
SHRINK = 2.0**-20

TR, TC = 128, 256
FR, FC = 160, 384
SPEC = 256

highest = lax.Precision.HIGHEST


def sine(count):
    k = np.arange(1, count + 1, dtype=np.float64)
    basis = np.sqrt(2.0 / (count + 1.0)) * np.sin(np.pi * k[:, None] * k[None, :] / (count + 1.0))
    return basis, 2.0 - 2.0 * np.cos(np.pi * k / (count + 1.0))


def block_constants():
    basis, eig = sine(EXT)
    rows = np.roll(basis, -OV, 0)
    cols = np.pad(basis, ((0, SPEC - EXT), (0, SPEC - EXT)))
    scale = np.pad((eig[:, None] + eig[None, :]) ** 2, ((0, 0), (0, SPEC - EXT)))
    wide = lambda x: np.pad(x, ((0, 0), (0, 2 * SPEC - x.shape[1])))
    high = rows.T.astype(ml_dtypes.bfloat16).astype(np.float64)
    low = (rows.T - high).astype(ml_dtypes.bfloat16).astype(np.float64)
    tile = np.concatenate([x[:, :SUB] for x in (high, high, low)], 1)
    halo = np.concatenate([x[:, SUB:] for x in (high, high, low)], 1)
    inner = np.concatenate([x[:, 16:112] for x in (high, high, low)], 1)
    at = [*range(136, 144), *range(16), *range(112, 136)]
    edge = np.concatenate([x[:, at] for x in (high, high, low)], 1)
    turned = np.hstack([rows.T, np.zeros((EXT, 256 - EXT)), edge])
    return [np.tile(scale, (1, 2)), *(wide(x) for x in (rows, turned, cols, inner, np.hstack([tile, halo])))]


def rows_part(ref):
    return ref[EXT : 2 * EXT, :EXT]


def rows_t_part(ref):
    return ref[2 * EXT : 3 * EXT, :256]


def cols_part(ref):
    return ref[3 * EXT : 3 * EXT + SPEC, :SPEC]


def inner_rows(ref):
    at = 3 * EXT + SPEC
    return ref[at : at + EXT, : 3 * 96]


def edge_rows(ref):
    return ref[2 * EXT : 3 * EXT, 256 : 256 + 3 * 48]


def tile_rows(ref):
    at = 4 * EXT + SPEC
    return ref[at : at + EXT, : 3 * SUB]


def halo_rows(ref):
    at = 4 * EXT + SPEC
    return ref[at : at + EXT, 3 * SUB : 3 * EXT]


def coarse_part(ref, width):
    at, lanes = 5 * EXT + SPEC, 2 * SPEC
    parts = [ref[at + k * width : at + (k + 1) * width] for k in range(-(-width // lanes))]
    return (parts[0] if len(parts) == 1 else jnp.concatenate(parts, axis=1))[:, :width]


def constants(nr, nc, width):
    lanes = 2 * SPEC
    inverse = coarse_inverse(nr, nc, -(-width // lanes) * lanes)[:width]
    parts = [*block_constants(), *np.split(inverse, inverse.shape[1] // lanes, 1)]
    return np.concatenate(parts).astype(np.float32)


def coarse_inverse(nr, nc, width):
    br, er = sine(nr)
    bc, ec = sine(nc)
    both = np.kron(br, bc).reshape(nr, nc // 2, 2, nr * nc).transpose(2, 0, 1, 3)
    both = both.reshape(nr * nc, nr * nc)
    scale = (er[:, None] + ec[None, :]) / (SUB * SUB)
    values = (SUB * SUB * (DAMP + scale * scale)).reshape(-1)
    whole = np.zeros((width, width), np.float32)
    whole[: nr * nc, : nr * nc] = (both / values) @ both.T
    return whole


def dot(a, b, side=0):
    return lax.dot_general(
        a, b, (((1,), (side,)), ((), ())), precision=highest, preferred_element_type=jnp.float32
    )


def lap(x):
    rows, lanes = x.shape
    beside = pltpu.roll(x, 1, 0) + pltpu.roll(x, rows - 1, 0)
    beside = beside + (pltpu.roll(x, 1, 1) + pltpu.roll(x, lanes - 1, 1))
    return 4.0 * x - beside


def lanes_of(shape):
    return lax.broadcasted_iota(jnp.int32, shape, 1)


def rows_of(shape):
    return lax.broadcasted_iota(jnp.int32, shape, 0)


def total(x):
    return jnp.sum(jnp.sum(x, axis=0, keepdims=True), axis=1, keepdims=True)


def place():
    return lax.axis_index("row"), lax.axis_index("col")


def is_even(index):
    return lax.rem(index, 2) == 0


def column_mask(counts):
    j = lax.axis_index("col")
    lane = lanes_of((1, FC))
    right = jnp.where(j < counts[1] - 1, 320, 256)
    left = jnp.where(j > 0, 320, 384)
    return (lane < right) | (lane >= left)


def edge_mask(counts):
    i = lax.axis_index("row")
    row = rows_of((80, 1))
    first = jnp.where(i > 0, 0, 16)
    last = jnp.where(i < counts[0] - 1, 80, 64)
    return (row >= first) & (row < last) & column_mask(counts)


def table_shape(counts):
    return (-(-2 * counts[0] * counts[1] // 1024) * 8, 128)


def table_of(values, counts):
    i, j = place()
    devices = counts[0] * counts[1]
    shape = table_shape(counts)
    at = rows_of(shape) * 128 + lanes_of(shape) - (i * counts[1] + j)
    return jnp.where(at == 0, values[0], jnp.where(at == devices, values[1], 0.0))


def merged(table, *others):
    for other in others:
        table = jnp.where(table != 0.0, table, other)
    return table


def as_row(table, width):
    return jnp.concatenate([table[k : k + 1] for k in range(width // 128)], axis=1)


def row_of(pairs):
    lane = lanes_of((1, 128))
    row = jnp.zeros((1, 128), jnp.float32)
    for k, (left, right) in enumerate(pairs):
        row = jnp.where(lane == k, left, jnp.where(lane == 64 + k, right, row))
    return row


def near_inverse(counts, inverse):
    i, j = place()
    nr, nc = counts[0], 2 * counts[1]
    shape = (16, inverse.shape[0])
    which = rows_of(shape)
    r = i - 1 + which // 4
    c = 2 * j - 1 + which % 4
    inside = (r >= 0) & (r < nr) & (c >= 0) & (c < nc) & (which < 12)
    at = lax.rem(c + 2, 2) * (nr * counts[1]) + r * counts[1] + (c + 2) // 2 - 1
    return dot(jnp.where(inside & (lanes_of(shape) == at), 1.0, 0.0), inverse)


def as_bands(values):
    lane = lanes_of((1, FC))
    bands = []
    for d in range(3):
        left, first, second, right = values[4 * d : 4 * d + 4]
        bands.append(
            jnp.where(
                lane < 128,
                first,
                jnp.where(lane < 256, second, jnp.where(lane < 320, right, left)),
            )
        )
    return bands


def edge_bands(bands):
    above, on, below = bands
    return jnp.concatenate(
        [
            jnp.broadcast_to(above, (16, FC)),
            jnp.broadcast_to(on, (48, FC)),
            jnp.broadcast_to(below, (16, FC)),
        ],
        axis=0,
    )


def jumps(row):
    step = row - pltpu.roll(row, 1, 1)
    lane = lanes_of((1, FC))
    at = [jnp.sum(jnp.where(lane == k, step, 0.0), axis=1, keepdims=True) for k in (0, 128, 256)]
    return jnp.where(
        (lane < 64) | (lane >= 320), at[0], jnp.where(lane < 192, at[1], at[2])
    )


def edge_steps():
    lane = lanes_of((1, FC))
    up = (lane == 0) | (lane == 128) | (lane == 256)
    down = (lane == FC - 1) | (lane == 127) | (lane == 255)
    return jnp.where(up, 1.0, jnp.where(down, -1.0, 0.0))


def halves_of(x):
    high = x.astype(jnp.bfloat16)
    return high, (x - high.astype(jnp.float32)).astype(jnp.bfloat16)


def product(a, b):
    return lax.dot_general(a, b, (((1,), (0,)), ((), ())), preferred_element_type=jnp.float32)


def column_transform(w, basis_ref):
    high, low = halves_of(pltpu.roll(w, OV, 1))
    cols, rest = halves_of(cols_part(basis_ref))
    cols = jnp.concatenate([cols, rest, cols], axis=0)

    def block(at):
        part = slice(at, at + SPEC)
        return product(jnp.concatenate([high[:, part], high[:, part], low[:, part]], axis=1), cols)

    return jnp.concatenate([block(0), block(128)], axis=1)


def row_transform(u, basis_ref, part):
    high, low = halves_of(u)
    rows = part(basis_ref).astype(jnp.bfloat16)
    return product(rows, jnp.concatenate([high, low, high], axis=0))


def weights(means, basis_ref):
    lane = lanes_of((1, 2 * SPEC))
    mean = jnp.where(lane < SPEC, means[0], means[1])
    return 1.0 / (DAMP + mean * basis_ref[:EXT])


def strips_of(t, basis_ref, deep):
    cols = cols_part(basis_ref)
    left = dot(cols[:deep], t[:, :SPEC], 1)
    right = dot(cols[EXT - deep : EXT], t[:, SPEC:], 1)
    both = dot(jnp.concatenate([left, right], axis=0), rows_t_part(basis_ref)[:, :EXT])
    return both[:deep], both[deep:]


def solution_of(t, basis_ref):
    v = dot(rows_part(basis_ref), t)
    cols = cols_part(basis_ref)
    first, second = dot(v[:, :SPEC], cols), dot(v[:, SPEC:], cols)
    y = jnp.concatenate(
        [first[:, :128], first[:, 128:] + second[:, :128], second[:, 128:]], axis=1
    )
    return pltpu.roll(y, FC - OV, 1)


def core_sums(x):
    return [total(x[:, :128]), total(x[:, 128:256])]


def add_columns(y, from_left, from_right):
    far = from_left.shape[0] - OV
    gap = jnp.zeros((56 - far, EXT), jnp.float32)
    turned = jnp.concatenate(
        [from_right[8:], gap, from_right[:8], from_left[far:], gap, from_left[:far]], axis=0
    )
    back = turned.T
    lane = lanes_of((EXT, 128))
    rolled = pltpu.roll(back, 64, 1)
    first = y[:, :128] + jnp.where(lane < 8, rolled, 0.0)
    second = y[:, 128:256] + jnp.where(lane >= 120, rolled, 0.0)
    third = y[:, 256:] + jnp.where((lane < 16) | (lane >= 112), back, 0.0)
    return jnp.concatenate([first, second, third], axis=1)


def pack_rows(y, deep):
    return jnp.concatenate([y[136:], y[: deep - 8]], axis=0), y[136 - deep : 136]


def edges(y, from_above, from_below):
    far = from_above.shape[0] - OV
    none = jnp.zeros((8, FC), jnp.float32)
    return jnp.concatenate(
        [
            from_above[:8] if far == 16 else none,
            y[136:] + from_above[far - 8 : far],
            y[:8] + from_above[far:],
            y[8:24],
            y[104:120],
            y[120:136] + from_below[:16],
            from_below[16:] if far == 16 else none,
        ],
        axis=0,
    )


def edge_part(frame):
    return jnp.concatenate([frame[144:], frame[:24], frame[104:144]], axis=0)


def with_edges(edge, inner):
    return jnp.concatenate([edge[16:32, :TC], inner, edge[48:64, :TC]], axis=0)


def sides(index, count, a, b):
    even = is_even(index)
    before = jnp.where(index > 0, jnp.where(even, b, a), 0.0)
    after = jnp.where(index < count - 1, jnp.where(even, a, b), 0.0)
    return before, after


def send(index, a_ref, b_ref, before, after):
    even = is_even(index)
    a_ref[...] = jnp.where(even, after, before)
    b_ref[...] = jnp.where(even, before, after)


def begin_kernel(counts, both_ref, b_ref, a_ref, table_ref):
    r, h = both_ref[:TR], both_ref[TR:]
    lane = lanes_of((128, 128))
    packed = jnp.where(
        lane < 16,
        r[:, :128],
        jnp.where(
            lane < 64,
            pltpu.roll(h[:, :128], 16, 1),
            jnp.where(lane < 112, pltpu.roll(h[:, 128:], 112, 1), r[:, 128:]),
        ),
    )
    turned = packed.T
    table = table_of(core_sums(r), counts)
    table_ref[...] = table
    send(
        lax.axis_index("col"),
        a_ref,
        b_ref,
        jnp.concatenate([turned[:32], table], axis=0),
        jnp.concatenate([turned[96:], table], axis=0),
    )


def widen_kernel(counts, both_ref, own_ref, gb_ref, ga_ref, r3_ref, h3_ref, b_ref, a_ref, table_ref):
    i, j = place()
    from_left, from_right = sides(j, counts[1], ga_ref[:32], gb_ref[:32])
    turned = jnp.concatenate([from_right, jnp.zeros((64, 128), jnp.float32), from_left], axis=0)
    back = turned.T
    lane = lanes_of((128, 128))
    edge = (lane < 16) | (lane >= 112)
    r3 = jnp.where(edge, back, 0.0)
    h3 = jnp.where(
        lane < 16, pltpu.roll(back, 112, 1), jnp.where(lane >= 112, pltpu.roll(back, 16, 1), 0.0)
    )
    r3_ref[...] = r3
    h3_ref[...] = h3
    r, h = both_ref[:TR], both_ref[TR:]
    table = merged(own_ref[...], ga_ref[32:], gb_ref[32:])
    table_ref[...] = table
    wide = jnp.concatenate([table, jnp.zeros((table.shape[0], FC - 128), jnp.float32)], axis=1)

    def strip(r_rows, h_rows):
        return jnp.concatenate(
            [
                jnp.concatenate([r[r_rows], r3[r_rows]], axis=1),
                jnp.concatenate([h[h_rows], h3[h_rows]], axis=1),
                wide,
            ],
            axis=0,
        )

    send(i, a_ref, b_ref, strip(slice(0, 8), slice(0, 16)), strip(slice(120, 128), slice(112, 128)))


def weights_kernel(both_ref, table_ref, basis_ref, weights_ref, table_out):
    h = both_ref[TR:]
    means = [x / (SUB * SUB) for x in core_sums(h * h * h)]
    weights_ref[...] = weights(means, basis_ref)
    table_out[...] = table_ref[...]


def forward_kernel(both_ref, r3_ref, basis_ref, t_ref):
    r = both_ref[:TR]
    u = column_transform(jnp.concatenate([r, r3_ref[...]], axis=1), basis_ref)
    t_ref[...] = row_transform(u, basis_ref, tile_rows)


def first_kernel(
    counts,
    gb_ref,
    ga_ref,
    tile_ref,
    weights_ref,
    basis_ref,
    table_ref,
    t_ref,
    table_out,
    b_ref,
    a_ref,
):
    i, j = place()
    above, below = sides(i, counts[0], ga_ref[:8], gb_ref[:8])
    u = column_transform(jnp.concatenate([below, above], axis=0), basis_ref)
    t = (tile_ref[...] + row_transform(u, basis_ref, halo_rows)) * weights_ref[...]
    t_ref[...] = t
    table = merged(table_ref[...], ga_ref[24:, :128], gb_ref[24:, :128])
    table_out[...] = table
    wide = jnp.concatenate([table, jnp.zeros((table.shape[0], EXT - 128), jnp.float32)], axis=1)
    strips = (jnp.concatenate([x, wide], axis=0) for x in strips_of(t, basis_ref, 24))
    send(j, a_ref, b_ref, *strips)


def inverse_kernel(
    counts, t_ref, basis_ref, both_ref, h3_ref, gb_ref, ga_ref, table_ref, y_ref, m_ref, table_out
):
    table_out[...] = table_ref[...]
    y_ref[...] = solution_of(t_ref[...], basis_ref)
    above, below = sides(lax.axis_index("row"), counts[0], ga_ref[8:24], gb_ref[8:24])
    h = jnp.concatenate([both_ref[TR:], h3_ref[...]], axis=1)
    tall = jnp.concatenate([h, below, above], axis=0)
    m_ref[...] = tall * tall * tall


def columns_kernel(counts, y_ref, gb_ref, ga_ref, *refs):
    i, j = place()
    deep = 24 if len(refs) == 6 else 16
    y = add_columns(y_ref[...], *sides(j, counts[1], ga_ref[:deep], gb_ref[:deep]))
    strips = pack_rows(y, deep)
    if len(refs) == 6:
        table_ref, far_ref, out_ref, table_out, b_ref, a_ref = refs
        table = merged(table_ref[...], far_ref[...], ga_ref[24:, :128], gb_ref[24:, :128])
        table_out[...] = table
        wide = jnp.concatenate([table, jnp.zeros((table.shape[0], FC - 128), jnp.float32)], axis=1)
        strips = [jnp.concatenate([x, wide], axis=0) for x in strips]
    else:
        out_ref, b_ref, a_ref = refs
    out_ref[...] = y
    send(i, a_ref, b_ref, *strips)


def inner_kernel(counts, width, y_ref, m_ref, basis_ref, w_ref, f_ref, gw_ref, gf_ref, near_ref):
    mask = column_mask(counts)
    s = jnp.where(mask, y_ref[8:120], 0.0)
    m = m_ref[8:120]
    w = DAMP * s + lap(m * lap(s))
    w = jnp.where(mask, w[8:104], 0.0) * SHRINK
    f = lap(m * edge_steps())
    f = jnp.where(mask, f[8:104], 0.0) * SHRINK
    w_ref[...] = w[:, :TC]
    f_ref[...] = f[:, :TC]
    gw_ref[...] = row_transform(w, basis_ref, inner_rows)
    gf_ref[...] = row_transform(f, basis_ref, inner_rows)
    near_ref[...] = near_inverse(counts, coarse_part(basis_ref, width))


def second_kernel(
    counts,
    width,
    y_ref,
    m_ref,
    gb_ref,
    ga_ref,
    table_ref,
    farther_ref,
    inner_w_ref,
    f_ref,
    gw_ref,
    gf_ref,
    near_ref,
    weights_ref,
    basis_ref,
    z_ref,
    w_ref,
    t_ref,
    b_ref,
    a_ref,
):
    i, j = place()
    y = y_ref[...]
    mask = edge_mask(counts)
    s = edges(y, *sides(i, counts[0], ga_ref[:24], gb_ref[:24]))
    s = jnp.where(mask, s, 0.0)
    table = merged(table_ref[...], farther_ref[...], ga_ref[24:, :128], gb_ref[24:, :128])
    picked = jnp.sum(near_ref[...] * as_row(table, width), axis=1, keepdims=True)
    bands = as_bands([picked[k : k + 1] for k in range(12)])
    coarse = edge_bands(bands)
    m = edge_part(m_ref)
    flow = m * (lap(s) + lap(coarse))
    z = s + coarse
    w = jnp.where(mask, DAMP * z + lap(flow), 0.0) * SHRINK
    step = jumps(bands[1])
    damped = (DAMP * SHRINK) * bands[1]
    z_ref[...] = with_edges(z, y[16:112, :TC] + bands[1][:, :TC])
    w_ref[...] = with_edges(w, inner_w_ref[...] + step[:, :TC] * f_ref[...] + damped[:, :TC])
    lane = lanes_of((EXT, 256))
    ones = jnp.where((lane >= 16) & (lane < 112), rows_t_part(basis_ref), 0.0)
    ones = jnp.sum(ones, axis=1, keepdims=True)
    u = gw_ref[...] + step * gf_ref[...] + ones * damped
    u = u + row_transform(jnp.concatenate([w[8:32], w[48:72]], axis=0), basis_ref, edge_rows)
    t = column_transform(u, basis_ref) * weights_ref[...]
    t_ref[...] = t
    send(j, a_ref, b_ref, *strips_of(t, basis_ref, 16))


def inverse_stats_kernel(t_ref, basis_ref, both_ref, m_ref, z_ref, w_ref, y_ref, stats_ref):
    y_ref[...] = solution_of(t_ref[...], basis_ref)
    rt, mt, zt, wt = both_ref[:TR], m_ref[:TR, :TC], z_ref[...], w_ref[...]
    lane, row = lanes_of((1, 256)), rows_of((128, 1))
    along = (lane % 128 != 0) & (lane % 128 != 127)
    top, low = mt[:1], mt[127:]
    side = jnp.sum(jnp.where((row > 0) & (row < 127), mt, 0.0), axis=0, keepdims=True)

    def halves(x):
        return [
            jnp.sum(x[:, :128], axis=1, keepdims=True),
            jnp.sum(x[:, 128:], axis=1, keepdims=True),
        ]

    first, last = lane % 128 == 0, lane % 128 == 127
    zero = jnp.zeros((1, 1), jnp.float32)
    stats_ref[...] = row_of(
        [
            core_sums(rt * zt),
            core_sums(zt * wt),
            core_sums(wt),
            halves(jnp.where(along, top, 0.0)),
            halves(jnp.where(along, low, 0.0)),
            halves(jnp.where(first, side, 0.0)),
            halves(jnp.where(last, side, 0.0)),
            halves(jnp.where(first, top, 0.0)),
            halves(jnp.where(last, top, 0.0)),
            halves(jnp.where(first, low, 0.0)),
            halves(jnp.where(last, low, 0.0)),
            *[[zero, zero]] * 4,
            core_sums(rt),
        ]
    )


def inner_dots_kernel(counts, y_ref, m_ref, both_ref, w_ref, stats_ref, v_ref, stats_out):
    q = jnp.where(column_mask(counts), y_ref[8:120], 0.0)
    v = (DAMP * q + lap(m_ref[8:120] * lap(q)))[8:104, :TC]
    q = q[8:104, :TC]
    v_ref[...] = v
    rest = [
        core_sums(v),
        core_sums(both_ref[16:112] * q),
        core_sums(w_ref[16:112] * q),
        core_sums(v * q),
    ]
    zero = jnp.zeros((1, 1), jnp.float32)
    stats_out[...] = stats_ref[...] + row_of([[zero, zero]] * 11 + rest)


def dots_kernel(
    counts, y_ref, m_ref, gb_ref, ga_ref, both_ref, w_ref, stats_ref, inner_v_ref, q_ref, v_ref, stats_out
):
    i, j = place()
    y = y_ref[...]
    q = edges(y, *sides(i, counts[0], ga_ref[...], gb_ref[...]))
    q = jnp.where(edge_mask(counts), q, 0.0)
    v = DAMP * q + lap(edge_part(m_ref) * lap(q))
    q_ref[...] = with_edges(q, y[16:112, :TC])
    v_ref[...] = with_edges(v, inner_v_ref[...])
    qe, ve = (jnp.concatenate([x[16:32, :TC], x[48:64, :TC]], axis=0) for x in (q, v))
    re = jnp.concatenate([both_ref[:16], both_ref[112:128]], axis=0)
    we = jnp.concatenate([w_ref[:16], w_ref[112:]], axis=0)
    rest = [core_sums(ve), core_sums(re * qe), core_sums(we * qe), core_sums(ve * qe)]
    zero = jnp.zeros((1, 1), jnp.float32)
    row = stats_ref[...] + row_of([[zero, zero]] * 11 + rest)
    stats_out[...] = jnp.broadcast_to(row, stats_out.shape)


def end_kernel(
    counts,
    width,
    stats_ref,
    basis_ref,
    m_ref,
    f_ref,
    both_ref,
    z_ref,
    w_ref,
    q_ref,
    v_ref,
    solution_ref,
    residual_ref,
):
    i, j = place()
    tiles_c = counts[1]
    devices = counts[0] * tiles_c
    rows = stats_ref[...]
    st = jnp.concatenate([rows, pltpu.roll(rows, 64, 1)], axis=0)
    inverse = coarse_part(basis_ref, width)[: 2 * devices, : 2 * devices]
    g = jnp.broadcast_to(dot(inverse, st)[:, 2:3], st.shape)
    lane, row = lanes_of(st.shape), rows_of(st.shape)
    device = row % devices
    column = device % tiles_c
    on_left = row < devices

    def from_row(distance):
        return pltpu.roll(g, distance % (2 * devices), 0)

    up = jnp.where(device >= tiles_c, from_row(tiles_c), 0.0)
    down = jnp.where(device < devices - tiles_c, from_row(-tiles_c), 0.0)
    left = jnp.where(on_left, jnp.where(column > 0, from_row(1 - devices), 0.0), from_row(devices))
    right = jnp.where(
        on_left, from_row(-devices), jnp.where(column < tiles_c - 1, from_row(devices - 1), 0.0)
    )
    du, dd, dl, dr = g - up, g - down, g - left, g - right
    across = jnp.where(
        (lane == 3) | (lane == 7) | (lane == 8),
        du,
        jnp.where((lane == 4) | (lane == 9) | (lane == 10), dd, 0.0),
    )
    across = across + jnp.where(
        (lane == 5) | (lane == 7) | (lane == 9),
        dl,
        jnp.where((lane == 6) | (lane == 8) | (lane == 10), dr, 0.0),
    )
    factor = jnp.where((lane == 2) | (lane == 15), g, across * across)
    factor = jnp.where(lane == 11, 2.0 * g, factor)
    factor = jnp.where((lane < 2) | ((lane >= 12) & (lane < 15)), 1.0, factor)
    terms = jnp.where(lane == 16, (DAMP * SUB * SUB) * g * g, st * factor)
    sums = jnp.sum(terms, axis=0, keepdims=True)

    def whole(wanted):
        return jnp.sum(jnp.where(wanted, sums, 0.0), axis=1, keepdims=True)

    at = lanes_of((1, 128))
    rz, zw = whole(at == 0), whole(at == 1)
    ry = whole((at == 12) | (at == 15))
    yw = whole((at == 13) | (at == 2))
    yv = whole(((at >= 3) & (at < 12)) | (at == 14) | (at == 16))
    a = rz / zw
    rz1 = rz - a * ry - a * zw + a * a * yw
    beta1 = 1.0 + rz1 / rz
    dad = (beta1 * beta1 * zw - 2.0 * a * beta1 * yw) * (1.0 / SHRINK) + a * a * yv
    a1 = rz1 / dad
    r = i - 1 + lane // 4
    c = 2 * j - 1 + lane % 4
    inside = (r >= 0) & (r < counts[0]) & (c >= 0) & (c < 2 * tiles_c) & (lane < 12)
    where = lax.rem(c + 2, 2) * devices + r * tiles_c + (c + 2) // 2 - 1
    picked = jnp.sum(jnp.where(inside & (row == where), g, 0.0), axis=0, keepdims=True)
    bands = as_bands([picked[:, k : k + 1] for k in range(12)])
    on = bands[1][:, :TC]
    coarse = edge_bands(bands)
    image = DAMP * coarse + lap(edge_part(m_ref) * lap(coarse))
    image = with_edges(image, (jumps(bands[1]) * (1.0 / SHRINK))[:, :TC] * f_ref[...] + DAMP * on)
    y = q_ref[...] + on
    v = v_ref[...] + image
    z, w = z_ref[...], w_ref[...]
    solution_ref[...] = (a * SHRINK) * z + a1 * (beta1 * z - a * y)
    residual_ref[...] = both_ref[:TR] - a * w - a1 * ((beta1 * (1.0 / SHRINK)) * w - a * v)


def call(kernel, outs, *args, flops=10**9):
    shapes = [jax.ShapeDtypeStruct(s, jnp.float32) for s in outs]
    return pl.pallas_call(
        kernel,
        out_shape=shapes,
        compiler_params=pltpu.CompilerParams(vmem_limit_bytes=48 * 1024 * 1024),
        cost_estimate=pl.CostEstimate(flops=flops, bytes_accessed=10**6, transcendentals=0),
    )(*args)


def pairs_from(count, offset):
    found = []
    for k in range(offset, count, 2):
        found += [(k, (k + 1) % count), ((k + 1) % count, k)]
    return found


def odd_pairs(counts, axis, bit):
    found = []
    for i in range(counts[0]):
        for j in range(counts[1]):
            at = [i, j]
            if bit and at[axis] in (0, counts[axis] - 1):
                at[1 - axis] ^= bit
            else:
                at[axis] = (at[axis] + (1 if at[axis] % 2 else -1)) % counts[axis]
            found.append((i * counts[1] + j, at[0] * counts[1] + at[1]))
    return found


def xor_pairs(counts, rows, cols):
    flat = [(i, j) for i in range(counts[0]) for j in range(counts[1])]
    return [(i * counts[1] + j, (i ^ rows) * counts[1] + (j ^ cols)) for i, j in flat]


def spreads(counts):
    known = np.eye(counts[0] * counts[1], dtype=bool)

    def meet(*swaps):
        return np.logical_or.reduce([known, *(known[[b for _, b in pairs]] for pairs in swaps)])

    even = [xor_pairs(counts, 0, 1), xor_pairs(counts, 1, 0)]
    known = meet(even[0], odd_pairs(counts, 1, 0))
    first = meet(xor_pairs(counts, 4, 0))
    known = meet(even[1], odd_pairs(counts, 0, 0))
    second = meet(xor_pairs(counts, 4, 2))
    known = meet(even[0], odd_pairs(counts, 1, 1)) | first
    return (meet(even[1], odd_pairs(counts, 0, 0)) | second).all()


def body(counts, height, noise):
    nr, nc = counts
    devices = nr * nc
    width = max(128, devices * 2)
    basis = jnp.asarray(constants(nr, 2 * nc, width))
    both_axes = ("row", "col")
    depth = table_shape(counts)[0]

    def swap(a, b, axis, bit=0):
        gb = lax.ppermute(b, both_axes, odd_pairs(counts, both_axes.index(axis), bit))
        return lax.ppermute(a, axis, pairs_from(lax.axis_size(axis), 0)), gb

    def small_swap(x, rows, cols):
        return lax.ppermute(x, both_axes, xor_pairs(counts, rows, cols))

    both = jnp.pad(noise, ((0, TR), (0, 0))) + jnp.pad(height, ((TR, 0), (0, 0)))
    b, a, table = call(
        functools.partial(begin_kernel, counts), [(32 + depth, 128)] * 2 + [(depth, 128)], both
    )
    if not spreads(counts):
        for axis, count in enumerate(counts):
            bit = 1
            while bit < count:
                table = table + small_swap(table, *((0, bit) if axis else (bit, 0)))
                bit *= 2
    ga, gb = swap(a, b, "col")
    r3, h3, b, a, table = call(
        functools.partial(widen_kernel, counts),
        [(128, 128)] * 2 + [(24 + depth, FC)] * 2 + [(depth, 128)],
        both,
        table,
        gb,
        ga,
    )
    ga, gb = swap(a, b, "row")
    weight, table = call(weights_kernel, [(EXT, 2 * SPEC), (depth, 128)], both, table, basis)
    far = small_swap(table, 4, 0)
    t = call(forward_kernel, [(EXT, 2 * SPEC)], both, r3, basis)[0]
    t, table, b, a = call(
        functools.partial(first_kernel, counts),
        [(EXT, 2 * SPEC), (depth, 128)] + [(24 + depth, EXT)] * 2,
        gb,
        ga,
        t,
        weight,
        basis,
        table,
    )
    y, m, table_too = call(
        functools.partial(inverse_kernel, counts),
        [(EXT, FC), (FR, FC), (depth, 128)],
        t,
        basis,
        both,
        h3,
        gb,
        ga,
        table,
    )
    ga, gb = swap(a, b, "col", 1)
    farther = small_swap(table_too, 4, 2)
    y, table, b, a = call(
        functools.partial(columns_kernel, counts),
        [(EXT, FC), (depth, 128)] + [(24 + depth, FC)] * 2,
        y,
        gb,
        ga,
        table,
        far,
    )
    ga, gb = swap(a, b, "row")
    inner_w, f, gw, gf, near = call(
        functools.partial(inner_kernel, counts, width),
        [(96, TC)] * 2 + [(EXT, FC)] * 2 + [(16, width)],
        y,
        m,
        basis,
    )
    z, w, t, b, a = call(
        functools.partial(second_kernel, counts, width),
        [(TR, TC)] * 2 + [(EXT, 2 * SPEC)] + [(16, EXT)] * 2,
        y,
        m,
        gb,
        ga,
        table,
        farther,
        inner_w,
        f,
        gw,
        gf,
        near,
        weight,
        basis,
    )
    ga, gb = swap(a, b, "col", 1)
    y, stats = call(inverse_stats_kernel, [(EXT, FC), (1, 128)], t, basis, both, m, z, w)
    y, b, a = call(
        functools.partial(columns_kernel, counts), [(EXT, FC)] + [(16, FC)] * 2, y, gb, ga
    )
    ga, gb = swap(a, b, "row", 1)
    inner_v, stats = call(
        functools.partial(inner_dots_kernel, counts),
        [(96, TC), (1, 128)],
        y,
        m,
        both,
        w,
        stats,
    )
    q, v, stats = call(
        functools.partial(dots_kernel, counts),
        [(TR, TC)] * 2 + [(devices, 128)],
        y,
        m,
        gb,
        ga,
        both,
        w,
        stats,
        inner_v,
    )
    stats = lax.all_to_all(stats, both_axes, 0, 0, tiled=True)
    return tuple(
        call(
            functools.partial(end_kernel, counts, width),
            [(TR, TC)] * 2,
            stats,
            basis,
            m,
            f,
            both,
            z,
            w,
            q,
            v,
        )
    )


def solution(mesh):
    counts = (mesh.shape["row"], mesh.shape["col"])
    spec = P("row", "col")
    return jax.shard_map(
        functools.partial(body, counts),
        mesh=mesh,
        in_specs=(spec, spec),
        out_specs=(spec, spec),
        check_vma=False,
    )
```

```python
import functools

import jax
import jax.numpy as jnp
import ml_dtypes
import numpy as np
from jax import lax
from jax.experimental import pallas as pl
from jax.experimental.pallas import tpu as pltpu
from jax.sharding import PartitionSpec as P

SUB = 128
OV = 8
EXT = SUB + 2 * OV
DAMP = 2.0**-28
SHRINK = 2.0**-20

TR, TC = 128, 256
FR, FC = 160, 384
SPEC = 256

highest = lax.Precision.HIGHEST


def sine(count):
    k = np.arange(1, count + 1, dtype=np.float64)
    basis = np.sqrt(2.0 / (count + 1.0)) * np.sin(np.pi * k[:, None] * k[None, :] / (count + 1.0))
    return basis, 2.0 - 2.0 * np.cos(np.pi * k / (count + 1.0))


def block_constants():
    basis, eig = sine(EXT)
    rows = np.roll(basis, -OV, 0)
    cols = np.pad(basis, ((0, SPEC - EXT), (0, SPEC - EXT)))
    scale = np.pad((eig[:, None] + eig[None, :]) ** 2, ((0, 0), (0, SPEC - EXT)))
    wide = lambda x: np.pad(x, ((0, 0), (0, 2 * SPEC - x.shape[1])))
    high = rows.T.astype(ml_dtypes.bfloat16).astype(np.float64)
    low = (rows.T - high).astype(ml_dtypes.bfloat16).astype(np.float64)
    tile = np.concatenate([x[:, :SUB] for x in (high, high, low)], 1)
    halo = np.concatenate([x[:, SUB:] for x in (high, high, low)], 1)
    inner = np.concatenate([x[:, 16:112] for x in (high, high, low)], 1)
    at = [*range(136, 144), *range(16), *range(112, 136)]
    edge = np.concatenate([x[:, at] for x in (high, high, low)], 1)
    turned = np.hstack([rows.T, np.zeros((EXT, 256 - EXT)), edge])
    return [np.tile(scale, (1, 2)), *(wide(x) for x in (rows, turned, cols, inner, np.hstack([tile, halo])))]


def rows_part(ref):
    return ref[EXT : 2 * EXT, :EXT]


def rows_t_part(ref):
    return ref[2 * EXT : 3 * EXT, :256]


def cols_part(ref):
    return ref[3 * EXT : 3 * EXT + SPEC, :SPEC]


def inner_rows(ref):
    at = 3 * EXT + SPEC
    return ref[at : at + EXT, : 3 * 96]


def edge_rows(ref):
    return ref[2 * EXT : 3 * EXT, 256 : 256 + 3 * 48]


def tile_rows(ref):
    at = 4 * EXT + SPEC
    return ref[at : at + EXT, : 3 * SUB]


def halo_rows(ref):
    at = 4 * EXT + SPEC
    return ref[at : at + EXT, 3 * SUB : 3 * EXT]


def coarse_part(ref, width):
    at, lanes = 5 * EXT + SPEC, 2 * SPEC
    parts = [ref[at + k * width : at + (k + 1) * width] for k in range(-(-width // lanes))]
    return (parts[0] if len(parts) == 1 else jnp.concatenate(parts, axis=1))[:, :width]


def constants(nr, nc, width):
    lanes = 2 * SPEC
    inverse = coarse_inverse(nr, nc, -(-width // lanes) * lanes)[:width]
    parts = [*block_constants(), *np.split(inverse, inverse.shape[1] // lanes, 1)]
    return np.concatenate(parts).astype(np.float32)


def coarse_inverse(nr, nc, width):
    br, er = sine(nr)
    bc, ec = sine(nc)
    both = np.kron(br, bc).reshape(nr, nc // 2, 2, nr * nc).transpose(2, 0, 1, 3)
    both = both.reshape(nr * nc, nr * nc)
    scale = (er[:, None] + ec[None, :]) / (SUB * SUB)
    values = (SUB * SUB * (DAMP + scale * scale)).reshape(-1)
    whole = np.zeros((width, width), np.float32)
    whole[: nr * nc, : nr * nc] = (both / values) @ both.T
    return whole


def dot(a, b, side=0):
    return lax.dot_general(
        a, b, (((1,), (side,)), ((), ())), precision=highest, preferred_element_type=jnp.float32
    )


def lap(x):
    rows, lanes = x.shape
    beside = pltpu.roll(x, 1, 0) + pltpu.roll(x, rows - 1, 0)
    beside = beside + (pltpu.roll(x, 1, 1) + pltpu.roll(x, lanes - 1, 1))
    return 4.0 * x - beside


def lanes_of(shape):
    return lax.broadcasted_iota(jnp.int32, shape, 1)


def rows_of(shape):
    return lax.broadcasted_iota(jnp.int32, shape, 0)


def total(x):
    return jnp.sum(jnp.sum(x, axis=0, keepdims=True), axis=1, keepdims=True)


def place():
    return lax.axis_index("row"), lax.axis_index("col")


def is_even(index):
    return lax.rem(index, 2) == 0


def column_mask(counts):
    j = lax.axis_index("col")
    lane = lanes_of((1, FC))
    right = jnp.where(j < counts[1] - 1, 320, 256)
    left = jnp.where(j > 0, 320, 384)
    return (lane < right) | (lane >= left)


def edge_mask(counts):
    i = lax.axis_index("row")
    row = rows_of((80, 1))
    first = jnp.where(i > 0, 0, 16)
    last = jnp.where(i < counts[0] - 1, 80, 64)
    return (row >= first) & (row < last) & column_mask(counts)


def table_shape(counts):
    return (-(-2 * counts[0] * counts[1] // 1024) * 8, 128)


def table_of(values, counts):
    i, j = place()
    devices = counts[0] * counts[1]
    shape = table_shape(counts)
    at = rows_of(shape) * 128 + lanes_of(shape) - (i * counts[1] + j)
    return jnp.where(at == 0, values[0], jnp.where(at == devices, values[1], 0.0))


def merged(table, *others):
    for other in others:
        table = jnp.where(table != 0.0, table, other)
    return table


def as_row(table, width):
    return jnp.concatenate([table[k : k + 1] for k in range(width // 128)], axis=1)


def row_of(pairs):
    lane = lanes_of((1, 128))
    row = jnp.zeros((1, 128), jnp.float32)
    for k, (left, right) in enumerate(pairs):
        row = jnp.where(lane == k, left, jnp.where(lane == 64 + k, right, row))
    return row


def near_inverse(counts, inverse):
    i, j = place()
    nr, nc = counts[0], 2 * counts[1]
    shape = (16, inverse.shape[0])
    which = rows_of(shape)
    r = i - 1 + which // 4
    c = 2 * j - 1 + which % 4
    inside = (r >= 0) & (r < nr) & (c >= 0) & (c < nc) & (which < 12)
    at = lax.rem(c + 2, 2) * (nr * counts[1]) + r * counts[1] + (c + 2) // 2 - 1
    return dot(jnp.where(inside & (lanes_of(shape) == at), 1.0, 0.0), inverse)


def as_bands(values):
    lane = lanes_of((1, FC))
    bands = []
    for d in range(3):
        left, first, second, right = values[4 * d : 4 * d + 4]
        bands.append(
            jnp.where(
                lane < 128,
                first,
                jnp.where(lane < 256, second, jnp.where(lane < 320, right, left)),
            )
        )
    return bands


def edge_bands(bands):
    above, on, below = bands
    return jnp.concatenate(
        [
            jnp.broadcast_to(above, (16, FC)),
            jnp.broadcast_to(on, (48, FC)),
            jnp.broadcast_to(below, (16, FC)),
        ],
        axis=0,
    )


def jumps(row):
    step = row - pltpu.roll(row, 1, 1)
    lane = lanes_of((1, FC))
    at = [jnp.sum(jnp.where(lane == k, step, 0.0), axis=1, keepdims=True) for k in (0, 128, 256)]
    return jnp.where(
        (lane < 64) | (lane >= 320), at[0], jnp.where(lane < 192, at[1], at[2])
    )


def edge_steps():
    lane = lanes_of((1, FC))
    up = (lane == 0) | (lane == 128) | (lane == 256)
    down = (lane == FC - 1) | (lane == 127) | (lane == 255)
    return jnp.where(up, 1.0, jnp.where(down, -1.0, 0.0))


def halves_of(x):
    high = x.astype(jnp.bfloat16)
    return high, (x - high.astype(jnp.float32)).astype(jnp.bfloat16)


def product(a, b):
    return lax.dot_general(a, b, (((1,), (0,)), ((), ())), preferred_element_type=jnp.float32)


def column_transform(w, basis_ref):
    high, low = halves_of(pltpu.roll(w, OV, 1))
    cols, rest = halves_of(cols_part(basis_ref))
    cols = jnp.concatenate([cols, rest, cols], axis=0)

    def block(at):
        part = slice(at, at + SPEC)
        return product(jnp.concatenate([high[:, part], high[:, part], low[:, part]], axis=1), cols)

    return jnp.concatenate([block(0), block(128)], axis=1)


def row_transform(u, basis_ref, part):
    high, low = halves_of(u)
    rows = part(basis_ref).astype(jnp.bfloat16)
    return product(rows, jnp.concatenate([high, low, high], axis=0))


def weights(means, basis_ref):
    lane = lanes_of((1, 2 * SPEC))
    mean = jnp.where(lane < SPEC, means[0], means[1])
    return 1.0 / (DAMP + mean * basis_ref[:EXT])


def strips_of(t, basis_ref, deep):
    cols = cols_part(basis_ref)
    left = dot(cols[:deep], t[:, :SPEC], 1)
    right = dot(cols[EXT - deep : EXT], t[:, SPEC:], 1)
    both = dot(jnp.concatenate([left, right], axis=0), rows_t_part(basis_ref)[:, :EXT])
    return both[:deep], both[deep:]


def solution_of(t, basis_ref):
    v = dot(rows_part(basis_ref), t)
    cols = cols_part(basis_ref)
    first, second = dot(v[:, :SPEC], cols), dot(v[:, SPEC:], cols)
    y = jnp.concatenate(
        [first[:, :128], first[:, 128:] + second[:, :128], second[:, 128:]], axis=1
    )
    return pltpu.roll(y, FC - OV, 1)


def core_sums(x):
    return [total(x[:, :128]), total(x[:, 128:256])]


def add_columns(y, from_left, from_right):
    far = from_left.shape[0] - OV
    gap = jnp.zeros((56 - far, EXT), jnp.float32)
    turned = jnp.concatenate(
        [from_right[8:], gap, from_right[:8], from_left[far:], gap, from_left[:far]], axis=0
    )
    back = turned.T
    lane = lanes_of((EXT, 128))
    rolled = pltpu.roll(back, 64, 1)
    first = y[:, :128] + jnp.where(lane < 8, rolled, 0.0)
    second = y[:, 128:256] + jnp.where(lane >= 120, rolled, 0.0)
    third = y[:, 256:] + jnp.where((lane < 16) | (lane >= 112), back, 0.0)
    return jnp.concatenate([first, second, third], axis=1)


def pack_rows(y, deep):
    return jnp.concatenate([y[136:], y[: deep - 8]], axis=0), y[136 - deep : 136]


def edges(y, from_above, from_below):
    far = from_above.shape[0] - OV
    none = jnp.zeros((8, FC), jnp.float32)
    return jnp.concatenate(
        [
            from_above[:8] if far == 16 else none,
            y[136:] + from_above[far - 8 : far],
            y[:8] + from_above[far:],
            y[8:24],
            y[104:120],
            y[120:136] + from_below[:16],
            from_below[16:] if far == 16 else none,
        ],
        axis=0,
    )


def edge_part(frame):
    return jnp.concatenate([frame[144:], frame[:24], frame[104:144]], axis=0)


def with_edges(edge, inner):
    return jnp.concatenate([edge[16:32, :TC], inner, edge[48:64, :TC]], axis=0)


def sides(index, count, a, b):
    even = is_even(index)
    before = jnp.where(index > 0, jnp.where(even, b, a), 0.0)
    after = jnp.where(index < count - 1, jnp.where(even, a, b), 0.0)
    return before, after


def send(index, a_ref, b_ref, before, after):
    even = is_even(index)
    a_ref[...] = jnp.where(even, after, before)
    b_ref[...] = jnp.where(even, before, after)


def begin_kernel(counts, both_ref, b_ref, a_ref, table_ref):
    r, h = both_ref[:TR], both_ref[TR:]
    lane = lanes_of((128, 128))
    packed = jnp.where(
        lane < 16,
        r[:, :128],
        jnp.where(
            lane < 64,
            pltpu.roll(h[:, :128], 16, 1),
            jnp.where(lane < 112, pltpu.roll(h[:, 128:], 112, 1), r[:, 128:]),
        ),
    )
    turned = packed.T
    table = table_of(core_sums(r), counts)
    table_ref[...] = table
    send(
        lax.axis_index("col"),
        a_ref,
        b_ref,
        jnp.concatenate([turned[:32], table], axis=0),
        jnp.concatenate([turned[96:], table], axis=0),
    )


def widen_kernel(counts, both_ref, own_ref, gb_ref, ga_ref, r3_ref, h3_ref, b_ref, a_ref, table_ref):
    i, j = place()
    from_left, from_right = sides(j, counts[1], ga_ref[:32], gb_ref[:32])
    turned = jnp.concatenate([from_right, jnp.zeros((64, 128), jnp.float32), from_left], axis=0)
    back = turned.T
    lane = lanes_of((128, 128))
    edge = (lane < 16) | (lane >= 112)
    r3 = jnp.where(edge, back, 0.0)
    h3 = jnp.where(
        lane < 16, pltpu.roll(back, 112, 1), jnp.where(lane >= 112, pltpu.roll(back, 16, 1), 0.0)
    )
    r3_ref[...] = r3
    h3_ref[...] = h3
    r, h = both_ref[:TR], both_ref[TR:]
    table = merged(own_ref[...], ga_ref[32:], gb_ref[32:])
    table_ref[...] = table
    wide = jnp.concatenate([table, jnp.zeros((table.shape[0], FC - 128), jnp.float32)], axis=1)

    def strip(r_rows, h_rows):
        return jnp.concatenate(
            [
                jnp.concatenate([r[r_rows], r3[r_rows]], axis=1),
                jnp.concatenate([h[h_rows], h3[h_rows]], axis=1),
                wide,
            ],
            axis=0,
        )

    send(i, a_ref, b_ref, strip(slice(0, 8), slice(0, 16)), strip(slice(120, 128), slice(112, 128)))


def weights_kernel(both_ref, table_ref, basis_ref, weights_ref, table_out):
    h = both_ref[TR:]
    means = [x / (SUB * SUB) for x in core_sums(h * h * h)]
    weights_ref[...] = weights(means, basis_ref)
    table_out[...] = table_ref[...]


def forward_kernel(both_ref, r3_ref, basis_ref, t_ref):
    r = both_ref[:TR]
    u = column_transform(jnp.concatenate([r, r3_ref[...]], axis=1), basis_ref)
    t_ref[...] = row_transform(u, basis_ref, tile_rows)


def first_kernel(
    counts,
    gb_ref,
    ga_ref,
    tile_ref,
    weights_ref,
    basis_ref,
    table_ref,
    t_ref,
    table_out,
    b_ref,
    a_ref,
):
    i, j = place()
    above, below = sides(i, counts[0], ga_ref[:8], gb_ref[:8])
    u = column_transform(jnp.concatenate([below, above], axis=0), basis_ref)
    t = (tile_ref[...] + row_transform(u, basis_ref, halo_rows)) * weights_ref[...]
    t_ref[...] = t
    table = merged(table_ref[...], ga_ref[24:, :128], gb_ref[24:, :128])
    table_out[...] = table
    wide = jnp.concatenate([table, jnp.zeros((table.shape[0], EXT - 128), jnp.float32)], axis=1)
    strips = (jnp.concatenate([x, wide], axis=0) for x in strips_of(t, basis_ref, 24))
    send(j, a_ref, b_ref, *strips)


def inverse_kernel(
    counts, t_ref, basis_ref, both_ref, h3_ref, gb_ref, ga_ref, table_ref, y_ref, m_ref, table_out
):
    table_out[...] = table_ref[...]
    y_ref[...] = solution_of(t_ref[...], basis_ref)
    above, below = sides(lax.axis_index("row"), counts[0], ga_ref[8:24], gb_ref[8:24])
    h = jnp.concatenate([both_ref[TR:], h3_ref[...]], axis=1)
    tall = jnp.concatenate([h, below, above], axis=0)
    m_ref[...] = tall * tall * tall


def columns_kernel(counts, y_ref, gb_ref, ga_ref, *refs):
    i, j = place()
    deep = 24 if len(refs) == 6 else 16
    y = add_columns(y_ref[...], *sides(j, counts[1], ga_ref[:deep], gb_ref[:deep]))
    strips = pack_rows(y, deep)
    if len(refs) == 6:
        table_ref, far_ref, out_ref, table_out, b_ref, a_ref = refs
        table = merged(table_ref[...], far_ref[...], ga_ref[24:, :128], gb_ref[24:, :128])
        table_out[...] = table
        wide = jnp.concatenate([table, jnp.zeros((table.shape[0], FC - 128), jnp.float32)], axis=1)
        strips = [jnp.concatenate([x, wide], axis=0) for x in strips]
    else:
        out_ref, b_ref, a_ref = refs
    out_ref[...] = y
    send(i, a_ref, b_ref, *strips)


def inner_kernel(counts, width, y_ref, m_ref, basis_ref, w_ref, f_ref, gw_ref, gf_ref, near_ref):
    mask = column_mask(counts)
    s = jnp.where(mask, y_ref[8:120], 0.0)
    m = m_ref[8:120]
    w = DAMP * s + lap(m * lap(s))
    w = jnp.where(mask, w[8:104], 0.0) * SHRINK
    f = lap(m * edge_steps())
    f = jnp.where(mask, f[8:104], 0.0) * SHRINK
    w_ref[...] = w[:, :TC]
    f_ref[...] = f[:, :TC]
    gw_ref[...] = row_transform(w, basis_ref, inner_rows)
    gf_ref[...] = row_transform(f, basis_ref, inner_rows)
    near_ref[...] = near_inverse(counts, coarse_part(basis_ref, width))


def second_kernel(
    counts,
    width,
    y_ref,
    m_ref,
    gb_ref,
    ga_ref,
    table_ref,
    farther_ref,
    farthest_ref,
    inner_w_ref,
    f_ref,
    gw_ref,
    gf_ref,
    near_ref,
    weights_ref,
    basis_ref,
    z_ref,
    w_ref,
    t_ref,
    b_ref,
    a_ref,
):
    i, j = place()
    y = y_ref[...]
    mask = edge_mask(counts)
    s = edges(y, *sides(i, counts[0], ga_ref[:24], gb_ref[:24]))
    s = jnp.where(mask, s, 0.0)
    table = merged(table_ref[...], farther_ref[...], farthest_ref[...])
    table = merged(table, ga_ref[24:, :128], gb_ref[24:, :128])
    picked = jnp.sum(near_ref[...] * as_row(table, width), axis=1, keepdims=True)
    bands = as_bands([picked[k : k + 1] for k in range(12)])
    coarse = edge_bands(bands)
    m = edge_part(m_ref)
    flow = m * (lap(s) + lap(coarse))
    z = s + coarse
    w = jnp.where(mask, DAMP * z + lap(flow), 0.0) * SHRINK
    step = jumps(bands[1])
    damped = (DAMP * SHRINK) * bands[1]
    z_ref[...] = with_edges(z, y[16:112, :TC] + bands[1][:, :TC])
    w_ref[...] = with_edges(w, inner_w_ref[...] + step[:, :TC] * f_ref[...] + damped[:, :TC])
    lane = lanes_of((EXT, 256))
    ones = jnp.where((lane >= 16) & (lane < 112), rows_t_part(basis_ref), 0.0)
    ones = jnp.sum(ones, axis=1, keepdims=True)
    u = gw_ref[...] + step * gf_ref[...] + ones * damped
    u = u + row_transform(jnp.concatenate([w[8:32], w[48:72]], axis=0), basis_ref, edge_rows)
    t = column_transform(u, basis_ref) * weights_ref[...]
    t_ref[...] = t
    send(j, a_ref, b_ref, *strips_of(t, basis_ref, 16))


def inverse_stats_kernel(t_ref, basis_ref, both_ref, m_ref, z_ref, w_ref, y_ref, stats_ref):
    y_ref[...] = solution_of(t_ref[...], basis_ref)
    rt, mt, zt, wt = both_ref[:TR], m_ref[:TR, :TC], z_ref[...], w_ref[...]
    lane, row = lanes_of((1, 256)), rows_of((128, 1))
    along = (lane % 128 != 0) & (lane % 128 != 127)
    top, low = mt[:1], mt[127:]
    side = jnp.sum(jnp.where((row > 0) & (row < 127), mt, 0.0), axis=0, keepdims=True)

    def halves(x):
        return [
            jnp.sum(x[:, :128], axis=1, keepdims=True),
            jnp.sum(x[:, 128:], axis=1, keepdims=True),
        ]

    first, last = lane % 128 == 0, lane % 128 == 127
    zero = jnp.zeros((1, 1), jnp.float32)
    stats_ref[...] = row_of(
        [
            core_sums(rt * zt),
            core_sums(zt * wt),
            core_sums(wt),
            halves(jnp.where(along, top, 0.0)),
            halves(jnp.where(along, low, 0.0)),
            halves(jnp.where(first, side, 0.0)),
            halves(jnp.where(last, side, 0.0)),
            halves(jnp.where(first, top, 0.0)),
            halves(jnp.where(last, top, 0.0)),
            halves(jnp.where(first, low, 0.0)),
            halves(jnp.where(last, low, 0.0)),
            *[[zero, zero]] * 4,
            core_sums(rt),
        ]
    )


def inner_dots_kernel(counts, y_ref, m_ref, both_ref, w_ref, stats_ref, v_ref, stats_out):
    q = jnp.where(column_mask(counts), y_ref[8:120], 0.0)
    v = (DAMP * q + lap(m_ref[8:120] * lap(q)))[8:104, :TC]
    q = q[8:104, :TC]
    v_ref[...] = v
    rest = [
        core_sums(v),
        core_sums(both_ref[16:112] * q),
        core_sums(w_ref[16:112] * q),
        core_sums(v * q),
    ]
    zero = jnp.zeros((1, 1), jnp.float32)
    stats_out[...] = stats_ref[...] + row_of([[zero, zero]] * 11 + rest)


def dots_kernel(
    counts, y_ref, m_ref, gb_ref, ga_ref, both_ref, w_ref, stats_ref, inner_v_ref, q_ref, v_ref, stats_out
):
    i, j = place()
    y = y_ref[...]
    q = edges(y, *sides(i, counts[0], ga_ref[...], gb_ref[...]))
    q = jnp.where(edge_mask(counts), q, 0.0)
    v = DAMP * q + lap(edge_part(m_ref) * lap(q))
    q_ref[...] = with_edges(q, y[16:112, :TC])
    v_ref[...] = with_edges(v, inner_v_ref[...])
    qe, ve = (jnp.concatenate([x[16:32, :TC], x[48:64, :TC]], axis=0) for x in (q, v))
    re = jnp.concatenate([both_ref[:16], both_ref[112:128]], axis=0)
    we = jnp.concatenate([w_ref[:16], w_ref[112:]], axis=0)
    rest = [core_sums(ve), core_sums(re * qe), core_sums(we * qe), core_sums(ve * qe)]
    zero = jnp.zeros((1, 1), jnp.float32)
    row = stats_ref[...] + row_of([[zero, zero]] * 11 + rest)
    stats_out[...] = jnp.broadcast_to(row, stats_out.shape)


def end_kernel(
    counts,
    width,
    stats_ref,
    basis_ref,
    m_ref,
    f_ref,
    both_ref,
    z_ref,
    w_ref,
    q_ref,
    v_ref,
    solution_ref,
    residual_ref,
):
    i, j = place()
    tiles_c = counts[1]
    devices = counts[0] * tiles_c
    rows = stats_ref[...]
    st = jnp.concatenate([rows, pltpu.roll(rows, 64, 1)], axis=0)
    inverse = coarse_part(basis_ref, width)[: 2 * devices, : 2 * devices]
    g = jnp.broadcast_to(dot(inverse, st)[:, 2:3], st.shape)
    lane, row = lanes_of(st.shape), rows_of(st.shape)
    device = row % devices
    column = device % tiles_c
    on_left = row < devices

    def from_row(distance):
        return pltpu.roll(g, distance % (2 * devices), 0)

    up = jnp.where(device >= tiles_c, from_row(tiles_c), 0.0)
    down = jnp.where(device < devices - tiles_c, from_row(-tiles_c), 0.0)
    left = jnp.where(on_left, jnp.where(column > 0, from_row(1 - devices), 0.0), from_row(devices))
    right = jnp.where(
        on_left, from_row(-devices), jnp.where(column < tiles_c - 1, from_row(devices - 1), 0.0)
    )
    du, dd, dl, dr = g - up, g - down, g - left, g - right
    across = jnp.where(
        (lane == 3) | (lane == 7) | (lane == 8),
        du,
        jnp.where((lane == 4) | (lane == 9) | (lane == 10), dd, 0.0),
    )
    across = across + jnp.where(
        (lane == 5) | (lane == 7) | (lane == 9),
        dl,
        jnp.where((lane == 6) | (lane == 8) | (lane == 10), dr, 0.0),
    )
    factor = jnp.where((lane == 2) | (lane == 15), g, across * across)
    factor = jnp.where(lane == 11, 2.0 * g, factor)
    factor = jnp.where((lane < 2) | ((lane >= 12) & (lane < 15)), 1.0, factor)
    terms = jnp.where(lane == 16, (DAMP * SUB * SUB) * g * g, st * factor)
    sums = jnp.sum(terms, axis=0, keepdims=True)

    def whole(wanted):
        return jnp.sum(jnp.where(wanted, sums, 0.0), axis=1, keepdims=True)

    at = lanes_of((1, 128))
    rz, zw = whole(at == 0), whole(at == 1)
    ry = whole((at == 12) | (at == 15))
    yw = whole((at == 13) | (at == 2))
    yv = whole(((at >= 3) & (at < 12)) | (at == 14) | (at == 16))
    a = rz / zw
    rz1 = rz - a * ry - a * zw + a * a * yw
    beta1 = 1.0 + rz1 / rz
    dad = (beta1 * beta1 * zw - 2.0 * a * beta1 * yw) * (1.0 / SHRINK) + a * a * yv
    a1 = rz1 / dad
    r = i - 1 + lane // 4
    c = 2 * j - 1 + lane % 4
    inside = (r >= 0) & (r < counts[0]) & (c >= 0) & (c < 2 * tiles_c) & (lane < 12)
    where = lax.rem(c + 2, 2) * devices + r * tiles_c + (c + 2) // 2 - 1
    picked = jnp.sum(jnp.where(inside & (row == where), g, 0.0), axis=0, keepdims=True)
    bands = as_bands([picked[:, k : k + 1] for k in range(12)])
    on = bands[1][:, :TC]
    coarse = edge_bands(bands)
    image = DAMP * coarse + lap(edge_part(m_ref) * lap(coarse))
    image = with_edges(image, (jumps(bands[1]) * (1.0 / SHRINK))[:, :TC] * f_ref[...] + DAMP * on)
    y = q_ref[...] + on
    v = v_ref[...] + image
    z, w = z_ref[...], w_ref[...]
    solution_ref[...] = (a * SHRINK) * z + a1 * (beta1 * z - a * y)
    residual_ref[...] = both_ref[:TR] - a * w - a1 * ((beta1 * (1.0 / SHRINK)) * w - a * v)


def call(kernel, outs, *args, flops=10**9):
    shapes = [jax.ShapeDtypeStruct(s, jnp.float32) for s in outs]
    return pl.pallas_call(
        kernel,
        out_shape=shapes,
        compiler_params=pltpu.CompilerParams(vmem_limit_bytes=48 * 1024 * 1024),
        cost_estimate=pl.CostEstimate(flops=flops, bytes_accessed=10**6, transcendentals=0),
    )(*args)


def pairs_from(count, offset):
    found = []
    for k in range(offset, count, 2):
        found += [(k, (k + 1) % count), ((k + 1) % count, k)]
    return found


def odd_pairs(counts, axis, bit):
    found = []
    for i in range(counts[0]):
        for j in range(counts[1]):
            at = [i, j]
            if bit and at[axis] in (0, counts[axis] - 1):
                at[1 - axis] ^= bit
            else:
                at[axis] = (at[axis] + (1 if at[axis] % 2 else -1)) % counts[axis]
            found.append((i * counts[1] + j, at[0] * counts[1] + at[1]))
    return found


def xor_pairs(counts, rows, cols):
    flat = [(i, j) for i in range(counts[0]) for j in range(counts[1])]
    return [(i * counts[1] + j, (i ^ rows) * counts[1] + (j ^ cols)) for i, j in flat]


def spreads(counts):
    known = np.eye(counts[0] * counts[1], dtype=bool)

    def meet(*swaps):
        return np.logical_or.reduce([known, *(known[[b for _, b in pairs]] for pairs in swaps)])

    even = [xor_pairs(counts, 0, 1), xor_pairs(counts, 1, 0)]
    known = meet(even[0], odd_pairs(counts, 1, 0))
    first = meet(xor_pairs(counts, 6, 0))
    known = meet(even[1], odd_pairs(counts, 0, 0))
    second = meet(xor_pairs(counts, 4, 0), xor_pairs(counts, 4, 2))
    known = meet(even[0], odd_pairs(counts, 1, 1)) | first
    return (meet(even[1], odd_pairs(counts, 0, 1)) | second).all()


def body(counts, height, noise):
    nr, nc = counts
    devices = nr * nc
    width = max(128, devices * 2)
    basis = jnp.asarray(constants(nr, 2 * nc, width))
    both_axes = ("row", "col")
    depth = table_shape(counts)[0]

    def swap(a, b, axis, bit=0):
        gb = lax.ppermute(b, both_axes, odd_pairs(counts, both_axes.index(axis), bit))
        return lax.ppermute(a, axis, pairs_from(lax.axis_size(axis), 0)), gb

    def small_swap(x, rows, cols):
        return lax.ppermute(x, both_axes, xor_pairs(counts, rows, cols))

    both = jnp.pad(noise, ((0, TR), (0, 0))) + jnp.pad(height, ((TR, 0), (0, 0)))
    b, a, table = call(
        functools.partial(begin_kernel, counts), [(32 + depth, 128)] * 2 + [(depth, 128)], both
    )
    if not spreads(counts):
        for axis, count in enumerate(counts):
            bit = 1
            while bit < count:
                table = table + small_swap(table, *((0, bit) if axis else (bit, 0)))
                bit *= 2
    ga, gb = swap(a, b, "col")
    r3, h3, b, a, table = call(
        functools.partial(widen_kernel, counts),
        [(128, 128)] * 2 + [(24 + depth, FC)] * 2 + [(depth, 128)],
        both,
        table,
        gb,
        ga,
    )
    ga, gb = swap(a, b, "row")
    weight, table = call(weights_kernel, [(EXT, 2 * SPEC), (depth, 128)], both, table, basis)
    far = small_swap(table, 6, 0)
    t = call(forward_kernel, [(EXT, 2 * SPEC)], both, r3, basis)[0]
    t, table, b, a = call(
        functools.partial(first_kernel, counts),
        [(EXT, 2 * SPEC), (depth, 128)] + [(24 + depth, EXT)] * 2,
        gb,
        ga,
        t,
        weight,
        basis,
        table,
    )
    y, m, table_too = call(
        functools.partial(inverse_kernel, counts),
        [(EXT, FC), (FR, FC), (depth, 128)],
        t,
        basis,
        both,
        h3,
        gb,
        ga,
        table,
    )
    ga, gb = swap(a, b, "col", 1)
    farther = small_swap(table_too, 4, 0), small_swap(table_too, 4, 2)
    y, table, b, a = call(
        functools.partial(columns_kernel, counts),
        [(EXT, FC), (depth, 128)] + [(24 + depth, FC)] * 2,
        y,
        gb,
        ga,
        table,
        far,
    )
    ga, gb = swap(a, b, "row", 1)
    inner_w, f, gw, gf, near = call(
        functools.partial(inner_kernel, counts, width),
        [(96, TC)] * 2 + [(EXT, FC)] * 2 + [(16, width)],
        y,
        m,
        basis,
    )
    z, w, t, b, a = call(
        functools.partial(second_kernel, counts, width),
        [(TR, TC)] * 2 + [(EXT, 2 * SPEC)] + [(16, EXT)] * 2,
        y,
        m,
        gb,
        ga,
        table,
        *farther,
        inner_w,
        f,
        gw,
        gf,
        near,
        weight,
        basis,
    )
    ga, gb = swap(a, b, "col", 1)
    y, stats = call(inverse_stats_kernel, [(EXT, FC), (1, 128)], t, basis, both, m, z, w)
    y, b, a = call(
        functools.partial(columns_kernel, counts), [(EXT, FC)] + [(16, FC)] * 2, y, gb, ga
    )
    ga, gb = swap(a, b, "row", 1)
    inner_v, stats = call(
        functools.partial(inner_dots_kernel, counts),
        [(96, TC), (1, 128)],
        y,
        m,
        both,
        w,
        stats,
    )
    q, v, stats = call(
        functools.partial(dots_kernel, counts),
        [(TR, TC)] * 2 + [(devices, 128)],
        y,
        m,
        gb,
        ga,
        both,
        w,
        stats,
        inner_v,
    )
    stats = lax.all_to_all(stats, both_axes, 0, 0, tiled=True)
    return tuple(
        call(
            functools.partial(end_kernel, counts, width),
            [(TR, TC)] * 2,
            stats,
            basis,
            m,
            f,
            both,
            z,
            w,
            q,
            v,
        )
    )


def solution(mesh):
    counts = (mesh.shape["row"], mesh.shape["col"])
    spec = P("row", "col")
    return jax.shard_map(
        functools.partial(body, counts),
        mesh=mesh,
        in_specs=(spec, spec),
        out_specs=(spec, spec),
        check_vma=False,
    )
```

```python
import functools

import jax
import jax.numpy as jnp
import ml_dtypes
import numpy as np
from jax import lax
from jax.experimental import pallas as pl
from jax.experimental.pallas import tpu as pltpu
from jax.sharding import PartitionSpec as P

SUB = 128
OV = 8
EXT = SUB + 2 * OV
DAMP = 2.0**-28
SHRINK = 2.0**-20

TR, TC = 128, 256
FR, FC = 160, 384
SPEC = 256

highest = lax.Precision.HIGHEST


def sine(count):
    k = np.arange(1, count + 1, dtype=np.float64)
    basis = np.sqrt(2.0 / (count + 1.0)) * np.sin(np.pi * k[:, None] * k[None, :] / (count + 1.0))
    return basis, 2.0 - 2.0 * np.cos(np.pi * k / (count + 1.0))


def block_constants():
    basis, eig = sine(EXT)
    rows = np.roll(basis, -OV, 0)
    cols = np.pad(basis, ((0, SPEC - EXT), (0, SPEC - EXT)))
    scale = np.pad((eig[:, None] + eig[None, :]) ** 2, ((0, 0), (0, SPEC - EXT)))
    wide = lambda x: np.pad(x, ((0, 0), (0, 2 * SPEC - x.shape[1])))
    high = rows.T.astype(ml_dtypes.bfloat16).astype(np.float64)
    low = (rows.T - high).astype(ml_dtypes.bfloat16).astype(np.float64)
    tile = np.concatenate([x[:, :SUB] for x in (high, high, low)], 1)
    halo = np.concatenate([x[:, SUB:] for x in (high, high, low)], 1)
    inner = np.concatenate([x[:, 16:112] for x in (high, high, low)], 1)
    at = [*range(136, 144), *range(16), *range(112, 136)]
    edge = np.concatenate([x[:, at] for x in (high, high, low)], 1)
    turned = np.hstack([rows.T, np.zeros((EXT, 256 - EXT)), edge])
    return [np.tile(scale, (1, 2)), *(wide(x) for x in (rows, turned, cols, inner, np.hstack([tile, halo])))]


def rows_part(ref):
    return ref[EXT : 2 * EXT, :EXT]


def rows_t_part(ref):
    return ref[2 * EXT : 3 * EXT, :256]


def cols_part(ref):
    return ref[3 * EXT : 3 * EXT + SPEC, :SPEC]


def inner_rows(ref):
    at = 3 * EXT + SPEC
    return ref[at : at + EXT, : 3 * 96]


def edge_rows(ref):
    return ref[2 * EXT : 3 * EXT, 256 : 256 + 3 * 48]


def tile_rows(ref):
    at = 4 * EXT + SPEC
    return ref[at : at + EXT, : 3 * SUB]


def halo_rows(ref):
    at = 4 * EXT + SPEC
    return ref[at : at + EXT, 3 * SUB : 3 * EXT]


def coarse_part(ref, width):
    at, lanes = 5 * EXT + SPEC, 2 * SPEC
    parts = [ref[at + k * width : at + (k + 1) * width] for k in range(-(-width // lanes))]
    return (parts[0] if len(parts) == 1 else jnp.concatenate(parts, axis=1))[:, :width]


def constants(nr, nc, width):
    lanes = 2 * SPEC
    inverse = coarse_inverse(nr, nc, -(-width // lanes) * lanes)[:width]
    parts = [*block_constants(), *np.split(inverse, inverse.shape[1] // lanes, 1)]
    return np.concatenate(parts).astype(np.float32)


def coarse_inverse(nr, nc, width):
    br, er = sine(nr)
    bc, ec = sine(nc)
    both = np.kron(br, bc).reshape(nr, nc // 2, 2, nr * nc).transpose(2, 0, 1, 3)
    both = both.reshape(nr * nc, nr * nc)
    scale = (er[:, None] + ec[None, :]) / (SUB * SUB)
    values = (SUB * SUB * (DAMP + scale * scale)).reshape(-1)
    whole = np.zeros((width, width), np.float32)
    whole[: nr * nc, : nr * nc] = (both / values) @ both.T
    return whole


def dot(a, b, side=0):
    return lax.dot_general(
        a, b, (((1,), (side,)), ((), ())), precision=highest, preferred_element_type=jnp.float32
    )


def lap(x):
    rows, lanes = x.shape
    beside = pltpu.roll(x, 1, 0) + pltpu.roll(x, rows - 1, 0)
    beside = beside + (pltpu.roll(x, 1, 1) + pltpu.roll(x, lanes - 1, 1))
    return 4.0 * x - beside


def lanes_of(shape):
    return lax.broadcasted_iota(jnp.int32, shape, 1)


def rows_of(shape):
    return lax.broadcasted_iota(jnp.int32, shape, 0)


def total(x):
    return jnp.sum(jnp.sum(x, axis=0, keepdims=True), axis=1, keepdims=True)


def place():
    return lax.axis_index("row"), lax.axis_index("col")


def is_even(index):
    return lax.rem(index, 2) == 0


def column_mask(counts):
    j = lax.axis_index("col")
    lane = lanes_of((1, FC))
    right = jnp.where(j < counts[1] - 1, 320, 256)
    left = jnp.where(j > 0, 320, 384)
    return (lane < right) | (lane >= left)


def edge_mask(counts):
    i = lax.axis_index("row")
    row = rows_of((80, 1))
    first = jnp.where(i > 0, 0, 16)
    last = jnp.where(i < counts[0] - 1, 80, 64)
    return (row >= first) & (row < last) & column_mask(counts)


def table_shape(counts):
    return (-(-2 * counts[0] * counts[1] // 1024) * 8, 128)


def table_of(values, counts):
    i, j = place()
    devices = counts[0] * counts[1]
    shape = table_shape(counts)
    at = rows_of(shape) * 128 + lanes_of(shape) - (i * counts[1] + j)
    return jnp.where(at == 0, values[0], jnp.where(at == devices, values[1], 0.0))


def merged(table, *others):
    for other in others:
        table = jnp.where(table != 0.0, table, other)
    return table


def as_row(table, width):
    return jnp.concatenate([table[k : k + 1] for k in range(width // 128)], axis=1)


def row_of(pairs):
    lane = lanes_of((1, 128))
    row = jnp.zeros((1, 128), jnp.float32)
    for k, (left, right) in enumerate(pairs):
        row = jnp.where(lane == k, left, jnp.where(lane == 64 + k, right, row))
    return row


def near_inverse(counts, inverse):
    i, j = place()
    nr, nc = counts[0], 2 * counts[1]
    shape = (16, inverse.shape[0])
    which = rows_of(shape)
    r = i - 1 + which // 4
    c = 2 * j - 1 + which % 4
    inside = (r >= 0) & (r < nr) & (c >= 0) & (c < nc) & (which < 12)
    at = lax.rem(c + 2, 2) * (nr * counts[1]) + r * counts[1] + (c + 2) // 2 - 1
    return dot(jnp.where(inside & (lanes_of(shape) == at), 1.0, 0.0), inverse)


def as_bands(values):
    lane = lanes_of((1, FC))
    bands = []
    for d in range(3):
        left, first, second, right = values[4 * d : 4 * d + 4]
        bands.append(
            jnp.where(
                lane < 128,
                first,
                jnp.where(lane < 256, second, jnp.where(lane < 320, right, left)),
            )
        )
    return bands


def edge_bands(bands):
    above, on, below = bands
    return jnp.concatenate(
        [
            jnp.broadcast_to(above, (16, FC)),
            jnp.broadcast_to(on, (48, FC)),
            jnp.broadcast_to(below, (16, FC)),
        ],
        axis=0,
    )


def jumps(row):
    step = row - pltpu.roll(row, 1, 1)
    lane = lanes_of((1, FC))
    at = [jnp.sum(jnp.where(lane == k, step, 0.0), axis=1, keepdims=True) for k in (0, 128, 256)]
    return jnp.where(
        (lane < 64) | (lane >= 320), at[0], jnp.where(lane < 192, at[1], at[2])
    )


def edge_steps():
    lane = lanes_of((1, FC))
    up = (lane == 0) | (lane == 128) | (lane == 256)
    down = (lane == FC - 1) | (lane == 127) | (lane == 255)
    return jnp.where(up, 1.0, jnp.where(down, -1.0, 0.0))


def halves_of(x):
    high = x.astype(jnp.bfloat16)
    return high, (x - high.astype(jnp.float32)).astype(jnp.bfloat16)


def product(a, b):
    return lax.dot_general(a, b, (((1,), (0,)), ((), ())), preferred_element_type=jnp.float32)


def column_transform(w, basis_ref):
    high, low = halves_of(pltpu.roll(w, OV, 1))
    cols, rest = halves_of(cols_part(basis_ref))
    cols = jnp.concatenate([cols, rest, cols], axis=0)

    def block(at):
        part = slice(at, at + SPEC)
        return product(jnp.concatenate([high[:, part], high[:, part], low[:, part]], axis=1), cols)

    return jnp.concatenate([block(0), block(128)], axis=1)


def row_transform(u, basis_ref, part):
    high, low = halves_of(u)
    rows = part(basis_ref).astype(jnp.bfloat16)
    return product(rows, jnp.concatenate([high, low, high], axis=0))


def weights(means, basis_ref):
    lane = lanes_of((1, 2 * SPEC))
    mean = jnp.where(lane < SPEC, means[0], means[1])
    return 1.0 / (DAMP + mean * basis_ref[:EXT])


def strips_of(t, basis_ref, deep):
    cols = cols_part(basis_ref)
    left = dot(cols[:deep], t[:, :SPEC], 1)
    right = dot(cols[EXT - deep : EXT], t[:, SPEC:], 1)
    both = dot(jnp.concatenate([left, right], axis=0), rows_t_part(basis_ref)[:, :EXT])
    return both[:deep], both[deep:]


def solution_of(t, basis_ref):
    v = dot(rows_part(basis_ref), t)
    cols = cols_part(basis_ref)
    first, second = dot(v[:, :SPEC], cols), dot(v[:, SPEC:], cols)
    y = jnp.concatenate(
        [first[:, :128], first[:, 128:] + second[:, :128], second[:, 128:]], axis=1
    )
    return pltpu.roll(y, FC - OV, 1)


def core_sums(x):
    return [total(x[:, :128]), total(x[:, 128:256])]


def add_columns(y, from_left, from_right):
    far = from_left.shape[0] - OV
    gap = jnp.zeros((56 - far, EXT), jnp.float32)
    turned = jnp.concatenate(
        [from_right[8:], gap, from_right[:8], from_left[far:], gap, from_left[:far]], axis=0
    )
    back = turned.T
    lane = lanes_of((EXT, 128))
    rolled = pltpu.roll(back, 64, 1)
    first = y[:, :128] + jnp.where(lane < 8, rolled, 0.0)
    second = y[:, 128:256] + jnp.where(lane >= 120, rolled, 0.0)
    third = y[:, 256:] + jnp.where((lane < 16) | (lane >= 112), back, 0.0)
    return jnp.concatenate([first, second, third], axis=1)


def pack_rows(y, deep):
    return jnp.concatenate([y[136:], y[: deep - 8]], axis=0), y[136 - deep : 136]


def edges(y, from_above, from_below):
    far = from_above.shape[0] - OV
    none = jnp.zeros((8, FC), jnp.float32)
    return jnp.concatenate(
        [
            from_above[:8] if far == 16 else none,
            y[136:] + from_above[far - 8 : far],
            y[:8] + from_above[far:],
            y[8:24],
            y[104:120],
            y[120:136] + from_below[:16],
            from_below[16:] if far == 16 else none,
        ],
        axis=0,
    )


def edge_part(frame):
    return jnp.concatenate([frame[144:], frame[:24], frame[104:144]], axis=0)


def with_edges(edge, inner):
    return jnp.concatenate([edge[16:32, :TC], inner, edge[48:64, :TC]], axis=0)


def sides(index, count, a, b):
    even = is_even(index)
    before = jnp.where(index > 0, jnp.where(even, b, a), 0.0)
    after = jnp.where(index < count - 1, jnp.where(even, a, b), 0.0)
    return before, after


def crossed(a, b):
    odd = lax.rem(lax.axis_index("row"), 2) == 1
    return jnp.where(odd, b, a), jnp.where(odd, a, b)


def send_columns(index, a_ref, b_ref, before, after):
    even = is_even(index)
    a_ref[...], b_ref[...] = crossed(
        jnp.where(even, after, before), jnp.where(even, before, after)
    )


def send(index, a_ref, b_ref, before, after):
    even = is_even(index)
    a_ref[...] = jnp.where(even, after, before)
    b_ref[...] = jnp.where(even, before, after)


def begin_kernel(counts, both_ref, b_ref, a_ref, table_ref):
    r, h = both_ref[:TR], both_ref[TR:]
    lane = lanes_of((128, 128))
    packed = jnp.where(
        lane < 16,
        r[:, :128],
        jnp.where(
            lane < 64,
            pltpu.roll(h[:, :128], 16, 1),
            jnp.where(lane < 112, pltpu.roll(h[:, 128:], 112, 1), r[:, 128:]),
        ),
    )
    turned = packed.T
    table = table_of(core_sums(r), counts)
    table_ref[...] = table
    send_columns(
        lax.axis_index("col"),
        a_ref,
        b_ref,
        jnp.concatenate([turned[:32], table], axis=0),
        jnp.concatenate([turned[96:], table], axis=0),
    )


def widen_kernel(counts, both_ref, own_ref, gb_ref, ga_ref, r3_ref, h3_ref, b_ref, a_ref, table_ref):
    i, j = place()
    from_left, from_right = sides(j, counts[1], *crossed(ga_ref[:32], gb_ref[:32]))
    turned = jnp.concatenate([from_right, jnp.zeros((64, 128), jnp.float32), from_left], axis=0)
    back = turned.T
    lane = lanes_of((128, 128))
    edge = (lane < 16) | (lane >= 112)
    r3 = jnp.where(edge, back, 0.0)
    h3 = jnp.where(
        lane < 16, pltpu.roll(back, 112, 1), jnp.where(lane >= 112, pltpu.roll(back, 16, 1), 0.0)
    )
    r3_ref[...] = r3
    h3_ref[...] = h3
    r, h = both_ref[:TR], both_ref[TR:]
    table = merged(own_ref[...], ga_ref[32:], gb_ref[32:])
    table_ref[...] = table
    wide = jnp.concatenate([table, jnp.zeros((table.shape[0], FC - 128), jnp.float32)], axis=1)

    def strip(r_rows, h_rows):
        return jnp.concatenate(
            [
                jnp.concatenate([r[r_rows], r3[r_rows]], axis=1),
                jnp.concatenate([h[h_rows], h3[h_rows]], axis=1),
                wide,
            ],
            axis=0,
        )

    send(i, a_ref, b_ref, strip(slice(0, 8), slice(0, 16)), strip(slice(120, 128), slice(112, 128)))


def weights_kernel(both_ref, table_ref, basis_ref, weights_ref, table_out):
    h = both_ref[TR:]
    means = [x / (SUB * SUB) for x in core_sums(h * h * h)]
    weights_ref[...] = weights(means, basis_ref)
    table_out[...] = table_ref[...]


def forward_kernel(both_ref, r3_ref, basis_ref, t_ref):
    r = both_ref[:TR]
    u = column_transform(jnp.concatenate([r, r3_ref[...]], axis=1), basis_ref)
    t_ref[...] = row_transform(u, basis_ref, tile_rows)


def first_kernel(
    counts,
    gb_ref,
    ga_ref,
    tile_ref,
    weights_ref,
    basis_ref,
    table_ref,
    t_ref,
    table_out,
    b_ref,
    a_ref,
):
    i, j = place()
    above, below = sides(i, counts[0], ga_ref[:8], gb_ref[:8])
    u = column_transform(jnp.concatenate([below, above], axis=0), basis_ref)
    t = (tile_ref[...] + row_transform(u, basis_ref, halo_rows)) * weights_ref[...]
    t_ref[...] = t
    send_columns(j, a_ref, b_ref, *strips_of(t, basis_ref, 24))
    table_out[...] = merged(table_ref[...], ga_ref[24:, :128], gb_ref[24:, :128])


def inverse_kernel(counts, t_ref, basis_ref, both_ref, h3_ref, gb_ref, ga_ref, y_ref, m_ref):
    y_ref[...] = solution_of(t_ref[...], basis_ref)
    above, below = sides(lax.axis_index("row"), counts[0], ga_ref[8:24], gb_ref[8:24])
    h = jnp.concatenate([both_ref[TR:], h3_ref[...]], axis=1)
    tall = jnp.concatenate([h, below, above], axis=0)
    m_ref[...] = tall * tall * tall


def columns_kernel(counts, y_ref, *refs):
    i, j = place()
    (ga_ref, gb_ref), refs = (refs[:2] if len(refs) == 7 else refs[1::-1]), refs[2:]
    deep = 24 if len(refs) == 5 else 16
    y = add_columns(y_ref[...], *sides(j, counts[1], *crossed(ga_ref[:deep], gb_ref[:deep])))
    strips = pack_rows(y, deep)
    if len(refs) == 5:
        table_ref, out_ref, table_out, b_ref, a_ref = refs
        table = merged(table_ref[...], ga_ref[24:, :128], gb_ref[24:, :128])
        table_out[...] = table
        wide = jnp.concatenate([table, jnp.zeros((table.shape[0], FC - 128), jnp.float32)], axis=1)
        strips = [jnp.concatenate([x, wide], axis=0) for x in strips]
    else:
        out_ref, b_ref, a_ref = refs
    out_ref[...] = y
    send(i, a_ref, b_ref, *strips)


def inner_kernel(counts, width, y_ref, m_ref, basis_ref, w_ref, f_ref, gw_ref, gf_ref, near_ref):
    mask = column_mask(counts)
    s = jnp.where(mask, y_ref[8:120], 0.0)
    m = m_ref[8:120]
    w = DAMP * s + lap(m * lap(s))
    w = jnp.where(mask, w[8:104], 0.0) * SHRINK
    f = lap(m * edge_steps())
    f = jnp.where(mask, f[8:104], 0.0) * SHRINK
    w_ref[...] = w[:, :TC]
    f_ref[...] = f[:, :TC]
    gw_ref[...] = row_transform(w, basis_ref, inner_rows)
    gf_ref[...] = row_transform(f, basis_ref, inner_rows)
    near_ref[...] = near_inverse(counts, coarse_part(basis_ref, width))


def second_kernel(
    counts,
    width,
    y_ref,
    m_ref,
    gb_ref,
    ga_ref,
    table_ref,
    inner_w_ref,
    f_ref,
    gw_ref,
    gf_ref,
    near_ref,
    weights_ref,
    basis_ref,
    z_ref,
    w_ref,
    t_ref,
    b_ref,
    a_ref,
):
    i, j = place()
    y = y_ref[...]
    mask = edge_mask(counts)
    s = edges(y, *sides(i, counts[0], ga_ref[:24], gb_ref[:24]))
    s = jnp.where(mask, s, 0.0)
    table = merged(table_ref[...], ga_ref[24:, :128], gb_ref[24:, :128])
    picked = jnp.sum(near_ref[...] * as_row(table, width), axis=1, keepdims=True)
    bands = as_bands([picked[k : k + 1] for k in range(12)])
    coarse = edge_bands(bands)
    m = edge_part(m_ref)
    flow = m * (lap(s) + lap(coarse))
    z = s + coarse
    w = jnp.where(mask, DAMP * z + lap(flow), 0.0) * SHRINK
    step = jumps(bands[1])
    damped = (DAMP * SHRINK) * bands[1]
    z_ref[...] = with_edges(z, y[16:112, :TC] + bands[1][:, :TC])
    w_ref[...] = with_edges(w, inner_w_ref[...] + step[:, :TC] * f_ref[...] + damped[:, :TC])
    lane = lanes_of((EXT, 256))
    ones = jnp.where((lane >= 16) & (lane < 112), rows_t_part(basis_ref), 0.0)
    ones = jnp.sum(ones, axis=1, keepdims=True)
    u = gw_ref[...] + step * gf_ref[...] + ones * damped
    u = u + row_transform(jnp.concatenate([w[8:32], w[48:72]], axis=0), basis_ref, edge_rows)
    t = column_transform(u, basis_ref) * weights_ref[...]
    t_ref[...] = t
    send_columns(j, a_ref, b_ref, *strips_of(t, basis_ref, 16))


def inverse_stats_kernel(t_ref, basis_ref, both_ref, m_ref, z_ref, w_ref, y_ref, stats_ref):
    y_ref[...] = solution_of(t_ref[...], basis_ref)
    rt, mt, zt, wt = both_ref[:TR], m_ref[:TR, :TC], z_ref[...], w_ref[...]
    lane, row = lanes_of((1, 256)), rows_of((128, 1))
    along = (lane % 128 != 0) & (lane % 128 != 127)
    top, low = mt[:1], mt[127:]
    side = jnp.sum(jnp.where((row > 0) & (row < 127), mt, 0.0), axis=0, keepdims=True)

    def halves(x):
        return [
            jnp.sum(x[:, :128], axis=1, keepdims=True),
            jnp.sum(x[:, 128:], axis=1, keepdims=True),
        ]

    first, last = lane % 128 == 0, lane % 128 == 127
    zero = jnp.zeros((1, 1), jnp.float32)
    stats_ref[...] = row_of(
        [
            core_sums(rt * zt),
            core_sums(zt * wt),
            core_sums(wt),
            halves(jnp.where(along, top, 0.0)),
            halves(jnp.where(along, low, 0.0)),
            halves(jnp.where(first, side, 0.0)),
            halves(jnp.where(last, side, 0.0)),
            halves(jnp.where(first, top, 0.0)),
            halves(jnp.where(last, top, 0.0)),
            halves(jnp.where(first, low, 0.0)),
            halves(jnp.where(last, low, 0.0)),
            *[[zero, zero]] * 4,
            core_sums(rt),
        ]
    )


def inner_dots_kernel(counts, y_ref, m_ref, both_ref, w_ref, stats_ref, v_ref, stats_out):
    q = jnp.where(column_mask(counts), y_ref[8:120], 0.0)
    v = (DAMP * q + lap(m_ref[8:120] * lap(q)))[8:104, :TC]
    q = q[8:104, :TC]
    v_ref[...] = v
    rest = [
        core_sums(v),
        core_sums(both_ref[16:112] * q),
        core_sums(w_ref[16:112] * q),
        core_sums(v * q),
    ]
    zero = jnp.zeros((1, 1), jnp.float32)
    stats_out[...] = stats_ref[...] + row_of([[zero, zero]] * 11 + rest)


def dots_kernel(
    counts, y_ref, m_ref, gb_ref, ga_ref, both_ref, w_ref, stats_ref, inner_v_ref, q_ref, v_ref, stats_out
):
    i, j = place()
    y = y_ref[...]
    q = edges(y, *sides(i, counts[0], ga_ref[...], gb_ref[...]))
    q = jnp.where(edge_mask(counts), q, 0.0)
    v = DAMP * q + lap(edge_part(m_ref) * lap(q))
    q_ref[...] = with_edges(q, y[16:112, :TC])
    v_ref[...] = with_edges(v, inner_v_ref[...])
    qe, ve = (jnp.concatenate([x[16:32, :TC], x[48:64, :TC]], axis=0) for x in (q, v))
    re = jnp.concatenate([both_ref[:16], both_ref[112:128]], axis=0)
    we = jnp.concatenate([w_ref[:16], w_ref[112:]], axis=0)
    rest = [core_sums(ve), core_sums(re * qe), core_sums(we * qe), core_sums(ve * qe)]
    zero = jnp.zeros((1, 1), jnp.float32)
    row = stats_ref[...] + row_of([[zero, zero]] * 11 + rest)
    stats_out[...] = jnp.broadcast_to(row, stats_out.shape)


def end_kernel(
    counts,
    width,
    stats_ref,
    basis_ref,
    m_ref,
    f_ref,
    both_ref,
    z_ref,
    w_ref,
    q_ref,
    v_ref,
    solution_ref,
    residual_ref,
):
    i, j = place()
    tiles_c = counts[1]
    devices = counts[0] * tiles_c
    rows = stats_ref[...]
    st = jnp.concatenate([rows, pltpu.roll(rows, 64, 1)], axis=0)
    inverse = coarse_part(basis_ref, width)[: 2 * devices, : 2 * devices]
    g = jnp.broadcast_to(dot(inverse, st)[:, 2:3], st.shape)
    lane, row = lanes_of(st.shape), rows_of(st.shape)
    device = row % devices
    column = device % tiles_c
    on_left = row < devices

    def from_row(distance):
        return pltpu.roll(g, distance % (2 * devices), 0)

    up = jnp.where(device >= tiles_c, from_row(tiles_c), 0.0)
    down = jnp.where(device < devices - tiles_c, from_row(-tiles_c), 0.0)
    left = jnp.where(on_left, jnp.where(column > 0, from_row(1 - devices), 0.0), from_row(devices))
    right = jnp.where(
        on_left, from_row(-devices), jnp.where(column < tiles_c - 1, from_row(devices - 1), 0.0)
    )
    du, dd, dl, dr = g - up, g - down, g - left, g - right
    across = jnp.where(
        (lane == 3) | (lane == 7) | (lane == 8),
        du,
        jnp.where((lane == 4) | (lane == 9) | (lane == 10), dd, 0.0),
    )
    across = across + jnp.where(
        (lane == 5) | (lane == 7) | (lane == 9),
        dl,
        jnp.where((lane == 6) | (lane == 8) | (lane == 10), dr, 0.0),
    )
    factor = jnp.where((lane == 2) | (lane == 15), g, across * across)
    factor = jnp.where(lane == 11, 2.0 * g, factor)
    factor = jnp.where((lane < 2) | ((lane >= 12) & (lane < 15)), 1.0, factor)
    terms = jnp.where(lane == 16, (DAMP * SUB * SUB) * g * g, st * factor)
    sums = jnp.sum(terms, axis=0, keepdims=True)

    def whole(wanted):
        return jnp.sum(jnp.where(wanted, sums, 0.0), axis=1, keepdims=True)

    at = lanes_of((1, 128))
    rz, zw = whole(at == 0), whole(at == 1)
    ry = whole((at == 12) | (at == 15))
    yw = whole((at == 13) | (at == 2))
    yv = whole(((at >= 3) & (at < 12)) | (at == 14) | (at == 16))
    a = rz / zw
    rz1 = rz - a * ry - a * zw + a * a * yw
    beta1 = 1.0 + rz1 / rz
    dad = (beta1 * beta1 * zw - 2.0 * a * beta1 * yw) * (1.0 / SHRINK) + a * a * yv
    a1 = rz1 / dad
    r = i - 1 + lane // 4
    c = 2 * j - 1 + lane % 4
    inside = (r >= 0) & (r < counts[0]) & (c >= 0) & (c < 2 * tiles_c) & (lane < 12)
    where = lax.rem(c + 2, 2) * devices + r * tiles_c + (c + 2) // 2 - 1
    picked = jnp.sum(jnp.where(inside & (row == where), g, 0.0), axis=0, keepdims=True)
    bands = as_bands([picked[:, k : k + 1] for k in range(12)])
    on = bands[1][:, :TC]
    coarse = edge_bands(bands)
    image = DAMP * coarse + lap(edge_part(m_ref) * lap(coarse))
    image = with_edges(image, (jumps(bands[1]) * (1.0 / SHRINK))[:, :TC] * f_ref[...] + DAMP * on)
    y = q_ref[...] + on
    v = v_ref[...] + image
    z, w = z_ref[...], w_ref[...]
    solution_ref[...] = (a * SHRINK) * z + a1 * (beta1 * z - a * y)
    residual_ref[...] = both_ref[:TR] - a * w - a1 * ((beta1 * (1.0 / SHRINK)) * w - a * v)


def call(kernel, outs, *args, flops=10**9):
    shapes = [jax.ShapeDtypeStruct(s, jnp.float32) for s in outs]
    return pl.pallas_call(
        kernel,
        out_shape=shapes,
        compiler_params=pltpu.CompilerParams(vmem_limit_bytes=48 * 1024 * 1024),
        cost_estimate=pl.CostEstimate(flops=flops, bytes_accessed=10**6, transcendentals=0),
    )(*args)


def pairs_from(count, offset):
    found = []
    for k in range(offset, count, 2):
        found += [(k, (k + 1) % count), ((k + 1) % count, k)]
    return found


def odd_pairs(counts, axis, bit):
    found = []
    for i in range(counts[0]):
        for j in range(counts[1]):
            at = [i, j]
            if bit and at[axis] in (0, counts[axis] - 1):
                at[1 - axis] ^= bit
            else:
                at[axis] = (at[axis] + (1 if at[axis] % 2 else -1)) % counts[axis]
            found.append((i * counts[1] + j, at[0] * counts[1] + at[1]))
    return found


def xor_pairs(counts, rows, cols):
    flat = [(i, j) for i in range(counts[0]) for j in range(counts[1])]
    return [(i * counts[1] + j, (i ^ rows) * counts[1] + (j ^ cols)) for i, j in flat]


def spreads(counts):
    known = np.eye(counts[0] * counts[1], dtype=bool)

    def meet(*swaps):
        return np.logical_or.reduce([known, *(known[[b for _, b in pairs]] for pairs in swaps)])

    even = [xor_pairs(counts, 0, 1), xor_pairs(counts, 1, 0)]
    known = meet(even[0], odd_pairs(counts, 1, 0))
    known = meet(even[1], odd_pairs(counts, 0, 0), xor_pairs(counts, 4, 0))
    known = meet(even[0], odd_pairs(counts, 1, 2))
    return meet(even[1], odd_pairs(counts, 0, 0)).all()


def body(counts, height, noise):
    nr, nc = counts
    devices = nr * nc
    width = max(128, devices * 2)
    basis = jnp.asarray(constants(nr, 2 * nc, width))
    both_axes = ("row", "col")
    depth = table_shape(counts)[0]

    def swap_columns(a, b, bit=0):
        even, odd = xor_pairs(counts, 0, 1), odd_pairs(counts, 1, bit)
        rows = [k // nc % 2 for k in range(devices)]
        first = [(even if row else odd)[k] for k, row in enumerate(rows)]
        second = [(odd if row else even)[k] for k, row in enumerate(rows)]
        gb = lax.ppermute(b, both_axes, first)
        return lax.ppermute(a, both_axes, second), gb

    def swap(a, b, axis, bit=0):
        gb = lax.ppermute(b, both_axes, odd_pairs(counts, both_axes.index(axis), bit))
        return lax.ppermute(a, axis, pairs_from(lax.axis_size(axis), 0)), gb

    def small_swap(x, rows, cols):
        return lax.ppermute(x, both_axes, xor_pairs(counts, rows, cols))

    both = jnp.pad(noise, ((0, TR), (0, 0))) + jnp.pad(height, ((TR, 0), (0, 0)))
    b, a, table = call(
        functools.partial(begin_kernel, counts), [(32 + depth, 128)] * 2 + [(depth, 128)], both
    )
    if not spreads(counts):
        for axis, count in enumerate(counts):
            bit = 1
            while bit < count:
                table = table + small_swap(table, *((0, bit) if axis else (bit, 0)))
                bit *= 2
    ga, gb = swap_columns(a, b)
    r3, h3, b, a, table = call(
        functools.partial(widen_kernel, counts),
        [(128, 128)] * 2 + [(24 + depth, FC)] * 2 + [(depth, 128)],
        both,
        table,
        gb,
        ga,
    )
    ga, gb = swap(a, b, "row")
    weight, table = call(weights_kernel, [(EXT, 2 * SPEC), (depth, 128)], both, table, basis)
    far = small_swap(table, 4, 0)
    t = call(forward_kernel, [(EXT, 2 * SPEC)], both, r3, basis)[0]
    t, table, b, a = call(
        functools.partial(first_kernel, counts),
        [(EXT, 2 * SPEC), (depth, 128)] + [(24, EXT)] * 2,
        gb,
        ga,
        t,
        weight,
        basis,
        table,
    )
    table = merged(table, far)
    wide = jnp.pad(table, ((0, 0), (0, EXT - 128)))
    y, m = call(
        functools.partial(inverse_kernel, counts),
        [(EXT, FC), (FR, FC)],
        t,
        basis,
        both,
        h3,
        gb,
        ga,
    )
    ga, gb = swap_columns(*(jnp.concatenate([x, wide], axis=0) for x in (a, b)), 2)
    y, table, b, a = call(
        functools.partial(columns_kernel, counts),
        [(EXT, FC), (depth, 128)] + [(24 + depth, FC)] * 2,
        y,
        ga,
        gb,
        table,
    )
    ga, gb = swap(a, b, "row")
    inner_w, f, gw, gf, near = call(
        functools.partial(inner_kernel, counts, width),
        [(96, TC)] * 2 + [(EXT, FC)] * 2 + [(16, width)],
        y,
        m,
        basis,
    )
    z, w, t, b, a = call(
        functools.partial(second_kernel, counts, width),
        [(TR, TC)] * 2 + [(EXT, 2 * SPEC)] + [(16, EXT)] * 2,
        y,
        m,
        gb,
        ga,
        table,
        inner_w,
        f,
        gw,
        gf,
        near,
        weight,
        basis,
    )
    ga, gb = swap_columns(a, b, 2)
    y, stats = call(inverse_stats_kernel, [(EXT, FC), (1, 128)], t, basis, both, m, z, w)
    y, b, a = call(
        functools.partial(columns_kernel, counts), [(EXT, FC)] + [(16, FC)] * 2, y, gb, ga
    )
    ga, gb = swap(a, b, "row", 1)
    inner_v, stats = call(
        functools.partial(inner_dots_kernel, counts),
        [(96, TC), (1, 128)],
        y,
        m,
        both,
        w,
        stats,
    )
    q, v, stats = call(
        functools.partial(dots_kernel, counts),
        [(TR, TC)] * 2 + [(devices, 128)],
        y,
        m,
        gb,
        ga,
        both,
        w,
        stats,
        inner_v,
    )
    stats = lax.all_to_all(stats, both_axes, 0, 0, tiled=True)
    return tuple(
        call(
            functools.partial(end_kernel, counts, width),
            [(TR, TC)] * 2,
            stats,
            basis,
            m,
            f,
            both,
            z,
            w,
            q,
            v,
        )
    )


def solution(mesh):
    counts = (mesh.shape["row"], mesh.shape["col"])
    spec = P("row", "col")
    return jax.shard_map(
        functools.partial(body, counts),
        mesh=mesh,
        in_specs=(spec, spec),
        out_specs=(spec, spec),
        check_vma=False,
    )
```

```python
import functools

import jax
import jax.numpy as jnp
import ml_dtypes
import numpy as np
from jax import lax
from jax.experimental import pallas as pl
from jax.experimental.pallas import tpu as pltpu
from jax.sharding import PartitionSpec as P

SUB = 128
OV = 8
EXT = SUB + 2 * OV
DAMP = 2.0**-28
SHRINK = 2.0**-20

TR, TC = 128, 256
FR, FC = 160, 384
SPEC = 256

highest = lax.Precision.HIGHEST


def sine(count):
    k = np.arange(1, count + 1, dtype=np.float64)
    basis = np.sqrt(2.0 / (count + 1.0)) * np.sin(np.pi * k[:, None] * k[None, :] / (count + 1.0))
    return basis, 2.0 - 2.0 * np.cos(np.pi * k / (count + 1.0))


def block_constants():
    basis, eig = sine(EXT)
    rows = np.roll(basis, -OV, 0)
    cols = np.pad(basis, ((0, SPEC - EXT), (0, SPEC - EXT)))
    scale = np.pad((eig[:, None] + eig[None, :]) ** 2, ((0, 0), (0, SPEC - EXT)))
    wide = lambda x: np.pad(x, ((0, 0), (0, 2 * SPEC - x.shape[1])))
    high = rows.T.astype(ml_dtypes.bfloat16).astype(np.float64)
    low = (rows.T - high).astype(ml_dtypes.bfloat16).astype(np.float64)
    tile = np.concatenate([x[:, :SUB] for x in (high, high, low)], 1)
    halo = np.concatenate([x[:, SUB:] for x in (high, high, low)], 1)
    inner = np.concatenate([x[:, 16:112] for x in (high, high, low)], 1)
    at = [*range(136, 144), *range(16), *range(112, 136)]
    edge = np.concatenate([x[:, at] for x in (high, high, low)], 1)
    turned = np.hstack([rows.T, np.zeros((EXT, 256 - EXT)), edge])
    return [np.tile(scale, (1, 2)), *(wide(x) for x in (rows, turned, cols, inner, np.hstack([tile, halo])))]


def rows_part(ref):
    return ref[EXT : 2 * EXT, :EXT]


def rows_t_part(ref):
    return ref[2 * EXT : 3 * EXT, :256]


def cols_part(ref):
    return ref[3 * EXT : 3 * EXT + SPEC, :SPEC]


def inner_rows(ref):
    at = 3 * EXT + SPEC
    return ref[at : at + EXT, : 3 * 96]


def edge_rows(ref):
    return ref[2 * EXT : 3 * EXT, 256 : 256 + 3 * 48]


def tile_rows(ref):
    at = 4 * EXT + SPEC
    return ref[at : at + EXT, : 3 * SUB]


def halo_rows(ref):
    at = 4 * EXT + SPEC
    return ref[at : at + EXT, 3 * SUB : 3 * EXT]


def coarse_part(ref, width):
    at, lanes = 5 * EXT + SPEC, 2 * SPEC
    parts = [ref[at + k * width : at + (k + 1) * width] for k in range(-(-width // lanes))]
    return (parts[0] if len(parts) == 1 else jnp.concatenate(parts, axis=1))[:, :width]


def constants(nr, nc, width):
    lanes = 2 * SPEC
    inverse = coarse_inverse(nr, nc, -(-width // lanes) * lanes)[:width]
    parts = [*block_constants(), *np.split(inverse, inverse.shape[1] // lanes, 1)]
    return np.concatenate(parts).astype(np.float32)


def coarse_inverse(nr, nc, width):
    br, er = sine(nr)
    bc, ec = sine(nc)
    both = np.kron(br, bc).reshape(nr, nc // 2, 2, nr * nc).transpose(2, 0, 1, 3)
    both = both.reshape(nr * nc, nr * nc)
    scale = (er[:, None] + ec[None, :]) / (SUB * SUB)
    values = (SUB * SUB * (DAMP + scale * scale)).reshape(-1)
    whole = np.zeros((width, width), np.float32)
    whole[: nr * nc, : nr * nc] = (both / values) @ both.T
    return whole


def dot(a, b, side=0):
    return lax.dot_general(
        a, b, (((1,), (side,)), ((), ())), precision=highest, preferred_element_type=jnp.float32
    )


def lap(x):
    rows, lanes = x.shape
    beside = pltpu.roll(x, 1, 0) + pltpu.roll(x, rows - 1, 0)
    beside = beside + (pltpu.roll(x, 1, 1) + pltpu.roll(x, lanes - 1, 1))
    return 4.0 * x - beside


def lanes_of(shape):
    return lax.broadcasted_iota(jnp.int32, shape, 1)


def rows_of(shape):
    return lax.broadcasted_iota(jnp.int32, shape, 0)


def total(x):
    return jnp.sum(jnp.sum(x, axis=0, keepdims=True), axis=1, keepdims=True)


def place():
    return lax.axis_index("row"), lax.axis_index("col")


def is_even(index):
    return lax.rem(index, 2) == 0


def column_mask(counts):
    j = lax.axis_index("col")
    lane = lanes_of((1, FC))
    right = jnp.where(j < counts[1] - 1, 320, 256)
    left = jnp.where(j > 0, 320, 384)
    return (lane < right) | (lane >= left)


def edge_mask(counts):
    i = lax.axis_index("row")
    row = rows_of((80, 1))
    first = jnp.where(i > 0, 0, 16)
    last = jnp.where(i < counts[0] - 1, 80, 64)
    return (row >= first) & (row < last) & column_mask(counts)


def table_shape(counts):
    return (-(-2 * counts[0] * counts[1] // 1024) * 8, 128)


def table_of(values, counts):
    i, j = place()
    devices = counts[0] * counts[1]
    shape = table_shape(counts)
    at = rows_of(shape) * 128 + lanes_of(shape) - (i * counts[1] + j)
    return jnp.where(at == 0, values[0], jnp.where(at == devices, values[1], 0.0))


def merged(table, *others):
    for other in others:
        table = jnp.where(table != 0.0, table, other)
    return table


def as_row(table, width):
    return jnp.concatenate([table[k : k + 1] for k in range(width // 128)], axis=1)


def row_of(pairs):
    lane = lanes_of((1, 128))
    row = jnp.zeros((1, 128), jnp.float32)
    for k, (left, right) in enumerate(pairs):
        row = jnp.where(lane == k, left, jnp.where(lane == 64 + k, right, row))
    return row


def near_inverse(counts, inverse):
    i, j = place()
    nr, nc = counts[0], 2 * counts[1]
    shape = (16, inverse.shape[0])
    which = rows_of(shape)
    r = i - 1 + which // 4
    c = 2 * j - 1 + which % 4
    inside = (r >= 0) & (r < nr) & (c >= 0) & (c < nc) & (which < 12)
    at = lax.rem(c + 2, 2) * (nr * counts[1]) + r * counts[1] + (c + 2) // 2 - 1
    return dot(jnp.where(inside & (lanes_of(shape) == at), 1.0, 0.0), inverse)


def as_bands(values):
    lane = lanes_of((1, FC))
    bands = []
    for d in range(3):
        left, first, second, right = values[4 * d : 4 * d + 4]
        bands.append(
            jnp.where(
                lane < 128,
                first,
                jnp.where(lane < 256, second, jnp.where(lane < 320, right, left)),
            )
        )
    return bands


def edge_bands(bands):
    above, on, below = bands
    return jnp.concatenate(
        [
            jnp.broadcast_to(above, (16, FC)),
            jnp.broadcast_to(on, (48, FC)),
            jnp.broadcast_to(below, (16, FC)),
        ],
        axis=0,
    )


def jumps(row):
    step = row - pltpu.roll(row, 1, 1)
    lane = lanes_of((1, FC))
    at = [jnp.sum(jnp.where(lane == k, step, 0.0), axis=1, keepdims=True) for k in (0, 128, 256)]
    return jnp.where(
        (lane < 64) | (lane >= 320), at[0], jnp.where(lane < 192, at[1], at[2])
    )


def edge_steps():
    lane = lanes_of((1, FC))
    up = (lane == 0) | (lane == 128) | (lane == 256)
    down = (lane == FC - 1) | (lane == 127) | (lane == 255)
    return jnp.where(up, 1.0, jnp.where(down, -1.0, 0.0))


def halves_of(x):
    high = x.astype(jnp.bfloat16)
    return high, (x - high.astype(jnp.float32)).astype(jnp.bfloat16)


def product(a, b):
    return lax.dot_general(a, b, (((1,), (0,)), ((), ())), preferred_element_type=jnp.float32)


def column_transform(w, basis_ref):
    high, low = halves_of(pltpu.roll(w, OV, 1))
    cols, rest = halves_of(cols_part(basis_ref))
    cols = jnp.concatenate([cols, rest, cols], axis=0)

    def block(at):
        part = slice(at, at + SPEC)
        return product(jnp.concatenate([high[:, part], high[:, part], low[:, part]], axis=1), cols)

    return jnp.concatenate([block(0), block(128)], axis=1)


def row_transform(u, basis_ref, part):
    high, low = halves_of(u)
    rows = part(basis_ref).astype(jnp.bfloat16)
    return product(rows, jnp.concatenate([high, low, high], axis=0))


def weights(means, basis_ref):
    lane = lanes_of((1, 2 * SPEC))
    mean = jnp.where(lane < SPEC, means[0], means[1])
    return 1.0 / (DAMP + mean * basis_ref[:EXT])


def strips_of(t, basis_ref, deep):
    cols = cols_part(basis_ref)
    left = dot(cols[:deep], t[:, :SPEC], 1)
    right = dot(cols[EXT - deep : EXT], t[:, SPEC:], 1)
    both = dot(jnp.concatenate([left, right], axis=0), rows_t_part(basis_ref)[:, :EXT])
    return both[:deep], both[deep:]


def solution_of(t, basis_ref):
    v = dot(rows_part(basis_ref), t)
    cols = cols_part(basis_ref)
    first, second = dot(v[:, :SPEC], cols), dot(v[:, SPEC:], cols)
    y = jnp.concatenate(
        [first[:, :128], first[:, 128:] + second[:, :128], second[:, 128:]], axis=1
    )
    return pltpu.roll(y, FC - OV, 1)


def core_sums(x):
    return [total(x[:, :128]), total(x[:, 128:256])]


def add_columns(y, from_left, from_right):
    far = from_left.shape[0] - OV
    gap = jnp.zeros((56 - far, EXT), jnp.float32)
    turned = jnp.concatenate(
        [from_right[8:], gap, from_right[:8], from_left[far:], gap, from_left[:far]], axis=0
    )
    back = turned.T
    lane = lanes_of((EXT, 128))
    rolled = pltpu.roll(back, 64, 1)
    first = y[:, :128] + jnp.where(lane < 8, rolled, 0.0)
    second = y[:, 128:256] + jnp.where(lane >= 120, rolled, 0.0)
    third = y[:, 256:] + jnp.where((lane < 16) | (lane >= 112), back, 0.0)
    return jnp.concatenate([first, second, third], axis=1)


def pack_rows(y, deep):
    return jnp.concatenate([y[136:], y[: deep - 8]], axis=0), y[136 - deep : 136]


def edges(y, from_above, from_below):
    far = from_above.shape[0] - OV
    none = jnp.zeros((8, FC), jnp.float32)
    return jnp.concatenate(
        [
            from_above[:8] if far == 16 else none,
            y[136:] + from_above[far - 8 : far],
            y[:8] + from_above[far:],
            y[8:24],
            y[104:120],
            y[120:136] + from_below[:16],
            from_below[16:] if far == 16 else none,
        ],
        axis=0,
    )


def edge_part(frame):
    return jnp.concatenate([frame[144:], frame[:24], frame[104:144]], axis=0)


def with_edges(edge, inner):
    return jnp.concatenate([edge[16:32, :TC], inner, edge[48:64, :TC]], axis=0)


def sides(index, count, a, b):
    even = is_even(index)
    before = jnp.where(index > 0, jnp.where(even, b, a), 0.0)
    after = jnp.where(index < count - 1, jnp.where(even, a, b), 0.0)
    return before, after


def send(index, a_ref, b_ref, before, after):
    even = is_even(index)
    a_ref[...] = jnp.where(even, after, before)
    b_ref[...] = jnp.where(even, before, after)


def begin_kernel(counts, both_ref, b_ref, a_ref, table_ref):
    r, h = both_ref[:TR], both_ref[TR:]
    lane = lanes_of((128, 128))
    packed = jnp.where(
        lane < 16,
        r[:, :128],
        jnp.where(
            lane < 64,
            pltpu.roll(h[:, :128], 16, 1),
            jnp.where(lane < 112, pltpu.roll(h[:, 128:], 112, 1), r[:, 128:]),
        ),
    )
    turned = packed.T
    table = table_of(core_sums(r), counts)
    table_ref[...] = table
    send(
        lax.axis_index("col"),
        a_ref,
        b_ref,
        jnp.concatenate([turned[:32], table], axis=0),
        jnp.concatenate([turned[96:], table], axis=0),
    )


def widen_kernel(counts, both_ref, own_ref, gb_ref, ga_ref, r3_ref, h3_ref, b_ref, a_ref, table_ref):
    i, j = place()
    from_left, from_right = sides(j, counts[1], ga_ref[:32], gb_ref[:32])
    turned = jnp.concatenate([from_right, jnp.zeros((64, 128), jnp.float32), from_left], axis=0)
    back = turned.T
    lane = lanes_of((128, 128))
    edge = (lane < 16) | (lane >= 112)
    r3 = jnp.where(edge, back, 0.0)
    h3 = jnp.where(
        lane < 16, pltpu.roll(back, 112, 1), jnp.where(lane >= 112, pltpu.roll(back, 16, 1), 0.0)
    )
    r3_ref[...] = r3
    h3_ref[...] = h3
    r, h = both_ref[:TR], both_ref[TR:]
    table = merged(own_ref[...], ga_ref[32:], gb_ref[32:])
    table_ref[...] = table
    wide = jnp.concatenate([table, jnp.zeros((table.shape[0], FC - 128), jnp.float32)], axis=1)

    def strip(r_rows, h_rows):
        return jnp.concatenate(
            [
                jnp.concatenate([r[r_rows], r3[r_rows]], axis=1),
                jnp.concatenate([h[h_rows], h3[h_rows]], axis=1),
                wide,
            ],
            axis=0,
        )

    send(i, a_ref, b_ref, strip(slice(0, 8), slice(0, 16)), strip(slice(120, 128), slice(112, 128)))


def weights_kernel(both_ref, table_ref, basis_ref, weights_ref, table_out):
    h = both_ref[TR:]
    means = [x / (SUB * SUB) for x in core_sums(h * h * h)]
    weights_ref[...] = weights(means, basis_ref)
    table_out[...] = table_ref[...]


def forward_kernel(both_ref, r3_ref, basis_ref, t_ref):
    r = both_ref[:TR]
    u = column_transform(jnp.concatenate([r, r3_ref[...]], axis=1), basis_ref)
    t_ref[...] = row_transform(u, basis_ref, tile_rows)


def first_kernel(
    counts,
    gb_ref,
    ga_ref,
    tile_ref,
    weights_ref,
    basis_ref,
    table_ref,
    t_ref,
    table_out,
    b_ref,
    a_ref,
):
    i, j = place()
    above, below = sides(i, counts[0], ga_ref[:8], gb_ref[:8])
    u = column_transform(jnp.concatenate([below, above], axis=0), basis_ref)
    t = (tile_ref[...] + row_transform(u, basis_ref, halo_rows)) * weights_ref[...]
    t_ref[...] = t
    send(j, a_ref, b_ref, *strips_of(t, basis_ref, 24))
    table_out[...] = merged(table_ref[...], ga_ref[24:, :128], gb_ref[24:, :128])


def inverse_kernel(counts, t_ref, basis_ref, both_ref, h3_ref, gb_ref, ga_ref, y_ref, m_ref):
    y_ref[...] = solution_of(t_ref[...], basis_ref)
    above, below = sides(lax.axis_index("row"), counts[0], ga_ref[8:24], gb_ref[8:24])
    h = jnp.concatenate([both_ref[TR:], h3_ref[...]], axis=1)
    tall = jnp.concatenate([h, below, above], axis=0)
    m_ref[...] = tall * tall * tall


def columns_kernel(counts, y_ref, *refs):
    i, j = place()
    (ga_ref, gb_ref), refs = (refs[:2] if len(refs) == 7 else refs[1::-1]), refs[2:]
    deep = 24 if len(refs) == 5 else 16
    y = add_columns(y_ref[...], *sides(j, counts[1], ga_ref[:deep], gb_ref[:deep]))
    strips = pack_rows(y, deep)
    if len(refs) == 5:
        table_ref, out_ref, table_out, b_ref, a_ref = refs
        table = merged(table_ref[...], ga_ref[24:, :128], gb_ref[24:, :128])
        table_out[...] = table
        wide = jnp.concatenate([table, jnp.zeros((table.shape[0], FC - 128), jnp.float32)], axis=1)
        strips = [jnp.concatenate([x, wide], axis=0) for x in strips]
    else:
        out_ref, b_ref, a_ref = refs
    out_ref[...] = y
    send(i, a_ref, b_ref, *strips)


def inner_kernel(counts, width, y_ref, m_ref, basis_ref, w_ref, f_ref, gw_ref, gf_ref, near_ref):
    mask = column_mask(counts)
    s = jnp.where(mask, y_ref[8:120], 0.0)
    m = m_ref[8:120]
    w = DAMP * s + lap(m * lap(s))
    w = jnp.where(mask, w[8:104], 0.0) * SHRINK
    f = lap(m * edge_steps())
    f = jnp.where(mask, f[8:104], 0.0) * SHRINK
    w_ref[...] = w[:, :TC]
    f_ref[...] = f[:, :TC]
    gw_ref[...] = row_transform(w, basis_ref, inner_rows)
    gf_ref[...] = row_transform(f, basis_ref, inner_rows)
    near_ref[...] = near_inverse(counts, coarse_part(basis_ref, width))


def second_kernel(
    counts,
    width,
    y_ref,
    m_ref,
    gb_ref,
    ga_ref,
    table_ref,
    gw_ref,
    gf_ref,
    near_ref,
    weights_ref,
    basis_ref,
    z_ref,
    w_ref,
    band_ref,
    t_ref,
    b_ref,
    a_ref,
):
    i, j = place()
    y = y_ref[...]
    mask = edge_mask(counts)
    s = edges(y, *sides(i, counts[0], ga_ref[:24], gb_ref[:24]))
    s = jnp.where(mask, s, 0.0)
    table = merged(table_ref[...], ga_ref[24:, :128], gb_ref[24:, :128])
    picked = jnp.sum(near_ref[...] * as_row(table, width), axis=1, keepdims=True)
    bands = as_bands([picked[k : k + 1] for k in range(12)])
    coarse = edge_bands(bands)
    m = edge_part(m_ref)
    flow = m * (lap(s) + lap(coarse))
    z = s + coarse
    w = jnp.where(mask, DAMP * z + lap(flow), 0.0) * SHRINK
    step = jumps(bands[1])
    damped = (DAMP * SHRINK) * bands[1]
    z_ref[...] = jnp.concatenate([z[16:32, :TC], z[48:64, :TC]], axis=0)
    w_ref[...] = jnp.concatenate([w[16:32, :TC], w[48:64, :TC]], axis=0)
    band_ref[...] = jnp.concatenate([bands[1], step, damped, jnp.zeros((5, FC), jnp.float32)], axis=0)
    lane = lanes_of((EXT, 256))
    ones = jnp.where((lane >= 16) & (lane < 112), rows_t_part(basis_ref), 0.0)
    ones = jnp.sum(ones, axis=1, keepdims=True)
    u = gw_ref[...] + step * gf_ref[...] + ones * damped
    u = u + row_transform(jnp.concatenate([w[8:32], w[48:72]], axis=0), basis_ref, edge_rows)
    t = column_transform(u, basis_ref) * weights_ref[...]
    t_ref[...] = t
    send(j, a_ref, b_ref, *strips_of(t, basis_ref, 16))


def tile_of(edge, inner):
    return jnp.concatenate([edge[:16], inner, edge[16:]], axis=0)


def inverse_stats_kernel(
    t_ref,
    basis_ref,
    both_ref,
    m_ref,
    first_ref,
    inner_w_ref,
    f_ref,
    edge_z_ref,
    edge_w_ref,
    band_ref,
    y_ref,
    stats_ref,
    z_ref,
    w_ref,
):
    on, step, damped = (band_ref[k : k + 1, :TC] for k in range(3))
    z_ref[...] = tile_of(edge_z_ref, first_ref[16:112, :TC] + on)
    w_ref[...] = tile_of(edge_w_ref, inner_w_ref[...] + step * f_ref[...] + damped)
    y_ref[...] = solution_of(t_ref[...], basis_ref)
    rt, mt, zt, wt = both_ref[:TR], m_ref[:TR, :TC], z_ref[...], w_ref[...]
    lane, row = lanes_of((1, 256)), rows_of((128, 1))
    along = (lane % 128 != 0) & (lane % 128 != 127)
    top, low = mt[:1], mt[127:]
    side = jnp.sum(jnp.where((row > 0) & (row < 127), mt, 0.0), axis=0, keepdims=True)

    def halves(x):
        return [
            jnp.sum(x[:, :128], axis=1, keepdims=True),
            jnp.sum(x[:, 128:], axis=1, keepdims=True),
        ]

    first, last = lane % 128 == 0, lane % 128 == 127
    zero = jnp.zeros((1, 1), jnp.float32)
    stats_ref[...] = row_of(
        [
            core_sums(rt * zt),
            core_sums(zt * wt),
            core_sums(wt),
            halves(jnp.where(along, top, 0.0)),
            halves(jnp.where(along, low, 0.0)),
            halves(jnp.where(first, side, 0.0)),
            halves(jnp.where(last, side, 0.0)),
            halves(jnp.where(first, top, 0.0)),
            halves(jnp.where(last, top, 0.0)),
            halves(jnp.where(first, low, 0.0)),
            halves(jnp.where(last, low, 0.0)),
            *[[zero, zero]] * 4,
            core_sums(rt),
        ]
    )


def inner_dots_kernel(counts, y_ref, m_ref, both_ref, w_ref, stats_ref, v_ref, stats_out):
    q = jnp.where(column_mask(counts), y_ref[8:120], 0.0)
    v = (DAMP * q + lap(m_ref[8:120] * lap(q)))[8:104, :TC]
    q = q[8:104, :TC]
    v_ref[...] = v
    rest = [
        core_sums(v),
        core_sums(both_ref[16:112] * q),
        core_sums(w_ref[16:112] * q),
        core_sums(v * q),
    ]
    zero = jnp.zeros((1, 1), jnp.float32)
    stats_out[...] = stats_ref[...] + row_of([[zero, zero]] * 11 + rest)


def dots_kernel(
    counts, y_ref, m_ref, gb_ref, ga_ref, both_ref, w_ref, stats_ref, q_ref, v_ref, stats_out
):
    i, j = place()
    y = y_ref[...]
    q = edges(y, *sides(i, counts[0], ga_ref[...], gb_ref[...]))
    q = jnp.where(edge_mask(counts), q, 0.0)
    v = DAMP * q + lap(edge_part(m_ref) * lap(q))
    qe, ve = (jnp.concatenate([x[16:32, :TC], x[48:64, :TC]], axis=0) for x in (q, v))
    q_ref[...] = qe
    v_ref[...] = ve
    re = jnp.concatenate([both_ref[:16], both_ref[112:128]], axis=0)
    we = jnp.concatenate([w_ref[:16], w_ref[112:]], axis=0)
    rest = [core_sums(ve), core_sums(re * qe), core_sums(we * qe), core_sums(ve * qe)]
    zero = jnp.zeros((1, 1), jnp.float32)
    row = stats_ref[...] + row_of([[zero, zero]] * 11 + rest)
    stats_out[...] = jnp.broadcast_to(row, stats_out.shape)


def end_kernel(
    counts,
    width,
    stats_ref,
    basis_ref,
    m_ref,
    f_ref,
    both_ref,
    z_ref,
    w_ref,
    y_ref,
    inner_v_ref,
    q_ref,
    v_ref,
    solution_ref,
    residual_ref,
):
    i, j = place()
    tiles_c = counts[1]
    devices = counts[0] * tiles_c
    rows = stats_ref[...]
    st = jnp.concatenate([rows, pltpu.roll(rows, 64, 1)], axis=0)
    inverse = coarse_part(basis_ref, width)[: 2 * devices, : 2 * devices]
    g = jnp.broadcast_to(dot(inverse, st)[:, 2:3], st.shape)
    lane, row = lanes_of(st.shape), rows_of(st.shape)
    device = row % devices
    column = device % tiles_c
    on_left = row < devices

    def from_row(distance):
        return pltpu.roll(g, distance % (2 * devices), 0)

    up = jnp.where(device >= tiles_c, from_row(tiles_c), 0.0)
    down = jnp.where(device < devices - tiles_c, from_row(-tiles_c), 0.0)
    left = jnp.where(on_left, jnp.where(column > 0, from_row(1 - devices), 0.0), from_row(devices))
    right = jnp.where(
        on_left, from_row(-devices), jnp.where(column < tiles_c - 1, from_row(devices - 1), 0.0)
    )
    du, dd, dl, dr = g - up, g - down, g - left, g - right
    across = jnp.where(
        (lane == 3) | (lane == 7) | (lane == 8),
        du,
        jnp.where((lane == 4) | (lane == 9) | (lane == 10), dd, 0.0),
    )
    across = across + jnp.where(
        (lane == 5) | (lane == 7) | (lane == 9),
        dl,
        jnp.where((lane == 6) | (lane == 8) | (lane == 10), dr, 0.0),
    )
    factor = jnp.where((lane == 2) | (lane == 15), g, across * across)
    factor = jnp.where(lane == 11, 2.0 * g, factor)
    factor = jnp.where((lane < 2) | ((lane >= 12) & (lane < 15)), 1.0, factor)
    terms = jnp.where(lane == 16, (DAMP * SUB * SUB) * g * g, st * factor)
    sums = jnp.sum(terms, axis=0, keepdims=True)

    def whole(wanted):
        return jnp.sum(jnp.where(wanted, sums, 0.0), axis=1, keepdims=True)

    at = lanes_of((1, 128))
    rz, zw = whole(at == 0), whole(at == 1)
    ry = whole((at == 12) | (at == 15))
    yw = whole((at == 13) | (at == 2))
    yv = whole(((at >= 3) & (at < 12)) | (at == 14) | (at == 16))
    a = rz / zw
    rz1 = rz - a * ry - a * zw + a * a * yw
    beta1 = 1.0 + rz1 / rz
    dad = (beta1 * beta1 * zw - 2.0 * a * beta1 * yw) * (1.0 / SHRINK) + a * a * yv
    a1 = rz1 / dad
    r = i - 1 + lane // 4
    c = 2 * j - 1 + lane % 4
    inside = (r >= 0) & (r < counts[0]) & (c >= 0) & (c < 2 * tiles_c) & (lane < 12)
    where = lax.rem(c + 2, 2) * devices + r * tiles_c + (c + 2) // 2 - 1
    picked = jnp.sum(jnp.where(inside & (row == where), g, 0.0), axis=0, keepdims=True)
    bands = as_bands([picked[:, k : k + 1] for k in range(12)])
    on = bands[1][:, :TC]
    coarse = edge_bands(bands)
    image = DAMP * coarse + lap(edge_part(m_ref) * lap(coarse))
    image = with_edges(image, (jumps(bands[1]) * (1.0 / SHRINK))[:, :TC] * f_ref[...] + DAMP * on)
    y = tile_of(q_ref, y_ref[16:112, :TC]) + on
    v = tile_of(v_ref, inner_v_ref[...]) + image
    z, w = z_ref[...], w_ref[...]
    solution_ref[...] = (a * SHRINK) * z + a1 * (beta1 * z - a * y)
    residual_ref[...] = both_ref[:TR] - a * w - a1 * ((beta1 * (1.0 / SHRINK)) * w - a * v)


def call(kernel, outs, *args, flops=10**9):
    shapes = [jax.ShapeDtypeStruct(s, jnp.float32) for s in outs]
    return pl.pallas_call(
        kernel,
        out_shape=shapes,
        compiler_params=pltpu.CompilerParams(vmem_limit_bytes=48 * 1024 * 1024),
        cost_estimate=pl.CostEstimate(flops=flops, bytes_accessed=10**6, transcendentals=0),
    )(*args)


def pairs_from(count, offset):
    found = []
    for k in range(offset, count, 2):
        found += [(k, (k + 1) % count), ((k + 1) % count, k)]
    return found


def odd_pairs(counts, axis, bit):
    found = []
    for i in range(counts[0]):
        for j in range(counts[1]):
            at = [i, j]
            if bit and at[axis] in (0, counts[axis] - 1):
                at[1 - axis] ^= bit
            else:
                at[axis] = (at[axis] + (1 if at[axis] % 2 else -1)) % counts[axis]
            found.append((i * counts[1] + j, at[0] * counts[1] + at[1]))
    return found


def xor_pairs(counts, rows, cols):
    flat = [(i, j) for i in range(counts[0]) for j in range(counts[1])]
    return [(i * counts[1] + j, (i ^ rows) * counts[1] + (j ^ cols)) for i, j in flat]


def spreads(counts):
    known = np.eye(counts[0] * counts[1], dtype=bool)

    def meet(*swaps):
        return np.logical_or.reduce([known, *(known[[b for _, b in pairs]] for pairs in swaps)])

    even = [xor_pairs(counts, 0, 1), xor_pairs(counts, 1, 0)]
    known = meet(even[0], odd_pairs(counts, 1, 0))
    known = meet(even[1], odd_pairs(counts, 0, 0), xor_pairs(counts, 4, 0))
    known = meet(even[0], odd_pairs(counts, 1, 1))
    return meet(even[1], odd_pairs(counts, 0, 0)).all()


def body(counts, height, noise):
    nr, nc = counts
    devices = nr * nc
    width = max(128, devices * 2)
    basis = jnp.asarray(constants(nr, 2 * nc, width))
    both_axes = ("row", "col")
    depth = table_shape(counts)[0]

    def swap(a, b, axis, bit=0):
        gb = lax.ppermute(b, both_axes, odd_pairs(counts, both_axes.index(axis), bit))
        return lax.ppermute(a, axis, pairs_from(lax.axis_size(axis), 0)), gb

    def small_swap(x, rows, cols):
        return lax.ppermute(x, both_axes, xor_pairs(counts, rows, cols))

    both = jnp.pad(noise, ((0, TR), (0, 0))) + jnp.pad(height, ((TR, 0), (0, 0)))
    b, a, table = call(
        functools.partial(begin_kernel, counts), [(32 + depth, 128)] * 2 + [(depth, 128)], both
    )
    if not spreads(counts):
        for axis, count in enumerate(counts):
            bit = 1
            while bit < count:
                table = table + small_swap(table, *((0, bit) if axis else (bit, 0)))
                bit *= 2
    ga, gb = swap(a, b, "col")
    r3, h3, b, a, table = call(
        functools.partial(widen_kernel, counts),
        [(128, 128)] * 2 + [(24 + depth, FC)] * 2 + [(depth, 128)],
        both,
        table,
        gb,
        ga,
    )
    ga, gb = swap(a, b, "row")
    weight, table = call(weights_kernel, [(EXT, 2 * SPEC), (depth, 128)], both, table, basis)
    far = small_swap(table, 4, 0)
    t = call(forward_kernel, [(EXT, 2 * SPEC)], both, r3, basis)[0]
    t, table, b, a = call(
        functools.partial(first_kernel, counts),
        [(EXT, 2 * SPEC), (depth, 128)] + [(24, EXT)] * 2,
        gb,
        ga,
        t,
        weight,
        basis,
        table,
    )
    table = merged(table, far)
    wide = jnp.pad(table, ((0, 0), (0, EXT - 128)))
    y, m = call(
        functools.partial(inverse_kernel, counts),
        [(EXT, FC), (FR, FC)],
        t,
        basis,
        both,
        h3,
        gb,
        ga,
    )
    ga, gb = swap(*(jnp.concatenate([x, wide], axis=0) for x in (a, b)), "col", 1)
    y, table, b, a = call(
        functools.partial(columns_kernel, counts),
        [(EXT, FC), (depth, 128)] + [(24 + depth, FC)] * 2,
        y,
        ga,
        gb,
        table,
    )
    ga, gb = swap(a, b, "row")
    inner_w, f, gw, gf, near = call(
        functools.partial(inner_kernel, counts, width),
        [(96, TC)] * 2 + [(EXT, FC)] * 2 + [(16, width)],
        y,
        m,
        basis,
    )
    edge_z, edge_w, band, t, b, a = call(
        functools.partial(second_kernel, counts, width),
        [(32, TC)] * 2 + [(8, FC), (EXT, 2 * SPEC)] + [(16, EXT)] * 2,
        y,
        m,
        gb,
        ga,
        table,
        gw,
        gf,
        near,
        weight,
        basis,
    )
    ga, gb = swap(a, b, "col", 1)
    y, stats, z, w = call(
        inverse_stats_kernel,
        [(EXT, FC), (1, 128)] + [(TR, TC)] * 2,
        t,
        basis,
        both,
        m,
        y,
        inner_w,
        f,
        edge_z,
        edge_w,
        band,
    )
    y, b, a = call(
        functools.partial(columns_kernel, counts), [(EXT, FC)] + [(16, FC)] * 2, y, gb, ga
    )
    ga, gb = swap(a, b, "row", 1)
    inner_v, stats = call(
        functools.partial(inner_dots_kernel, counts),
        [(96, TC), (1, 128)],
        y,
        m,
        both,
        w,
        stats,
    )
    q, v, stats = call(
        functools.partial(dots_kernel, counts),
        [(32, TC)] * 2 + [(devices, 128)],
        y,
        m,
        gb,
        ga,
        both,
        w,
        stats,
    )
    stats = lax.all_to_all(stats, both_axes, 0, 0, tiled=True)
    return tuple(
        call(
            functools.partial(end_kernel, counts, width),
            [(TR, TC)] * 2,
            stats,
            basis,
            m,
            f,
            both,
            z,
            w,
            y,
            inner_v,
            q,
            v,
        )
    )


def solution(mesh):
    counts = (mesh.shape["row"], mesh.shape["col"])
    spec = P("row", "col")
    return jax.shard_map(
        functools.partial(body, counts),
        mesh=mesh,
        in_specs=(spec, spec),
        out_specs=(spec, spec),
        check_vma=False,
    )
```

```python
import functools

import jax
import jax.numpy as jnp
import ml_dtypes
import numpy as np
from jax import lax
from jax.experimental import pallas as pl
from jax.experimental.pallas import tpu as pltpu
from jax.sharding import PartitionSpec as P

SUB = 128
OV = 8
EXT = SUB + 2 * OV
DAMP = 2.0**-28
SHRINK = 2.0**-20

TR, TC = 128, 256
FR, FC = 160, 384
SPEC = 256

highest = lax.Precision.HIGHEST


def sine(count):
    k = np.arange(1, count + 1, dtype=np.float64)
    basis = np.sqrt(2.0 / (count + 1.0)) * np.sin(np.pi * k[:, None] * k[None, :] / (count + 1.0))
    return basis, 2.0 - 2.0 * np.cos(np.pi * k / (count + 1.0))


def block_constants():
    basis, eig = sine(EXT)
    rows = np.roll(basis, -OV, 0)
    cols = np.pad(basis, ((0, SPEC - EXT), (0, SPEC - EXT)))
    scale = np.pad((eig[:, None] + eig[None, :]) ** 2, ((0, 0), (0, SPEC - EXT)))
    wide = lambda x: np.pad(x, ((0, 0), (0, 2 * SPEC - x.shape[1])))
    high = rows.T.astype(ml_dtypes.bfloat16).astype(np.float64)
    low = (rows.T - high).astype(ml_dtypes.bfloat16).astype(np.float64)
    tile = np.concatenate([x[:, :SUB] for x in (high, high, low)], 1)
    halo = np.concatenate([x[:, SUB:] for x in (high, high, low)], 1)
    inner = np.concatenate([x[:, 16:112] for x in (high, high, low)], 1)
    at = [*range(136, 144), *range(16), *range(112, 136)]
    edge = np.concatenate([x[:, at] for x in (high, high, low)], 1)
    turned = np.hstack([rows.T, np.zeros((EXT, 256 - EXT)), edge])
    return [np.tile(scale, (1, 2)), *(wide(x) for x in (rows, turned, cols, inner, np.hstack([tile, halo])))]


def rows_part(ref):
    return ref[EXT : 2 * EXT, :EXT]


def rows_t_part(ref):
    return ref[2 * EXT : 3 * EXT, :256]


def cols_part(ref):
    return ref[3 * EXT : 3 * EXT + SPEC, :SPEC]


def inner_rows(ref):
    at = 3 * EXT + SPEC
    return ref[at : at + EXT, : 3 * 96]


def edge_rows(ref):
    return ref[2 * EXT : 3 * EXT, 256 : 256 + 3 * 48]


def tile_rows(ref):
    at = 4 * EXT + SPEC
    return ref[at : at + EXT, : 3 * SUB]


def halo_rows(ref):
    at = 4 * EXT + SPEC
    return ref[at : at + EXT, 3 * SUB : 3 * EXT]


def coarse_part(ref, width):
    at, lanes = 5 * EXT + SPEC, 2 * SPEC
    parts = [ref[at + k * width : at + (k + 1) * width] for k in range(-(-width // lanes))]
    return (parts[0] if len(parts) == 1 else jnp.concatenate(parts, axis=1))[:, :width]


def constants(nr, nc, width):
    lanes = 2 * SPEC
    inverse = coarse_inverse(nr, nc, -(-width // lanes) * lanes)[:width]
    parts = [*block_constants(), *np.split(inverse, inverse.shape[1] // lanes, 1)]
    return np.concatenate(parts).astype(np.float32)


def coarse_inverse(nr, nc, width):
    br, er = sine(nr)
    bc, ec = sine(nc)
    both = np.kron(br, bc).reshape(nr, nc // 2, 2, nr * nc).transpose(2, 0, 1, 3)
    both = both.reshape(nr * nc, nr * nc)
    scale = (er[:, None] + ec[None, :]) / (SUB * SUB)
    values = (SUB * SUB * (DAMP + scale * scale)).reshape(-1)
    whole = np.zeros((width, width), np.float32)
    whole[: nr * nc, : nr * nc] = (both / values) @ both.T
    return whole


def dot(a, b, side=0):
    return lax.dot_general(
        a, b, (((1,), (side,)), ((), ())), precision=highest, preferred_element_type=jnp.float32
    )


def lap(x):
    rows, lanes = x.shape
    beside = pltpu.roll(x, 1, 0) + pltpu.roll(x, rows - 1, 0)
    beside = beside + (pltpu.roll(x, 1, 1) + pltpu.roll(x, lanes - 1, 1))
    return 4.0 * x - beside


def lanes_of(shape):
    return lax.broadcasted_iota(jnp.int32, shape, 1)


def rows_of(shape):
    return lax.broadcasted_iota(jnp.int32, shape, 0)


def total(x):
    return jnp.sum(jnp.sum(x, axis=0, keepdims=True), axis=1, keepdims=True)


def place():
    return lax.axis_index("row"), lax.axis_index("col")


def is_even(index):
    return lax.rem(index, 2) == 0


def column_mask(counts):
    j = lax.axis_index("col")
    lane = lanes_of((1, FC))
    right = jnp.where(j < counts[1] - 1, 320, 256)
    left = jnp.where(j > 0, 320, 384)
    return (lane < right) | (lane >= left)


def edge_mask(counts):
    i = lax.axis_index("row")
    row = rows_of((80, 1))
    first = jnp.where(i > 0, 0, 16)
    last = jnp.where(i < counts[0] - 1, 80, 64)
    return (row >= first) & (row < last) & column_mask(counts)


def table_shape(counts):
    return (-(-2 * counts[0] * counts[1] // 1024) * 8, 128)


def table_of(values, counts):
    i, j = place()
    devices = counts[0] * counts[1]
    shape = table_shape(counts)
    at = rows_of(shape) * 128 + lanes_of(shape) - (i * counts[1] + j)
    return jnp.where(at == 0, values[0], jnp.where(at == devices, values[1], 0.0))


def merged(table, *others):
    for other in others:
        table = jnp.where(table != 0.0, table, other)
    return table


def as_row(table, width):
    return jnp.concatenate([table[k : k + 1] for k in range(width // 128)], axis=1)


def row_of(pairs):
    lane = lanes_of((1, 128))
    row = jnp.zeros((1, 128), jnp.float32)
    for k, (left, right) in enumerate(pairs):
        row = jnp.where(lane == k, left, jnp.where(lane == 64 + k, right, row))
    return row


def near_inverse(counts, inverse):
    i, j = place()
    nr, nc = counts[0], 2 * counts[1]
    shape = (16, inverse.shape[0])
    which = rows_of(shape)
    r = i - 1 + which // 4
    c = 2 * j - 1 + which % 4
    inside = (r >= 0) & (r < nr) & (c >= 0) & (c < nc) & (which < 12)
    at = lax.rem(c + 2, 2) * (nr * counts[1]) + r * counts[1] + (c + 2) // 2 - 1
    return dot(jnp.where(inside & (lanes_of(shape) == at), 1.0, 0.0), inverse)


def as_bands(values):
    lane = lanes_of((1, FC))
    bands = []
    for d in range(3):
        left, first, second, right = values[4 * d : 4 * d + 4]
        bands.append(
            jnp.where(
                lane < 128,
                first,
                jnp.where(lane < 256, second, jnp.where(lane < 320, right, left)),
            )
        )
    return bands


def edge_bands(bands):
    above, on, below = bands
    return jnp.concatenate(
        [
            jnp.broadcast_to(above, (16, FC)),
            jnp.broadcast_to(on, (48, FC)),
            jnp.broadcast_to(below, (16, FC)),
        ],
        axis=0,
    )


def jumps(row):
    step = row - pltpu.roll(row, 1, 1)
    lane = lanes_of((1, FC))
    at = [jnp.sum(jnp.where(lane == k, step, 0.0), axis=1, keepdims=True) for k in (0, 128, 256)]
    return jnp.where(
        (lane < 64) | (lane >= 320), at[0], jnp.where(lane < 192, at[1], at[2])
    )


def edge_steps():
    lane = lanes_of((1, FC))
    up = (lane == 0) | (lane == 128) | (lane == 256)
    down = (lane == FC - 1) | (lane == 127) | (lane == 255)
    return jnp.where(up, 1.0, jnp.where(down, -1.0, 0.0))


def halves_of(x):
    high = x.astype(jnp.bfloat16)
    return high, (x - high.astype(jnp.float32)).astype(jnp.bfloat16)


def product(a, b):
    return lax.dot_general(a, b, (((1,), (0,)), ((), ())), preferred_element_type=jnp.float32)


def column_transform(w, basis_ref):
    high, low = halves_of(pltpu.roll(w, OV, 1))
    cols, rest = halves_of(cols_part(basis_ref))
    cols = jnp.concatenate([cols, rest, cols], axis=0)

    def block(at):
        part = slice(at, at + SPEC)
        return product(jnp.concatenate([high[:, part], high[:, part], low[:, part]], axis=1), cols)

    return jnp.concatenate([block(0), block(128)], axis=1)


def row_transform(u, basis_ref, part):
    high, low = halves_of(u)
    rows = part(basis_ref).astype(jnp.bfloat16)
    return product(rows, jnp.concatenate([high, low, high], axis=0))


def weights(means, basis_ref):
    lane = lanes_of((1, 2 * SPEC))
    mean = jnp.where(lane < SPEC, means[0], means[1])
    return 1.0 / (DAMP + mean * basis_ref[:EXT])


def strips_of(t, basis_ref, deep):
    cols = cols_part(basis_ref)
    left = dot(cols[:deep], t[:, :SPEC], 1)
    right = dot(cols[EXT - deep : EXT], t[:, SPEC:], 1)
    both = dot(jnp.concatenate([left, right], axis=0), rows_t_part(basis_ref)[:, :EXT])
    return both[:deep], both[deep:]


def solution_of(t, basis_ref):
    v = dot(rows_part(basis_ref), t)
    cols = cols_part(basis_ref)
    first, second = dot(v[:, :SPEC], cols), dot(v[:, SPEC:], cols)
    y = jnp.concatenate(
        [first[:, :128], first[:, 128:] + second[:, :128], second[:, 128:]], axis=1
    )
    return pltpu.roll(y, FC - OV, 1)


def core_sums(x):
    return [total(x[:, :128]), total(x[:, 128:256])]


def add_columns(y, from_left, from_right):
    far = from_left.shape[0] - OV
    gap = jnp.zeros((56 - far, EXT), jnp.float32)
    turned = jnp.concatenate(
        [from_right[8:], gap, from_right[:8], from_left[far:], gap, from_left[:far]], axis=0
    )
    back = turned.T
    lane = lanes_of((EXT, 128))
    rolled = pltpu.roll(back, 64, 1)
    first = y[:, :128] + jnp.where(lane < 8, rolled, 0.0)
    second = y[:, 128:256] + jnp.where(lane >= 120, rolled, 0.0)
    third = y[:, 256:] + jnp.where((lane < 16) | (lane >= 112), back, 0.0)
    return jnp.concatenate([first, second, third], axis=1)


def pack_rows(y, deep):
    return jnp.concatenate([y[136:], y[: deep - 8]], axis=0), y[136 - deep : 136]


def edges(y, from_above, from_below):
    far = from_above.shape[0] - OV
    none = jnp.zeros((8, FC), jnp.float32)
    return jnp.concatenate(
        [
            from_above[:8] if far == 16 else none,
            y[136:] + from_above[far - 8 : far],
            y[:8] + from_above[far:],
            y[8:24],
            y[104:120],
            y[120:136] + from_below[:16],
            from_below[16:] if far == 16 else none,
        ],
        axis=0,
    )


def edge_part(frame):
    return jnp.concatenate([frame[144:], frame[:24], frame[104:144]], axis=0)


def with_edges(edge, inner):
    return jnp.concatenate([edge[16:32, :TC], inner, edge[48:64, :TC]], axis=0)


def sides(index, count, a, b):
    even = is_even(index)
    before = jnp.where(index > 0, jnp.where(even, b, a), 0.0)
    after = jnp.where(index < count - 1, jnp.where(even, a, b), 0.0)
    return before, after


def fold(rows, table):
    lane = lanes_of((8, 128))
    free = (lane >= 32) & (lane < 96)
    third = jnp.concatenate(
        [
            jnp.where(free, pltpu.roll(table, 32, 1), rows[:8, 256:]),
            jnp.where(free, pltpu.roll(table, 96, 1), rows[8:16, 256:]),
            rows[16:, 256:],
        ],
        axis=0,
    )
    return jnp.concatenate([rows[:, :256], third], axis=1)


def unfold(ref):
    low, high = ref[:8, 256:], ref[8:16, 256:]
    return jnp.where(lanes_of((8, 128)) < 64, pltpu.roll(low, 96, 1), pltpu.roll(high, 32, 1))


def row_sides(index, count, ga_ref, gb_ref, rows):
    lane = lanes_of((1, FC))
    used = (lane < 288) | (lane >= 352)
    return [jnp.where(used, x, 0.0) for x in sides(index, count, ga_ref[rows], gb_ref[rows])]


def send(index, a_ref, b_ref, before, after):
    even = is_even(index)
    a_ref[...] = jnp.where(even, after, before)
    b_ref[...] = jnp.where(even, before, after)


def begin_kernel(counts, both_ref, b_ref, a_ref, table_ref):
    r, h = both_ref[:TR], both_ref[TR:]
    lane = lanes_of((128, 128))
    packed = jnp.where(
        lane < 16,
        r[:, :128],
        jnp.where(
            lane < 64,
            pltpu.roll(h[:, :128], 16, 1),
            jnp.where(lane < 112, pltpu.roll(h[:, 128:], 112, 1), r[:, 128:]),
        ),
    )
    turned = packed.T
    table = table_of(core_sums(r), counts)
    table_ref[...] = table
    send(
        lax.axis_index("col"),
        a_ref,
        b_ref,
        jnp.concatenate([turned[:32], table], axis=0),
        jnp.concatenate([turned[96:], table], axis=0),
    )


def widen_kernel(counts, both_ref, own_ref, gb_ref, ga_ref, r3_ref, h3_ref, b_ref, a_ref, table_ref):
    i, j = place()
    from_left, from_right = sides(j, counts[1], ga_ref[:32], gb_ref[:32])
    turned = jnp.concatenate([from_right, jnp.zeros((64, 128), jnp.float32), from_left], axis=0)
    back = turned.T
    lane = lanes_of((128, 128))
    edge = (lane < 16) | (lane >= 112)
    r3 = jnp.where(edge, back, 0.0)
    h3 = jnp.where(
        lane < 16, pltpu.roll(back, 112, 1), jnp.where(lane >= 112, pltpu.roll(back, 16, 1), 0.0)
    )
    r3_ref[...] = r3
    h3_ref[...] = h3
    r, h = both_ref[:TR], both_ref[TR:]
    table = merged(own_ref[...], ga_ref[32:], gb_ref[32:])
    table_ref[...] = table

    def strip(r_rows, h_rows):
        rows = jnp.concatenate(
            [
                jnp.concatenate([r[r_rows], r3[r_rows]], axis=1),
                jnp.concatenate([h[h_rows], h3[h_rows]], axis=1),
            ],
            axis=0,
        )
        return fold(rows, table)

    send(i, a_ref, b_ref, strip(slice(0, 8), slice(0, 16)), strip(slice(120, 128), slice(112, 128)))


def weights_kernel(both_ref, table_ref, basis_ref, weights_ref, table_out):
    h = both_ref[TR:]
    means = [x / (SUB * SUB) for x in core_sums(h * h * h)]
    weights_ref[...] = weights(means, basis_ref)
    table_out[...] = table_ref[...]


def forward_kernel(both_ref, r3_ref, basis_ref, t_ref):
    r = both_ref[:TR]
    u = column_transform(jnp.concatenate([r, r3_ref[...]], axis=1), basis_ref)
    t_ref[...] = row_transform(u, basis_ref, tile_rows)


def first_kernel(
    counts,
    gb_ref,
    ga_ref,
    tile_ref,
    weights_ref,
    basis_ref,
    table_ref,
    t_ref,
    table_out,
    b_ref,
    a_ref,
):
    i, j = place()
    above, below = row_sides(i, counts[0], ga_ref, gb_ref, slice(0, 8))
    u = column_transform(jnp.concatenate([below, above], axis=0), basis_ref)
    t = (tile_ref[...] + row_transform(u, basis_ref, halo_rows)) * weights_ref[...]
    t_ref[...] = t
    table = merged(table_ref[...], unfold(ga_ref), unfold(gb_ref))
    table_out[...] = table
    wide = jnp.concatenate([table, jnp.zeros((table.shape[0], EXT - 128), jnp.float32)], axis=1)
    strips = (jnp.concatenate([x, wide], axis=0) for x in strips_of(t, basis_ref, 24))
    send(j, a_ref, b_ref, *strips)


def inverse_kernel(
    counts, t_ref, basis_ref, both_ref, h3_ref, gb_ref, ga_ref, table_ref, y_ref, m_ref, table_out
):
    table_out[...] = table_ref[...]
    y_ref[...] = solution_of(t_ref[...], basis_ref)
    above, below = row_sides(lax.axis_index("row"), counts[0], ga_ref, gb_ref, slice(8, 24))
    h = jnp.concatenate([both_ref[TR:], h3_ref[...]], axis=1)
    tall = jnp.concatenate([h, below, above], axis=0)
    m_ref[...] = tall * tall * tall


def columns_kernel(counts, y_ref, gb_ref, ga_ref, *refs):
    i, j = place()
    deep = 24 if len(refs) == 6 else 16
    y = add_columns(y_ref[...], *sides(j, counts[1], ga_ref[:deep], gb_ref[:deep]))
    strips = pack_rows(y, deep)
    if len(refs) == 6:
        table_ref, far_ref, out_ref, table_out, b_ref, a_ref = refs
        table = merged(table_ref[...], far_ref[...], ga_ref[24:, :128], gb_ref[24:, :128])
        table_out[...] = table
        strips = [fold(x, table) for x in strips]
    else:
        out_ref, b_ref, a_ref = refs
    out_ref[...] = y
    send(i, a_ref, b_ref, *strips)


def inner_kernel(counts, width, y_ref, m_ref, basis_ref, w_ref, f_ref, gw_ref, gf_ref, near_ref):
    mask = column_mask(counts)
    s = jnp.where(mask, y_ref[8:120], 0.0)
    m = m_ref[8:120]
    w = DAMP * s + lap(m * lap(s))
    w = jnp.where(mask, w[8:104], 0.0) * SHRINK
    f = lap(m * edge_steps())
    f = jnp.where(mask, f[8:104], 0.0) * SHRINK
    w_ref[...] = w[:, :TC]
    f_ref[...] = f[:, :TC]
    gw_ref[...] = row_transform(w, basis_ref, inner_rows)
    gf_ref[...] = row_transform(f, basis_ref, inner_rows)
    near_ref[...] = near_inverse(counts, coarse_part(basis_ref, width))


def second_kernel(
    counts,
    width,
    y_ref,
    m_ref,
    gb_ref,
    ga_ref,
    table_ref,
    farther_ref,
    inner_w_ref,
    f_ref,
    gw_ref,
    gf_ref,
    near_ref,
    weights_ref,
    basis_ref,
    z_ref,
    w_ref,
    t_ref,
    b_ref,
    a_ref,
):
    i, j = place()
    y = y_ref[...]
    mask = edge_mask(counts)
    s = edges(y, *row_sides(i, counts[0], ga_ref, gb_ref, slice(0, 24)))
    s = jnp.where(mask, s, 0.0)
    table = merged(table_ref[...], farther_ref[...], unfold(ga_ref), unfold(gb_ref))
    picked = jnp.sum(near_ref[...] * as_row(table, width), axis=1, keepdims=True)
    bands = as_bands([picked[k : k + 1] for k in range(12)])
    coarse = edge_bands(bands)
    m = edge_part(m_ref)
    flow = m * (lap(s) + lap(coarse))
    z = s + coarse
    w = jnp.where(mask, DAMP * z + lap(flow), 0.0) * SHRINK
    step = jumps(bands[1])
    damped = (DAMP * SHRINK) * bands[1]
    z_ref[...] = with_edges(z, y[16:112, :TC] + bands[1][:, :TC])
    w_ref[...] = with_edges(w, inner_w_ref[...] + step[:, :TC] * f_ref[...] + damped[:, :TC])
    lane = lanes_of((EXT, 256))
    ones = jnp.where((lane >= 16) & (lane < 112), rows_t_part(basis_ref), 0.0)
    ones = jnp.sum(ones, axis=1, keepdims=True)
    u = gw_ref[...] + step * gf_ref[...] + ones * damped
    u = u + row_transform(jnp.concatenate([w[8:32], w[48:72]], axis=0), basis_ref, edge_rows)
    t = column_transform(u, basis_ref) * weights_ref[...]
    t_ref[...] = t
    send(j, a_ref, b_ref, *strips_of(t, basis_ref, 16))


def inverse_stats_kernel(t_ref, basis_ref, both_ref, m_ref, z_ref, w_ref, y_ref, stats_ref):
    y_ref[...] = solution_of(t_ref[...], basis_ref)
    rt, mt, zt, wt = both_ref[:TR], m_ref[:TR, :TC], z_ref[...], w_ref[...]
    lane, row = lanes_of((1, 256)), rows_of((128, 1))
    along = (lane % 128 != 0) & (lane % 128 != 127)
    top, low = mt[:1], mt[127:]
    side = jnp.sum(jnp.where((row > 0) & (row < 127), mt, 0.0), axis=0, keepdims=True)

    def halves(x):
        return [
            jnp.sum(x[:, :128], axis=1, keepdims=True),
            jnp.sum(x[:, 128:], axis=1, keepdims=True),
        ]

    first, last = lane % 128 == 0, lane % 128 == 127
    zero = jnp.zeros((1, 1), jnp.float32)
    stats_ref[...] = row_of(
        [
            core_sums(rt * zt),
            core_sums(zt * wt),
            core_sums(wt),
            halves(jnp.where(along, top, 0.0)),
            halves(jnp.where(along, low, 0.0)),
            halves(jnp.where(first, side, 0.0)),
            halves(jnp.where(last, side, 0.0)),
            halves(jnp.where(first, top, 0.0)),
            halves(jnp.where(last, top, 0.0)),
            halves(jnp.where(first, low, 0.0)),
            halves(jnp.where(last, low, 0.0)),
            *[[zero, zero]] * 4,
            core_sums(rt),
        ]
    )


def inner_dots_kernel(counts, y_ref, m_ref, both_ref, w_ref, stats_ref, v_ref, stats_out):
    q = jnp.where(column_mask(counts), y_ref[8:120], 0.0)
    v = (DAMP * q + lap(m_ref[8:120] * lap(q)))[8:104, :TC]
    q = q[8:104, :TC]
    v_ref[...] = v
    rest = [
        core_sums(v),
        core_sums(both_ref[16:112] * q),
        core_sums(w_ref[16:112] * q),
        core_sums(v * q),
    ]
    zero = jnp.zeros((1, 1), jnp.float32)
    stats_out[...] = stats_ref[...] + row_of([[zero, zero]] * 11 + rest)


def dots_kernel(
    counts, y_ref, m_ref, gb_ref, ga_ref, both_ref, w_ref, stats_ref, inner_v_ref, q_ref, v_ref, stats_out
):
    i, j = place()
    y = y_ref[...]
    q = edges(y, *sides(i, counts[0], ga_ref[...], gb_ref[...]))
    q = jnp.where(edge_mask(counts), q, 0.0)
    v = DAMP * q + lap(edge_part(m_ref) * lap(q))
    q_ref[...] = with_edges(q, y[16:112, :TC])
    v_ref[...] = with_edges(v, inner_v_ref[...])
    qe, ve = (jnp.concatenate([x[16:32, :TC], x[48:64, :TC]], axis=0) for x in (q, v))
    re = jnp.concatenate([both_ref[:16], both_ref[112:128]], axis=0)
    we = jnp.concatenate([w_ref[:16], w_ref[112:]], axis=0)
    rest = [core_sums(ve), core_sums(re * qe), core_sums(we * qe), core_sums(ve * qe)]
    zero = jnp.zeros((1, 1), jnp.float32)
    row = stats_ref[...] + row_of([[zero, zero]] * 11 + rest)
    stats_out[...] = jnp.broadcast_to(row, stats_out.shape)


def end_kernel(
    counts,
    width,
    stats_ref,
    basis_ref,
    m_ref,
    f_ref,
    both_ref,
    z_ref,
    w_ref,
    q_ref,
    v_ref,
    solution_ref,
    residual_ref,
):
    i, j = place()
    tiles_c = counts[1]
    devices = counts[0] * tiles_c
    rows = stats_ref[...]
    st = jnp.concatenate([rows, pltpu.roll(rows, 64, 1)], axis=0)
    inverse = coarse_part(basis_ref, width)[: 2 * devices, : 2 * devices]
    g = jnp.broadcast_to(dot(inverse, st)[:, 2:3], st.shape)
    lane, row = lanes_of(st.shape), rows_of(st.shape)
    device = row % devices
    column = device % tiles_c
    on_left = row < devices

    def from_row(distance):
        return pltpu.roll(g, distance % (2 * devices), 0)

    up = jnp.where(device >= tiles_c, from_row(tiles_c), 0.0)
    down = jnp.where(device < devices - tiles_c, from_row(-tiles_c), 0.0)
    left = jnp.where(on_left, jnp.where(column > 0, from_row(1 - devices), 0.0), from_row(devices))
    right = jnp.where(
        on_left, from_row(-devices), jnp.where(column < tiles_c - 1, from_row(devices - 1), 0.0)
    )
    du, dd, dl, dr = g - up, g - down, g - left, g - right
    across = jnp.where(
        (lane == 3) | (lane == 7) | (lane == 8),
        du,
        jnp.where((lane == 4) | (lane == 9) | (lane == 10), dd, 0.0),
    )
    across = across + jnp.where(
        (lane == 5) | (lane == 7) | (lane == 9),
        dl,
        jnp.where((lane == 6) | (lane == 8) | (lane == 10), dr, 0.0),
    )
    factor = jnp.where((lane == 2) | (lane == 15), g, across * across)
    factor = jnp.where(lane == 11, 2.0 * g, factor)
    factor = jnp.where((lane < 2) | ((lane >= 12) & (lane < 15)), 1.0, factor)
    terms = jnp.where(lane == 16, (DAMP * SUB * SUB) * g * g, st * factor)
    sums = jnp.sum(terms, axis=0, keepdims=True)

    def whole(wanted):
        return jnp.sum(jnp.where(wanted, sums, 0.0), axis=1, keepdims=True)

    at = lanes_of((1, 128))
    rz, zw = whole(at == 0), whole(at == 1)
    ry = whole((at == 12) | (at == 15))
    yw = whole((at == 13) | (at == 2))
    yv = whole(((at >= 3) & (at < 12)) | (at == 14) | (at == 16))
    a = rz / zw
    rz1 = rz - a * ry - a * zw + a * a * yw
    beta1 = 1.0 + rz1 / rz
    dad = (beta1 * beta1 * zw - 2.0 * a * beta1 * yw) * (1.0 / SHRINK) + a * a * yv
    a1 = rz1 / dad
    r = i - 1 + lane // 4
    c = 2 * j - 1 + lane % 4
    inside = (r >= 0) & (r < counts[0]) & (c >= 0) & (c < 2 * tiles_c) & (lane < 12)
    where = lax.rem(c + 2, 2) * devices + r * tiles_c + (c + 2) // 2 - 1
    picked = jnp.sum(jnp.where(inside & (row == where), g, 0.0), axis=0, keepdims=True)
    bands = as_bands([picked[:, k : k + 1] for k in range(12)])
    on = bands[1][:, :TC]
    coarse = edge_bands(bands)
    image = DAMP * coarse + lap(edge_part(m_ref) * lap(coarse))
    image = with_edges(image, (jumps(bands[1]) * (1.0 / SHRINK))[:, :TC] * f_ref[...] + DAMP * on)
    y = q_ref[...] + on
    v = v_ref[...] + image
    z, w = z_ref[...], w_ref[...]
    solution_ref[...] = (a * SHRINK) * z + a1 * (beta1 * z - a * y)
    residual_ref[...] = both_ref[:TR] - a * w - a1 * ((beta1 * (1.0 / SHRINK)) * w - a * v)


def call(kernel, outs, *args, flops=10**9):
    shapes = [jax.ShapeDtypeStruct(s, jnp.float32) for s in outs]
    return pl.pallas_call(
        kernel,
        out_shape=shapes,
        compiler_params=pltpu.CompilerParams(vmem_limit_bytes=48 * 1024 * 1024),
        cost_estimate=pl.CostEstimate(flops=flops, bytes_accessed=10**6, transcendentals=0),
    )(*args)


def pairs_from(count, offset):
    found = []
    for k in range(offset, count, 2):
        found += [(k, (k + 1) % count), ((k + 1) % count, k)]
    return found


def odd_pairs(counts, axis, bit):
    found = []
    for i in range(counts[0]):
        for j in range(counts[1]):
            at = [i, j]
            if bit and at[axis] in (0, counts[axis] - 1):
                at[1 - axis] ^= bit
            else:
                at[axis] = (at[axis] + (1 if at[axis] % 2 else -1)) % counts[axis]
            found.append((i * counts[1] + j, at[0] * counts[1] + at[1]))
    return found


def xor_pairs(counts, rows, cols):
    flat = [(i, j) for i in range(counts[0]) for j in range(counts[1])]
    return [(i * counts[1] + j, (i ^ rows) * counts[1] + (j ^ cols)) for i, j in flat]


def spreads(counts):
    known = np.eye(counts[0] * counts[1], dtype=bool)

    def meet(*swaps):
        return np.logical_or.reduce([known, *(known[[b for _, b in pairs]] for pairs in swaps)])

    even = [xor_pairs(counts, 0, 1), xor_pairs(counts, 1, 0)]
    known = meet(even[0], odd_pairs(counts, 1, 0))
    first = meet(xor_pairs(counts, 4, 0))
    known = meet(even[1], odd_pairs(counts, 0, 0))
    second = meet(xor_pairs(counts, 4, 2))
    known = meet(even[0], odd_pairs(counts, 1, 1)) | first
    return (meet(even[1], odd_pairs(counts, 0, 0)) | second).all()


def body(counts, height, noise):
    nr, nc = counts
    devices = nr * nc
    width = max(128, devices * 2)
    basis = jnp.asarray(constants(nr, 2 * nc, width))
    both_axes = ("row", "col")
    depth = table_shape(counts)[0]

    def swap(a, b, axis, bit=0):
        gb = lax.ppermute(b, both_axes, odd_pairs(counts, both_axes.index(axis), bit))
        return lax.ppermute(a, axis, pairs_from(lax.axis_size(axis), 0)), gb

    def small_swap(x, rows, cols):
        return lax.ppermute(x, both_axes, xor_pairs(counts, rows, cols))

    both = jnp.pad(noise, ((0, TR), (0, 0))) + jnp.pad(height, ((TR, 0), (0, 0)))
    b, a, table = call(
        functools.partial(begin_kernel, counts), [(32 + depth, 128)] * 2 + [(depth, 128)], both
    )
    if not spreads(counts):
        for axis, count in enumerate(counts):
            bit = 1
            while bit < count:
                table = table + small_swap(table, *((0, bit) if axis else (bit, 0)))
                bit *= 2
    ga, gb = swap(a, b, "col")
    r3, h3, b, a, table = call(
        functools.partial(widen_kernel, counts),
        [(128, 128)] * 2 + [(24, FC)] * 2 + [(depth, 128)],
        both,
        table,
        gb,
        ga,
    )
    ga, gb = swap(a, b, "row")
    weight, table = call(weights_kernel, [(EXT, 2 * SPEC), (depth, 128)], both, table, basis)
    far = small_swap(table, 4, 0)
    t = call(forward_kernel, [(EXT, 2 * SPEC)], both, r3, basis, flops=5 * 10**8)[0]
    t, table, b, a = call(
        functools.partial(first_kernel, counts),
        [(EXT, 2 * SPEC), (depth, 128)] + [(24 + depth, EXT)] * 2,
        gb,
        ga,
        t,
        weight,
        basis,
        table,
    )
    y, m, table_too = call(
        functools.partial(inverse_kernel, counts),
        [(EXT, FC), (FR, FC), (depth, 128)],
        t,
        basis,
        both,
        h3,
        gb,
        ga,
        table,
    )
    ga, gb = swap(a, b, "col", 1)
    farther = small_swap(table_too, 4, 2)
    y, table, b, a = call(
        functools.partial(columns_kernel, counts),
        [(EXT, FC), (depth, 128)] + [(24, FC)] * 2,
        y,
        gb,
        ga,
        table,
        far,
    )
    ga, gb = swap(a, b, "row")
    inner_w, f, gw, gf, near = call(
        functools.partial(inner_kernel, counts, width),
        [(96, TC)] * 2 + [(EXT, FC)] * 2 + [(16, width)],
        y,
        m,
        basis,
    )
    z, w, t, b, a = call(
        functools.partial(second_kernel, counts, width),
        [(TR, TC)] * 2 + [(EXT, 2 * SPEC)] + [(16, EXT)] * 2,
        y,
        m,
        gb,
        ga,
        table,
        farther,
        inner_w,
        f,
        gw,
        gf,
        near,
        weight,
        basis,
    )
    ga, gb = swap(a, b, "col", 1)
    y, stats = call(inverse_stats_kernel, [(EXT, FC), (1, 128)], t, basis, both, m, z, w)
    y, b, a = call(
        functools.partial(columns_kernel, counts), [(EXT, FC)] + [(16, FC)] * 2, y, gb, ga
    )
    ga, gb = swap(a, b, "row", 1)
    inner_v, stats = call(
        functools.partial(inner_dots_kernel, counts),
        [(96, TC), (1, 128)],
        y,
        m,
        both,
        w,
        stats,
    )
    q, v, stats = call(
        functools.partial(dots_kernel, counts),
        [(TR, TC)] * 2 + [(devices, 128)],
        y,
        m,
        gb,
        ga,
        both,
        w,
        stats,
        inner_v,
    )
    stats = lax.all_to_all(stats, both_axes, 0, 0, tiled=True)
    return tuple(
        call(
            functools.partial(end_kernel, counts, width),
            [(TR, TC)] * 2,
            stats,
            basis,
            m,
            f,
            both,
            z,
            w,
            q,
            v,
        )
    )


def solution(mesh):
    counts = (mesh.shape["row"], mesh.shape["col"])
    spec = P("row", "col")
    return jax.shard_map(
        functools.partial(body, counts),
        mesh=mesh,
        in_specs=(spec, spec),
        out_specs=(spec, spec),
        check_vma=False,
    )
```

```python
import functools

import jax
import jax.numpy as jnp
import ml_dtypes
import numpy as np
from jax import lax
from jax.experimental import pallas as pl
from jax.experimental.pallas import tpu as pltpu
from jax.sharding import PartitionSpec as P

SUB = 128
OV = 8
EXT = SUB + 2 * OV
DAMP = 2.0**-28
SHRINK = 2.0**-20

TR, TC = 128, 256
FR, FC = 160, 384
SPEC = 256

highest = lax.Precision.HIGHEST


def sine(count):
    k = np.arange(1, count + 1, dtype=np.float64)
    basis = np.sqrt(2.0 / (count + 1.0)) * np.sin(np.pi * k[:, None] * k[None, :] / (count + 1.0))
    return basis, 2.0 - 2.0 * np.cos(np.pi * k / (count + 1.0))


def block_constants():
    basis, eig = sine(EXT)
    rows = np.roll(basis, -OV, 0)
    cols = np.pad(basis, ((0, SPEC - EXT), (0, SPEC - EXT)))
    scale = np.pad((eig[:, None] + eig[None, :]) ** 2, ((0, 0), (0, SPEC - EXT)))
    wide = lambda x: np.pad(x, ((0, 0), (0, 2 * SPEC - x.shape[1])))
    high = rows.T.astype(ml_dtypes.bfloat16).astype(np.float64)
    low = (rows.T - high).astype(ml_dtypes.bfloat16).astype(np.float64)
    tile = np.concatenate([x[:, :SUB] for x in (high, high, low)], 1)
    halo = np.concatenate([x[:, SUB:] for x in (high, high, low)], 1)
    inner = np.concatenate([x[:, 16:112] for x in (high, high, low)], 1)
    at = [*range(136, 144), *range(16), *range(112, 136)]
    edge = np.concatenate([x[:, at] for x in (high, high, low)], 1)
    turned = np.hstack([rows.T, np.zeros((EXT, 256 - EXT)), edge])
    return [np.tile(scale, (1, 2)), *(wide(x) for x in (rows, turned, cols, inner, np.hstack([tile, halo])))]


def rows_part(ref):
    return ref[EXT : 2 * EXT, :EXT]


def rows_t_part(ref):
    return ref[2 * EXT : 3 * EXT, :256]


def cols_part(ref):
    return ref[3 * EXT : 3 * EXT + SPEC, :SPEC]


def inner_rows(ref):
    at = 3 * EXT + SPEC
    return ref[at : at + EXT, : 3 * 96]


def edge_rows(ref):
    return ref[2 * EXT : 3 * EXT, 256 : 256 + 3 * 48]


def tile_rows(ref):
    at = 4 * EXT + SPEC
    return ref[at : at + EXT, : 3 * SUB]


def halo_rows(ref):
    at = 4 * EXT + SPEC
    return ref[at : at + EXT, 3 * SUB : 3 * EXT]


def coarse_part(ref, width):
    at, lanes = 5 * EXT + SPEC, 2 * SPEC
    parts = [ref[at + k * width : at + (k + 1) * width] for k in range(-(-width // lanes))]
    return (parts[0] if len(parts) == 1 else jnp.concatenate(parts, axis=1))[:, :width]


def constants(nr, nc, width):
    lanes = 2 * SPEC
    inverse = coarse_inverse(nr, nc, -(-width // lanes) * lanes)[:width]
    parts = [*block_constants(), *np.split(inverse, inverse.shape[1] // lanes, 1)]
    return np.concatenate(parts).astype(np.float32)


def coarse_inverse(nr, nc, width):
    br, er = sine(nr)
    bc, ec = sine(nc)
    both = np.kron(br, bc).reshape(nr, nc // 2, 2, nr * nc).transpose(2, 0, 1, 3)
    both = both.reshape(nr * nc, nr * nc)
    scale = (er[:, None] + ec[None, :]) / (SUB * SUB)
    values = (SUB * SUB * (DAMP + scale * scale)).reshape(-1)
    whole = np.zeros((width, width), np.float32)
    whole[: nr * nc, : nr * nc] = (both / values) @ both.T
    return whole


def dot(a, b, side=0):
    return lax.dot_general(
        a, b, (((1,), (side,)), ((), ())), precision=highest, preferred_element_type=jnp.float32
    )


def lap(x):
    rows, lanes = x.shape
    beside = pltpu.roll(x, 1, 0) + pltpu.roll(x, rows - 1, 0)
    beside = beside + (pltpu.roll(x, 1, 1) + pltpu.roll(x, lanes - 1, 1))
    return 4.0 * x - beside


def lanes_of(shape):
    return lax.broadcasted_iota(jnp.int32, shape, 1)


def rows_of(shape):
    return lax.broadcasted_iota(jnp.int32, shape, 0)


def total(x):
    return jnp.sum(jnp.sum(x, axis=0, keepdims=True), axis=1, keepdims=True)


def place():
    return lax.axis_index("row"), lax.axis_index("col")


def is_even(index):
    return lax.rem(index, 2) == 0


def column_mask(counts):
    j = lax.axis_index("col")
    lane = lanes_of((1, FC))
    right = jnp.where(j < counts[1] - 1, 320, 256)
    left = jnp.where(j > 0, 320, 384)
    return (lane < right) | (lane >= left)


def edge_mask(counts):
    i = lax.axis_index("row")
    row = rows_of((80, 1))
    first = jnp.where(i > 0, 0, 16)
    last = jnp.where(i < counts[0] - 1, 80, 64)
    return (row >= first) & (row < last) & column_mask(counts)


def table_shape(counts):
    return (-(-2 * counts[0] * counts[1] // 1024) * 8, 128)


def table_of(values, counts):
    i, j = place()
    devices = counts[0] * counts[1]
    shape = table_shape(counts)
    at = rows_of(shape) * 128 + lanes_of(shape) - (i * counts[1] + j)
    return jnp.where(at == 0, values[0], jnp.where(at == devices, values[1], 0.0))


def merged(table, *others):
    for other in others:
        table = jnp.where(table != 0.0, table, other)
    return table


def as_row(table, width):
    return jnp.concatenate([table[k : k + 1] for k in range(width // 128)], axis=1)


def row_of(pairs):
    lane = lanes_of((1, 128))
    row = jnp.zeros((1, 128), jnp.float32)
    for k, (left, right) in enumerate(pairs):
        row = jnp.where(lane == k, left, jnp.where(lane == 64 + k, right, row))
    return row


def near_inverse(counts, inverse):
    i, j = place()
    nr, nc = counts[0], 2 * counts[1]
    shape = (16, inverse.shape[0])
    which = rows_of(shape)
    r = i - 1 + which // 4
    c = 2 * j - 1 + which % 4
    inside = (r >= 0) & (r < nr) & (c >= 0) & (c < nc) & (which < 12)
    at = lax.rem(c + 2, 2) * (nr * counts[1]) + r * counts[1] + (c + 2) // 2 - 1
    return dot(jnp.where(inside & (lanes_of(shape) == at), 1.0, 0.0), inverse)


def as_bands(values):
    lane = lanes_of((1, FC))
    bands = []
    for d in range(3):
        left, first, second, right = values[4 * d : 4 * d + 4]
        bands.append(
            jnp.where(
                lane < 128,
                first,
                jnp.where(lane < 256, second, jnp.where(lane < 320, right, left)),
            )
        )
    return bands


def edge_bands(bands):
    above, on, below = bands
    return jnp.concatenate(
        [
            jnp.broadcast_to(above, (16, FC)),
            jnp.broadcast_to(on, (48, FC)),
            jnp.broadcast_to(below, (16, FC)),
        ],
        axis=0,
    )


def jumps(row):
    step = row - pltpu.roll(row, 1, 1)
    lane = lanes_of((1, FC))
    at = [jnp.sum(jnp.where(lane == k, step, 0.0), axis=1, keepdims=True) for k in (0, 128, 256)]
    return jnp.where(
        (lane < 64) | (lane >= 320), at[0], jnp.where(lane < 192, at[1], at[2])
    )


def edge_steps():
    lane = lanes_of((1, FC))
    up = (lane == 0) | (lane == 128) | (lane == 256)
    down = (lane == FC - 1) | (lane == 127) | (lane == 255)
    return jnp.where(up, 1.0, jnp.where(down, -1.0, 0.0))


def halves_of(x):
    high = x.astype(jnp.bfloat16)
    return high, (x - high.astype(jnp.float32)).astype(jnp.bfloat16)


def product(a, b):
    return lax.dot_general(a, b, (((1,), (0,)), ((), ())), preferred_element_type=jnp.float32)


def column_transform(w, basis_ref):
    high, low = halves_of(pltpu.roll(w, OV, 1))
    cols, rest = halves_of(cols_part(basis_ref))
    cols = jnp.concatenate([cols, rest, cols], axis=0)

    def block(at):
        part = slice(at, at + SPEC)
        return product(jnp.concatenate([high[:, part], high[:, part], low[:, part]], axis=1), cols)

    return jnp.concatenate([block(0), block(128)], axis=1)


def row_transform(u, basis_ref, part):
    high, low = halves_of(u)
    rows = part(basis_ref).astype(jnp.bfloat16)
    return product(rows, jnp.concatenate([high, low, high], axis=0))


def weights(means, basis_ref):
    lane = lanes_of((1, 2 * SPEC))
    mean = jnp.where(lane < SPEC, means[0], means[1])
    return 1.0 / (DAMP + mean * basis_ref[:EXT])


def strips_of(t, basis_ref, deep):
    cols = cols_part(basis_ref)
    left = dot(cols[:deep], t[:, :SPEC], 1)
    right = dot(cols[EXT - deep : EXT], t[:, SPEC:], 1)
    both = dot(jnp.concatenate([left, right], axis=0), rows_t_part(basis_ref)[:, :EXT])
    return both[:deep], both[deep:]


def solution_of(t, basis_ref):
    v = dot(rows_part(basis_ref), t)
    cols = cols_part(basis_ref)
    first, second = dot(v[:, :SPEC], cols), dot(v[:, SPEC:], cols)
    y = jnp.concatenate(
        [first[:, :128], first[:, 128:] + second[:, :128], second[:, 128:]], axis=1
    )
    return pltpu.roll(y, FC - OV, 1)


def core_sums(x):
    return [total(x[:, :128]), total(x[:, 128:256])]


def add_columns(y, from_left, from_right):
    far = from_left.shape[0] - OV
    gap = jnp.zeros((56 - far, EXT), jnp.float32)
    turned = jnp.concatenate(
        [from_right[8:], gap, from_right[:8], from_left[far:], gap, from_left[:far]], axis=0
    )
    back = turned.T
    lane = lanes_of((EXT, 128))
    rolled = pltpu.roll(back, 64, 1)
    first = y[:, :128] + jnp.where(lane < 8, rolled, 0.0)
    second = y[:, 128:256] + jnp.where(lane >= 120, rolled, 0.0)
    third = y[:, 256:] + jnp.where((lane < 16) | (lane >= 112), back, 0.0)
    return jnp.concatenate([first, second, third], axis=1)


def pack_rows(y, deep):
    return jnp.concatenate([y[136:], y[: deep - 8]], axis=0), y[136 - deep : 136]


def edges(y, from_above, from_below):
    far = from_above.shape[0] - OV
    none = jnp.zeros((8, FC), jnp.float32)
    return jnp.concatenate(
        [
            from_above[:8] if far == 16 else none,
            y[136:] + from_above[far - 8 : far],
            y[:8] + from_above[far:],
            y[8:24],
            y[104:120],
            y[120:136] + from_below[:16],
            from_below[16:] if far == 16 else none,
        ],
        axis=0,
    )


def edge_part(frame):
    return jnp.concatenate([frame[144:], frame[:24], frame[104:144]], axis=0)


def with_edges(edge, inner):
    return jnp.concatenate([edge[16:32, :TC], inner, edge[48:64, :TC]], axis=0)


def sides(index, count, a, b):
    even = is_even(index)
    before = jnp.where(index > 0, jnp.where(even, b, a), 0.0)
    after = jnp.where(index < count - 1, jnp.where(even, a, b), 0.0)
    return before, after


def fold(rows, table):
    lane = lanes_of((8, 128))
    free = (lane >= 32) & (lane < 96)
    third = jnp.concatenate(
        [
            jnp.where(free, pltpu.roll(table, 32, 1), rows[:8, 256:]),
            jnp.where(free, pltpu.roll(table, 96, 1), rows[8:16, 256:]),
            rows[16:, 256:],
        ],
        axis=0,
    )
    return jnp.concatenate([rows[:, :256], third], axis=1)


def unfold(ref):
    low, high = ref[:8, 256:], ref[8:16, 256:]
    return jnp.where(lanes_of((8, 128)) < 64, pltpu.roll(low, 96, 1), pltpu.roll(high, 32, 1))


def row_sides(index, count, ga_ref, gb_ref, rows):
    lane = lanes_of((1, FC))
    used = (lane < 288) | (lane >= 352)
    return [jnp.where(used, x, 0.0) for x in sides(index, count, ga_ref[rows], gb_ref[rows])]


def send(index, a_ref, b_ref, before, after):
    even = is_even(index)
    a_ref[...] = jnp.where(even, after, before)
    b_ref[...] = jnp.where(even, before, after)


def begin_kernel(counts, both_ref, b_ref, a_ref, table_ref):
    r, h = both_ref[:TR], both_ref[TR:]
    lane = lanes_of((128, 128))
    packed = jnp.where(
        lane < 16,
        r[:, :128],
        jnp.where(
            lane < 64,
            pltpu.roll(h[:, :128], 16, 1),
            jnp.where(lane < 112, pltpu.roll(h[:, 128:], 112, 1), r[:, 128:]),
        ),
    )
    turned = packed.T
    table = table_of(core_sums(r), counts)
    table_ref[...] = table
    send(
        lax.axis_index("col"),
        a_ref,
        b_ref,
        jnp.concatenate([turned[:32], table], axis=0),
        jnp.concatenate([turned[96:], table], axis=0),
    )


def widen_kernel(counts, both_ref, own_ref, gb_ref, ga_ref, r3_ref, h3_ref, b_ref, a_ref, table_ref):
    i, j = place()
    from_left, from_right = sides(j, counts[1], ga_ref[:32], gb_ref[:32])
    turned = jnp.concatenate([from_right, jnp.zeros((64, 128), jnp.float32), from_left], axis=0)
    back = turned.T
    lane = lanes_of((128, 128))
    edge = (lane < 16) | (lane >= 112)
    r3 = jnp.where(edge, back, 0.0)
    h3 = jnp.where(
        lane < 16, pltpu.roll(back, 112, 1), jnp.where(lane >= 112, pltpu.roll(back, 16, 1), 0.0)
    )
    r3_ref[...] = r3
    h3_ref[...] = h3
    r, h = both_ref[:TR], both_ref[TR:]
    table = merged(own_ref[...], ga_ref[32:], gb_ref[32:])
    table_ref[...] = table

    def strip(r_rows, h_rows):
        rows = jnp.concatenate(
            [
                jnp.concatenate([r[r_rows], r3[r_rows]], axis=1),
                jnp.concatenate([h[h_rows], h3[h_rows]], axis=1),
            ],
            axis=0,
        )
        return fold(rows, table)

    send(i, a_ref, b_ref, strip(slice(0, 8), slice(0, 16)), strip(slice(120, 128), slice(112, 128)))


def weights_kernel(both_ref, table_ref, basis_ref, weights_ref, table_out):
    h = both_ref[TR:]
    means = [x / (SUB * SUB) for x in core_sums(h * h * h)]
    weights_ref[...] = weights(means, basis_ref)
    table_out[...] = table_ref[...]


def forward_kernel(both_ref, r3_ref, basis_ref, t_ref):
    r = both_ref[:TR]
    u = column_transform(jnp.concatenate([r, r3_ref[...]], axis=1), basis_ref)
    t_ref[...] = row_transform(u, basis_ref, tile_rows)


def first_kernel(
    counts,
    gb_ref,
    ga_ref,
    tile_ref,
    weights_ref,
    basis_ref,
    table_ref,
    t_ref,
    table_out,
    b_ref,
    a_ref,
):
    i, j = place()
    above, below = row_sides(i, counts[0], ga_ref, gb_ref, slice(0, 8))
    u = column_transform(jnp.concatenate([below, above], axis=0), basis_ref)
    t = (tile_ref[...] + row_transform(u, basis_ref, halo_rows)) * weights_ref[...]
    t_ref[...] = t
    table = merged(table_ref[...], unfold(ga_ref), unfold(gb_ref))
    table_out[...] = table
    wide = jnp.concatenate([table, jnp.zeros((table.shape[0], EXT - 128), jnp.float32)], axis=1)
    strips = (jnp.concatenate([x, wide], axis=0) for x in strips_of(t, basis_ref, 24))
    send(j, a_ref, b_ref, *strips)


def inverse_kernel(
    counts, t_ref, basis_ref, both_ref, h3_ref, gb_ref, ga_ref, table_ref, y_ref, m_ref, table_out
):
    table_out[...] = table_ref[...]
    y_ref[...] = solution_of(t_ref[...], basis_ref)
    above, below = row_sides(lax.axis_index("row"), counts[0], ga_ref, gb_ref, slice(8, 24))
    h = jnp.concatenate([both_ref[TR:], h3_ref[...]], axis=1)
    tall = jnp.concatenate([h, below, above], axis=0)
    m_ref[...] = tall * tall * tall


def columns_kernel(counts, y_ref, gb_ref, ga_ref, *refs):
    i, j = place()
    deep = 24 if len(refs) == 6 else 16
    y = add_columns(y_ref[...], *sides(j, counts[1], ga_ref[:deep], gb_ref[:deep]))
    strips = pack_rows(y, deep)
    if len(refs) == 6:
        table_ref, far_ref, out_ref, table_out, b_ref, a_ref = refs
        table = merged(table_ref[...], far_ref[...], ga_ref[24:, :128], gb_ref[24:, :128])
        table_out[...] = table
        strips = [fold(x, table) for x in strips]
    else:
        out_ref, b_ref, a_ref = refs
    out_ref[...] = y
    send(i, a_ref, b_ref, *strips)


def inner_kernel(counts, width, y_ref, m_ref, basis_ref, w_ref, f_ref, gw_ref, gf_ref, near_ref):
    mask = column_mask(counts)
    s = jnp.where(mask, y_ref[8:120], 0.0)
    m = m_ref[8:120]
    w = DAMP * s + lap(m * lap(s))
    w = jnp.where(mask, w[8:104], 0.0) * SHRINK
    f = lap(m * edge_steps())
    f = jnp.where(mask, f[8:104], 0.0) * SHRINK
    w_ref[...] = w[:, :TC]
    f_ref[...] = f[:, :TC]
    gw_ref[...] = row_transform(w, basis_ref, inner_rows)
    gf_ref[...] = row_transform(f, basis_ref, inner_rows)
    near_ref[...] = near_inverse(counts, coarse_part(basis_ref, width))


def second_kernel(
    counts,
    width,
    y_ref,
    m_ref,
    gb_ref,
    ga_ref,
    table_ref,
    farther_ref,
    gw_ref,
    gf_ref,
    near_ref,
    weights_ref,
    basis_ref,
    z_ref,
    w_ref,
    band_ref,
    t_ref,
    b_ref,
    a_ref,
):
    i, j = place()
    y = y_ref[...]
    mask = edge_mask(counts)
    s = edges(y, *row_sides(i, counts[0], ga_ref, gb_ref, slice(0, 24)))
    s = jnp.where(mask, s, 0.0)
    table = merged(table_ref[...], farther_ref[...], unfold(ga_ref), unfold(gb_ref))
    picked = jnp.sum(near_ref[...] * as_row(table, width), axis=1, keepdims=True)
    bands = as_bands([picked[k : k + 1] for k in range(12)])
    coarse = edge_bands(bands)
    m = edge_part(m_ref)
    flow = m * (lap(s) + lap(coarse))
    z = s + coarse
    w = jnp.where(mask, DAMP * z + lap(flow), 0.0) * SHRINK
    step = jumps(bands[1])
    damped = (DAMP * SHRINK) * bands[1]
    z_ref[...] = jnp.concatenate([z[16:32, :TC], z[48:64, :TC]], axis=0)
    w_ref[...] = jnp.concatenate([w[16:32, :TC], w[48:64, :TC]], axis=0)
    band_ref[...] = jnp.concatenate([bands[1], step, damped, jnp.zeros((5, FC), jnp.float32)], axis=0)
    lane = lanes_of((EXT, 256))
    ones = jnp.where((lane >= 16) & (lane < 112), rows_t_part(basis_ref), 0.0)
    ones = jnp.sum(ones, axis=1, keepdims=True)
    u = gw_ref[...] + step * gf_ref[...] + ones * damped
    u = u + row_transform(jnp.concatenate([w[8:32], w[48:72]], axis=0), basis_ref, edge_rows)
    t = column_transform(u, basis_ref) * weights_ref[...]
    t_ref[...] = t
    send(j, a_ref, b_ref, *strips_of(t, basis_ref, 16))


def tile_of(edge, inner):
    return jnp.concatenate([edge[:16], inner, edge[16:]], axis=0)


def inverse_stats_kernel(
    t_ref,
    basis_ref,
    both_ref,
    m_ref,
    first_ref,
    inner_w_ref,
    f_ref,
    edge_z_ref,
    edge_w_ref,
    band_ref,
    y_ref,
    stats_ref,
    z_ref,
    w_ref,
):
    on, step, damped = (band_ref[k : k + 1, :TC] for k in range(3))
    z_ref[...] = tile_of(edge_z_ref, first_ref[16:112, :TC] + on)
    w_ref[...] = tile_of(edge_w_ref, inner_w_ref[...] + step * f_ref[...] + damped)
    y_ref[...] = solution_of(t_ref[...], basis_ref)
    rt, mt, zt, wt = both_ref[:TR], m_ref[:TR, :TC], z_ref[...], w_ref[...]
    lane, row = lanes_of((1, 256)), rows_of((128, 1))
    along = (lane % 128 != 0) & (lane % 128 != 127)
    top, low = mt[:1], mt[127:]
    side = jnp.sum(jnp.where((row > 0) & (row < 127), mt, 0.0), axis=0, keepdims=True)

    def halves(x):
        return [
            jnp.sum(x[:, :128], axis=1, keepdims=True),
            jnp.sum(x[:, 128:], axis=1, keepdims=True),
        ]

    first, last = lane % 128 == 0, lane % 128 == 127
    zero = jnp.zeros((1, 1), jnp.float32)
    stats_ref[...] = row_of(
        [
            core_sums(rt * zt),
            core_sums(zt * wt),
            core_sums(wt),
            halves(jnp.where(along, top, 0.0)),
            halves(jnp.where(along, low, 0.0)),
            halves(jnp.where(first, side, 0.0)),
            halves(jnp.where(last, side, 0.0)),
            halves(jnp.where(first, top, 0.0)),
            halves(jnp.where(last, top, 0.0)),
            halves(jnp.where(first, low, 0.0)),
            halves(jnp.where(last, low, 0.0)),
            *[[zero, zero]] * 4,
            core_sums(rt),
        ]
    )


def inner_dots_kernel(counts, y_ref, m_ref, both_ref, w_ref, stats_ref, v_ref, stats_out):
    q = jnp.where(column_mask(counts), y_ref[8:120], 0.0)
    v = (DAMP * q + lap(m_ref[8:120] * lap(q)))[8:104, :TC]
    q = q[8:104, :TC]
    v_ref[...] = v
    rest = [
        core_sums(v),
        core_sums(both_ref[16:112] * q),
        core_sums(w_ref[16:112] * q),
        core_sums(v * q),
    ]
    zero = jnp.zeros((1, 1), jnp.float32)
    stats_out[...] = stats_ref[...] + row_of([[zero, zero]] * 11 + rest)


def dots_kernel(
    counts, y_ref, m_ref, gb_ref, ga_ref, both_ref, w_ref, stats_ref, q_ref, v_ref, stats_out
):
    i, j = place()
    y = y_ref[...]
    q = edges(y, *sides(i, counts[0], ga_ref[...], gb_ref[...]))
    q = jnp.where(edge_mask(counts), q, 0.0)
    v = DAMP * q + lap(edge_part(m_ref) * lap(q))
    qe, ve = (jnp.concatenate([x[16:32, :TC], x[48:64, :TC]], axis=0) for x in (q, v))
    q_ref[...] = qe
    v_ref[...] = ve
    re = jnp.concatenate([both_ref[:16], both_ref[112:128]], axis=0)
    we = jnp.concatenate([w_ref[:16], w_ref[112:]], axis=0)
    rest = [core_sums(ve), core_sums(re * qe), core_sums(we * qe), core_sums(ve * qe)]
    zero = jnp.zeros((1, 1), jnp.float32)
    row = stats_ref[...] + row_of([[zero, zero]] * 11 + rest)
    stats_out[...] = jnp.broadcast_to(row, stats_out.shape)


def end_kernel(
    counts,
    width,
    stats_ref,
    basis_ref,
    m_ref,
    f_ref,
    both_ref,
    z_ref,
    w_ref,
    y_ref,
    inner_v_ref,
    q_ref,
    v_ref,
    solution_ref,
    residual_ref,
):
    i, j = place()
    tiles_c = counts[1]
    devices = counts[0] * tiles_c
    rows = stats_ref[...]
    st = jnp.concatenate([rows, pltpu.roll(rows, 64, 1)], axis=0)
    inverse = coarse_part(basis_ref, width)[: 2 * devices, : 2 * devices]
    g = jnp.broadcast_to(dot(inverse, st)[:, 2:3], st.shape)
    lane, row = lanes_of(st.shape), rows_of(st.shape)
    device = row % devices
    column = device % tiles_c
    on_left = row < devices

    def from_row(distance):
        return pltpu.roll(g, distance % (2 * devices), 0)

    up = jnp.where(device >= tiles_c, from_row(tiles_c), 0.0)
    down = jnp.where(device < devices - tiles_c, from_row(-tiles_c), 0.0)
    left = jnp.where(on_left, jnp.where(column > 0, from_row(1 - devices), 0.0), from_row(devices))
    right = jnp.where(
        on_left, from_row(-devices), jnp.where(column < tiles_c - 1, from_row(devices - 1), 0.0)
    )
    du, dd, dl, dr = g - up, g - down, g - left, g - right
    across = jnp.where(
        (lane == 3) | (lane == 7) | (lane == 8),
        du,
        jnp.where((lane == 4) | (lane == 9) | (lane == 10), dd, 0.0),
    )
    across = across + jnp.where(
        (lane == 5) | (lane == 7) | (lane == 9),
        dl,
        jnp.where((lane == 6) | (lane == 8) | (lane == 10), dr, 0.0),
    )
    factor = jnp.where((lane == 2) | (lane == 15), g, across * across)
    factor = jnp.where(lane == 11, 2.0 * g, factor)
    factor = jnp.where((lane < 2) | ((lane >= 12) & (lane < 15)), 1.0, factor)
    terms = jnp.where(lane == 16, (DAMP * SUB * SUB) * g * g, st * factor)
    sums = jnp.sum(terms, axis=0, keepdims=True)

    def whole(wanted):
        return jnp.sum(jnp.where(wanted, sums, 0.0), axis=1, keepdims=True)

    at = lanes_of((1, 128))
    rz, zw = whole(at == 0), whole(at == 1)
    ry = whole((at == 12) | (at == 15))
    yw = whole((at == 13) | (at == 2))
    yv = whole(((at >= 3) & (at < 12)) | (at == 14) | (at == 16))
    a = rz / zw
    rz1 = rz - a * ry - a * zw + a * a * yw
    beta1 = 1.0 + rz1 / rz
    dad = (beta1 * beta1 * zw - 2.0 * a * beta1 * yw) * (1.0 / SHRINK) + a * a * yv
    a1 = rz1 / dad
    r = i - 1 + lane // 4
    c = 2 * j - 1 + lane % 4
    inside = (r >= 0) & (r < counts[0]) & (c >= 0) & (c < 2 * tiles_c) & (lane < 12)
    where = lax.rem(c + 2, 2) * devices + r * tiles_c + (c + 2) // 2 - 1
    picked = jnp.sum(jnp.where(inside & (row == where), g, 0.0), axis=0, keepdims=True)
    bands = as_bands([picked[:, k : k + 1] for k in range(12)])
    on = bands[1][:, :TC]
    coarse = edge_bands(bands)
    image = DAMP * coarse + lap(edge_part(m_ref) * lap(coarse))
    image = with_edges(image, (jumps(bands[1]) * (1.0 / SHRINK))[:, :TC] * f_ref[...] + DAMP * on)
    y = tile_of(q_ref, y_ref[16:112, :TC]) + on
    v = tile_of(v_ref, inner_v_ref[...]) + image
    z, w = z_ref[...], w_ref[...]
    solution_ref[...] = (a * SHRINK) * z + a1 * (beta1 * z - a * y)
    residual_ref[...] = both_ref[:TR] - a * w - a1 * ((beta1 * (1.0 / SHRINK)) * w - a * v)


def call(kernel, outs, *args, flops=10**9):
    shapes = [jax.ShapeDtypeStruct(s, jnp.float32) for s in outs]
    return pl.pallas_call(
        kernel,
        out_shape=shapes,
        compiler_params=pltpu.CompilerParams(vmem_limit_bytes=48 * 1024 * 1024),
        cost_estimate=pl.CostEstimate(flops=flops, bytes_accessed=10**6, transcendentals=0),
    )(*args)


def pairs_from(count, offset):
    found = []
    for k in range(offset, count, 2):
        found += [(k, (k + 1) % count), ((k + 1) % count, k)]
    return found


def odd_pairs(counts, axis, bit):
    found = []
    for i in range(counts[0]):
        for j in range(counts[1]):
            at = [i, j]
            if bit and at[axis] in (0, counts[axis] - 1):
                at[1 - axis] ^= bit
            else:
                at[axis] = (at[axis] + (1 if at[axis] % 2 else -1)) % counts[axis]
            found.append((i * counts[1] + j, at[0] * counts[1] + at[1]))
    return found


def xor_pairs(counts, rows, cols):
    flat = [(i, j) for i in range(counts[0]) for j in range(counts[1])]
    return [(i * counts[1] + j, (i ^ rows) * counts[1] + (j ^ cols)) for i, j in flat]


def spreads(counts):
    known = np.eye(counts[0] * counts[1], dtype=bool)

    def meet(*swaps):
        return np.logical_or.reduce([known, *(known[[b for _, b in pairs]] for pairs in swaps)])

    even = [xor_pairs(counts, 0, 1), xor_pairs(counts, 1, 0)]
    known = meet(even[0], odd_pairs(counts, 1, 0))
    first = meet(xor_pairs(counts, 4, 0))
    known = meet(even[1], odd_pairs(counts, 0, 0))
    second = meet(xor_pairs(counts, 4, 2))
    known = meet(even[0], odd_pairs(counts, 1, 1)) | first
    return (meet(even[1], odd_pairs(counts, 0, 0)) | second).all()


def body(counts, height, noise):
    nr, nc = counts
    devices = nr * nc
    width = max(128, devices * 2)
    basis = jnp.asarray(constants(nr, 2 * nc, width))
    both_axes = ("row", "col")
    depth = table_shape(counts)[0]

    def swap(a, b, axis, bit=0):
        gb = lax.ppermute(b, both_axes, odd_pairs(counts, both_axes.index(axis), bit))
        return lax.ppermute(a, axis, pairs_from(lax.axis_size(axis), 0)), gb

    def small_swap(x, rows, cols):
        return lax.ppermute(x, both_axes, xor_pairs(counts, rows, cols))

    both = jnp.pad(noise, ((0, TR), (0, 0))) + jnp.pad(height, ((TR, 0), (0, 0)))
    b, a, table = call(
        functools.partial(begin_kernel, counts), [(32 + depth, 128)] * 2 + [(depth, 128)], both
    )
    if not spreads(counts):
        for axis, count in enumerate(counts):
            bit = 1
            while bit < count:
                table = table + small_swap(table, *((0, bit) if axis else (bit, 0)))
                bit *= 2
    ga, gb = swap(a, b, "col")
    r3, h3, b, a, table = call(
        functools.partial(widen_kernel, counts),
        [(128, 128)] * 2 + [(24, FC)] * 2 + [(depth, 128)],
        both,
        table,
        gb,
        ga,
    )
    ga, gb = swap(a, b, "row")
    weight, table = call(weights_kernel, [(EXT, 2 * SPEC), (depth, 128)], both, table, basis)
    far = small_swap(table, 4, 0)
    t = call(forward_kernel, [(EXT, 2 * SPEC)], both, r3, basis, flops=5 * 10**8)[0]
    t, table, b, a = call(
        functools.partial(first_kernel, counts),
        [(EXT, 2 * SPEC), (depth, 128)] + [(24 + depth, EXT)] * 2,
        gb,
        ga,
        t,
        weight,
        basis,
        table,
    )
    y, m, table_too = call(
        functools.partial(inverse_kernel, counts),
        [(EXT, FC), (FR, FC), (depth, 128)],
        t,
        basis,
        both,
        h3,
        gb,
        ga,
        table,
    )
    ga, gb = swap(a, b, "col", 1)
    farther = small_swap(table_too, 4, 2)
    y, table, b, a = call(
        functools.partial(columns_kernel, counts),
        [(EXT, FC), (depth, 128)] + [(24, FC)] * 2,
        y,
        gb,
        ga,
        table,
        far,
    )
    ga, gb = swap(a, b, "row")
    inner_w, f, gw, gf, near = call(
        functools.partial(inner_kernel, counts, width),
        [(96, TC)] * 2 + [(EXT, FC)] * 2 + [(16, width)],
        y,
        m,
        basis,
    )
    edge_z, edge_w, band, t, b, a = call(
        functools.partial(second_kernel, counts, width),
        [(32, TC)] * 2 + [(8, FC), (EXT, 2 * SPEC)] + [(16, EXT)] * 2,
        y,
        m,
        gb,
        ga,
        table,
        farther,
        gw,
        gf,
        near,
        weight,
        basis,
    )
    ga, gb = swap(a, b, "col", 1)
    y, stats, z, w = call(
        inverse_stats_kernel,
        [(EXT, FC), (1, 128)] + [(TR, TC)] * 2,
        t,
        basis,
        both,
        m,
        y,
        inner_w,
        f,
        edge_z,
        edge_w,
        band,
    )
    y, b, a = call(
        functools.partial(columns_kernel, counts), [(EXT, FC)] + [(16, FC)] * 2, y, gb, ga
    )
    ga, gb = swap(a, b, "row", 1)
    inner_v, stats = call(
        functools.partial(inner_dots_kernel, counts),
        [(96, TC), (1, 128)],
        y,
        m,
        both,
        w,
        stats,
    )
    q, v, stats = call(
        functools.partial(dots_kernel, counts),
        [(32, TC)] * 2 + [(devices, 128)],
        y,
        m,
        gb,
        ga,
        both,
        w,
        stats,
    )
    stats = lax.all_to_all(stats, both_axes, 0, 0, tiled=True)
    return tuple(
        call(
            functools.partial(end_kernel, counts, width),
            [(TR, TC)] * 2,
            stats,
            basis,
            m,
            f,
            both,
            z,
            w,
            y,
            inner_v,
            q,
            v,
        )
    )


def solution(mesh):
    counts = (mesh.shape["row"], mesh.shape["col"])
    spec = P("row", "col")
    return jax.shard_map(
        functools.partial(body, counts),
        mesh=mesh,
        in_specs=(spec, spec),
        out_specs=(spec, spec),
        check_vma=False,
    )
```

```python
import functools

import jax
import jax.numpy as jnp
import ml_dtypes
import numpy as np
from jax import lax
from jax.experimental import pallas as pl
from jax.experimental.pallas import tpu as pltpu
from jax.sharding import PartitionSpec as P

SUB = 128
OV = 8
EXT = SUB + 2 * OV
DAMP = 2.0**-28
SHRINK = 2.0**-20

TR, TC = 128, 256
FR, FC = 160, 384
SPEC = 256

highest = lax.Precision.HIGHEST


def sine(count):
    k = np.arange(1, count + 1, dtype=np.float64)
    basis = np.sqrt(2.0 / (count + 1.0)) * np.sin(np.pi * k[:, None] * k[None, :] / (count + 1.0))
    return basis, 2.0 - 2.0 * np.cos(np.pi * k / (count + 1.0))


def block_constants():
    basis, eig = sine(EXT)
    rows = np.roll(basis, -OV, 0)
    cols = np.pad(basis, ((0, SPEC - EXT), (0, SPEC - EXT)))
    scale = np.pad((eig[:, None] + eig[None, :]) ** 2, ((0, 0), (0, SPEC - EXT)))
    wide = lambda x: np.pad(x, ((0, 0), (0, 2 * SPEC - x.shape[1])))
    high = rows.T.astype(ml_dtypes.bfloat16).astype(np.float64)
    low = (rows.T - high).astype(ml_dtypes.bfloat16).astype(np.float64)
    tile = np.concatenate([x[:, :SUB] for x in (high, high, low)], 1)
    halo = np.concatenate([x[:, SUB:] for x in (high, high, low)], 1)
    inner = np.concatenate([x[:, 16:112] for x in (high, high, low)], 1)
    at = [*range(136, 144), *range(16), *range(112, 136)]
    edge = np.concatenate([x[:, at] for x in (high, high, low)], 1)
    turned = np.hstack([rows.T, np.zeros((EXT, 256 - EXT)), edge])
    return [np.tile(scale, (1, 2)), *(wide(x) for x in (rows, turned, cols, inner, np.hstack([tile, halo])))]


def rows_part(ref):
    return ref[EXT : 2 * EXT, :EXT]


def rows_t_part(ref):
    return ref[2 * EXT : 3 * EXT, :256]


def cols_part(ref):
    return ref[3 * EXT : 3 * EXT + SPEC, :SPEC]


def inner_rows(ref):
    at = 3 * EXT + SPEC
    return ref[at : at + EXT, : 3 * 96]


def edge_rows(ref):
    return ref[2 * EXT : 3 * EXT, 256 : 256 + 3 * 48]


def tile_rows(ref):
    at = 4 * EXT + SPEC
    return ref[at : at + EXT, : 3 * SUB]


def halo_rows(ref):
    at = 4 * EXT + SPEC
    return ref[at : at + EXT, 3 * SUB : 3 * EXT]


def coarse_part(ref, width):
    at, lanes = 5 * EXT + SPEC, 2 * SPEC
    parts = [ref[at + k * width : at + (k + 1) * width] for k in range(-(-width // lanes))]
    return (parts[0] if len(parts) == 1 else jnp.concatenate(parts, axis=1))[:, :width]


def constants(nr, nc, width):
    lanes = 2 * SPEC
    inverse = coarse_inverse(nr, nc, -(-width // lanes) * lanes)[:width]
    parts = [*block_constants(), *np.split(inverse, inverse.shape[1] // lanes, 1)]
    return np.concatenate(parts).astype(np.float32)


def coarse_inverse(nr, nc, width):
    br, er = sine(nr)
    bc, ec = sine(nc)
    both = np.kron(br, bc).reshape(nr, nc // 2, 2, nr * nc).transpose(2, 0, 1, 3)
    both = both.reshape(nr * nc, nr * nc)
    scale = (er[:, None] + ec[None, :]) / (SUB * SUB)
    values = (SUB * SUB * (DAMP + scale * scale)).reshape(-1)
    whole = np.zeros((width, width), np.float32)
    whole[: nr * nc, : nr * nc] = (both / values) @ both.T
    return whole


def dot(a, b, side=0):
    return lax.dot_general(
        a, b, (((1,), (side,)), ((), ())), precision=highest, preferred_element_type=jnp.float32
    )


def lap(x):
    rows, lanes = x.shape
    beside = pltpu.roll(x, 1, 0) + pltpu.roll(x, rows - 1, 0)
    beside = beside + (pltpu.roll(x, 1, 1) + pltpu.roll(x, lanes - 1, 1))
    return 4.0 * x - beside


def lanes_of(shape):
    return lax.broadcasted_iota(jnp.int32, shape, 1)


def rows_of(shape):
    return lax.broadcasted_iota(jnp.int32, shape, 0)


def total(x):
    return jnp.sum(jnp.sum(x, axis=0, keepdims=True), axis=1, keepdims=True)


def place():
    return lax.axis_index("row"), lax.axis_index("col")


def is_even(index):
    return lax.rem(index, 2) == 0


def column_mask(counts):
    j = lax.axis_index("col")
    lane = lanes_of((1, FC))
    right = jnp.where(j < counts[1] - 1, 320, 256)
    left = jnp.where(j > 0, 320, 384)
    return (lane < right) | (lane >= left)


def edge_mask(counts):
    i = lax.axis_index("row")
    row = rows_of((80, 1))
    first = jnp.where(i > 0, 0, 16)
    last = jnp.where(i < counts[0] - 1, 80, 64)
    return (row >= first) & (row < last) & column_mask(counts)


def table_shape(counts):
    return (-(-2 * counts[0] * counts[1] // 1024) * 8, 128)


def table_of(values, counts):
    i, j = place()
    devices = counts[0] * counts[1]
    shape = table_shape(counts)
    at = rows_of(shape) * 128 + lanes_of(shape) - (i * counts[1] + j)
    return jnp.where(at == 0, values[0], jnp.where(at == devices, values[1], 0.0))


def merged(table, *others):
    for other in others:
        table = jnp.where(table != 0.0, table, other)
    return table


def as_row(table, width):
    return jnp.concatenate([table[k : k + 1] for k in range(width // 128)], axis=1)


def row_of(pairs):
    lane = lanes_of((1, 128))
    row = jnp.zeros((1, 128), jnp.float32)
    for k, (left, right) in enumerate(pairs):
        row = jnp.where(lane == k, left, jnp.where(lane == 64 + k, right, row))
    return row


def near_inverse(counts, inverse):
    i, j = place()
    nr, nc = counts[0], 2 * counts[1]
    shape = (16, inverse.shape[0])
    which = rows_of(shape)
    r = i - 1 + which // 4
    c = 2 * j - 1 + which % 4
    inside = (r >= 0) & (r < nr) & (c >= 0) & (c < nc) & (which < 12)
    at = lax.rem(c + 2, 2) * (nr * counts[1]) + r * counts[1] + (c + 2) // 2 - 1
    return dot(jnp.where(inside & (lanes_of(shape) == at), 1.0, 0.0), inverse)


def as_bands(values):
    lane = lanes_of((1, FC))
    bands = []
    for d in range(3):
        left, first, second, right = values[4 * d : 4 * d + 4]
        bands.append(
            jnp.where(
                lane < 128,
                first,
                jnp.where(lane < 256, second, jnp.where(lane < 320, right, left)),
            )
        )
    return bands


def edge_bands(bands):
    above, on, below = bands
    return jnp.concatenate(
        [
            jnp.broadcast_to(above, (16, FC)),
            jnp.broadcast_to(on, (48, FC)),
            jnp.broadcast_to(below, (16, FC)),
        ],
        axis=0,
    )


def jumps(row):
    step = row - pltpu.roll(row, 1, 1)
    lane = lanes_of((1, FC))
    at = [jnp.sum(jnp.where(lane == k, step, 0.0), axis=1, keepdims=True) for k in (0, 128, 256)]
    return jnp.where(
        (lane < 64) | (lane >= 320), at[0], jnp.where(lane < 192, at[1], at[2])
    )


def edge_steps():
    lane = lanes_of((1, FC))
    up = (lane == 0) | (lane == 128) | (lane == 256)
    down = (lane == FC - 1) | (lane == 127) | (lane == 255)
    return jnp.where(up, 1.0, jnp.where(down, -1.0, 0.0))


def halves_of(x):
    high = x.astype(jnp.bfloat16)
    return high, (x - high.astype(jnp.float32)).astype(jnp.bfloat16)


def product(a, b):
    return lax.dot_general(a, b, (((1,), (0,)), ((), ())), preferred_element_type=jnp.float32)


def column_transform(w, basis_ref):
    high, low = halves_of(pltpu.roll(w, OV, 1))
    cols, rest = halves_of(cols_part(basis_ref))
    cols = jnp.concatenate([cols, rest, cols], axis=0)

    def block(at):
        part = slice(at, at + SPEC)
        return product(jnp.concatenate([high[:, part], high[:, part], low[:, part]], axis=1), cols)

    return jnp.concatenate([block(0), block(128)], axis=1)


def row_transform(u, basis_ref, part):
    high, low = halves_of(u)
    rows = part(basis_ref).astype(jnp.bfloat16)
    return product(rows, jnp.concatenate([high, low, high], axis=0))


def weights(means, basis_ref):
    lane = lanes_of((1, 2 * SPEC))
    mean = jnp.where(lane < SPEC, means[0], means[1])
    return 1.0 / (DAMP + mean * basis_ref[:EXT])


def strips_of(t, basis_ref, deep):
    cols = cols_part(basis_ref)
    left = dot(cols[:deep], t[:, :SPEC], 1)
    right = dot(cols[EXT - deep : EXT], t[:, SPEC:], 1)
    both = dot(jnp.concatenate([left, right], axis=0), rows_t_part(basis_ref)[:, :EXT])
    return both[:deep], both[deep:]


def solution_of(t, basis_ref):
    v = dot(rows_part(basis_ref), t)
    cols = cols_part(basis_ref)
    first, second = dot(v[:, :SPEC], cols), dot(v[:, SPEC:], cols)
    y = jnp.concatenate(
        [first[:, :128], first[:, 128:] + second[:, :128], second[:, 128:]], axis=1
    )
    return pltpu.roll(y, FC - OV, 1)


def core_sums(x):
    return [total(x[:, :128]), total(x[:, 128:256])]


def add_columns(y, from_left, from_right):
    far = from_left.shape[0] - OV
    gap = jnp.zeros((56 - far, EXT), jnp.float32)
    turned = jnp.concatenate(
        [from_right[8:], gap, from_right[:8], from_left[far:], gap, from_left[:far]], axis=0
    )
    back = turned.T
    lane = lanes_of((EXT, 128))
    rolled = pltpu.roll(back, 64, 1)
    first = y[:, :128] + jnp.where(lane < 8, rolled, 0.0)
    second = y[:, 128:256] + jnp.where(lane >= 120, rolled, 0.0)
    third = y[:, 256:] + jnp.where((lane < 16) | (lane >= 112), back, 0.0)
    return jnp.concatenate([first, second, third], axis=1)


def pack_rows(y, deep):
    return jnp.concatenate([y[136:], y[: deep - 8]], axis=0), y[136 - deep : 136]


def edges(y, from_above, from_below):
    far = from_above.shape[0] - OV
    none = jnp.zeros((8, FC), jnp.float32)
    return jnp.concatenate(
        [
            from_above[:8] if far == 16 else none,
            y[136:] + from_above[far - 8 : far],
            y[:8] + from_above[far:],
            y[8:24],
            y[104:120],
            y[120:136] + from_below[:16],
            from_below[16:] if far == 16 else none,
        ],
        axis=0,
    )


def edge_part(frame):
    return jnp.concatenate([frame[144:], frame[:24], frame[104:144]], axis=0)


def with_edges(edge, inner):
    return jnp.concatenate([edge[16:32, :TC], inner, edge[48:64, :TC]], axis=0)


def sides(index, count, a, b):
    even = is_even(index)
    before = jnp.where(index > 0, jnp.where(even, b, a), 0.0)
    after = jnp.where(index < count - 1, jnp.where(even, a, b), 0.0)
    return before, after


def fold(rows, table):
    lane = lanes_of((8, 128))
    free = (lane >= 32) & (lane < 96)
    third = jnp.concatenate(
        [
            jnp.where(free, pltpu.roll(table, 32, 1), rows[:8, 256:]),
            jnp.where(free, pltpu.roll(table, 96, 1), rows[8:16, 256:]),
            rows[16:, 256:],
        ],
        axis=0,
    )
    return jnp.concatenate([rows[:, :256], third], axis=1)


def unfold(ref):
    low, high = ref[:8, 256:], ref[8:16, 256:]
    return jnp.where(lanes_of((8, 128)) < 64, pltpu.roll(low, 96, 1), pltpu.roll(high, 32, 1))


def row_sides(index, count, ga_ref, gb_ref, rows):
    lane = lanes_of((1, FC))
    used = (lane < 288) | (lane >= 352)
    return [jnp.where(used, x, 0.0) for x in sides(index, count, ga_ref[rows], gb_ref[rows])]


def send(index, a_ref, b_ref, before, after):
    even = is_even(index)
    a_ref[...] = jnp.where(even, after, before)
    b_ref[...] = jnp.where(even, before, after)


def begin_kernel(counts, both_ref, b_ref, a_ref, table_ref):
    r, h = both_ref[:TR], both_ref[TR:]
    lane = lanes_of((128, 128))
    packed = jnp.where(
        lane < 16,
        r[:, :128],
        jnp.where(
            lane < 64,
            pltpu.roll(h[:, :128], 16, 1),
            jnp.where(lane < 112, pltpu.roll(h[:, 128:], 112, 1), r[:, 128:]),
        ),
    )
    turned = packed.T
    table = table_of(core_sums(r), counts)
    table_ref[...] = table
    send(
        lax.axis_index("col"),
        a_ref,
        b_ref,
        jnp.concatenate([turned[:32], table], axis=0),
        jnp.concatenate([turned[96:], table], axis=0),
    )


def widen_kernel(counts, both_ref, own_ref, gb_ref, ga_ref, r3_ref, h3_ref, b_ref, a_ref, table_ref):
    i, j = place()
    from_left, from_right = sides(j, counts[1], ga_ref[:32], gb_ref[:32])
    turned = jnp.concatenate([from_right, jnp.zeros((64, 128), jnp.float32), from_left], axis=0)
    back = turned.T
    lane = lanes_of((128, 128))
    edge = (lane < 16) | (lane >= 112)
    r3 = jnp.where(edge, back, 0.0)
    h3 = jnp.where(
        lane < 16, pltpu.roll(back, 112, 1), jnp.where(lane >= 112, pltpu.roll(back, 16, 1), 0.0)
    )
    r3_ref[...] = r3
    h3_ref[...] = h3
    r, h = both_ref[:TR], both_ref[TR:]
    table = merged(own_ref[...], ga_ref[32:], gb_ref[32:])
    table_ref[...] = table

    def strip(r_rows, h_rows):
        rows = jnp.concatenate(
            [
                jnp.concatenate([r[r_rows], r3[r_rows]], axis=1),
                jnp.concatenate([h[h_rows], h3[h_rows]], axis=1),
            ],
            axis=0,
        )
        return fold(rows, table)

    send(i, a_ref, b_ref, strip(slice(0, 8), slice(0, 16)), strip(slice(120, 128), slice(112, 128)))


def weights_kernel(both_ref, table_ref, basis_ref, weights_ref, table_out):
    h = both_ref[TR:]
    means = [x / (SUB * SUB) for x in core_sums(h * h * h)]
    weights_ref[...] = weights(means, basis_ref)
    table_out[...] = table_ref[...]


def forward_kernel(both_ref, r3_ref, basis_ref, t_ref):
    r = both_ref[:TR]
    u = column_transform(jnp.concatenate([r, r3_ref[...]], axis=1), basis_ref)
    t_ref[...] = row_transform(u, basis_ref, tile_rows)


def first_kernel(
    counts,
    gb_ref,
    ga_ref,
    tile_ref,
    weights_ref,
    basis_ref,
    table_ref,
    t_ref,
    table_out,
    b_ref,
    a_ref,
):
    i, j = place()
    above, below = row_sides(i, counts[0], ga_ref, gb_ref, slice(0, 8))
    u = column_transform(jnp.concatenate([below, above], axis=0), basis_ref)
    t = (tile_ref[...] + row_transform(u, basis_ref, halo_rows)) * weights_ref[...]
    t_ref[...] = t
    table = merged(table_ref[...], unfold(ga_ref), unfold(gb_ref))
    table_out[...] = table
    wide = jnp.concatenate([table, jnp.zeros((table.shape[0], EXT - 128), jnp.float32)], axis=1)
    strips = (jnp.concatenate([x, wide], axis=0) for x in strips_of(t, basis_ref, 24))
    send(j, a_ref, b_ref, *strips)


def inverse_kernel(
    counts, t_ref, basis_ref, both_ref, h3_ref, gb_ref, ga_ref, table_ref, y_ref, m_ref, table_out
):
    table_out[...] = table_ref[...]
    y_ref[...] = solution_of(t_ref[...], basis_ref)
    above, below = row_sides(lax.axis_index("row"), counts[0], ga_ref, gb_ref, slice(8, 24))
    h = jnp.concatenate([both_ref[TR:], h3_ref[...]], axis=1)
    tall = jnp.concatenate([h, below, above], axis=0)
    m_ref[...] = tall * tall * tall


def columns_kernel(counts, y_ref, gb_ref, ga_ref, *refs):
    i, j = place()
    deep = 24 if len(refs) == 6 else 16
    y = add_columns(y_ref[...], *sides(j, counts[1], ga_ref[:deep], gb_ref[:deep]))
    strips = pack_rows(y, deep)
    if len(refs) == 6:
        table_ref, far_ref, out_ref, table_out, b_ref, a_ref = refs
        table = merged(table_ref[...], far_ref[...], ga_ref[24:, :128], gb_ref[24:, :128])
        table_out[...] = table
        strips = [fold(x, table) for x in strips]
    else:
        out_ref, b_ref, a_ref = refs
    out_ref[...] = y
    send(i, a_ref, b_ref, *strips)


def inner_kernel(counts, width, y_ref, m_ref, basis_ref, w_ref, f_ref, gw_ref, gf_ref, near_ref):
    mask = column_mask(counts)
    s = jnp.where(mask, y_ref[8:120], 0.0)
    m = m_ref[8:120]
    w = DAMP * s + lap(m * lap(s))
    w = jnp.where(mask, w[8:104], 0.0) * SHRINK
    f = lap(m * edge_steps())
    f = jnp.where(mask, f[8:104], 0.0) * SHRINK
    w_ref[...] = w[:, :TC]
    f_ref[...] = f[:, :TC]
    gw_ref[...] = row_transform(w, basis_ref, inner_rows)
    gf_ref[...] = row_transform(f, basis_ref, inner_rows)
    near_ref[...] = near_inverse(counts, coarse_part(basis_ref, width))


def second_kernel(
    counts,
    width,
    y_ref,
    m_ref,
    gb_ref,
    ga_ref,
    table_ref,
    farther_ref,
    inner_w_ref,
    f_ref,
    gw_ref,
    gf_ref,
    near_ref,
    weights_ref,
    basis_ref,
    z_ref,
    w_ref,
    t_ref,
    b_ref,
    a_ref,
):
    i, j = place()
    y = y_ref[...]
    mask = edge_mask(counts)
    s = edges(y, *row_sides(i, counts[0], ga_ref, gb_ref, slice(0, 24)))
    s = jnp.where(mask, s, 0.0)
    table = merged(table_ref[...], farther_ref[...], unfold(ga_ref), unfold(gb_ref))
    picked = jnp.sum(near_ref[...] * as_row(table, width), axis=1, keepdims=True)
    bands = as_bands([picked[k : k + 1] for k in range(12)])
    coarse = edge_bands(bands)
    m = edge_part(m_ref)
    flow = m * (lap(s) + lap(coarse))
    z = s + coarse
    w = jnp.where(mask, DAMP * z + lap(flow), 0.0) * SHRINK
    step = jumps(bands[1])
    damped = (DAMP * SHRINK) * bands[1]
    z_ref[...] = with_edges(z, y[16:112, :TC] + bands[1][:, :TC])
    w_ref[...] = with_edges(w, inner_w_ref[...] + step[:, :TC] * f_ref[...] + damped[:, :TC])
    lane = lanes_of((EXT, 256))
    ones = jnp.where((lane >= 16) & (lane < 112), rows_t_part(basis_ref), 0.0)
    ones = jnp.sum(ones, axis=1, keepdims=True)
    u = gw_ref[...] + step * gf_ref[...] + ones * damped
    u = u + row_transform(jnp.concatenate([w[8:32], w[48:72]], axis=0), basis_ref, edge_rows)
    t = column_transform(u, basis_ref) * weights_ref[...]
    t_ref[...] = t
    send(j, a_ref, b_ref, *strips_of(t, basis_ref, 16))


def inverse_stats_kernel(t_ref, basis_ref, both_ref, m_ref, z_ref, w_ref, y_ref, stats_ref):
    y_ref[...] = solution_of(t_ref[...], basis_ref)
    rt, mt, zt, wt = both_ref[:TR], m_ref[:TR, :TC], z_ref[...], w_ref[...]
    lane, row = lanes_of((1, 256)), rows_of((128, 1))
    along = (lane % 128 != 0) & (lane % 128 != 127)
    top, low = mt[:1], mt[127:]
    side = jnp.sum(jnp.where((row > 0) & (row < 127), mt, 0.0), axis=0, keepdims=True)

    def halves(x):
        return [
            jnp.sum(x[:, :128], axis=1, keepdims=True),
            jnp.sum(x[:, 128:], axis=1, keepdims=True),
        ]

    first, last = lane % 128 == 0, lane % 128 == 127
    zero = jnp.zeros((1, 1), jnp.float32)
    stats_ref[...] = row_of(
        [
            core_sums(rt * zt),
            core_sums(zt * wt),
            core_sums(wt),
            halves(jnp.where(along, top, 0.0)),
            halves(jnp.where(along, low, 0.0)),
            halves(jnp.where(first, side, 0.0)),
            halves(jnp.where(last, side, 0.0)),
            halves(jnp.where(first, top, 0.0)),
            halves(jnp.where(last, top, 0.0)),
            halves(jnp.where(first, low, 0.0)),
            halves(jnp.where(last, low, 0.0)),
            *[[zero, zero]] * 4,
            core_sums(rt),
        ]
    )


def inner_dots_kernel(counts, y_ref, m_ref, both_ref, w_ref, stats_ref, v_ref, stats_out):
    q = jnp.where(column_mask(counts), y_ref[8:120], 0.0)
    v = (DAMP * q + lap(m_ref[8:120] * lap(q)))[8:104, :TC]
    q = q[8:104, :TC]
    v_ref[...] = v
    rest = [
        core_sums(v),
        core_sums(both_ref[16:112] * q),
        core_sums(w_ref[16:112] * q),
        core_sums(v * q),
    ]
    zero = jnp.zeros((1, 1), jnp.float32)
    stats_out[...] = stats_ref[...] + row_of([[zero, zero]] * 11 + rest)


def dots_kernel(
    counts, y_ref, m_ref, gb_ref, ga_ref, both_ref, w_ref, stats_ref, inner_v_ref, q_ref, v_ref, stats_out
):
    i, j = place()
    y = y_ref[...]
    q = edges(y, *sides(i, counts[0], ga_ref[...], gb_ref[...]))
    q = jnp.where(edge_mask(counts), q, 0.0)
    v = DAMP * q + lap(edge_part(m_ref) * lap(q))
    q_ref[...] = with_edges(q, y[16:112, :TC])
    v_ref[...] = with_edges(v, inner_v_ref[...])
    qe, ve = (jnp.concatenate([x[16:32, :TC], x[48:64, :TC]], axis=0) for x in (q, v))
    re = jnp.concatenate([both_ref[:16], both_ref[112:128]], axis=0)
    we = jnp.concatenate([w_ref[:16], w_ref[112:]], axis=0)
    rest = [core_sums(ve), core_sums(re * qe), core_sums(we * qe), core_sums(ve * qe)]
    zero = jnp.zeros((1, 1), jnp.float32)
    row = stats_ref[...] + row_of([[zero, zero]] * 11 + rest)
    stats_out[...] = jnp.broadcast_to(row, stats_out.shape)


def end_kernel(
    counts,
    width,
    stats_ref,
    basis_ref,
    m_ref,
    f_ref,
    both_ref,
    z_ref,
    w_ref,
    q_ref,
    v_ref,
    solution_ref,
    residual_ref,
):
    i, j = place()
    tiles_c = counts[1]
    devices = counts[0] * tiles_c
    rows = stats_ref[...]
    st = jnp.concatenate([rows, pltpu.roll(rows, 64, 1)], axis=0)
    inverse = coarse_part(basis_ref, width)[: 2 * devices, : 2 * devices]
    g = jnp.broadcast_to(dot(inverse, st)[:, 2:3], st.shape)
    lane, row = lanes_of(st.shape), rows_of(st.shape)
    device = row % devices
    column = device % tiles_c
    on_left = row < devices

    def from_row(distance):
        return pltpu.roll(g, distance % (2 * devices), 0)

    up = jnp.where(device >= tiles_c, from_row(tiles_c), 0.0)
    down = jnp.where(device < devices - tiles_c, from_row(-tiles_c), 0.0)
    left = jnp.where(on_left, jnp.where(column > 0, from_row(1 - devices), 0.0), from_row(devices))
    right = jnp.where(
        on_left, from_row(-devices), jnp.where(column < tiles_c - 1, from_row(devices - 1), 0.0)
    )
    du, dd, dl, dr = g - up, g - down, g - left, g - right
    across = jnp.where(
        (lane == 3) | (lane == 7) | (lane == 8),
        du,
        jnp.where((lane == 4) | (lane == 9) | (lane == 10), dd, 0.0),
    )
    across = across + jnp.where(
        (lane == 5) | (lane == 7) | (lane == 9),
        dl,
        jnp.where((lane == 6) | (lane == 8) | (lane == 10), dr, 0.0),
    )
    factor = jnp.where((lane == 2) | (lane == 15), g, across * across)
    factor = jnp.where(lane == 11, 2.0 * g, factor)
    factor = jnp.where((lane < 2) | ((lane >= 12) & (lane < 15)), 1.0, factor)
    terms = jnp.where(lane == 16, (DAMP * SUB * SUB) * g * g, st * factor)
    sums = jnp.sum(terms, axis=0, keepdims=True)

    def whole(wanted):
        return jnp.sum(jnp.where(wanted, sums, 0.0), axis=1, keepdims=True)

    at = lanes_of((1, 128))
    rz, zw = whole(at == 0), whole(at == 1)
    ry = whole((at == 12) | (at == 15))
    yw = whole((at == 13) | (at == 2))
    yv = whole(((at >= 3) & (at < 12)) | (at == 14) | (at == 16))
    a = rz / zw
    rz1 = rz - a * ry - a * zw + a * a * yw
    beta1 = 1.0 + rz1 / rz
    dad = (beta1 * beta1 * zw - 2.0 * a * beta1 * yw) * (1.0 / SHRINK) + a * a * yv
    a1 = rz1 / dad
    r = i - 1 + lane // 4
    c = 2 * j - 1 + lane % 4
    inside = (r >= 0) & (r < counts[0]) & (c >= 0) & (c < 2 * tiles_c) & (lane < 12)
    where = lax.rem(c + 2, 2) * devices + r * tiles_c + (c + 2) // 2 - 1
    picked = jnp.sum(jnp.where(inside & (row == where), g, 0.0), axis=0, keepdims=True)
    bands = as_bands([picked[:, k : k + 1] for k in range(12)])
    on = bands[1][:, :TC]
    coarse = edge_bands(bands)
    image = DAMP * coarse + lap(edge_part(m_ref) * lap(coarse))
    image = with_edges(image, (jumps(bands[1]) * (1.0 / SHRINK))[:, :TC] * f_ref[...] + DAMP * on)
    y = q_ref[...] + on
    v = v_ref[...] + image
    z, w = z_ref[...], w_ref[...]
    solution_ref[...] = (a * SHRINK) * z + a1 * (beta1 * z - a * y)
    residual_ref[...] = both_ref[:TR] - a * w - a1 * ((beta1 * (1.0 / SHRINK)) * w - a * v)


def call(kernel, outs, *args, flops=10**9):
    shapes = [jax.ShapeDtypeStruct(s, jnp.float32) for s in outs]
    return pl.pallas_call(
        kernel,
        out_shape=shapes,
        compiler_params=pltpu.CompilerParams(vmem_limit_bytes=48 * 1024 * 1024),
        cost_estimate=pl.CostEstimate(flops=flops, bytes_accessed=10**6, transcendentals=0),
    )(*args)


def pairs_from(count, offset):
    found = []
    for k in range(offset, count, 2):
        found += [(k, (k + 1) % count), ((k + 1) % count, k)]
    return found


def odd_pairs(counts, axis, bit):
    found = []
    for i in range(counts[0]):
        for j in range(counts[1]):
            at = [i, j]
            if bit and at[axis] in (0, counts[axis] - 1):
                at[1 - axis] ^= bit
            else:
                at[axis] = (at[axis] + (1 if at[axis] % 2 else -1)) % counts[axis]
            found.append((i * counts[1] + j, at[0] * counts[1] + at[1]))
    return found


def xor_pairs(counts, rows, cols):
    flat = [(i, j) for i in range(counts[0]) for j in range(counts[1])]
    return [(i * counts[1] + j, (i ^ rows) * counts[1] + (j ^ cols)) for i, j in flat]


def spreads(counts):
    known = np.eye(counts[0] * counts[1], dtype=bool)

    def meet(*swaps):
        return np.logical_or.reduce([known, *(known[[b for _, b in pairs]] for pairs in swaps)])

    even = [xor_pairs(counts, 0, 1), xor_pairs(counts, 1, 0)]
    known = meet(even[0], odd_pairs(counts, 1, 0))
    first = meet(xor_pairs(counts, 4, 0))
    known = meet(even[1], odd_pairs(counts, 0, 0))
    second = meet(xor_pairs(counts, 4, 1))
    known = meet(even[0], odd_pairs(counts, 1, 1)) | first
    return (meet(even[1], odd_pairs(counts, 0, 0)) | second).all()


def body(counts, height, noise):
    nr, nc = counts
    devices = nr * nc
    width = max(128, devices * 2)
    basis = jnp.asarray(constants(nr, 2 * nc, width))
    both_axes = ("row", "col")
    depth = table_shape(counts)[0]

    def swap(a, b, axis, bit=0):
        gb = lax.ppermute(b, both_axes, odd_pairs(counts, both_axes.index(axis), bit))
        return lax.ppermute(a, axis, pairs_from(lax.axis_size(axis), 0)), gb

    def small_swap(x, rows, cols):
        return lax.ppermute(x, both_axes, xor_pairs(counts, rows, cols))

    both = jnp.pad(noise, ((0, TR), (0, 0))) + jnp.pad(height, ((TR, 0), (0, 0)))
    b, a, table = call(
        functools.partial(begin_kernel, counts), [(32 + depth, 128)] * 2 + [(depth, 128)], both
    )
    if not spreads(counts):
        for axis, count in enumerate(counts):
            bit = 1
            while bit < count:
                table = table + small_swap(table, *((0, bit) if axis else (bit, 0)))
                bit *= 2
    ga, gb = swap(a, b, "col")
    r3, h3, b, a, table = call(
        functools.partial(widen_kernel, counts),
        [(128, 128)] * 2 + [(24, FC)] * 2 + [(depth, 128)],
        both,
        table,
        gb,
        ga,
    )
    ga, gb = swap(a, b, "row")
    weight, table = call(weights_kernel, [(EXT, 2 * SPEC), (depth, 128)], both, table, basis)
    far = small_swap(table, 4, 0)
    t = call(forward_kernel, [(EXT, 2 * SPEC)], both, r3, basis, flops=5 * 10**8)[0]
    t, table, b, a = call(
        functools.partial(first_kernel, counts),
        [(EXT, 2 * SPEC), (depth, 128)] + [(24 + depth, EXT)] * 2,
        gb,
        ga,
        t,
        weight,
        basis,
        table,
    )
    y, m, table_too = call(
        functools.partial(inverse_kernel, counts),
        [(EXT, FC), (FR, FC), (depth, 128)],
        t,
        basis,
        both,
        h3,
        gb,
        ga,
        table,
    )
    ga, gb = swap(a, b, "col", 1)
    farther = small_swap(table_too, 4, 1)
    y, table, b, a = call(
        functools.partial(columns_kernel, counts),
        [(EXT, FC), (depth, 128)] + [(24, FC)] * 2,
        y,
        gb,
        ga,
        table,
        far,
    )
    ga, gb = swap(a, b, "row")
    inner_w, f, gw, gf, near = call(
        functools.partial(inner_kernel, counts, width),
        [(96, TC)] * 2 + [(EXT, FC)] * 2 + [(16, width)],
        y,
        m,
        basis,
    )
    z, w, t, b, a = call(
        functools.partial(second_kernel, counts, width),
        [(TR, TC)] * 2 + [(EXT, 2 * SPEC)] + [(16, EXT)] * 2,
        y,
        m,
        gb,
        ga,
        table,
        farther,
        inner_w,
        f,
        gw,
        gf,
        near,
        weight,
        basis,
    )
    ga, gb = swap(a, b, "col", 1)
    y, stats = call(inverse_stats_kernel, [(EXT, FC), (1, 128)], t, basis, both, m, z, w)
    y, b, a = call(
        functools.partial(columns_kernel, counts), [(EXT, FC)] + [(16, FC)] * 2, y, gb, ga
    )
    ga, gb = swap(a, b, "row", 1)
    inner_v, stats = call(
        functools.partial(inner_dots_kernel, counts),
        [(96, TC), (1, 128)],
        y,
        m,
        both,
        w,
        stats,
    )
    q, v, stats = call(
        functools.partial(dots_kernel, counts),
        [(TR, TC)] * 2 + [(devices, 128)],
        y,
        m,
        gb,
        ga,
        both,
        w,
        stats,
        inner_v,
    )
    stats = lax.all_to_all(stats, both_axes, 0, 0, tiled=True)
    return tuple(
        call(
            functools.partial(end_kernel, counts, width),
            [(TR, TC)] * 2,
            stats,
            basis,
            m,
            f,
            both,
            z,
            w,
            q,
            v,
        )
    )


def solution(mesh):
    counts = (mesh.shape["row"], mesh.shape["col"])
    spec = P("row", "col")
    return jax.shard_map(
        functools.partial(body, counts),
        mesh=mesh,
        in_specs=(spec, spec),
        out_specs=(spec, spec),
        check_vma=False,
    )
```
